128 devices in a mesh: section: 2 (over core), ctx: 16 (over x, y), fsdp: 4 (over z).
Axes of the slice: x: 4, y: 4, z: 4, core: 2. Of those that a mesh axis runs over, the one named last changes fastest.
Arguments:
- tokens: float32 [2, 4, 2048, 896], P(None, 'fsdp', 'ctx'), may hold values from -6 to 6
- cotangent: float32 [2, 4, 2048, 896], P(None, 'fsdp', 'ctx'), may hold values from -6 to 6
- pair_of: int32 [16], P('ctx'), may hold values from 0 to 15, each once
- attn_gain: bfloat16 [2, 896], P('section', 'fsdp'), may hold values from 0.099609375 to 1.8984375
- ffn_gain: bfloat16 [2, 896], P('section', 'fsdp'), may hold values from 0.099609375 to 1.8984375
- qkv_weight: bfloat16 [2, 896, 1152], P('section', 'fsdp'), may hold values from -0.1875 to 0.1875
- qkv_bias: bfloat16 [2, 1152], P('section', 'fsdp'), may hold values from -2 to 2
- out_weight: bfloat16 [2, 896, 896], P('section', 'fsdp'), may hold values from -1.5 to 1.5
- gate_weight: bfloat16 [2, 896, 4864], P('section', 'fsdp'), may hold values from -0.1875 to 0.1875
- up_weight: bfloat16 [2, 896, 4864], P('section', 'fsdp'), may hold values from -0.1875 to 0.1875
- down_weight: bfloat16 [2, 4864, 896], P('section', 'fsdp'), may hold values from -0.078125 to 0.078125
Outputs:
- layer_out: float32 [2, 2, 4, 2048, 896], P('section', None, 'fsdp', 'ctx')
- input_grad: float32 [2, 2, 4, 2048, 896], P('section', None, 'fsdp', 'ctx')
- attn_gain_grad: float32 [2, 896], P('section', 'fsdp')
- ffn_gain_grad: float32 [2, 896], P('section', 'fsdp')
- qkv_weight_grad: float32 [2, 896, 1152], P('section', 'fsdp')
- qkv_bias_grad: float32 [2, 1152], P('section', 'fsdp')
- out_weight_grad: float32 [2, 896, 896], P('section', 'fsdp')
- gate_weight_grad: float32 [2, 896, 4864], P('section', 'fsdp')
- up_weight_grad: float32 [2, 896, 4864], P('section', 'fsdp')
- down_weight_grad: float32 [2, 4864, 896], P('section', 'fsdp')
The draws below stay inside these ranges and needn't reach their ends.
Inputs may be any that keep to these rules, and one draw needn't show every extreme that they name: pair_of is a permutation of the ctx ranks: rank r holds the causal blocks pair_of[r] and 31 - pair_of[r] of each sequence, 64 tokens each.
All inputs are finite; a program needn't handle non-finite values.
Results may differ from the reference program's by a relative error of at most 0.02.
Values may be sent and summed in bfloat16 or wider, within the bound.
A program may use at most 320 MiB of HBM per device.

```python
import jax
import jax.numpy as jnp
from jax import lax

D = 896
HEADS = 14
KV_HEADS = 2
HEAD_DIM = 64
FF = 4864
MICRO = 2
BLK = 64
SEQ = 2048
SEQS = 4
LAYERS = 2
QKV = 1152
N_CTX = 16


def block_scale(stream_key, extent, split, low, largest):
    loudness = 1.0
    for dim, parts in split:
        steps = jax.random.uniform(jax.random.fold_in(jax.random.fold_in(stream_key, 6), dim), (parts,), jnp.float32, low / len(split), largest / len(split))
        loudness = loudness * jnp.repeat(jnp.exp(steps), extent[dim] // parts).reshape((-1,) + (1,) * (len(extent) - 1 - dim))
    return loudness


def centred(key, dims, width, bound, split=(), held_as=jnp.bfloat16):
    loudness = block_scale(key, dims, split, -0.22, 0.18) if split else 1.0
    entries = jax.random.normal(key, dims, jnp.float32) * width * loudness
    return jnp.minimum(jnp.maximum(entries, -bound), bound).astype(held_as)


def setup_inputs(seed: int = 0) -> dict:
    key_list = jax.random.split(jax.random.key(seed), 12)
    tokens = centred(key_list[0], (MICRO, SEQS, SEQ, D), 1.0, 6.0, ((1, 4), (2, 16)), jnp.float32)
    cotangent = centred(key_list[1], (MICRO, SEQS, SEQ, D), 1.0, 6.0, ((1, 4), (2, 16)), jnp.float32)
    pair_of = jax.random.permutation(key_list[2], N_CTX).astype(jnp.int32)
    attn_gain = jnp.clip(1.0 + 0.18 * jax.random.normal(key_list[3], (LAYERS, D), jnp.float32), 0.099609375, 1.8984375).astype(jnp.bfloat16)
    ffn_gain = jnp.clip(1.0 + 0.18 * jax.random.normal(key_list[4], (LAYERS, D), jnp.float32), 0.099609375, 1.8984375).astype(jnp.bfloat16)
    qkv_weight = centred(key_list[5], (LAYERS, D, QKV), D ** -0.5, 0.1875, ((0, 2), (1, 4)))
    qkv_bias = centred(key_list[6], (LAYERS, QKV), 0.3, 2.0, ((0, 2), (1, 4)))
    out_weight = centred(key_list[7], (LAYERS, HEADS * HEAD_DIM, D), (HEADS * HEAD_DIM // 64) ** -0.5, 1.5, ((0, 2), (1, 4)))
    gate_weight = centred(key_list[8], (LAYERS, D, FF), D ** -0.5, 0.1875, ((0, 2), (1, 4)))
    up_weight = centred(key_list[9], (LAYERS, D, FF), D ** -0.5, 0.1875, ((0, 2), (1, 4)))
    down_weight = centred(key_list[10], (LAYERS, FF, D), FF ** -0.5, 0.078125, ((0, 2), (1, 4)))
    return {"tokens": tokens, "cotangent": cotangent, "pair_of": pair_of, "attn_gain": attn_gain, "ffn_gain": ffn_gain, "qkv_weight": qkv_weight, "qkv_bias": qkv_bias, "out_weight": out_weight, "gate_weight": gate_weight, "up_weight": up_weight, "down_weight": down_weight}


EPS = 1e-06
THETA = 1000000.0

@jax.custom_vjp
def low(v):
    return lax.optimization_barrier(v.astype(jnp.bfloat16)).astype(jnp.float32)

@jax.custom_vjp
def low_back(v):
    return v

def low_keep(v):
    return (low(v), None)

def low_pass(kept, grad):
    return (grad,)

def back_keep(v):
    return (v, None)

def back_low(kept, grad):
    return (low(grad),)
low.defvjp(low_keep, low_pass)
low_back.defvjp(back_keep, back_low)

def matmul_high(left, right):
    return jnp.dot(left, right, precision=lax.Precision.HIGHEST)

def dealt_positions(pair_of):
    offsets = jnp.arange(SEQ, dtype=jnp.int32)
    owner = offsets // (2 * BLK)
    within = offsets % (2 * BLK)
    chosen = pair_of[owner].astype(jnp.int32)
    first = chosen * BLK + within
    second = (2 * N_CTX - 1 - chosen) * BLK + within - BLK
    return jnp.where(within < BLK, first, second).astype(jnp.int32)

def rope_tables(positions):
    freq_index = jnp.arange(HEAD_DIM // 2, dtype=jnp.float32)
    inverse = THETA ** (-2.0 * freq_index / HEAD_DIM)
    angles = positions.astype(jnp.float32)[:, None] * inverse[None, :]
    angles = jnp.concatenate([angles, angles], -1)
    return (jnp.cos(angles), jnp.sin(angles))

def rotate(field, cosine, sine):
    half_width = HEAD_DIM // 2
    turned = jnp.concatenate([-field[..., half_width:], field[..., :half_width]], -1)
    return field * cosine[:, None, :] + turned * sine[:, None, :]

def layer(inputs, attn_gain, ffn_gain, qkv_weight, qkv_bias, out_weight, gate_weight, up_weight, down_weight, cosine, sine, positions):
    factor_one = lax.rsqrt(lax.optimization_barrier(jnp.mean(inputs * inputs, -1, keepdims=True)) + EPS)
    normed = low(inputs * factor_one * attn_gain)
    linear = low_back(matmul_high(normed, qkv_weight) + qkv_bias)
    width_query = HEADS * HEAD_DIM
    width_key = KV_HEADS * HEAD_DIM
    group_size = HEADS // KV_HEADS
    queries = low(rotate(linear[:, :width_query].reshape(SEQ, HEADS, HEAD_DIM), cosine, sine))
    keys_rot = low(rotate(linear[:, width_query:width_query + width_key].reshape(SEQ, KV_HEADS, HEAD_DIM), cosine, sine))
    values = low(linear[:, width_query + width_key:].reshape(SEQ, KV_HEADS, HEAD_DIM))
    grouped = queries.reshape(SEQ, KV_HEADS, group_size, HEAD_DIM)
    block_rows = min(512, SEQ)
    scale_factor = HEAD_DIM ** (-0.5)

    def attend(start):
        block_query = lax.dynamic_slice_in_dim(grouped, start, block_rows, 0)
        block_pos = lax.dynamic_slice_in_dim(positions, start, block_rows, 0)
        scores = low_back(jnp.einsum('qgjd,kgd->gjqk', block_query, keys_rot, precision=lax.Precision.HIGHEST) * scale_factor)
        allowed = positions[None, :] <= block_pos[:, None]
        scores = jnp.where(allowed, scores, -1e+30)
        top_score = lax.optimization_barrier(jnp.max(scores, -1, keepdims=True))
        weights = jnp.exp(scores - top_score)
        probs = weights / lax.optimization_barrier(jnp.sum(weights, -1, keepdims=True))
        mixed = jnp.einsum('gjqk,kgd->qgjd', low(probs), values, precision=lax.Precision.HIGHEST)
        return mixed.reshape(block_rows, HEADS * HEAD_DIM)
    starts = jnp.arange(0, SEQ, block_rows, dtype=jnp.int32)
    attended = lax.map(jax.checkpoint(attend), starts).reshape(SEQ, HEADS * HEAD_DIM)
    attended = low_back(low(attended))
    middle = inputs + low_back(matmul_high(attended, out_weight))
    factor_two = lax.rsqrt(lax.optimization_barrier(jnp.mean(middle * middle, -1, keepdims=True)) + EPS)
    normed_two = low(middle * factor_two * ffn_gain)
    gate = low_back(matmul_high(normed_two, gate_weight))
    up_part = low_back(matmul_high(normed_two, up_weight))
    hidden = low(jax.nn.silu(gate) * up_part)
    return middle + low_back(matmul_high(hidden, down_weight))

def reference(tokens, cotangent, pair_of, attn_gain, ffn_gain, qkv_weight, qkv_bias, out_weight, gate_weight, up_weight, down_weight):
    positions = dealt_positions(pair_of)
    cosine, sine = rope_tables(positions)
    stacked = (attn_gain, ffn_gain, qkv_weight, qkv_bias, out_weight, gate_weight, up_weight, down_weight)
    params = [tuple((item[level].astype(jnp.float32) for item in stacked)) for level in range(LAYERS)]

    def apply_layer(source, *weights):
        return layer(source, *weights, cosine, sine, positions)

    def one_sequence(carry, pieces):
        source, upstream = pieces
        outputs = []
        backs = []
        current = source
        for level in range(LAYERS):
            result, back_fn = jax.vjp(apply_layer, current, *params[level])
            outputs.append(result)
            backs.append(back_fn)
            current = low(result)
        input_grads = [None] * LAYERS
        new_carry = [None] * LAYERS
        flowing = upstream
        for level in range(LAYERS - 1, -1, -1):
            grads = backs[level](flowing)
            input_grads[level] = grads[0]
            new_carry[level] = tuple((total + part for total, part in zip(carry[level], grads[1:])))
            flowing = low(grads[0])
        return (tuple(new_carry), (jnp.stack(outputs), jnp.stack(input_grads)))
    start_carry = tuple((tuple((jnp.zeros_like(item) for item in params[level])) for level in range(LAYERS)))
    sources = tokens.astype(jnp.float32).reshape(MICRO * SEQS, SEQ, D)
    upstreams = cotangent.astype(jnp.float32).reshape(MICRO * SEQS, SEQ, D)
    totals, (outputs, input_grads) = lax.scan(one_sequence, start_carry, (sources, upstreams))
    layer_out = jnp.transpose(outputs.reshape(MICRO, SEQS, LAYERS, SEQ, D), (2, 0, 1, 3, 4))
    input_grad = jnp.transpose(input_grads.reshape(MICRO, SEQS, LAYERS, SEQ, D), (2, 0, 1, 3, 4))
    grads = [jnp.stack([totals[level][member] for level in range(LAYERS)]) for member in range(8)]
    return (layer_out, input_grad, grads[0], grads[1], grads[2], grads[3], grads[4], grads[5], grads[6], grads[7])
```

```python
import functools

import jax
import jax.numpy as jnp
from jax import lax
from jax.experimental import pallas as pl
from jax.experimental.pallas import tpu as pltpu
from jax.sharding import PartitionSpec as P

D = 896
HEADS = 14
KV_HEADS = 2
HEAD_DIM = 64
GROUP = HEADS // KV_HEADS
FF = 4864
QKV = 1152
EPS = 1e-06
THETA = 1000000.0
LANES = 128
TILES = D // LANES
WIN = 1280
NEG = -1e30
F32 = jnp.float32
BF16 = jnp.bfloat16
MESH = pl.DeviceIdType.MESH
VMEM_LIMIT = 56 * 2**20


def mm(a, b):
    return jnp.dot(a, b, preferred_element_type=F32)


def mm_nt(a, b):
    return lax.dot_general(a, b, (((1,), (1,)), ((), ())), preferred_element_type=F32)


def greet(axis, n):
    me = lax.axis_index(axis)
    bar = pltpu.get_barrier_semaphore()

    def one(k, c):
        pl.semaphore_signal(
            bar, inc=1, device_id={axis: lax.rem(me + k, n)}, device_id_type=MESH
        )
        return c

    lax.fori_loop(1, n, one, 0)
    return bar


def push(src, dst, ssem, rsem, axis, to):
    return pltpu.make_async_remote_copy(
        src_ref=src,
        dst_ref=dst,
        send_sem=ssem,
        recv_sem=rsem,
        device_id={axis: to},
        device_id_type=MESH,
    )


def rope(u, cos, sa, sb):
    return u * cos + pltpu.roll(u, 96, 1) * sa + pltpu.roll(u, 32, 1) * sb


def unrope(u, cos, sa, sb):
    return u * cos - pltpu.roll(u, 96, 1) * sa - pltpu.roll(u, 32, 1) * sb


def spread(ref, t, tile_t):
    half = HEAD_DIM
    zero = jnp.zeros((half, LANES), BF16)
    for j in range(2):
        h = 2 * t + j
        slab = tile_t[j * half : (j + 1) * half, :].astype(BF16)
        both = [slab, zero] if h // GROUP == 0 else [zero, slab]
        ref[:, h * LANES : (h + 1) * LANES] = jnp.concatenate(both, 0)


def gathered_tile(wide, t):
    half = HEAD_DIM
    rows = []
    for j in range(2):
        g = (2 * t + j) // GROUP
        rows.append(wide[g * half : (g + 1) * half, j * LANES : (j + 1) * LANES])
    return jnp.concatenate(rows, 0).T


def attn_fwd_kernel(
    n, x_ref, g1_ref, g2_ref, wqkv_ref, bias_ref, cos_ref, sa_ref, sb_ref, kpos_ref, qpos_ref, wout_ref,
    mid_ref, n2_ref, n1_ref, qst_ref, kv_ref, lse_ref, att_ref,
    m_s, l_s, acc_s, ssem, rsem,
):
    me = lax.axis_index("ctx")
    bar = greet("ctx", n)
    x = x_ref[...]
    r1 = lax.rsqrt(jnp.mean(x * x, -1, keepdims=True) + EPS)
    n1 = (x * r1 * g1_ref[...]).astype(BF16)
    n1_ref[...] = n1
    cos, sa, sb = cos_ref[...], sa_ref[...], sb_ref[...]
    lin = mm(n1, wqkv_ref[:, D:]) + bias_ref[:, D:]
    kv_ref[me] = jnp.concatenate(
        [rope(lin[:, :LANES], cos, sa, sb), lin[:, LANES:]], 1
    ).astype(BF16)
    pl.semaphore_wait(bar, n - 1)

    def start(k, c):
        push(kv_ref.at[me], kv_ref.at[me], ssem.at[k], rsem.at[k], "ctx", lax.rem(me + k, n)).start()
        return c

    lax.fori_loop(1, n, start, 0)
    linq = mm(n1, wqkv_ref[:, :D]) + bias_ref[:, :D]
    for t in range(TILES):
        q = rope(linq[:, t * LANES : (t + 1) * LANES], cos, sa, sb) * HEAD_DIM ** (-0.5)
        spread(qst_ref, t, q.T)
    m_s[...] = jnp.full_like(m_s, NEG)
    l_s[...] = jnp.zeros_like(l_s)
    acc_s[...] = jnp.zeros_like(acc_s)
    qpos = qpos_ref[...]

    def block(src):
        keys = kv_ref[src, :, :LANES]
        vals_t = kv_ref[src, :, LANES:].astype(F32).T.astype(BF16)
        hide = jnp.where(kpos_ref[src] <= qpos, 0.0, NEG)
        hide = jnp.concatenate([hide, hide], 1)
        for t in range(TILES):
            cols = slice(2 * t * LANES, 2 * (t + 1) * LANES)
            s = mm(keys, qst_ref[:, cols]) + hide
            m_old = m_s[:, cols]
            m_new = jnp.maximum(m_old, jnp.max(s, 0, keepdims=True))
            p = jnp.exp(s - m_new)
            alpha = jnp.exp(m_old - m_new)
            m_s[:, cols] = m_new
            l_s[:, cols] = l_s[:, cols] * alpha + jnp.sum(p, 0, keepdims=True)
            acc_s[:, cols] = acc_s[:, cols] * alpha + mm(vals_t, p.astype(BF16))

    block(me)

    def step(k, c):
        src = lax.rem(me + n - k, n)
        push(kv_ref.at[src], kv_ref.at[src], ssem.at[k], rsem.at[k], "ctx", lax.rem(me + k, n)).wait_recv()
        block(src)
        return c

    lax.fori_loop(1, n, step, 0)
    lse_ref[...] = m_s[...] + jnp.log(l_s[...])
    for t in range(TILES):
        cols = slice(2 * t * LANES, 2 * (t + 1) * LANES)
        wide = acc_s[:, cols] / l_s[:, cols]
        att_ref[:, t * LANES : (t + 1) * LANES] = gathered_tile(wide, t).astype(BF16)
    mid = x + mm(att_ref[...], wout_ref[...])
    mid_ref[...] = mid
    r2 = lax.rsqrt(jnp.mean(mid * mid, -1, keepdims=True) + EPS)
    n2_ref[...] = (mid * r2 * g2_ref[...]).astype(BF16)

    def done(k, c):
        push(kv_ref.at[me], kv_ref.at[me], ssem.at[k], rsem.at[k], "ctx", lax.rem(me + k, n)).wait_send()
        return c

    lax.fori_loop(1, n, done, 0)


def attn_bwd_kernel(
    n, gm_ref, x_ref, g1_ref, wqkv_ref, wout_ref, qst_ref, kv_ref, lse_ref, att_ref,
    cos_ref, sa_ref, sb_ref, kpos_ref, qpos_ref,
    gx_ref, glin_ref, gmb_ref, dg1_ref,
    gst_s, delta_s, gq_s, send_s, land_s, ssem, rsem,
):
    me = lax.axis_index("ctx")
    bar = greet("ctx", n)
    half = HEAD_DIM
    gm = gm_ref[...]
    gmb = gm.astype(BF16)
    gmb_ref[...] = gmb
    ga = mm_nt(gmb, wout_ref[...])
    for t in range(TILES):
        tile = slice(t * LANES, (t + 1) * LANES)
        ga_t = ga[:, tile].T
        spread(gst_s, t, ga_t)
        prod = ga_t * att_ref[:, tile].astype(F32).T
        delta_s[:, 2 * t * LANES : (2 * t + 1) * LANES] = jnp.sum(prod[:half], 0, keepdims=True)
        delta_s[:, (2 * t + 1) * LANES : (2 * t + 2) * LANES] = jnp.sum(prod[half:], 0, keepdims=True)
    gq_s[...] = jnp.zeros_like(gq_s)
    qpos = qpos_ref[...]
    pl.semaphore_wait(bar, n - 1)

    def block(src):
        keys = kv_ref[src, :, :LANES]
        vals = kv_ref[src, :, LANES:]
        keys_t = keys.astype(F32).T.astype(BF16)
        hide = jnp.where(kpos_ref[src] <= qpos, 0.0, NEG)
        hide = jnp.concatenate([hide, hide], 1)
        gk = jnp.zeros((LANES, LANES), F32)
        gv = jnp.zeros((LANES, LANES), F32)
        for t in range(TILES):
            cols = slice(2 * t * LANES, 2 * (t + 1) * LANES)
            qs, gs = qst_ref[:, cols], gst_s[:, cols]
            p = jnp.exp(mm(keys, qs) + hide - lse_ref[:, cols])
            ds = (p * (mm(vals, gs) - delta_s[:, cols])).astype(BF16)
            gv = gv + mm_nt(p.astype(BF16), gs)
            gk = gk + mm_nt(ds, qs)
            gq_s[:, cols] += mm(keys_t, ds)
        return jnp.concatenate([gk, gv], 1)

    def step(k, c):
        to = lax.rem(me + k, n)
        send_s[k] = block(to).astype(BF16)
        push(send_s.at[k], land_s.at[k], ssem.at[k], rsem.at[k], "ctx", to).start()
        return c

    lax.fori_loop(1, n, step, 0)
    own = block(me)

    def take(k, total):
        push(send_s.at[k], land_s.at[k], ssem.at[k], rsem.at[k], "ctx", lax.rem(me + k, n)).wait_recv()
        return total + land_s[k].astype(F32)

    own = lax.fori_loop(1, n, take, own)
    cos, sa, sb = cos_ref[...], sa_ref[...], sb_ref[...]
    for t in range(TILES):
        wide = gq_s[:, 2 * t * LANES : 2 * (t + 1) * LANES]
        gq = gathered_tile(wide, t) * HEAD_DIM ** (-0.5)
        glin_ref[:, t * LANES : (t + 1) * LANES] = unrope(gq, cos, sa, sb).astype(BF16)
    glin_ref[:, D : D + LANES] = unrope(own[:, :LANES], cos, sa, sb).astype(BF16)
    glin_ref[:, D + LANES :] = own[:, LANES:].astype(BF16)
    gn1 = mm_nt(glin_ref[...], wqkv_ref[...])
    x = x_ref[...]
    r1 = lax.rsqrt(jnp.mean(x * x, -1, keepdims=True) + EPS)
    unit = x * r1
    dg1_ref[...] = jnp.sum(gn1 * unit, 0, keepdims=True)
    dz = gn1 * g1_ref[...]
    gx_ref[...] = gm + r1 * (dz - unit * jnp.mean(dz * unit, -1, keepdims=True))

    def done(k, c):
        push(send_s.at[k], land_s.at[k], ssem.at[k], rsem.at[k], "ctx", lax.rem(me + k, n)).wait_send()
        return c

    lax.fori_loop(1, n, done, 0)


def ffn_fwd_kernel(
    n, n2_ref, mid_ref, wg_ref, wu_ref, wd_ref,
    y_ref, all_ref, gate_ref, up_ref,
    send_s, land_s, ssem, rsem, ssem2, rsem2,
):
    me = lax.axis_index("fsdp")
    bar = greet("fsdp", n)
    all_ref[me] = n2_ref[...]
    order = [k for k in (1, 3, 2) if k < n]
    pl.semaphore_wait(bar, n - 1)

    def first(k):
        return push(all_ref.at[me], all_ref.at[me], ssem.at[k], rsem.at[k], "fsdp", lax.rem(me + k, n))

    def second(k):
        return push(send_s.at[k], land_s.at[k], ssem2.at[k], rsem2.at[k], "fsdp", lax.rem(me + n - k, n))

    for k in order:
        first(k).start()

    def block(src):
        a = all_ref[src]
        gate = mm(a, wg_ref[...])
        up = mm(a, wu_ref[...])
        gate_ref[src] = gate
        up_ref[src] = up
        hidden = (gate * jax.nn.sigmoid(gate) * up).astype(BF16)
        return mm(hidden, wd_ref[...])

    y_ref[...] = mid_ref[...] + block(me)
    for k in order:
        first(k).wait_recv()
        send_s[k] = block(lax.rem(me + n - k, n)).astype(BF16)
        second(k).start()
    for k in order:
        second(k).wait_recv()
        y_ref[...] += land_s[k].astype(F32)
    for k in order:
        first(k).wait_send()
        second(k).wait_send()


def ffn_bwd_kernel(
    n, gy_ref, mid_ref, g2_ref, wg_ref, wu_ref, wd_ref, gate_ref, up_ref,
    gm_ref, all_ref, hid_ref, ggate_ref, gup_ref, dg2_ref,
    own_s, send_s, land_s, ssem, rsem, ssem2, rsem2,
):
    me = lax.axis_index("fsdp")
    bar = greet("fsdp", n)
    all_ref[me] = gy_ref[...].astype(BF16)
    order = [k for k in (1, 3, 2) if k < n]
    pl.semaphore_wait(bar, n - 1)

    def first(k):
        return push(all_ref.at[me], all_ref.at[me], ssem.at[k], rsem.at[k], "fsdp", lax.rem(me + k, n))

    def second(k):
        return push(send_s.at[k], land_s.at[k], ssem2.at[k], rsem2.at[k], "fsdp", lax.rem(me + n - k, n))

    for k in order:
        first(k).start()

    def block(src):
        gh = mm_nt(all_ref[src], wd_ref[...])
        gate, up = gate_ref[src], up_ref[src]
        sg = jax.nn.sigmoid(gate)
        act = gate * sg
        hid_ref[src] = (act * up).astype(BF16)
        ggate = (gh * up * sg * (1.0 + gate * (1.0 - sg))).astype(BF16)
        gup = (gh * act).astype(BF16)
        ggate_ref[src] = ggate
        gup_ref[src] = gup
        return mm_nt(ggate, wg_ref[...]) + mm_nt(gup, wu_ref[...])

    own_s[...] = block(me)
    for k in order:
        first(k).wait_recv()
        send_s[k] = block(lax.rem(me + n - k, n)).astype(BF16)
        second(k).start()
    for k in order:
        second(k).wait_recv()
        own_s[...] += land_s[k].astype(F32)
    gn2 = own_s[...]
    mid = mid_ref[...]
    r2 = lax.rsqrt(jnp.mean(mid * mid, -1, keepdims=True) + EPS)
    unit = mid * r2
    dg2_ref[...] = jnp.sum(gn2 * unit, 0, keepdims=True)
    dz = gn2 * g2_ref[...]
    gm_ref[...] = gy_ref[...] + r2 * (dz - unit * jnp.mean(dz * unit, -1, keepdims=True))
    for k in order:
        first(k).wait_send()
        second(k).wait_send()


def call(kernel, n, ins, outs, scratch, cid, name, flops):
    vm = pl.BlockSpec(memory_space=pltpu.VMEM)
    moved = sum(a.size * a.dtype.itemsize for a in ins)
    return pl.pallas_call(
        functools.partial(kernel, n),
        out_shape=[jax.ShapeDtypeStruct(s, t) for s, t in outs],
        in_specs=[vm] * len(ins),
        out_specs=[vm] * len(outs),
        scratch_shapes=scratch,
        compiler_params=pltpu.CompilerParams(
            collective_id=cid, has_side_effects=True, vmem_limit_bytes=VMEM_LIMIT
        ),
        cost_estimate=pl.CostEstimate(flops=flops, bytes_accessed=moved, transcendentals=0),
        name=name,
    )(*ins)


def attn_fwd(x, g1, g2, wqkv, bias, tabs, wout):
    n = lax.axis_size("ctx")
    tok = x.shape[0]
    wide = HEADS * LANES
    cos, sa, sb, kpos, qpos = tabs
    dma = pltpu.SemaphoreType.DMA
    return call(
        attn_fwd_kernel, n,
        (x, g1, g2, wqkv, bias, cos, sa, sb, kpos, qpos, wout),
        [((tok, D), F32), ((tok, D), BF16), ((tok, D), BF16), ((LANES, wide), BF16),
         ((n, tok, 2 * LANES), BF16), ((1, wide), F32), ((tok, D), BF16)],
        [pltpu.VMEM((1, wide), F32), pltpu.VMEM((1, wide), F32), pltpu.VMEM((LANES, wide), F32), dma((n,)), dma((n,))],
        1, "attn_fwd", 10 * 10**9,
    )


def attn_bwd(gm, x, g1, wqkv, wout, saved, tabs):
    n = lax.axis_size("ctx")
    tok = x.shape[0]
    wide = HEADS * LANES
    cos, sa, sb, kpos, qpos = tabs
    qst, kv, lse, att = saved
    dma = pltpu.SemaphoreType.DMA
    return call(
        attn_bwd_kernel, n,
        (gm, x, g1, wqkv, wout, qst, kv, lse, att, cos, sa, sb, kpos, qpos),
        [((tok, D), F32), ((tok, QKV), BF16), ((tok, D), BF16), ((1, D), F32)],
        [pltpu.VMEM((LANES, wide), BF16), pltpu.VMEM((1, wide), F32), pltpu.VMEM((LANES, wide), F32),
         pltpu.VMEM((n, tok, 2 * LANES), BF16), pltpu.VMEM((n, tok, 2 * LANES), BF16), dma((n,)), dma((n,))],
        2, "attn_bwd", 20 * 10**9,
    )


def ffn_fwd(n2, mid, wg, wu, wd):
    n = lax.axis_size("fsdp")
    tok = n2.shape[0]
    dma = pltpu.SemaphoreType.DMA
    return call(
        ffn_fwd_kernel, n, (n2, mid, wg, wu, wd),
        [((tok, D), F32), ((n, tok, D), BF16), ((n, tok, WIN), F32), ((n, tok, WIN), F32)],
        [pltpu.VMEM((n, tok, D), BF16), pltpu.VMEM((n, tok, D), BF16), dma((n,)), dma((n,)), dma((n,)), dma((n,))],
        3, "ffn_fwd", 10 * 10**9,
    )


def ffn_bwd(gy, mid, g2, wg, wu, wd, gate, up):
    n = lax.axis_size("fsdp")
    tok = gy.shape[0]
    dma = pltpu.SemaphoreType.DMA
    return call(
        ffn_bwd_kernel, n, (gy, mid, g2, wg, wu, wd, gate, up),
        [((tok, D), F32), ((n, tok, D), BF16), ((n, tok, WIN), BF16), ((n, tok, WIN), BF16),
         ((n, tok, WIN), BF16), ((1, D), F32)],
        [pltpu.VMEM((tok, D), F32), pltpu.VMEM((n, tok, D), BF16), pltpu.VMEM((n, tok, D), BF16),
         dma((n,)), dma((n,)), dma((n,)), dma((n,))],
        4, "ffn_bwd", 20 * 10**9,
    )


def dealt_positions(chosen_pair, block_len, ctx_count):
    within = jnp.arange(2 * block_len, dtype=jnp.int32)
    first = chosen_pair * block_len + within
    second = (2 * ctx_count - 1 - chosen_pair) * block_len + within - block_len
    return jnp.where(within < block_len, first, second)


def tables(pair_of):
    n = lax.axis_size("ctx")
    block_len = 64
    all_pairs = lax.all_gather(pair_of, "ctx", axis=0, tiled=True)
    own = dealt_positions(pair_of[0], block_len, n)
    kpos = jax.vmap(lambda p: dealt_positions(p, block_len, n))(all_pairs)
    freq = jnp.arange(HEAD_DIM // 2, dtype=F32)
    inverse = THETA ** (-2.0 * freq / HEAD_DIM)
    angles = own.astype(F32)[:, None] * inverse[None, :]
    cos, sin = jnp.cos(angles), jnp.sin(angles)
    zero = jnp.zeros_like(sin)
    return (
        jnp.concatenate([cos] * 4, -1),
        jnp.concatenate([-sin, zero] * 2, -1),
        jnp.concatenate([zero, sin] * 2, -1),
        kpos[:, :, None],
        own[None, :],
    )


def window_starts():
    n = lax.axis_size("fsdp")
    share = FF // n
    return [(i * share // LANES) * LANES for i in range(n)]


def local(
    tokens, cotangent, pair_of, attn_gain, ffn_gain, qkv_weight, qkv_bias, out_weight, gate_weight, up_weight, down_weight,
):
    s = lax.axis_index("section")
    z = lax.axis_index("fsdp")
    nz = lax.axis_size("fsdp")
    share = FF // nz
    starts = window_starts()
    tabs = tables(pair_of)
    both = ("section", "fsdp")

    small = jnp.concatenate([attn_gain[0], ffn_gain[0], qkv_bias[0]])
    small = lax.all_gather(small, both, axis=0, tiled=False).reshape(2, nz, -1)
    qd = D // nz
    gain1 = small[:, :, :qd].reshape(2, 1, D).astype(F32)
    gain2 = small[:, :, qd : 2 * qd].reshape(2, 1, D).astype(F32)
    bias = small[:, :, 2 * qd :].reshape(2, 1, QKV).astype(F32)
    wqkv = lax.all_gather(qkv_weight[0], both, axis=0).reshape(2, D, QKV)
    wout = lax.all_gather(out_weight[0], both, axis=0).reshape(2, D, D)

    def windows(w):
        return jnp.stack([w[:, a : a + WIN] for a in starts])

    gu = jnp.stack([windows(gate_weight[0]), windows(up_weight[0])], 1)
    gu = lax.all_to_all(gu, "fsdp", 0, 0)
    gu = gu.transpose(1, 0, 2, 3).reshape(2, D, WIN)
    gu = lax.all_gather(gu, "section", axis=0)
    pad = (WIN - share) * lax.rem(z, 2)
    down = jnp.pad(down_weight[0], ((WIN - share, WIN - share), (0, 0)))
    down = lax.dynamic_slice_in_dim(down, WIN - share - pad, WIN, 0)
    wd = lax.all_gather(down, "section", axis=0)

    x = jnp.where(s == 0, tokens[0, 0], tokens[1, 0])
    saved = []
    outs = []
    for l in range(2):
        mid, n2, n1, qst, kv, lse, att = attn_fwd(x, gain1[l], gain2[l], wqkv[l], bias[l], tabs, wout[l])
        y, n2_all, gate, up = ffn_fwd(n2, mid, gu[l, 0], gu[l, 1], wd[l])
        saved.append((x, mid, n1, (qst, kv, lse, att), n2_all, gate, up))
        outs.append(y)
        x = y.astype(BF16).astype(F32)

    gy = jnp.where(s == 0, cotangent[0, 0], cotangent[1, 0])
    grads = [None, None]
    gxs = [None, None]
    for l in (1, 0):
        x, mid, n1, attn_saved, n2_all, gate, up = saved[l]
        gm, gy_all, hid, ggate, gup, dg2 = ffn_bwd(gy, mid, gain2[l], gu[l, 0], gu[l, 1], wd[l], gate, up)
        gx, glin, gmb, dg1 = attn_bwd(gm, x, gain1[l], wqkv[l], wout[l], attn_saved, tabs)
        gxs[l] = gx
        gy = gx.astype(BF16).astype(F32)
        ddown = jnp.einsum("stf,std->fd", hid, gy_all, preferred_element_type=F32)
        dgate = jnp.einsum("std,stf->df", n2_all, ggate, preferred_element_type=F32)
        dup = jnp.einsum("std,stf->df", n2_all, gup, preferred_element_type=F32)
        dqkv = jnp.einsum("td,te->de", n1, glin, preferred_element_type=F32)
        dout = jnp.einsum("td,te->de", attn_saved[3], gmb, preferred_element_type=F32)
        dbias = jnp.sum(glin.astype(F32), 0)
        ddown = lax.dynamic_slice_in_dim(ddown, pad, share, 0)
        grads[l] = (ddown, dgate, dup, dqkv, dout, dg1[0], dg2[0], dbias)

    def over_sections(index):
        pair = jnp.stack([grads[0][index], grads[1][index]]).astype(BF16)
        return lax.psum_scatter(pair, "section", scatter_dimension=0, tiled=False)

    ddown, dgate, dup, dqkv, dout = (over_sections(i) for i in range(5))
    ddown = lax.psum(ddown, "ctx").astype(F32)
    dqkv = lax.psum_scatter(dqkv, "fsdp", scatter_dimension=0, tiled=True)
    dout = lax.psum_scatter(dout, "fsdp", scatter_dimension=0, tiled=True)
    dqkv, dout = lax.psum((dqkv, dout), "ctx")
    gu_grad = jnp.concatenate([dgate.reshape(nz, qd, WIN), dup.reshape(nz, qd, WIN)], 2)
    gu_grad = lax.psum_scatter(gu_grad, "ctx", scatter_dimension=2, tiled=True)
    gu_grad = lax.all_to_all(gu_grad, "fsdp", 0, 0)
    gu_grad = lax.all_gather(gu_grad, "ctx", axis=2, tiled=True).astype(F32)

    def assembled(w):
        total = jnp.zeros((qd, FF), F32)
        for i, a in enumerate(starts):
            total = total.at[:, a : a + WIN].add(w[i])
        return total

    small_grad = jnp.stack(
        [jnp.concatenate([g[5].reshape(nz, -1), g[6].reshape(nz, -1), g[7].reshape(nz, -1)], 1) for g in grads]
    )
    small_grad = lax.psum(small_grad, ("section", "ctx", "fsdp"))
    small_grad = lax.dynamic_slice(small_grad, (s, z, 0), (1, 1, small_grad.shape[2]))[0, 0]

    def by_layer(pair):
        theirs = jnp.where(s == 0, pair[1], pair[0])
        mine = jnp.where(s == 0, pair[0], pair[1])
        got = lax.ppermute(theirs, "section", [(0, 1), (1, 0)])
        return jnp.where(s == 0, jnp.stack([mine, got]), jnp.stack([got, mine]))[None, :, None]

    return (
        by_layer(outs),
        by_layer(gxs),
        small_grad[None, :qd],
        small_grad[None, qd : 2 * qd],
        dqkv.astype(F32)[None],
        small_grad[None, 2 * qd :],
        dout.astype(F32)[None],
        assembled(gu_grad[:, :, :WIN])[None],
        assembled(gu_grad[:, :, WIN:])[None],
        ddown[None],
    )


def solution(mesh):
    return jax.shard_map(
        local,
        mesh=mesh,
        in_specs=(
            P(None, "fsdp", "ctx", None),
            P(None, "fsdp", "ctx", None),
            P("ctx"),
            P("section", "fsdp"),
            P("section", "fsdp"),
            P("section", "fsdp", None),
            P("section", "fsdp"),
            P("section", "fsdp", None),
            P("section", "fsdp", None),
            P("section", "fsdp", None),
            P("section", "fsdp", None),
        ),
        out_specs=(
            P("section", None, "fsdp", "ctx", None),
            P("section", None, "fsdp", "ctx", None),
            P("section", "fsdp"),
            P("section", "fsdp"),
            P("section", "fsdp", None),
            P("section", "fsdp"),
            P("section", "fsdp", None),
            P("section", "fsdp", None),
            P("section", "fsdp", None),
            P("section", "fsdp", None),
        ),
        check_vma=False,
    )
```

```python
import functools

import jax
import jax.numpy as jnp
from jax import lax
from jax.experimental import pallas as pl
from jax.experimental.pallas import tpu as pltpu
from jax.sharding import PartitionSpec as P

D = 896
HEADS = 14
KV_HEADS = 2
HEAD_DIM = 64
GROUP = HEADS // KV_HEADS
FF = 4864
QKV = 1152
EPS = 1e-06
THETA = 1000000.0
LANES = 128
TILES = D // LANES
WIN = 1280
NEG = -1e30
F32 = jnp.float32
BF16 = jnp.bfloat16
MESH = pl.DeviceIdType.MESH
VMEM_LIMIT = 56 * 2**20
UNIT = 16
SIDE = 4
GATE_PER = (5, 4)
DOWN_PER = (8, 9)
Q_PER = (4, 4)
Q_ROWS = 16 * sum(Q_PER) * UNIT


def mm(a, b):
    return jnp.dot(a, b, preferred_element_type=F32)


def mm_nt(a, b):
    return lax.dot_general(a, b, (((1,), (1,)), ((), ())), preferred_element_type=F32)


def mm_tn(a, b):
    return lax.dot_general(a, b, (((0,), (0,)), ((), ())), preferred_element_type=F32)


def greet(axis, n):
    me = lax.axis_index(axis)
    bar = pltpu.get_barrier_semaphore()

    def one(k, c):
        pl.semaphore_signal(
            bar, inc=1, device_id={axis: lax.rem(me + k, n)}, device_id_type=MESH
        )
        return c

    lax.fori_loop(1, n, one, 0)
    return bar


def push(src, dst, ssem, rsem, axis, to):
    return pltpu.make_async_remote_copy(
        src_ref=src,
        dst_ref=dst,
        send_sem=ssem,
        recv_sem=rsem,
        device_id={axis: to},
        device_id_type=MESH,
    )


def rope(u, cos, sa, sb):
    return u * cos + pltpu.roll(u, 96, 1) * sa + pltpu.roll(u, 32, 1) * sb


def unrope(u, cos, sa, sb):
    return u * cos - pltpu.roll(u, 96, 1) * sa - pltpu.roll(u, 32, 1) * sb


def spread(ref, t, tile_t):
    half = HEAD_DIM
    zero = jnp.zeros((half, LANES), BF16)
    for j in range(2):
        h = 2 * t + j
        slab = tile_t[j * half : (j + 1) * half, :].astype(BF16)
        both = [slab, zero] if h // GROUP == 0 else [zero, slab]
        ref[:, h * LANES : (h + 1) * LANES] = jnp.concatenate(both, 0)


def gathered_tile(wide, t):
    half = HEAD_DIM
    rows = []
    for j in range(2):
        g = (2 * t + j) // GROUP
        rows.append(wide[g * half : (g + 1) * half, j * LANES : (j + 1) * LANES])
    return jnp.concatenate(rows, 0).T


def attn_fwd_kernel(
    n, x_ref, g1_ref, g2_ref, wqkv_ref, bias_ref, cos_ref, sa_ref, sb_ref, kpos_ref, qpos_ref, wout_ref,
    mid_ref, n2_ref, n1_ref, qst_ref, kv_ref, lse_ref, att_ref,
    m_s, l_s, acc_s, ssem, rsem,
):
    me = lax.axis_index("ctx")
    bar = greet("ctx", n)
    x = x_ref[...]
    r1 = lax.rsqrt(jnp.mean(x * x, -1, keepdims=True) + EPS)
    n1 = (x * r1 * g1_ref[...]).astype(BF16)
    n1_ref[...] = n1
    cos, sa, sb = cos_ref[...], sa_ref[...], sb_ref[...]
    lin = mm(n1, wqkv_ref[:, D:]) + bias_ref[:, D:]
    kv_ref[me] = jnp.concatenate(
        [rope(lin[:, :LANES], cos, sa, sb), lin[:, LANES:]], 1
    ).astype(BF16)
    pl.semaphore_wait(bar, n - 1)

    def start(k, c):
        push(kv_ref.at[me], kv_ref.at[me], ssem.at[k], rsem.at[k], "ctx", lax.rem(me + k, n)).start()
        return c

    lax.fori_loop(1, n, start, 0)
    linq = mm(n1, wqkv_ref[:, :D]) + bias_ref[:, :D]
    for t in range(TILES):
        q = rope(linq[:, t * LANES : (t + 1) * LANES], cos, sa, sb) * HEAD_DIM ** (-0.5)
        spread(qst_ref, t, q.T)
    m_s[...] = jnp.full_like(m_s, NEG)
    l_s[...] = jnp.zeros_like(l_s)
    acc_s[...] = jnp.zeros_like(acc_s)
    qpos = qpos_ref[...]

    def block(src):
        keys = kv_ref[src, :, :LANES]
        vals_t = kv_ref[src, :, LANES:].astype(F32).T.astype(BF16)
        hide = jnp.where(kpos_ref[src] <= qpos, 0.0, NEG)
        hide = jnp.concatenate([hide, hide], 1)
        for t in range(TILES):
            cols = slice(2 * t * LANES, 2 * (t + 1) * LANES)
            s = mm(keys, qst_ref[:, cols]) + hide
            m_old = m_s[:, cols]
            m_new = jnp.maximum(m_old, jnp.max(s, 0, keepdims=True))
            p = jnp.exp(s - m_new)
            alpha = jnp.exp(m_old - m_new)
            m_s[:, cols] = m_new
            l_s[:, cols] = l_s[:, cols] * alpha + jnp.sum(p, 0, keepdims=True)
            acc_s[:, cols] = acc_s[:, cols] * alpha + mm(vals_t, p.astype(BF16))

    block(me)

    def step(k, c):
        src = lax.rem(me + n - k, n)
        push(kv_ref.at[src], kv_ref.at[src], ssem.at[k], rsem.at[k], "ctx", lax.rem(me + k, n)).wait_recv()
        block(src)
        return c

    lax.fori_loop(1, n, step, 0)
    lse_ref[...] = m_s[...] + jnp.log(l_s[...])
    for t in range(TILES):
        cols = slice(2 * t * LANES, 2 * (t + 1) * LANES)
        wide = acc_s[:, cols] / l_s[:, cols]
        att_ref[:, t * LANES : (t + 1) * LANES] = gathered_tile(wide, t).astype(BF16)
    mid = x + mm(att_ref[...], wout_ref[...])
    mid_ref[...] = mid
    r2 = lax.rsqrt(jnp.mean(mid * mid, -1, keepdims=True) + EPS)
    n2_ref[...] = (mid * r2 * g2_ref[...]).astype(BF16)

    def done(k, c):
        push(kv_ref.at[me], kv_ref.at[me], ssem.at[k], rsem.at[k], "ctx", lax.rem(me + k, n)).wait_send()
        return c

    lax.fori_loop(1, n, done, 0)


def attn_bwd_kernel(
    n, gm_ref, x_ref, g1_ref, wqkv_ref, wout_ref, qst_ref, kv_ref, lse_ref, att_ref,
    cos_ref, sa_ref, sb_ref, kpos_ref, qpos_ref, n1_ref, dg2_ref,
    gx_ref, q_ref,
    gst_s, delta_s, gq_s, glin_ref, small_s, send_s, land_s, ssem, rsem,
):
    me = lax.axis_index("ctx")
    bar = greet("ctx", n)
    half = HEAD_DIM
    gm = gm_ref[...]
    gmb = gm.astype(BF16)
    ga = mm_nt(gmb, wout_ref[...])
    for t in range(TILES):
        tile = slice(t * LANES, (t + 1) * LANES)
        ga_t = ga[:, tile].T
        spread(gst_s, t, ga_t)
        prod = ga_t * att_ref[:, tile].astype(F32).T
        delta_s[:, 2 * t * LANES : (2 * t + 1) * LANES] = jnp.sum(prod[:half], 0, keepdims=True)
        delta_s[:, (2 * t + 1) * LANES : (2 * t + 2) * LANES] = jnp.sum(prod[half:], 0, keepdims=True)
    gq_s[...] = jnp.zeros_like(gq_s)
    qpos = qpos_ref[...]
    pl.semaphore_wait(bar, n - 1)

    def block(src):
        keys = kv_ref[src, :, :LANES]
        vals = kv_ref[src, :, LANES:]
        keys_t = keys.astype(F32).T.astype(BF16)
        hide = jnp.where(kpos_ref[src] <= qpos, 0.0, NEG)
        hide = jnp.concatenate([hide, hide], 1)
        gk = jnp.zeros((LANES, LANES), F32)
        gv = jnp.zeros((LANES, LANES), F32)
        for t in range(TILES):
            cols = slice(2 * t * LANES, 2 * (t + 1) * LANES)
            qs, gs = qst_ref[:, cols], gst_s[:, cols]
            p = jnp.exp(mm(keys, qs) + hide - lse_ref[:, cols])
            ds = (p * (mm(vals, gs) - delta_s[:, cols])).astype(BF16)
            gv = gv + mm_nt(p.astype(BF16), gs)
            gk = gk + mm_nt(ds, qs)
            gq_s[:, cols] += mm(keys_t, ds)
        return jnp.concatenate([gk, gv], 1)

    def step(k, c):
        to = lax.rem(me + k, n)
        send_s[k] = block(to).astype(BF16)
        push(send_s.at[k], land_s.at[k], ssem.at[k], rsem.at[k], "ctx", to).start()
        return c

    lax.fori_loop(1, n, step, 0)
    own = block(me)

    def take(k, total):
        push(send_s.at[k], land_s.at[k], ssem.at[k], rsem.at[k], "ctx", lax.rem(me + k, n)).wait_recv()
        return total + land_s[k].astype(F32)

    own = lax.fori_loop(1, n, take, own)
    cos, sa, sb = cos_ref[...], sa_ref[...], sb_ref[...]
    for t in range(TILES):
        wide = gq_s[:, 2 * t * LANES : 2 * (t + 1) * LANES]
        gq = gathered_tile(wide, t) * HEAD_DIM ** (-0.5)
        glin_ref[:, t * LANES : (t + 1) * LANES] = unrope(gq, cos, sa, sb).astype(BF16)
    glin_ref[:, D : D + LANES] = unrope(own[:, :LANES], cos, sa, sb).astype(BF16)
    glin_ref[:, D + LANES :] = own[:, LANES:].astype(BF16)
    gn1 = mm_nt(glin_ref[...], wqkv_ref[...])
    x = x_ref[...]
    r1 = lax.rsqrt(jnp.mean(x * x, -1, keepdims=True) + EPS)
    unit = x * r1
    dg1 = jnp.sum(gn1 * unit, 0, keepdims=True)
    dz = gn1 * g1_ref[...]
    gx_ref[...] = gm + r1 * (dz - unit * jnp.mean(dz * unit, -1, keepdims=True))
    dbias = jnp.sum(glin_ref[...].astype(F32), 0, keepdims=True)
    small_s[...] = jnp.zeros_like(small_s)
    row = 0
    for part in (dg1, dg2_ref[...], dbias):
        for t in range(part.shape[1] // LANES):
            small_s[row : row + 1, :] = part[:, t * LANES : (t + 1) * LANES]
            row += 1
    small = small_s[...].astype(BF16)
    parts = q_ref.shape[1]
    share = D // parts
    for j in range(0, QKV // LANES + TILES, 8):
        for t in range(j, j + 8):
            if t < QKV // LANES:
                d = mm_tn(n1_ref[...], glin_ref[:, t * LANES : (t + 1) * LANES])
            else:
                u = t - QKV // LANES
                d = mm_tn(att_ref[...], gmb[:, u * LANES : (u + 1) * LANES])
            d = d.astype(BF16)
            for i in range(parts):
                q_ref[j // 8, i, (t % 8) * share : (t % 8 + 1) * share, :] = d[i * share : (i + 1) * share, :]
        for i in range(parts):
            q_ref[j // 8, i, 8 * share : 8 * share + 2 * UNIT, :] = small if j == 0 else jnp.zeros_like(small)
            q_ref[j // 8, i, 8 * share + 2 * UNIT :, :] = jnp.zeros((Q_ROWS - 8 * share - 2 * UNIT, LANES), BF16)

    def done(k, c):
        push(send_s.at[k], land_s.at[k], ssem.at[k], rsem.at[k], "ctx", lax.rem(me + k, n)).wait_send()
        return c

    lax.fori_loop(1, n, done, 0)


def ffn_fwd_kernel(
    n, n2_ref, mid_ref, wg_ref, wu_ref, wd_ref,
    y_ref, all_ref, gate_ref, up_ref,
    send_s, land_s, ssem, rsem, ssem2, rsem2,
):
    me = lax.axis_index("fsdp")
    bar = greet("fsdp", n)
    all_ref[me] = n2_ref[...]
    order = [k for k in (1, 3, 2) if k < n]
    pl.semaphore_wait(bar, n - 1)

    def first(k):
        return push(all_ref.at[me], all_ref.at[me], ssem.at[k], rsem.at[k], "fsdp", lax.rem(me + k, n))

    def second(k):
        return push(send_s.at[k], land_s.at[k], ssem2.at[k], rsem2.at[k], "fsdp", lax.rem(me + n - k, n))

    for k in order:
        first(k).start()

    def block(src):
        a = all_ref[src]
        gate = mm(a, wg_ref[...])
        up = mm(a, wu_ref[...])
        gate_ref[src] = gate
        up_ref[src] = up
        hidden = (gate * jax.nn.sigmoid(gate) * up).astype(BF16)
        return mm(hidden, wd_ref[...])

    y_ref[...] = mid_ref[...] + block(me)
    for k in order:
        first(k).wait_recv()
        send_s[k] = block(lax.rem(me + n - k, n)).astype(BF16)
        second(k).start()
    for k in order:
        second(k).wait_recv()
        y_ref[...] += land_s[k].astype(F32)
    for k in order:
        first(k).wait_send()
        second(k).wait_send()


def dealt(a_per, b_per):
    where = [(0, u // a_per, u % a_per) for u in range(16 * a_per)]
    return where + [(1, v // b_per, v % b_per) for v in range(16 * b_per)]


def unit_runs(first, count, per):
    where = dealt(*per)
    found = []
    for i in range(count):
        part, piece, slot = where[first + i]
        if found and found[-1][0] == part and found[-1][1] == piece:
            found[-1][4] += 1
        else:
            found.append([part, piece, slot, i, 1])
    return found


def put_units(refs, section, base, per, first, rows):
    for part, piece, slot, i, m in unit_runs(first, rows.shape[0] // UNIT, per):
        at = base[part] + slot * UNIT
        refs[part][section, piece // SIDE, piece % SIDE, at : at + m * UNIT, :] = rows[i * UNIT : (i + m) * UNIT, :]


def ffn_bwd_kernel(
    n, gy_ref, mid_ref, g2_ref, wg_ref, wu_ref, wd_ref, gate_ref, up_ref, n2_ref,
    gm_ref, dg2_ref, fa_ref, fb_ref,
    all_s, hid_s, ggate_s, gup_s, down_s, own_s, send_s, land_s, ssem, rsem, ssem2, rsem2,
):
    me = lax.axis_index("fsdp")
    bar = greet("fsdp", n)
    tok = gy_ref.shape[0]
    order = [k for k in (1, 3, 2) if k < n]

    def rows_of(i):
        return pl.ds(pl.multiple_of(i * tok, tok), tok)

    all_s[rows_of(me), :] = gy_ref[...].astype(BF16)
    pl.semaphore_wait(bar, n - 1)

    def first(k):
        mine = all_s.at[rows_of(me), :]
        return push(mine, mine, ssem.at[k], rsem.at[k], "fsdp", lax.rem(me + k, n))

    def second(k):
        return push(send_s.at[k], land_s.at[k], ssem2.at[k], rsem2.at[k], "fsdp", lax.rem(me + n - k, n))

    for k in order:
        first(k).start()

    def block(src):
        rows = rows_of(src)
        gh = mm_nt(all_s[rows, :], wd_ref[...])
        gate, up = gate_ref[src], up_ref[src]
        sg = jax.nn.sigmoid(gate)
        act = gate * sg
        hid_s[rows, :] = (act * up).astype(BF16)
        ggate = (gh * up * sg * (1.0 + gate * (1.0 - sg))).astype(BF16)
        gup = (gh * act).astype(BF16)
        ggate_s[rows, :] = ggate
        gup_s[rows, :] = gup
        return mm_nt(ggate, wg_ref[...]) + mm_nt(gup, wu_ref[...])

    own_s[...] = block(me)
    for k in order:
        first(k).wait_recv()
        send_s[k] = block(lax.rem(me + n - k, n)).astype(BF16)
        second(k).start()

    refs = (fa_ref, fb_ref)
    share = D // n
    normed = jnp.concatenate([n2_ref[i] for i in range(n)], 0)
    for section, part in ((0, ggate_s), (1, gup_s)):
        for j in range(WIN // (2 * LANES)):
            d = mm_tn(normed, part[:, 2 * j * LANES : 2 * (j + 1) * LANES]).astype(BF16)
            for t in (2 * j, 2 * j + 1):
                tile = d[:, (t % 2) * LANES : (t % 2 + 1) * LANES]
                for i in range(n):
                    base = [i * per * UNIT for per in GATE_PER]
                    put_units(refs, section, base, GATE_PER, t * (share // UNIT), tile[i * share : (i + 1) * share, :])
        used = WIN // LANES * (share // UNIT)
        extra = 16 * sum(GATE_PER) - used
        for i in range(n):
            base = [i * per * UNIT for per in GATE_PER]
            put_units(refs, section, base, GATE_PER, used, jnp.zeros((extra * UNIT, LANES), BF16))
    for j in range(WIN // (2 * LANES)):
        cols = slice(2 * j * LANES, 2 * (j + 1) * LANES)
        down_s[cols, :] = mm_tn(hid_s[:, cols], all_s[...]).astype(BF16)
    pad = (WIN - FF // n) * lax.rem(me, 2)
    half = FF // n // 2
    base = [n * per * UNIT for per in GATE_PER]
    for section in range(2):
        rows = down_s[pl.ds(pl.multiple_of(pad + section * half, UNIT), half), :]
        for t in range(TILES):
            put_units(refs, section, base, DOWN_PER, t * (half // UNIT), rows[:, t * LANES : (t + 1) * LANES])
        used = TILES * (half // UNIT)
        extra = 16 * sum(DOWN_PER) - used
        put_units(refs, section, base, DOWN_PER, used, jnp.zeros((extra * UNIT, LANES), BF16))

    for k in order:
        second(k).wait_recv()
        own_s[...] += land_s[k].astype(F32)
    gn2 = own_s[...]
    mid = mid_ref[...]
    r2 = lax.rsqrt(jnp.mean(mid * mid, -1, keepdims=True) + EPS)
    unit = mid * r2
    dg2_ref[...] = jnp.sum(gn2 * unit, 0, keepdims=True)
    dz = gn2 * g2_ref[...]
    gm_ref[...] = gy_ref[...] + r2 * (dz - unit * jnp.mean(dz * unit, -1, keepdims=True))
    for k in order:
        first(k).wait_send()
        second(k).wait_send()


class Stages:
    def __init__(self, ssem, rsem):
        self.s = lax.axis_index("section")
        c = lax.axis_index("ctx")
        self.x, self.y = c // SIDE, lax.rem(c, SIDE)
        self.z = lax.axis_index("fsdp")
        self.nz = lax.axis_size("fsdp")
        self.ssem, self.rsem = ssem, rsem
        self.used = 0
        self.sent = []

    def along(self, axis, k):
        own, n = {"x": (self.x, SIDE), "y": (self.y, SIDE), "z": (self.z, self.nz)}[axis]
        return lax.rem(own + k, n)

    def peer(self, axis, k, section=None):
        if axis == "s":
            return {"section": 1 - self.s}
        if axis == "z":
            return {"fsdp": self.along("z", k)}
        to = self.along("x", k) * SIDE + self.y if axis == "x" else self.x * SIDE + self.along("y", k)
        return {"ctx": to} if section is None else {"ctx": to, "section": section}

    def greet(self, owners):
        ids = [self.peer("s", 0)]
        for k in range(1, SIDE):
            for axis in ("x", "y"):
                ids.append(self.peer(axis, k))
                if owners:
                    ids.append(self.peer(axis, k, 1 - self.s))
        ids += [self.peer("z", k) for k in range(1, self.nz)]
        bar = pltpu.get_barrier_semaphore()
        for i in ids:
            pl.semaphore_signal(bar, inc=1, device_id=i, device_id_type=MESH)
        pl.semaphore_wait(bar, len(ids))

    def take(self, count):
        self.used += count
        return self.used - count

    def copy(self, src, dst, at, to, recv_at=None):
        return pltpu.make_async_remote_copy(
            src_ref=src,
            dst_ref=dst,
            send_sem=self.ssem.at[at],
            recv_sem=self.rsem.at[at if recv_at is None else recv_at],
            device_id=to,
            device_id_type=MESH,
        )

    def begin(self, copies):
        for c in copies:
            c.start()
        self.sent += copies
        return copies

    def drain(self):
        for c in self.sent:
            c.wait_send()

    def swap(self, src, land):
        return self.begin([self.copy(src.at[1 - self.s], land, self.take(1), self.peer("s", 0))])

    def scatter(self, axis, src, land, peers=None):
        at = self.take(SIDE - 1)
        return self.begin(
            [self.copy(src.at[self.along(axis, k)], land.at[k - 1], at + k - 1, self.peer(axis, k)) for k in range(1, SIDE)]
        )

    def gather(self, axis, ref):
        at = self.take(SIDE - 1)
        mine = ref.at[self.along(axis, 0)]
        return self.begin([self.copy(mine, mine, at + k - 1, self.peer(axis, k)) for k in range(1, SIDE)])

    def deal(self, src, dst, rows):
        at = self.take(self.nz - 1)
        mine = dst.at[self.block(self.z, rows), :]
        return self.begin(
            [
                self.copy(src.at[self.block(self.along("z", k), rows), :], mine, at + k - 1, self.peer("z", k))
                for k in range(1, self.nz)
            ]
        )

    def block(self, i, rows):
        return pl.ds(pl.multiple_of(i * rows, UNIT), rows)

    def hand_over(self, axis, src, dst, layer):
        at = self.take(2 * SIDE)
        mine = dst.at[self.s, self.along(axis, 0)]
        copies = self.begin(
            [
                self.copy(src, mine, at + k, self.peer(axis, k, layer), at + self.s * SIDE + k)
                for k in range(1, SIDE)
            ]
        )
        beside = self.copy(src, mine, at, {"section": layer}, at + self.s * SIDE)

        @pl.when(self.s != layer)
        def _():
            beside.start()

        @pl.when(self.s == layer)
        def _():
            mine[...] = src[...]

        def finish():
            @pl.when(self.s == layer)
            def _():
                for half in range(2):
                    for k in range(0 if half != layer else 1, SIDE):
                        self.copy(src, mine, at, {"section": layer}, at + half * SIDE + k).wait_recv()

            @pl.when(self.s != layer)
            def _():
                beside.wait_send()

        return finish


def arrived(copies):
    for c in copies:
        c.wait_recv()


def add_into(dst, parts):
    def one(i, c):
        total = parts[0][i].astype(F32)
        for p in parts[1:]:
            total = total + p[i].astype(F32)
        dst[i] = total.astype(dst.dtype)
        return c

    lax.fori_loop(0, dst.shape[0], one, 0)


def add_rows(dst, parts):
    total = parts[0][...].astype(F32)
    for p in parts[1:]:
        total = total + p[...].astype(F32)
    dst[...] = total.astype(dst.dtype)


AXES = (("x", "y"), ("y", "x"))


def reduce_kernel(
    layer, fa_ref, fb_ref, q_ref,
    ga_ref, gb_ref, qa_ref, qb_ref,
    sa, sb, l1a, l1b, l2a, l2b, t2a, t2b, g1a, g1b,
    sq, zq, qpa, qpb, q1a, q1b, q2a, q2b, qga, qgb, ssem, rsem,
):
    st = Stages(ssem, rsem)
    st.greet(True)
    f, sl, l1, l2, t2, g1, out = (fa_ref, fb_ref), (sa, sb), (l1a, l1b), (l2a, l2b), (t2a, t2b), (g1a, g1b), (ga_ref, gb_ref)
    qp, q1, q2, qg, qout = (qpa, qpb), (q1a, q1b), (q2a, q2b), (qga, qgb), (qa_ref, qb_ref)
    both = range(2)
    swaps = [st.swap(f[h], sl[h]) for h in both]
    qswap = st.swap(q_ref, sq)
    r1 = [None, None]
    for h in both:
        arrived(swaps[h])
        for i in range(SIDE):
            add_into(sl[h].at[i], [f[h].at[st.s, i], sl[h].at[i]])
        r1[h] = st.scatter(AXES[h][0], sl[h], l1[h])
    arrived(qswap)
    add_into(sq, [q_ref.at[st.s], sq])
    at = st.take(st.nz - 1)
    zr = st.begin([st.copy(sq.at[st.along("z", k)], zq.at[k - 1], at + k - 1, st.peer("z", k)) for k in range(1, st.nz)])
    r2 = [None, None]
    for h in both:
        arrived(r1[h])
        own = sl[h].at[st.along(AXES[h][0], 0)]
        add_into(own, [own] + [l1[h].at[k] for k in range(SIDE - 1)])
        r2[h] = st.scatter(AXES[h][1], own, l2[h])
    arrived(zr)
    parts = [sq.at[st.z]] + [zq.at[k] for k in range(st.nz - 1)]
    rows = Q_ROWS // 2 // 16
    qr1 = [None, None]
    for h in both:
        for i in range(16):
            total = jnp.zeros((rows, LANES), F32)
            for p in parts:
                total = total + p[h * Q_ROWS // 2 + i * rows : h * Q_ROWS // 2 + (i + 1) * rows, :].astype(F32)
            qp[h][i // SIDE, i % SIDE] = total.astype(BF16)
        qr1[h] = st.scatter(AXES[h][0], qp[h], q1[h])
    zs = [None, None]
    for h in both:
        arrived(r2[h])
        own = sl[h].at[st.along(AXES[h][0], 0), st.along(AXES[h][1], 0)]
        add_rows(t2[h], [own] + [l2[h].at[k] for k in range(SIDE - 1)])
        per = GATE_PER[h] * UNIT
        mine = g1[h].at[st.along(AXES[h][1], 0)]
        zs[h] = st.deal(t2[h], mine, per)
        mine[st.block(st.z, per), :] = t2[h][st.block(st.z, per), :]
        mine[st.nz * per :, :] = t2[h][st.nz * per :, :]
    qr2 = [None, None]
    for h in both:
        arrived(qr1[h])
        own = qp[h].at[st.along(AXES[h][0], 0)]
        add_into(own, [own] + [q1[h].at[k] for k in range(SIDE - 1)])
        qr2[h] = st.scatter(AXES[h][1], own, q2[h])
    ag = [None, None]
    for h in both:
        arrived(zs[h])
        ag[h] = st.gather(AXES[h][1], g1[h])
    qag = [None, None]
    for h in both:
        arrived(qr2[h])
        own = qp[h].at[st.along(AXES[h][0], 0), st.along(AXES[h][1], 0)]
        add_rows(qg[h].at[st.along(AXES[h][1], 0)], [own] + [q2[h].at[k] for k in range(SIDE - 1)])
        qag[h] = st.gather(AXES[h][1], qg[h])
    last = []
    for h in both:
        arrived(ag[h])
        last.append(st.hand_over(AXES[h][0], g1[h], out[h], layer))
    for h in both:
        arrived(qag[h])
        last.append(st.hand_over(AXES[h][0], qg[h], qout[h], layer))
    for finish in last:
        finish()
    st.drain()


def reduce_gradients(fa, fb, q, layer):
    ra, rb = fa.shape[3], fb.shape[3]
    rq = Q_ROWS // 2 // 16
    vm = pl.BlockSpec(memory_space=pltpu.VMEM)
    dma = pltpu.SemaphoreType.DMA

    def buf(*shape):
        return pltpu.VMEM(shape + (LANES,), BF16)

    sides = (SIDE, SIDE)
    nz = lax.axis_size("fsdp")
    return pl.pallas_call(
        functools.partial(reduce_kernel, layer),
        out_shape=[
            jax.ShapeDtypeStruct((2,) + sides + (r, LANES), BF16) for r in (ra, rb, rq, rq)
        ],
        in_specs=[vm] * 3,
        out_specs=[vm] * 4,
        scratch_shapes=[
            buf(*sides, ra), buf(*sides, rb),
            buf(SIDE - 1, SIDE, ra), buf(SIDE - 1, SIDE, rb),
            buf(SIDE - 1, ra), buf(SIDE - 1, rb),
            buf(ra), buf(rb),
            buf(SIDE, ra), buf(SIDE, rb),
            buf(nz, Q_ROWS), buf(nz - 1, Q_ROWS),
            buf(*sides, rq), buf(*sides, rq),
            buf(SIDE - 1, SIDE, rq), buf(SIDE - 1, SIDE, rq),
            buf(SIDE - 1, rq), buf(SIDE - 1, rq),
            buf(SIDE, rq), buf(SIDE, rq),
            dma((80,)), dma((80,)),
        ],
        compiler_params=pltpu.CompilerParams(
            collective_id=5 + layer, has_side_effects=True, vmem_limit_bytes=VMEM_LIMIT
        ),
        cost_estimate=pl.CostEstimate(flops=10**9, bytes_accessed=40 * 2**20, transcendentals=0),
        name=f"reduce_{layer}",
    )(fa, fb, q)


def assemble_kernel(nz, *refs):
    given, outs, held, sem = (refs[:4], refs[4:8]), refs[8:14], refs[14:18], refs[18]
    s = lax.axis_index("section")
    for layer in range(2):
        @pl.when(s == layer)
        def _():
            copies = [pltpu.make_async_copy(a, b, sem.at[i]) for i, (a, b) in enumerate(zip(given[layer], held))]
            for c in copies:
                c.start()
            for c in copies:
                c.wait()

    gate_ref, up_ref, down_ref, qkv_ref, out_ref, small_ref = outs
    share = D // nz
    starts = window_starts(nz)

    def units(refs, section, base, per, first, count):
        rows = []
        for part, piece, slot, _, m in unit_runs(first, count, per):
            at = base[part] + slot * UNIT
            rows.append(refs[part][section, piece // SIDE, piece % SIDE, at : at + m * UNIT, :].astype(F32))
        return jnp.concatenate(rows, 0) if len(rows) > 1 else rows[0]

    for section, ref in ((0, gate_ref), (1, up_ref)):
        tiles = {}
        for w, a in enumerate(starts):
            for t in range(WIN // LANES):
                tiles.setdefault(a // LANES + t, []).append((w, t))
        for col, sources in tiles.items():
            total = None
            for w, t in sources:
                base = [w * per * UNIT for per in GATE_PER]
                got = units(held[:2], section, base, GATE_PER, t * (share // UNIT), share // UNIT)
                total = got if total is None else total + got
            ref[:, col * LANES : (col + 1) * LANES] = total
    base = [nz * per * UNIT for per in GATE_PER]
    half = FF // nz // 2
    for section in range(2):
        for t in range(TILES):
            got = units(held[:2], section, base, DOWN_PER, t * (half // UNIT), half // UNIT)
            down_ref[section * half : (section + 1) * half, t * LANES : (t + 1) * LANES] = got
    for t in range(QKV // LANES + TILES):
        got = units(held[2:], t // 8, (0, 0), Q_PER, (t % 8) * (share // UNIT), share // UNIT)
        if t < QKV // LANES:
            qkv_ref[:, t * LANES : (t + 1) * LANES] = got
        else:
            u = t - QKV // LANES
            out_ref[:, u * LANES : (u + 1) * LANES] = got
    small_ref[...] = units(held[2:], 0, (0, 0), Q_PER, 8 * (share // UNIT), 2)


def assemble(given):
    nz = lax.axis_size("fsdp")
    vm = pl.BlockSpec(memory_space=pltpu.VMEM)
    share = D // nz
    shapes = [(share, FF), (share, FF), (FF // nz, D), (share, QKV), (share, D), (2 * UNIT, LANES)]
    flat = [a for one in given for a in one]
    return pl.pallas_call(
        functools.partial(assemble_kernel, nz),
        out_shape=[jax.ShapeDtypeStruct(a, F32) for a in shapes],
        in_specs=[pl.BlockSpec(memory_space=pl.ANY)] * len(flat),
        out_specs=[vm] * len(shapes),
        scratch_shapes=[pltpu.VMEM(a.shape, a.dtype) for a in given[0]] + [pltpu.SemaphoreType.DMA((4,))],
        compiler_params=pltpu.CompilerParams(vmem_limit_bytes=VMEM_LIMIT),
        name="assemble",
    )(*flat)


def call(kernel, n, ins, outs, scratch, cid, name, flops):
    vm = pl.BlockSpec(memory_space=pltpu.VMEM)
    moved = sum(a.size * a.dtype.itemsize for a in ins)
    return pl.pallas_call(
        functools.partial(kernel, n),
        out_shape=[jax.ShapeDtypeStruct(s, t) for s, t in outs],
        in_specs=[vm] * len(ins),
        out_specs=[vm] * len(outs),
        scratch_shapes=scratch,
        compiler_params=pltpu.CompilerParams(
            collective_id=cid, has_side_effects=True, vmem_limit_bytes=VMEM_LIMIT
        ),
        cost_estimate=pl.CostEstimate(flops=flops, bytes_accessed=moved, transcendentals=0),
        name=name,
    )(*ins)


def attn_fwd(x, g1, g2, wqkv, bias, tabs, wout):
    n = lax.axis_size("ctx")
    tok = x.shape[0]
    wide = HEADS * LANES
    cos, sa, sb, kpos, qpos = tabs
    dma = pltpu.SemaphoreType.DMA
    return call(
        attn_fwd_kernel, n,
        (x, g1, g2, wqkv, bias, cos, sa, sb, kpos, qpos, wout),
        [((tok, D), F32), ((tok, D), BF16), ((tok, D), BF16), ((LANES, wide), BF16),
         ((n, tok, 2 * LANES), BF16), ((1, wide), F32), ((tok, D), BF16)],
        [pltpu.VMEM((1, wide), F32), pltpu.VMEM((1, wide), F32), pltpu.VMEM((LANES, wide), F32), dma((n,)), dma((n,))],
        1, "attn_fwd", 10 * 10**9,
    )


def attn_bwd(gm, x, g1, wqkv, wout, saved, tabs, n1, dg2):
    n = lax.axis_size("ctx")
    nz = lax.axis_size("fsdp")
    tok = x.shape[0]
    wide = HEADS * LANES
    cos, sa, sb, kpos, qpos = tabs
    qst, kv, lse, att = saved
    dma = pltpu.SemaphoreType.DMA
    return call(
        attn_bwd_kernel, n,
        (gm, x, g1, wqkv, wout, qst, kv, lse, att, cos, sa, sb, kpos, qpos, n1, dg2),
        [((tok, D), F32), ((2, nz, Q_ROWS, LANES), BF16)],
        [pltpu.VMEM((LANES, wide), BF16), pltpu.VMEM((1, wide), F32), pltpu.VMEM((LANES, wide), F32),
         pltpu.VMEM((tok, QKV), BF16), pltpu.VMEM((2 * UNIT, LANES), F32),
         pltpu.VMEM((n, tok, 2 * LANES), BF16), pltpu.VMEM((n, tok, 2 * LANES), BF16), dma((n,)), dma((n,))],
        2, "attn_bwd", 20 * 10**9,
    )


def ffn_fwd(n2, mid, wg, wu, wd):
    n = lax.axis_size("fsdp")
    tok = n2.shape[0]
    dma = pltpu.SemaphoreType.DMA
    return call(
        ffn_fwd_kernel, n, (n2, mid, wg, wu, wd),
        [((tok, D), F32), ((n, tok, D), BF16), ((n, tok, WIN), F32), ((n, tok, WIN), F32)],
        [pltpu.VMEM((n, tok, D), BF16), pltpu.VMEM((n, tok, D), BF16), dma((n,)), dma((n,)), dma((n,)), dma((n,))],
        3, "ffn_fwd", 10 * 10**9,
    )


def ffn_bwd(gy, mid, g2, wg, wu, wd, gate, up, n2_all):
    n = lax.axis_size("fsdp")
    tok = gy.shape[0]
    dma = pltpu.SemaphoreType.DMA
    rows = [(n * g + d) * UNIT for g, d in zip(GATE_PER, DOWN_PER)]
    return call(
        ffn_bwd_kernel, n, (gy, mid, g2, wg, wu, wd, gate, up, n2_all),
        [((tok, D), F32), ((1, D), F32), ((2, SIDE, SIDE, rows[0], LANES), BF16), ((2, SIDE, SIDE, rows[1], LANES), BF16)],
        [pltpu.VMEM((n * tok, D), BF16), pltpu.VMEM((n * tok, WIN), BF16), pltpu.VMEM((n * tok, WIN), BF16),
         pltpu.VMEM((n * tok, WIN), BF16), pltpu.VMEM((WIN, D), BF16),
         pltpu.VMEM((tok, D), F32), pltpu.VMEM((n, tok, D), BF16), pltpu.VMEM((n, tok, D), BF16),
         dma((n,)), dma((n,)), dma((n,)), dma((n,))],
        4, "ffn_bwd", 20 * 10**9,
    )


def dealt_positions(chosen_pair, block_len, ctx_count):
    within = jnp.arange(2 * block_len, dtype=jnp.int32)
    first = chosen_pair * block_len + within
    second = (2 * ctx_count - 1 - chosen_pair) * block_len + within - block_len
    return jnp.where(within < block_len, first, second)


def tables(pair_of):
    n = lax.axis_size("ctx")
    block_len = 64
    all_pairs = lax.all_gather(pair_of, "ctx", axis=0, tiled=True)
    own = dealt_positions(pair_of[0], block_len, n)
    kpos = jax.vmap(lambda p: dealt_positions(p, block_len, n))(all_pairs)
    freq = jnp.arange(HEAD_DIM // 2, dtype=F32)
    inverse = THETA ** (-2.0 * freq / HEAD_DIM)
    angles = own.astype(F32)[:, None] * inverse[None, :]
    cos, sin = jnp.cos(angles), jnp.sin(angles)
    zero = jnp.zeros_like(sin)
    return (
        jnp.concatenate([cos] * 4, -1),
        jnp.concatenate([-sin, zero] * 2, -1),
        jnp.concatenate([zero, sin] * 2, -1),
        kpos[:, :, None],
        own[None, :],
    )


def window_starts(n):
    share = FF // n
    return [(i * share // LANES) * LANES for i in range(n)]


def local(
    tokens, cotangent, pair_of, attn_gain, ffn_gain, qkv_weight, qkv_bias, out_weight, gate_weight, up_weight, down_weight,
):
    s = lax.axis_index("section")
    z = lax.axis_index("fsdp")
    nz = lax.axis_size("fsdp")
    share = FF // nz
    starts = window_starts(nz)
    tabs = tables(pair_of)
    both = ("section", "fsdp")

    small = jnp.concatenate([attn_gain[0], ffn_gain[0], qkv_bias[0]])
    small = lax.all_gather(small, both, axis=0, tiled=False).reshape(2, nz, -1)
    qd = D // nz
    gain1 = small[:, :, :qd].reshape(2, 1, D).astype(F32)
    gain2 = small[:, :, qd : 2 * qd].reshape(2, 1, D).astype(F32)
    bias = small[:, :, 2 * qd :].reshape(2, 1, QKV).astype(F32)
    wqkv = lax.all_gather(qkv_weight[0], both, axis=0).reshape(2, D, QKV)
    wout = lax.all_gather(out_weight[0], both, axis=0).reshape(2, D, D)

    def windows(w):
        return jnp.stack([w[:, a : a + WIN] for a in starts])

    gu = jnp.stack([windows(gate_weight[0]), windows(up_weight[0])], 1)
    gu = lax.all_to_all(gu, "fsdp", 0, 0)
    gu = gu.transpose(1, 0, 2, 3).reshape(2, D, WIN)
    gu = lax.all_gather(gu, "section", axis=0)
    pad = (WIN - share) * lax.rem(z, 2)
    down = jnp.pad(down_weight[0], ((WIN - share, WIN - share), (0, 0)))
    down = lax.dynamic_slice_in_dim(down, WIN - share - pad, WIN, 0)
    wd = lax.all_gather(down, "section", axis=0)

    x = jnp.where(s == 0, tokens[0, 0], tokens[1, 0])
    saved = []
    outs = []
    for l in range(2):
        mid, n2, n1, qst, kv, lse, att = attn_fwd(x, gain1[l], gain2[l], wqkv[l], bias[l], tabs, wout[l])
        y, n2_all, gate, up = ffn_fwd(n2, mid, gu[l, 0], gu[l, 1], wd[l])
        saved.append((x, mid, n1, (qst, kv, lse, att), n2_all, gate, up))
        outs.append(y)
        x = y.astype(BF16).astype(F32)

    gy = jnp.where(s == 0, cotangent[0, 0], cotangent[1, 0])
    given = [None, None]
    gxs = [None, None]
    for l in (1, 0):
        x, mid, n1, attn_saved, n2_all, gate, up = saved[l]
        gm, dg2, fa, fb = ffn_bwd(gy, mid, gain2[l], gu[l, 0], gu[l, 1], wd[l], gate, up, n2_all)
        gx, q = attn_bwd(gm, x, gain1[l], wqkv[l], wout[l], attn_saved, tabs, n1, dg2)
        gxs[l] = gx
        gy = gx.astype(BF16).astype(F32)
        given[l] = reduce_gradients(fa, fb, q, l)
    dgate, dup, ddown, dqkv, dout, small_grad = assemble(given)
    small_grad = small_grad.reshape(-1)

    def mine(first, size):
        return lax.dynamic_slice_in_dim(small_grad, first + z * size, size, 0)[None]

    def by_layer(pair):
        theirs = jnp.where(s == 0, pair[1], pair[0])
        mine = jnp.where(s == 0, pair[0], pair[1])
        got = lax.ppermute(theirs, "section", [(0, 1), (1, 0)])
        return jnp.where(s == 0, jnp.stack([mine, got]), jnp.stack([got, mine]))[None, :, None]

    return (
        by_layer(outs),
        by_layer(gxs),
        mine(0, qd),
        mine(D, qd),
        dqkv[None],
        mine(2 * D, QKV // nz),
        dout[None],
        dgate[None],
        dup[None],
        ddown[None],
    )


def solution(mesh):
    return jax.shard_map(
        local,
        mesh=mesh,
        in_specs=(
            P(None, "fsdp", "ctx", None),
            P(None, "fsdp", "ctx", None),
            P("ctx"),
            P("section", "fsdp"),
            P("section", "fsdp"),
            P("section", "fsdp", None),
            P("section", "fsdp"),
            P("section", "fsdp", None),
            P("section", "fsdp", None),
            P("section", "fsdp", None),
            P("section", "fsdp", None),
        ),
        out_specs=(
            P("section", None, "fsdp", "ctx", None),
            P("section", None, "fsdp", "ctx", None),
            P("section", "fsdp"),
            P("section", "fsdp"),
            P("section", "fsdp", None),
            P("section", "fsdp"),
            P("section", "fsdp", None),
            P("section", "fsdp", None),
            P("section", "fsdp", None),
            P("section", "fsdp", None),
        ),
        check_vma=False,
    )
```

```python
import functools
import types

import jax
import jax.numpy as jnp
from jax import lax
from jax.experimental import pallas as pl
from jax.experimental.pallas import tpu as pltpu
from jax.sharding import PartitionSpec as P

D = 896
HEADS = 14
KV_HEADS = 2
HEAD_DIM = 64
GROUP = HEADS // KV_HEADS
FF = 4864
QKV = 1152
EPS = 1e-06
THETA = 1000000.0
LANES = 128
TILES = D // LANES
WIN = 1280
NEG = -1e30
F32 = jnp.float32
BF16 = jnp.bfloat16
MESH = pl.DeviceIdType.MESH
VMEM_LIMIT = 56 * 2**20
UNIT = 16
SIDE = 4
GATE_PER = (5, 4)
DOWN_PER = (8, 9)
Q_PER = (4, 4)
Q_ROWS = 16 * sum(Q_PER) * UNIT


def mm(a, b):
    return jnp.dot(a, b, preferred_element_type=F32)


def mm_nt(a, b):
    return lax.dot_general(a, b, (((1,), (1,)), ((), ())), preferred_element_type=F32)


def mm_tn(a, b):
    return lax.dot_general(a, b, (((0,), (0,)), ((), ())), preferred_element_type=F32)


ORDER = (1, 3, 2)
SMALL = 2 * D + QKV
AXES = (("x", "y"), ("y", "x"))


def push(src, dst, ssem, rsem, axis, to):
    return pltpu.make_async_remote_copy(
        src_ref=src,
        dst_ref=dst,
        send_sem=ssem,
        recv_sem=rsem,
        device_id={axis: to},
        device_id_type=MESH,
    )


def rope(u, cos, sa, sb):
    return u * cos + pltpu.roll(u, 96, 1) * sa + pltpu.roll(u, 32, 1) * sb


def unrope(u, cos, sa, sb):
    return u * cos - pltpu.roll(u, 96, 1) * sa - pltpu.roll(u, 32, 1) * sb


def spread(ref, t, tile_t):
    half = HEAD_DIM
    zero = jnp.zeros((half, LANES), BF16)
    for j in range(2):
        h = 2 * t + j
        slab = tile_t[j * half : (j + 1) * half, :].astype(BF16)
        both = [slab, zero] if h // GROUP == 0 else [zero, slab]
        ref[:, h * LANES : (h + 1) * LANES] = jnp.concatenate(both, 0)


def gathered_tile(wide, t):
    half = HEAD_DIM
    rows = []
    for j in range(2):
        g = (2 * t + j) // GROUP
        rows.append(wide[g * half : (g + 1) * half, j * LANES : (j + 1) * LANES])
    return jnp.concatenate(rows, 0).T


def dealt(a_per, b_per):
    where = [(0, u // a_per, u % a_per) for u in range(16 * a_per)]
    return where + [(1, v // b_per, v % b_per) for v in range(16 * b_per)]


def unit_runs(first, count, per):
    where = dealt(*per)
    found = []
    for i in range(count):
        part, piece, slot = where[first + i]
        if found and found[-1][0] == part and found[-1][1] == piece:
            found[-1][4] += 1
        else:
            found.append([part, piece, slot, i, 1])
    return found


def put_units(refs, section, base, per, first, rows):
    for part, piece, slot, i, m in unit_runs(first, rows.shape[0] // UNIT, per):
        at = base[part] + slot * UNIT
        refs[part][section, piece // SIDE, piece % SIDE, at : at + m * UNIT, :] = rows[i * UNIT : (i + m) * UNIT, :]


class Stages:
    def __init__(self, r):
        self.s = lax.axis_index("section")
        self.c = lax.axis_index("ctx")
        self.nc = lax.axis_size("ctx")
        self.x, self.y = self.c // SIDE, lax.rem(self.c, SIDE)
        self.z = lax.axis_index("fsdp")
        self.nz = lax.axis_size("fsdp")
        self.ssem, self.rsem, self.lsem = r.ssem, r.rsem, r.lsem
        self.used = 0
        self.local_used = 0
        self.sent = []

    def along(self, axis, k):
        own, n = {
            "x": (self.x, SIDE),
            "y": (self.y, SIDE),
            "z": (self.z, self.nz),
            "c": (self.c, self.nc),
        }[axis]
        return lax.rem(own + n + k, n)

    def peer(self, axis, k, section=None):
        if axis == "s":
            return {"section": 1 - self.s}
        if axis == "z":
            to = {"fsdp": self.along("z", k)}
        elif axis == "c":
            to = {"ctx": self.along("c", k)}
        elif axis == "x":
            to = {"ctx": self.along("x", k) * SIDE + self.y}
        else:
            to = {"ctx": self.x * SIDE + self.along("y", k)}
        if section is not None:
            to["section"] = section
        return to

    def hail(self, ids, ring=False):
        bar = pltpu.get_barrier_semaphore()
        for i in ids:
            pl.semaphore_signal(bar, inc=1, device_id=i, device_id_type=MESH)
        self.expected = len(ids)
        if ring:
            def one(k, c):
                pl.semaphore_signal(bar, inc=1, device_id=self.peer("c", k), device_id_type=MESH)
                return c

            lax.fori_loop(1, self.nc, one, 0)
            self.expected += self.nc - 1
        self.bar = bar

    def met(self):
        pl.semaphore_wait(self.bar, self.expected)

    def beside(self):
        return [self.peer("s", 0)]

    def upright(self, both=False):
        ids = [self.peer("z", k) for k in range(1, self.nz)]
        return ids + ([self.peer("z", k, 1 - self.s) for k in range(1, self.nz)] if both else [])

    def flat(self, both=False):
        ids = [self.peer(a, k) for a in "xy" for k in range(1, SIDE)]
        return ids + ([self.peer(a, k, 1 - self.s) for a in "xy" for k in range(1, SIDE)] if both else [])

    def take(self, count):
        self.used += count
        return self.used - count

    def copy(self, src, dst, at, to, recv_at=None):
        return pltpu.make_async_remote_copy(
            src_ref=src,
            dst_ref=dst,
            send_sem=self.ssem.at[at],
            recv_sem=self.rsem.at[at if recv_at is None else recv_at],
            device_id=to,
            device_id_type=MESH,
        )

    def begin(self, copies):
        for c in copies:
            c.start()
        self.sent += copies
        return copies

    def drain(self):
        for c in self.sent:
            c.wait_send()

    def swap(self, src, land):
        return self.begin([self.copy(src.at[1 - self.s], land, self.take(1), self.peer("s", 0))])

    def scatter(self, axis, src, land):
        n = self.nz if axis == "z" else SIDE
        at = self.take(n - 1)
        return self.begin(
            [self.copy(src.at[self.along(axis, k)], land.at[k - 1], at + k - 1, self.peer(axis, k)) for k in range(1, n)]
        )

    def gather(self, axis, ref):
        at = self.take(SIDE - 1)
        mine = ref.at[self.along(axis, 0)]
        return self.begin([self.copy(mine, mine, at + k - 1, self.peer(axis, k)) for k in range(1, SIDE)])

    def deal(self, src, dst, rows):
        at = self.take(self.nz - 1)
        mine = dst.at[self.block(self.z, rows), :]
        return self.begin(
            [
                self.copy(src.at[self.block(self.along("z", k), rows), :], mine, at + k - 1, self.peer("z", k))
                for k in range(1, self.nz)
            ]
        )

    def block(self, i, rows):
        return pl.ds(pl.multiple_of(i * rows, UNIT), rows)

    def hand_over(self, axis, src, dst, layer):
        at = self.take(2 * SIDE)
        mine = dst.at[self.s, self.along(axis, 0)]
        self.begin(
            [
                self.copy(src, mine, at + k, self.peer(axis, k, layer), at + self.s * SIDE + k)
                for k in range(1, SIDE)
            ]
        )
        beside = self.copy(src, mine, at, {"section": layer}, at + self.s * SIDE)

        @pl.when(self.s != layer)
        def _():
            beside.start()

        @pl.when(self.s == layer)
        def _():
            mine[...] = src[...]

        def finish():
            @pl.when(self.s == layer)
            def _():
                for half in range(2):
                    for k in range(0 if half != layer else 1, SIDE):
                        self.copy(src, mine, at, {"section": layer}, at + half * SIDE + k).wait_recv()

            @pl.when(self.s != layer)
            def _():
                beside.wait_send()

        return finish


class Feed:
    def __init__(self, st, layer, source, piece):
        self.st, self.layer, self.source, self.piece = st, layer, source, piece
        self.across = st.take(2 * (st.nz - 1))
        self.own = st.take(2)
        self.passed = st.take(st.nz - 1)
        self.local = st.local_used
        st.local_used += 2

    def out_copies(self):
        st = self.st
        found = []
        for k in ORDER:
            for h in range(2):
                found.append(
                    st.copy(
                        self.source(h, st.along("z", k)), self.piece(st.z, h), self.across + 2 * (k - 1) + h, st.peer("z", k, h)
                    )
                )
        for h in range(2):
            found.append(st.copy(self.source(h, st.z), self.piece(st.z, h), self.own + h, st.peer("s", 0)))
        return found

    def in_place(self):
        st = self.st
        return [
            pltpu.make_async_copy(self.source(h, st.z), self.piece(st.z, h), st.lsem.at[self.local + h]) for h in range(2)
        ]

    def start(self):
        @pl.when(self.st.s == self.layer)
        def _():
            for c in self.in_place() + self.out_copies():
                c.start()

    def pass_on(self, k):
        st = self.st
        p = self.piece(st.along("z", -k), st.s)
        st.copy(p, p, self.across + 2 * (k - 1) + st.s, st.peer("s", 0)).wait_recv()
        st.begin([st.copy(p, p, self.passed + k - 1, st.peer("s", 0))])

    def finish(self):
        st = self.st
        for k in ORDER:
            p = self.piece(st.along("z", -k), 1 - st.s)
            st.copy(p, p, self.passed + k - 1, st.peer("s", 0)).wait_recv()

        @pl.when(st.s == self.layer)
        def _():
            for c in self.in_place():
                c.wait()
            for c in self.out_copies():
                c.wait_send()

        @pl.when(st.s != self.layer)
        def _():
            for h in range(2):
                p = self.piece(st.z, h)
                st.copy(p, p, self.own + h, st.peer("s", 0)).wait_recv()


class FeedDown:
    def __init__(self, st, layer, src, dst):
        self.st, self.layer = st, layer
        share = src.shape[1]
        spare = WIN - share
        odd = lax.rem(st.z, 2)
        place = dst.at[pl.ds(pl.multiple_of(odd * spare, UNIT), share), :]
        dst[pl.ds(pl.multiple_of((1 - odd) * share, UNIT), spare), :] = jnp.zeros((spare, D), BF16)
        self.local = pltpu.make_async_copy(src.at[0], place, st.lsem.at[st.local_used])
        st.local_used += 1
        self.remote = st.copy(src.at[0], place, st.take(1), st.peer("s", 0))

    def start(self):
        @pl.when(self.st.s == self.layer)
        def _():
            self.local.start()
            self.remote.start()

    def finish(self):
        @pl.when(self.st.s == self.layer)
        def _():
            self.local.wait()
            self.remote.wait_send()

        @pl.when(self.st.s != self.layer)
        def _():
            self.remote.wait_recv()


def feed_rows(st, layer, src, dst):
    share = src.shape[1]
    half = share // 2

    def source(h, z_to):
        return src.at[0, h * half : (h + 1) * half, :]

    def piece(z_from, h):
        return dst.at[pl.ds(pl.multiple_of(z_from * share + h * half, UNIT), half), :]

    return Feed(st, layer, source, piece)


def feed_windows(st, layer, gate, up, dst):
    share = gate.shape[1]
    pace = FF // st.nz // (LANES // 2)

    def source(h, z_to):
        start = pl.multiple_of(z_to * pace // 2 * LANES, LANES)
        return (gate, up)[h].at[0, :, pl.ds(start, WIN)]

    def piece(z_from, h):
        return dst.at[h, pl.ds(pl.multiple_of(z_from * share, UNIT), share), :]

    return Feed(st, layer, source, piece)


def arrived(copies):
    for c in copies:
        c.wait_recv()


def add_into(dst, parts):
    def one(i, c):
        total = parts[0][i].astype(F32)
        for p in parts[1:]:
            total = total + p[i].astype(F32)
        dst[i] = total.astype(dst.dtype)
        return c

    lax.fori_loop(0, dst.shape[0], one, 0)


def add_rows(dst, parts):
    total = parts[0][...].astype(F32)
    for p in parts[1:]:
        total = total + p[...].astype(F32)
    dst[...] = total.astype(dst.dtype)


def swapped_sum(st, copies, given, land):
    arrived(copies)
    for i in range(SIDE):
        add_into(land.at[i], [given.at[st.s, i], land.at[i]])


def key_positions(pairs_ref, src, n):
    pair = pairs_ref[src, 0:1, :]
    i = lax.broadcasted_iota(jnp.int32, (LANES, LANES), 0)
    block = LANES // 2
    return jnp.where(i < block, pair * block + i, (2 * n - 1 - pair) * block + i - block)


def hidden_bias(pairs_ref, src, qpos, n):
    hide = jnp.where(key_positions(pairs_ref, src, n) <= qpos, 0.0, NEG)
    return jnp.concatenate([hide, hide], 1)


def row_positions(pairs_ref, me, n):
    pair = pairs_ref[me, 0:1, :]
    i = lax.broadcasted_iota(jnp.int32, (1, LANES), 1)
    block = LANES // 2
    return jnp.where(i < block, pair * block + i, (2 * n - 1 - pair) * block + i - block)


def attn_fwd_kernel(layer, r):
    st = Stages(r)
    n, me = st.nc, st.c
    st.hail(st.beside() + st.upright(True), ring=True)
    first = layer == 0
    x = r.x[...]
    r1 = lax.rsqrt(jnp.mean(x * x, -1, keepdims=True) + EPS)
    unit = x * r1
    if first:
        r.pairs[me] = jnp.broadcast_to(r.pair[...], r.pairs.shape[1:])
        r.parts[st.s, st.z] = r.small_own[...]
    st.met()
    wout = feed_rows(st, layer, r.wout_shard, r.wout)
    gu = feed_windows(st, layer, r.gate_shard, r.up_shard, r.gu)
    down = FeedDown(st, layer, r.down_shard, r.down)
    if first:
        qkv = feed_rows(st, layer, r.wqkv_shard, r.wqkv)
        qkv.start()
        at = st.take(2 * st.nz)
        mine = r.parts.at[st.s, st.z]
        st.begin(
            [st.copy(mine, mine, at + k, st.peer("z", k, st.s), at + st.s * st.nz + k) for k in range(1, st.nz)]
            + [st.copy(mine, mine, at + st.nz + k, st.peer("z", k, 1 - st.s), at + st.s * st.nz + k) for k in range(1, st.nz)]
            + [st.copy(mine, mine, at, st.peer("s", 0), at + st.s * st.nz)]
        )

        def tell(k, c):
            p = r.pairs.at[me]
            push(p, p, r.psem.at[k], r.psem2.at[k], "ctx", lax.rem(me + k, n)).start()
            return c

        lax.fori_loop(1, n, tell, 0)
        block = LANES // 2
        i = lax.broadcasted_iota(jnp.int32, (LANES, LANES), 0)
        pair = r.pairs[me, 0:1, :]
        pos = jnp.where(i < block, pair * block + i, (2 * n - 1 - pair) * block + i - block)
        angle = pos.astype(F32) * r.inverse[...]
        lane = lax.rem(lax.broadcasted_iota(jnp.int32, (LANES, LANES), 1), HEAD_DIM)
        sine = jnp.sin(angle)
        r.cos[...] = jnp.cos(angle)
        r.sa[...] = jnp.where(lane < HEAD_DIM // 2, -sine, 0.0)
        r.sb[...] = jnp.where(lane < HEAD_DIM // 2, 0.0, sine)
        for h in (st.s, 1 - st.s):
            for k in range(st.nz):
                if h is st.s and k == 0:
                    continue
                st.copy(mine, mine, at, st.peer("s", 0), at + h * st.nz + k).wait_recv()
        for h in range(2):
            total = r.parts[h, 0]
            for k in range(1, st.nz):
                total = total + r.parts[h, k]
            r.small[h] = total
        for k in ORDER:
            qkv.pass_on(k)
    wout.start()
    gu.start()
    down.start()
    small = r.small[layer]
    n1 = (unit * small[:, :D]).astype(BF16)
    r.n1[...] = n1
    bias = small[:, 2 * D :]
    if first:
        qkv.finish()
    cos, sa, sb = r.cos[...], r.sa[...], r.sb[...]
    lin = mm(n1, r.wqkv[:, D:]) + bias[:, D:]
    r.kv[me] = jnp.concatenate([rope(lin[:, :LANES], cos, sa, sb), lin[:, LANES:]], 1).astype(BF16)

    def keys_copy(k, src):
        return push(r.kv.at[src], r.kv.at[src], r.csem.at[k], r.csem2.at[k], "ctx", lax.rem(me + k, n))

    def start(k, c):
        keys_copy(k, me).start()
        return c

    lax.fori_loop(1, n, start, 0)
    linq = mm(n1, r.wqkv[:, :D]) + bias[:, :D]
    for t in range(TILES):
        q = rope(linq[:, t * LANES : (t + 1) * LANES], cos, sa, sb) * HEAD_DIM ** (-0.5)
        spread(r.qst, t, q.T)
    r.m_s[...] = jnp.full(r.m_s.shape, NEG, F32)
    r.l_s[...] = jnp.zeros(r.l_s.shape, F32)
    r.acc_s[...] = jnp.zeros(r.acc_s.shape, F32)
    qpos = row_positions(r.pairs, me, n)

    def block(src):
        keys = r.kv[src, :, :LANES]
        vals_t = r.kv[src, :, LANES:].astype(F32).T.astype(BF16)
        hide = hidden_bias(r.pairs, src, qpos, n)
        for t in range(TILES):
            cols = slice(2 * t * LANES, 2 * (t + 1) * LANES)
            s = mm(keys, r.qst[:, cols]) + hide
            m_old = r.m_s[:, cols]
            m_new = jnp.maximum(m_old, jnp.max(s, 0, keepdims=True))
            p = jnp.exp(s - m_new)
            alpha = jnp.exp(m_old - m_new)
            r.m_s[:, cols] = m_new
            r.l_s[:, cols] = r.l_s[:, cols] * alpha + jnp.sum(p, 0, keepdims=True)
            r.acc_s[:, cols] = r.acc_s[:, cols] * alpha + mm(vals_t, p.astype(BF16))

    block(me)

    def step(k, c):
        src = lax.rem(me + n - k, n)
        keys_copy(k, src).wait_recv()
        if first:
            p = r.pairs.at[src]
            push(p, p, r.psem.at[k], r.psem2.at[k], "ctx", lax.rem(me + k, n)).wait_recv()
        block(src)
        return c

    low = 1
    for high, feed, k in ((5, wout, 1), (6, wout, 3), (9, wout, 2), (13, gu, 1), (14, gu, 3)):
        lax.fori_loop(low, high, step, 0)
        feed.pass_on(k)
        low = high
    lax.fori_loop(low, n, step, 0)
    r.lse[...] = r.m_s[...] + jnp.log(r.l_s[...])
    for t in range(TILES):
        cols = slice(2 * t * LANES, 2 * (t + 1) * LANES)
        wide = r.acc_s[:, cols] / r.l_s[:, cols]
        r.att[:, t * LANES : (t + 1) * LANES] = gathered_tile(wide, t).astype(BF16)
    wout.finish()
    mid = x + mm(r.att[...], r.wout[...])
    r.mid[...] = mid
    r2 = lax.rsqrt(jnp.mean(mid * mid, -1, keepdims=True) + EPS)
    r.n2[...] = (mid * r2 * small[:, D : 2 * D]).astype(BF16)
    gu.pass_on(2)
    gu.finish()
    down.finish()
    st.drain()

    def done(k, c):
        keys_copy(k, me).wait_send()
        if first:
            p = r.pairs.at[me]
            push(p, p, r.psem.at[k], r.psem2.at[k], "ctx", lax.rem(me + k, n)).wait_send()
        return c

    lax.fori_loop(1, n, done, 0)


def attn_bwd_kernel(layer, r):
    st = Stages(r)
    n, me = st.nc, st.c
    last = layer == 0
    st.hail(st.beside() + (st.upright() if last else []), ring=True)
    half = HEAD_DIM
    gm = r.gm[...]
    gmb = gm.astype(BF16)
    ga = mm_nt(gmb, r.wout[...])
    for t in range(TILES):
        tile = slice(t * LANES, (t + 1) * LANES)
        ga_t = ga[:, tile].T
        spread(r.gst_s, t, ga_t)
        prod = ga_t * r.att[:, tile].astype(F32).T
        r.delta_s[:, 2 * t * LANES : (2 * t + 1) * LANES] = jnp.sum(prod[:half], 0, keepdims=True)
        r.delta_s[:, (2 * t + 1) * LANES : (2 * t + 2) * LANES] = jnp.sum(prod[half:], 0, keepdims=True)
    r.gq_s[...] = jnp.zeros(r.gq_s.shape, F32)
    qpos = row_positions(r.pairs, me, n)
    st.met()
    f, sl, l1, t1 = (r.fa, r.fb), (r.sla, r.slb), (r.l1a, r.l1b), (r.t1a, r.t1b)
    swaps = [st.swap(f[h], sl[h]) for h in range(2)]
    if last:
        qswap = st.swap(r.q_before, r.sq)

    def block(src):
        keys = r.kv[src, :, :LANES]
        vals = r.kv[src, :, LANES:]
        keys_t = keys.astype(F32).T.astype(BF16)
        hide = hidden_bias(r.pairs, src, qpos, n)
        gk = jnp.zeros((LANES, LANES), F32)
        gv = jnp.zeros((LANES, LANES), F32)
        for t in range(TILES):
            cols = slice(2 * t * LANES, 2 * (t + 1) * LANES)
            qs, gs = r.qst[:, cols], r.gst_s[:, cols]
            p = jnp.exp(mm(keys, qs) + hide - r.lse[:, cols])
            ds = (p * (mm(vals, gs) - r.delta_s[:, cols])).astype(BF16)
            gv = gv + mm_nt(p.astype(BF16), gs)
            gk = gk + mm_nt(ds, qs)
            r.gq_s[:, cols] += mm(keys_t, ds)
        return jnp.concatenate([gk, gv], 1)

    def sum_copy(k):
        return push(r.send_s.at[k], r.land_s.at[k], r.csem.at[k], r.csem2.at[k], "ctx", lax.rem(me + k, n))

    def step(k, c):
        r.send_s[k] = block(lax.rem(me + k, n)).astype(BF16)
        sum_copy(k).start()
        return c

    lax.fori_loop(1, 6, step, 0)
    r1 = [None, None]
    for h in range(2):
        swapped_sum(st, swaps[h], f[h], sl[h])
        r1[h] = st.scatter(AXES[h][0], sl[h], l1[h])
    lax.fori_loop(6, 9, step, 0)
    if last:
        arrived(qswap)
        add_into(r.sq, [r.q_before.at[st.s], r.sq])
        zr = st.scatter("z", r.sq, r.zq)
    lax.fori_loop(9, n, step, 0)
    own = block(me)

    def take(k, total):
        sum_copy(k).wait_recv()
        return total + r.land_s[k].astype(F32)

    own = lax.fori_loop(1, n, take, own)
    cos, sa, sb = r.cos[...], r.sa[...], r.sb[...]
    for t in range(TILES):
        wide = r.gq_s[:, 2 * t * LANES : 2 * (t + 1) * LANES]
        gq = gathered_tile(wide, t) * HEAD_DIM ** (-0.5)
        r.glin_s[:, t * LANES : (t + 1) * LANES] = unrope(gq, cos, sa, sb).astype(BF16)
    r.glin_s[:, D : D + LANES] = unrope(own[:, :LANES], cos, sa, sb).astype(BF16)
    r.glin_s[:, D + LANES :] = own[:, LANES:].astype(BF16)
    gn1 = mm_nt(r.glin_s[...], r.wqkv[...])
    x = r.x[...]
    r1_ = lax.rsqrt(jnp.mean(x * x, -1, keepdims=True) + EPS)
    unit = x * r1_
    dg1 = jnp.sum(gn1 * unit, 0, keepdims=True)
    dz = gn1 * r.small[layer][:, :D]
    r.gx[...] = gm + r1_ * (dz - unit * jnp.mean(dz * unit, -1, keepdims=True))
    dbias = jnp.sum(r.glin_s[...].astype(F32), 0, keepdims=True)
    r.small_s[...] = jnp.zeros(r.small_s.shape, F32)
    row = 0
    for part in (dg1, r.dg2[...], dbias):
        for t in range(part.shape[1] // LANES):
            r.small_s[row : row + 1, :] = part[:, t * LANES : (t + 1) * LANES]
            row += 1
    small = r.small_s[...].astype(BF16)
    share = D // st.nz
    for j in range(0, QKV // LANES + TILES, 8):
        for t in range(j, j + 8):
            if t < QKV // LANES:
                d = mm_tn(r.n1[...], r.glin_s[:, t * LANES : (t + 1) * LANES])
            else:
                u = t - QKV // LANES
                d = mm_tn(r.att[...], gmb[:, u * LANES : (u + 1) * LANES])
            d = d.astype(BF16)
            for i in range(st.nz):
                r.q[j // 8, i, (t % 8) * share : (t % 8 + 1) * share, :] = d[i * share : (i + 1) * share, :]
        for i in range(st.nz):
            r.q[j // 8, i, 8 * share : 8 * share + 2 * UNIT, :] = small if j == 0 else jnp.zeros_like(small)
            r.q[j // 8, i, 8 * share + 2 * UNIT :, :] = jnp.zeros((Q_ROWS - 8 * share - 2 * UNIT, LANES), BF16)
    for h in range(2):
        arrived(r1[h])
        mine = sl[h].at[st.along(AXES[h][0], 0)]
        add_into(t1[h], [mine] + [l1[h].at[k] for k in range(SIDE - 1)])
    if last:
        arrived(zr)
        fold_z(st, r.sq, r.zq, (r.qpa, r.qpb))
    st.drain()

    def done(k, c):
        sum_copy(k).wait_send()
        return c

    lax.fori_loop(1, n, done, 0)


def fold_z(st, sq, zq, out):
    parts = [sq.at[st.z]] + [zq.at[k] for k in range(st.nz - 1)]
    rows = Q_ROWS // 2 // 16
    for h in range(2):
        for i in range(16):
            at = (h * 16 + i) * rows
            total = jnp.zeros((rows, LANES), F32)
            for p in parts:
                total = total + p[at : at + rows, :].astype(F32)
            out[h][i // SIDE, i % SIDE] = total.astype(BF16)


def ffn_fwd_kernel(layer, r):
    st = Stages(r)
    n, me = st.nz, st.z
    carry = layer == 0
    st.hail(st.upright(carry) + (st.beside() if carry else []))
    r.all[me] = r.n2[...]
    st.met()
    at = st.take(2 * n)

    def first(k):
        return st.copy(r.all.at[me], r.all.at[me], at + k, st.peer("z", k))

    def second(k):
        return st.copy(r.send_s.at[k], r.land_s.at[k], at + n + k, st.peer("z", -k))

    for k in ORDER:
        first(k).start()
    if carry:
        qkv = feed_rows(st, 1, r.wqkv_shard, r.wqkv)
        qkv.start()

    def block(src):
        a = r.all[src]
        gate = mm(a, r.gu[0])
        up = mm(a, r.gu[1])
        r.gate[src] = gate
        r.up[src] = up
        hidden = (gate * jax.nn.sigmoid(gate) * up).astype(BF16)
        return mm(hidden, r.down[...])

    r.y[...] = r.mid[...] + block(me)
    for k in ORDER:
        first(k).wait_recv()
        r.send_s[k] = block(st.along("z", -k)).astype(BF16)
        second(k).start()
        if carry and k == 3:
            qkv.pass_on(1)
            qkv.pass_on(3)
    if carry:
        qkv.pass_on(2)
    for k in ORDER:
        second(k).wait_recv()
        r.y[...] += r.land_s[k].astype(F32)
    for k in ORDER:
        first(k).wait_send()
        second(k).wait_send()
    if carry:
        qkv.finish()
    st.drain()


def ffn_bwd_kernel(layer, r):
    st = Stages(r)
    n, me = st.nz, st.z
    carry = layer == 0
    st.hail(st.upright() + (st.beside() + st.flat(True) if carry else []))
    tok = r.gy.shape[0]

    def rows_of(i):
        return pl.ds(pl.multiple_of(i * tok, tok), tok)

    r.all_s[rows_of(me), :] = r.gy[...].astype(BF16)
    st.met()
    at = st.take(2 * n)

    def first(k):
        mine = r.all_s.at[rows_of(me), :]
        return st.copy(mine, mine, at + k, st.peer("z", k))

    def second(k):
        return st.copy(r.send_s.at[k], r.land_s.at[k], at + n + k, st.peer("z", -k))

    for k in ORDER:
        first(k).start()
    if carry:
        rest = Rest(st, (r.t1a, r.t1b), (r.l2a, r.l2b), (r.t2a, r.t2b), (r.g1a, r.g1b), (r.ga, r.gb), 1)

    def block(src):
        rows = rows_of(src)
        gh = mm_nt(r.all_s[rows, :], r.down[...])
        gate, up = r.gate[src], r.up[src]
        sg = jax.nn.sigmoid(gate)
        act = gate * sg
        r.hid_s[rows, :] = (act * up).astype(BF16)
        ggate = (gh * up * sg * (1.0 + gate * (1.0 - sg))).astype(BF16)
        gup = (gh * act).astype(BF16)
        r.ggate_s[rows, :] = ggate
        r.gup_s[rows, :] = gup
        return mm_nt(ggate, r.gu[0]) + mm_nt(gup, r.gu[1])

    r.own_s[...] = block(me)
    for k in ORDER:
        if carry:
            rest.advance()
        first(k).wait_recv()
        r.send_s[k] = block(st.along("z", -k)).astype(BF16)
        second(k).start()

    refs = (r.fa, r.fb)
    share = D // n
    normed = jnp.concatenate([r.n2_all[i] for i in range(n)], 0)
    for section, part in ((0, r.ggate_s), (1, r.gup_s)):
        for j in range(WIN // (2 * LANES)):
            d = mm_tn(normed, part[:, 2 * j * LANES : 2 * (j + 1) * LANES]).astype(BF16)
            for t in (2 * j, 2 * j + 1):
                tile = d[:, (t % 2) * LANES : (t % 2 + 1) * LANES]
                for i in range(n):
                    base = [i * per * UNIT for per in GATE_PER]
                    put_units(refs, section, base, GATE_PER, t * (share // UNIT), tile[i * share : (i + 1) * share, :])
        used = WIN // LANES * (share // UNIT)
        extra = 16 * sum(GATE_PER) - used
        for i in range(n):
            base = [i * per * UNIT for per in GATE_PER]
            put_units(refs, section, base, GATE_PER, used, jnp.zeros((extra * UNIT, LANES), BF16))
    for j in range(WIN // (2 * LANES)):
        cols = slice(2 * j * LANES, 2 * (j + 1) * LANES)
        r.down_s[cols, :] = mm_tn(r.hid_s[:, cols], r.all_s[...]).astype(BF16)
    pad = (WIN - FF // n) * lax.rem(me, 2)
    half = FF // n // 2
    base = [n * per * UNIT for per in GATE_PER]
    for section in range(2):
        rows = r.down_s[pl.ds(pl.multiple_of(pad + section * half, UNIT), half), :]
        for t in range(TILES):
            put_units(refs, section, base, DOWN_PER, t * (half // UNIT), rows[:, t * LANES : (t + 1) * LANES])
        used = TILES * (half // UNIT)
        extra = 16 * sum(DOWN_PER) - used
        put_units(refs, section, base, DOWN_PER, used, jnp.zeros((extra * UNIT, LANES), BF16))

    for k in ORDER:
        second(k).wait_recv()
        r.own_s[...] += r.land_s[k].astype(F32)
    gn2 = r.own_s[...]
    mid = r.mid[...]
    r2 = lax.rsqrt(jnp.mean(mid * mid, -1, keepdims=True) + EPS)
    unit = mid * r2
    r.dg2[...] = jnp.sum(gn2 * unit, 0, keepdims=True)
    dz = gn2 * r.small[layer][:, D : 2 * D]
    r.gm[...] = r.gy[...] + r2 * (dz - unit * jnp.mean(dz * unit, -1, keepdims=True))
    for k in ORDER:
        first(k).wait_send()
        second(k).wait_send()
    if carry:
        rest.finish()
    st.drain()


class Rest:
    def __init__(self, st, t1, l2, t2, g1, out, layer):
        self.st, self.t1, self.l2, self.t2, self.g1, self.out, self.layer = st, t1, l2, t2, g1, out, layer
        self.stage = 0
        self.moving = [st.scatter(AXES[h][1], t1[h], l2[h]) for h in range(2)]

    def advance(self):
        st = self.st
        for h in range(2):
            second = AXES[h][1]
            arrived(self.moving[h])
            mine = self.g1[h].at[st.along(second, 0)]
            if self.stage == 0:
                t2 = self.t2[h]
                add_rows(t2, [self.t1[h].at[st.along(second, 0)]] + [self.l2[h].at[k] for k in range(SIDE - 1)])
                per = GATE_PER[h] * UNIT
                self.moving[h] = st.deal(t2, mine, per)
                mine[st.block(st.z, per), :] = t2[st.block(st.z, per), :]
                mine[st.nz * per :, :] = t2[st.nz * per :, :]
            elif self.stage == 1:
                self.moving[h] = st.gather(second, self.g1[h])
            else:
                self.moving[h] = st.hand_over(AXES[h][0], self.g1[h], self.out[h], self.layer)
        self.stage += 1

    def finish(self):
        for h in range(2):
            self.moving[h]()


def reduce_kernel(layer, r):
    st = Stages(r)
    st.hail(st.beside() + st.upright() + st.flat(True))
    st.met()
    rest = Rest(st, (r.t1a, r.t1b), (r.l2a, r.l2b), (r.t2a, r.t2b), (r.g1a, r.g1b), (r.ga, r.gb), 0)
    qswap = st.swap(r.q0, r.sq)
    qp = {1: (r.q1a, r.q1b), 0: (r.qpa, r.qpb)}
    land = {1: (r.m1a, r.m1b), 0: (r.m0a, r.m0b)}
    land2 = {1: (r.w1a, r.w1b), 0: (r.w0a, r.w0b)}
    part = {1: (r.e1a, r.e1b), 0: (r.e0a, r.e0b)}
    wide = {1: (r.h1a, r.h1b), 0: (r.h0a, r.h0b)}
    out = (r.qa, r.qb)
    moving = {}

    def along_first(l):
        moving[l] = [st.scatter(AXES[h][0], qp[l][h], land[l][h]) for h in range(2)]

    def along_second(l):
        for h in range(2):
            arrived(moving[l][h])
            own = qp[l][h].at[st.along(AXES[h][0], 0)]
            add_into(part[l][h], [own] + [land[l][h].at[k] for k in range(SIDE - 1)])
            moving[l][h] = st.scatter(AXES[h][1], part[l][h], land2[l][h])

    def back_second(l):
        for h in range(2):
            arrived(moving[l][h])
            i = st.along(AXES[h][1], 0)
            add_rows(wide[l][h].at[i], [part[l][h].at[i]] + [land2[l][h].at[k] for k in range(SIDE - 1)])
            moving[l][h] = st.gather(AXES[h][1], wide[l][h])

    def back_first(l):
        for h in range(2):
            arrived(moving[l][h])
            moving[l][h] = st.hand_over(AXES[h][0], wide[l][h], out[h], l)

    along_first(1)
    rest.advance()
    arrived(qswap)
    add_into(r.sq, [r.q0.at[st.s], r.sq])
    zr = st.scatter("z", r.sq, r.zq)
    rest.advance()
    along_second(1)
    rest.advance()
    back_second(1)
    arrived(zr)
    fold_z(st, r.sq, r.zq, qp[0])
    along_first(0)
    back_first(1)
    along_second(0)
    back_second(0)
    back_first(0)
    rest.finish()
    for l in (1, 0):
        for h in range(2):
            moving[l][h]()
    st.drain()


def call(kernel, layer, cid, name, ins, outs, scratch, sems, hbm=(), flops=10**10):
    names = list(ins) + list(outs) + list(scratch)
    dma = pltpu.SemaphoreType.DMA
    counts = dict(ssem=sems, rsem=sems, lsem=8, csem=16, csem2=16, psem=16, psem2=16)

    def body(*refs):
        kernel(layer, types.SimpleNamespace(**dict(zip(names + list(counts), refs))))

    vm = pl.BlockSpec(memory_space=pltpu.VMEM)
    anywhere = pl.BlockSpec(memory_space=pl.ANY)
    made = pl.pallas_call(
        body,
        out_shape=[jax.ShapeDtypeStruct(s, t) for s, t in outs.values()],
        in_specs=[anywhere if k in hbm else vm for k in ins],
        out_specs=[vm] * len(outs),
        scratch_shapes=[pltpu.VMEM(s, t) for s, t in scratch.values()] + [dma((k,)) for k in counts.values()],
        compiler_params=pltpu.CompilerParams(
            collective_id=cid, has_side_effects=True, vmem_limit_bytes=VMEM_LIMIT
        ),
        cost_estimate=pl.CostEstimate(flops=flops, bytes_accessed=20 * 2**20, transcendentals=0),
        name=name,
    )(*ins.values())
    return dict(zip(outs, made))


FA_ROWS = tuple((4 * g + d) * UNIT for g, d in zip(GATE_PER, DOWN_PER))
RQ = Q_ROWS // 2 // 16
SIDES = (SIDE, SIDE)
WIDE = HEADS * LANES


def bf(*shape):
    return (shape, BF16)


def f4(*shape):
    return (shape, F32)


def rest_scratch():
    made = {}
    for h, rows in zip("ab", FA_ROWS):
        made["l2" + h] = bf(SIDE - 1, rows, LANES)
        made["t2" + h] = bf(rows, LANES)
        made["g1" + h] = bf(SIDE, rows, LANES)
    return made


def rest_outs():
    return {"g" + h: bf(2, *SIDES, rows, LANES) for h, rows in zip("ab", FA_ROWS)}


def assemble_kernel(nz, *refs):
    given, outs, held, sem = (refs[:2], refs[2:4]), refs[6:12], refs[12:14] + refs[4:6], refs[14]
    s = lax.axis_index("section")
    for layer in range(2):
        @pl.when(s == layer)
        def _():
            copies = [pltpu.make_async_copy(a, b, sem.at[i]) for i, (a, b) in enumerate(zip(given[layer], held))]
            for c in copies:
                c.start()
            for c in copies:
                c.wait()

    gate_ref, up_ref, down_ref, qkv_ref, out_ref, small_ref = outs
    share = D // nz
    starts = window_starts(nz)

    def units(refs, section, base, per, first, count):
        rows = []
        for part, piece, slot, _, m in unit_runs(first, count, per):
            at = base[part] + slot * UNIT
            rows.append(refs[part][section, piece // SIDE, piece % SIDE, at : at + m * UNIT, :].astype(F32))
        return jnp.concatenate(rows, 0) if len(rows) > 1 else rows[0]

    for section, ref in ((0, gate_ref), (1, up_ref)):
        tiles = {}
        for w, a in enumerate(starts):
            for t in range(WIN // LANES):
                tiles.setdefault(a // LANES + t, []).append((w, t))
        for col, sources in tiles.items():
            total = None
            for w, t in sources:
                base = [w * per * UNIT for per in GATE_PER]
                got = units(held[:2], section, base, GATE_PER, t * (share // UNIT), share // UNIT)
                total = got if total is None else total + got
            ref[:, col * LANES : (col + 1) * LANES] = total
    base = [nz * per * UNIT for per in GATE_PER]
    half = FF // nz // 2
    for section in range(2):
        for t in range(TILES):
            got = units(held[:2], section, base, DOWN_PER, t * (half // UNIT), half // UNIT)
            down_ref[section * half : (section + 1) * half, t * LANES : (t + 1) * LANES] = got
    for t in range(QKV // LANES + TILES):
        got = units(held[2:], t // 8, (0, 0), Q_PER, (t % 8) * (share // UNIT), share // UNIT)
        if t < QKV // LANES:
            qkv_ref[:, t * LANES : (t + 1) * LANES] = got
        else:
            u = t - QKV // LANES
            out_ref[:, u * LANES : (u + 1) * LANES] = got
    small_ref[...] = units(held[2:], 0, (0, 0), Q_PER, 8 * (share // UNIT), 2)


def assemble(zero, one, attn):
    nz = lax.axis_size("fsdp")
    vm = pl.BlockSpec(memory_space=pltpu.VMEM)
    anywhere = pl.BlockSpec(memory_space=pl.ANY)
    share = D // nz
    shapes = [(share, FF), (share, FF), (FF // nz, D), (share, QKV), (share, D), (2 * UNIT, LANES)]
    return pl.pallas_call(
        functools.partial(assemble_kernel, nz),
        out_shape=[jax.ShapeDtypeStruct(a, F32) for a in shapes],
        in_specs=[anywhere] * 4 + [vm] * 2,
        out_specs=[vm] * len(shapes),
        scratch_shapes=[pltpu.VMEM(a.shape, a.dtype) for a in zero] + [pltpu.SemaphoreType.DMA((2,))],
        compiler_params=pltpu.CompilerParams(vmem_limit_bytes=VMEM_LIMIT),
        name="assemble",
    )(*zero, *one, *attn)


def window_starts(n):
    share = FF // n
    return [(i * share // LANES) * LANES for i in range(n)]


def attn_fwd(layer, x, shards, small, pair, pairs, tabs, wqkv):
    n, nz = lax.axis_size("ctx"), lax.axis_size("fsdp")
    tok = x.shape[0]
    ins = dict(x=x, wout_shard=shards["out"], gate_shard=shards["gate"], up_shard=shards["up"], down_shard=shards["down"])
    outs = dict(
        mid=f4(tok, D), n2=bf(tok, D), n1=bf(tok, D), qst=bf(LANES, WIDE), kv=bf(n, tok, 2 * LANES), lse=f4(1, WIDE),
        att=bf(tok, D), wout=bf(D, D), gu=bf(2, D, WIN), down=bf(WIN, D),
    )
    scratch = dict(m_s=f4(1, WIDE), l_s=f4(1, WIDE), acc_s=f4(LANES, WIDE))
    if layer == 0:
        freq = jnp.arange(HEAD_DIM // 2, dtype=F32)
        inverse = jnp.tile(THETA ** (-2.0 * freq / HEAD_DIM), 4)[None, :]
        ins.update(wqkv_shard=shards["qkv"], small_own=small, pair=pair, inverse=inverse)
        outs.update(
            wqkv=bf(D, QKV), small=f4(2, 1, SMALL), pairs=((n, 8, LANES), jnp.int32),
            cos=f4(tok, LANES), sa=f4(tok, LANES), sb=f4(tok, LANES),
        )
        scratch.update(parts=f4(2, nz, 1, SMALL))
    else:
        ins.update(wqkv=wqkv, small=small, pairs=pairs, cos=tabs[0], sa=tabs[1], sb=tabs[2])
    hbm = ("wout_shard", "gate_shard", "up_shard", "down_shard", "wqkv_shard")
    return call(attn_fwd_kernel, layer, 1 + layer, f"attn_fwd_{layer}", ins, outs, scratch, 64, hbm)


def ffn_fwd(layer, a, qkv_shard):
    n = lax.axis_size("fsdp")
    tok = a["n2"].shape[0]
    ins = {k: a[k] for k in ("n2", "mid", "gu", "down")}
    outs = dict(y=f4(tok, D), all=bf(n, tok, D), gate=f4(n, tok, WIN), up=f4(n, tok, WIN))
    if layer == 0:
        ins.update(wqkv_shard=qkv_shard)
        outs.update(wqkv=bf(D, QKV))
    scratch = dict(send_s=bf(n, tok, D), land_s=bf(n, tok, D))
    return call(ffn_fwd_kernel, layer, 3 + layer, f"ffn_fwd_{layer}", ins, outs, scratch, 32, ("wqkv_shard",))


def ffn_bwd(layer, gy, a, f, small, before):
    n = lax.axis_size("fsdp")
    tok = gy.shape[0]
    ins = dict(gy=gy, mid=a["mid"], small=small, gu=a["gu"], down=a["down"], gate=f["gate"], up=f["up"], n2_all=f["all"])
    outs = dict(gm=f4(tok, D), dg2=f4(1, D))
    for h, rows in zip("ab", FA_ROWS):
        outs["f" + h] = bf(2, *SIDES, rows, LANES)
    scratch = dict(
        all_s=bf(n * tok, D), hid_s=bf(n * tok, WIN), ggate_s=bf(n * tok, WIN), gup_s=bf(n * tok, WIN), down_s=bf(WIN, D),
        own_s=f4(tok, D), send_s=bf(n, tok, D), land_s=bf(n, tok, D),
    )
    if layer == 0:
        ins.update(t1a=before["t1a"], t1b=before["t1b"])
        outs.update(rest_outs())
        scratch.update(rest_scratch())
    return call(ffn_bwd_kernel, layer, 5 + layer, f"ffn_bwd_{layer}", ins, outs, scratch, 64, flops=2 * 10**10)


def attn_bwd(layer, x, a, b, wqkv, small, pairs, tabs, before):
    n, nz = lax.axis_size("ctx"), lax.axis_size("fsdp")
    tok = x.shape[0]
    ins = dict(
        gm=b["gm"], dg2=b["dg2"], fa=b["fa"], fb=b["fb"], x=x, wqkv=wqkv, small=small, pairs=pairs,
        cos=tabs[0], sa=tabs[1], sb=tabs[2],
    )
    ins.update({k: a[k] for k in ("wout", "qst", "kv", "lse", "att", "n1")})
    outs = dict(gx=f4(tok, D), q=bf(2, nz, Q_ROWS, LANES))
    scratch = dict(
        gst_s=bf(LANES, WIDE), delta_s=f4(1, WIDE), gq_s=f4(LANES, WIDE), glin_s=bf(tok, QKV), small_s=f4(2 * UNIT, LANES),
        send_s=bf(n, tok, 2 * LANES), land_s=bf(n, tok, 2 * LANES),
    )
    for h, rows in zip("ab", FA_ROWS):
        outs["t1" + h] = bf(SIDE, rows, LANES)
        scratch["sl" + h] = bf(*SIDES, rows, LANES)
        scratch["l1" + h] = bf(SIDE - 1, SIDE, rows, LANES)
    if layer == 0:
        ins.update(q_before=before["q"])
        scratch.update(sq=bf(nz, Q_ROWS, LANES), zq=bf(nz - 1, Q_ROWS, LANES))
        outs.update(qpa=bf(*SIDES, RQ, LANES), qpb=bf(*SIDES, RQ, LANES))
    return call(attn_bwd_kernel, layer, 7 + layer, f"attn_bwd_{layer}", ins, outs, scratch, 32, flops=2 * 10**10)


def reduce_rest(last):
    nz = lax.axis_size("fsdp")
    ins = dict(t1a=last["t1a"], t1b=last["t1b"], q0=last["q"], q1a=last["qpa"], q1b=last["qpb"])
    outs = rest_outs()
    scratch = rest_scratch()
    scratch.update(sq=bf(nz, Q_ROWS, LANES), zq=bf(nz - 1, Q_ROWS, LANES), qpa=bf(*SIDES, RQ, LANES), qpb=bf(*SIDES, RQ, LANES))
    for h in "ab":
        outs["q" + h] = bf(2, *SIDES, RQ, LANES)
        for l in "01":
            scratch["m" + l + h] = bf(SIDE - 1, SIDE, RQ, LANES)
            scratch["w" + l + h] = bf(SIDE - 1, RQ, LANES)
            scratch["e" + l + h] = bf(SIDE, RQ, LANES)
            scratch["h" + l + h] = bf(SIDE, RQ, LANES)
    return call(reduce_kernel, 0, 9, "reduce", ins, outs, scratch, 128)


def local(
    tokens, cotangent, pair_of, attn_gain, ffn_gain, qkv_weight, qkv_bias, out_weight, gate_weight, up_weight, down_weight,
):
    s = lax.axis_index("section")
    z = lax.axis_index("fsdp")
    nz = lax.axis_size("fsdp")
    qd = D // nz
    shards = dict(qkv=qkv_weight, out=out_weight, gate=gate_weight, up=up_weight, down=down_weight)

    def placed(part, size):
        whole = jnp.zeros((1, size), F32)
        return lax.dynamic_update_slice(whole, part.astype(F32), (0, z * part.shape[1]))

    small_own = jnp.concatenate([placed(attn_gain, D), placed(ffn_gain, D), placed(qkv_bias, QKV)], 1)
    pair = jnp.broadcast_to(pair_of.reshape(1, 1), (8, LANES))
    x0 = jnp.where(s == 0, tokens[0, 0], tokens[1, 0])
    a0 = attn_fwd(0, x0, shards, small_own, pair, None, None, None)
    small, pairs, tabs = a0["small"], a0["pairs"], (a0["cos"], a0["sa"], a0["sb"])
    f0 = ffn_fwd(0, a0, qkv_weight)
    x1 = f0["y"].astype(BF16).astype(F32)
    a1 = attn_fwd(1, x1, shards, small, None, pairs, tabs, f0["wqkv"])
    f1 = ffn_fwd(1, a1, None)

    gy = jnp.where(s == 0, cotangent[0, 0], cotangent[1, 0])
    b1 = ffn_bwd(1, gy, a1, f1, small, None)
    c1 = attn_bwd(1, x1, a1, b1, f0["wqkv"], small, pairs, tabs, None)
    gy = c1["gx"].astype(BF16).astype(F32)
    b0 = ffn_bwd(0, gy, a0, f0, small, c1)
    c0 = attn_bwd(0, x0, a0, b0, a0["wqkv"], small, pairs, tabs, c1)
    t = reduce_rest(c0)
    dgate, dup, ddown, dqkv, dout, small_grad = assemble((t["ga"], t["gb"]), (b0["ga"], b0["gb"]), (t["qa"], t["qb"]))
    small_grad = small_grad.reshape(-1)

    def mine(first, size):
        return lax.dynamic_slice_in_dim(small_grad, first + z * size, size, 0)[None]

    def by_layer(pair):
        theirs = jnp.where(s == 0, pair[1], pair[0])
        mine = jnp.where(s == 0, pair[0], pair[1])
        got = lax.ppermute(theirs, "section", [(0, 1), (1, 0)])
        return jnp.where(s == 0, jnp.stack([mine, got]), jnp.stack([got, mine]))[None, :, None]

    return (
        by_layer((f0["y"], f1["y"])),
        by_layer((c0["gx"], c1["gx"])),
        mine(0, qd),
        mine(D, qd),
        dqkv[None],
        mine(2 * D, QKV // nz),
        dout[None],
        dgate[None],
        dup[None],
        ddown[None],
    )


def solution(mesh):
    return jax.shard_map(
        local,
        mesh=mesh,
        in_specs=(
            P(None, "fsdp", "ctx", None),
            P(None, "fsdp", "ctx", None),
            P("ctx"),
            P("section", "fsdp"),
            P("section", "fsdp"),
            P("section", "fsdp", None),
            P("section", "fsdp"),
            P("section", "fsdp", None),
            P("section", "fsdp", None),
            P("section", "fsdp", None),
            P("section", "fsdp", None),
        ),
        out_specs=(
            P("section", None, "fsdp", "ctx", None),
            P("section", None, "fsdp", "ctx", None),
            P("section", "fsdp"),
            P("section", "fsdp"),
            P("section", "fsdp", None),
            P("section", "fsdp"),
            P("section", "fsdp", None),
            P("section", "fsdp", None),
            P("section", "fsdp", None),
            P("section", "fsdp", None),
        ),
        check_vma=False,
    )
```

```python
import functools
import types

import jax
import jax.numpy as jnp
from jax import lax
from jax.experimental import pallas as pl
from jax.experimental.pallas import tpu as pltpu
from jax.sharding import PartitionSpec as P

D = 896
HEADS = 14
KV_HEADS = 2
HEAD_DIM = 64
GROUP = HEADS // KV_HEADS
FF = 4864
QKV = 1152
EPS = 1e-06
THETA = 1000000.0
LANES = 128
TILES = D // LANES
WIN = 1280
NEG = -1e30
F32 = jnp.float32
BF16 = jnp.bfloat16
MESH = pl.DeviceIdType.MESH
VMEM_LIMIT = 56 * 2**20
UNIT = 16
SIDE = 4
GATE_PER = (5, 4)
DOWN_PER = (8, 9)
Q_PER = (4, 4)
Q_ROWS = 16 * sum(Q_PER) * UNIT


def mm(a, b):
    return jnp.dot(a, b, preferred_element_type=F32)


def mm_nt(a, b):
    return lax.dot_general(a, b, (((1,), (1,)), ((), ())), preferred_element_type=F32)


def mm_tn(a, b):
    return lax.dot_general(a, b, (((0,), (0,)), ((), ())), preferred_element_type=F32)


ORDER = (1, 3, 2)
SMALL = 2 * D + QKV
AXES = (("x", "y"), ("y", "x"))
BATCH = 3
GROUPS = tuple(slice(a, min(a + 2 * LANES, HEADS * HEAD_DIM)) for a in range(0, HEADS * HEAD_DIM, 2 * LANES))


def push(src, dst, ssem, rsem, axis, to):
    return pltpu.make_async_remote_copy(
        src_ref=src,
        dst_ref=dst,
        send_sem=ssem,
        recv_sem=rsem,
        device_id={axis: to},
        device_id_type=MESH,
    )


def rope(u, cos, sa, sb):
    return u * cos + pltpu.roll(u, 96, 1) * sa + pltpu.roll(u, 32, 1) * sb


def unrope(u, cos, sa, sb):
    return u * cos - pltpu.roll(u, 96, 1) * sa - pltpu.roll(u, 32, 1) * sb


def halves(a0, a1):
    lane = lax.broadcasted_iota(jnp.int32, a0.shape, 1) < HEAD_DIM
    low = jnp.where(lane, a0, pltpu.roll(a1, HEAD_DIM, 1))
    high = jnp.where(lane, pltpu.roll(a0, HEAD_DIM, 1), a1)
    return low, high


def spread(ref, t, tile_t):
    half = HEAD_DIM
    zero = jnp.zeros((half, LANES), F32)
    cols = slice(t * LANES, (t + 1) * LANES)
    for g in range(KV_HEADS):
        pair = [tile_t[j * half : (j + 1) * half, :] if (2 * t + j) // GROUP == g else zero for j in range(2)]
        for part, content in enumerate(halves(*pair)):
            ref[part * LANES + g * half : part * LANES + (g + 1) * half, cols] = content.astype(BF16)


def gathered_tile(wide, t):
    half = HEAD_DIM
    rows = []
    for j in range(2):
        g = (2 * t + j) // GROUP
        low = wide[g * half : (g + 1) * half, :]
        high = wide[LANES + g * half : LANES + (g + 1) * half, :]
        rows.append(halves(low, high)[j])
    return jnp.concatenate(rows, 0)


def dealt(a_per, b_per):
    where = [(0, u // a_per, u % a_per) for u in range(16 * a_per)]
    return where + [(1, v // b_per, v % b_per) for v in range(16 * b_per)]


def unit_runs(first, count, per):
    where = dealt(*per)
    found = []
    for i in range(count):
        part, piece, slot = where[first + i]
        if found and found[-1][0] == part and found[-1][1] == piece:
            found[-1][4] += 1
        else:
            found.append([part, piece, slot, i, 1])
    return found


def put_units(refs, section, base, per, first, rows):
    for part, piece, slot, i, m in unit_runs(first, rows.shape[0] // UNIT, per):
        at = base[part] + slot * UNIT
        refs[part][section, piece // SIDE, piece % SIDE, at : at + m * UNIT, :] = rows[i * UNIT : (i + m) * UNIT, :]


class Stages:
    def __init__(self, r):
        self.s = lax.axis_index("section")
        self.c = lax.axis_index("ctx")
        self.nc = lax.axis_size("ctx")
        self.x, self.y = self.c // SIDE, lax.rem(self.c, SIDE)
        self.z = lax.axis_index("fsdp")
        self.nz = lax.axis_size("fsdp")
        self.ssem, self.rsem, self.lsem = r.ssem, r.rsem, r.lsem
        self.used = 0
        self.local_used = 0
        self.sent = []

    def along(self, axis, k):
        own, n = {
            "x": (self.x, SIDE),
            "y": (self.y, SIDE),
            "z": (self.z, self.nz),
            "c": (self.c, self.nc),
        }[axis]
        return lax.rem(own + n + k, n)

    def peer(self, axis, k, section=None):
        if axis == "s":
            return {"section": 1 - self.s}
        if axis == "z":
            to = {"fsdp": self.along("z", k)}
        elif axis == "c":
            to = {"ctx": self.along("c", k)}
        elif axis == "x":
            to = {"ctx": self.along("x", k) * SIDE + self.y}
        else:
            to = {"ctx": self.x * SIDE + self.along("y", k)}
        if section is not None:
            to["section"] = section
        return to

    def hail(self, ids, ring=False):
        bar = pltpu.get_barrier_semaphore()
        for i in ids:
            pl.semaphore_signal(bar, inc=1, device_id=i, device_id_type=MESH)
        self.expected = len(ids)
        if ring:
            def one(k, c):
                pl.semaphore_signal(bar, inc=1, device_id=self.peer("c", k), device_id_type=MESH)
                return c

            lax.fori_loop(1, self.nc, one, 0)
            self.expected += self.nc - 1
        self.bar = bar

    def met(self):
        pl.semaphore_wait(self.bar, self.expected)

    def beside(self):
        return [self.peer("s", 0)]

    def upright(self, both=False):
        ids = [self.peer("z", k) for k in range(1, self.nz)]
        return ids + ([self.peer("z", k, 1 - self.s) for k in range(1, self.nz)] if both else [])

    def flat(self, both=False):
        ids = [self.peer(a, k) for a in "xy" for k in range(1, SIDE)]
        return ids + ([self.peer(a, k, 1 - self.s) for a in "xy" for k in range(1, SIDE)] if both else [])

    def take(self, count):
        self.used += count
        return self.used - count

    def copy(self, src, dst, at, to, recv_at=None):
        return pltpu.make_async_remote_copy(
            src_ref=src,
            dst_ref=dst,
            send_sem=self.ssem.at[at],
            recv_sem=self.rsem.at[at if recv_at is None else recv_at],
            device_id=to,
            device_id_type=MESH,
        )

    def begin(self, copies):
        for c in copies:
            c.start()
        self.sent += copies
        return copies

    def drain(self):
        for c in self.sent:
            c.wait_send()

    def swap(self, src, land):
        return self.begin([self.copy(src.at[1 - self.s], land, self.take(1), self.peer("s", 0))])

    def scatter(self, axis, src, land):
        n = self.nz if axis == "z" else SIDE
        at = self.take(n - 1)
        return self.begin(
            [self.copy(src.at[self.along(axis, k)], land.at[k - 1], at + k - 1, self.peer(axis, k)) for k in range(1, n)]
        )

    def gather(self, axis, ref):
        at = self.take(SIDE - 1)
        mine = ref.at[self.along(axis, 0)]
        return self.begin([self.copy(mine, mine, at + k - 1, self.peer(axis, k)) for k in range(1, SIDE)])

    def deal(self, src, dst, rows):
        at = self.take(self.nz - 1)
        mine = dst.at[self.block(self.z, rows), :]
        return self.begin(
            [
                self.copy(src.at[self.block(self.along("z", k), rows), :], mine, at + k - 1, self.peer("z", k))
                for k in range(1, self.nz)
            ]
        )

    def block(self, i, rows):
        return pl.ds(pl.multiple_of(i * rows, UNIT), rows)

    def aside(self, j):
        x = lax.rem(self.x + (1 - self.s) * j, SIDE)
        y = lax.rem(self.y + self.s * j, SIDE)
        return {"ctx": x * SIDE + y}

    def quarter(self):
        return self.x * (1 - self.s) + self.y * self.s

    def hand_over(self, axis, src, dst, layer):
        at = self.take(2 * SIDE)
        mine = dst.at[self.s, self.along(axis, 0)]
        self.begin(
            [
                self.copy(src, mine, at + k, self.peer(axis, k, layer), at + self.s * SIDE + k)
                for k in range(1, SIDE)
            ]
        )
        beside = self.copy(src, mine, at, {"section": layer}, at + self.s * SIDE)
        within = pltpu.make_async_copy(src, mine, self.lsem.at[self.local_used])
        self.local_used += 1

        @pl.when(self.s != layer)
        def _():
            beside.start()

        @pl.when(self.s == layer)
        def _():
            within.start()

        def finish():
            @pl.when(self.s == layer)
            def _():
                within.wait()
                for half in range(2):
                    for k in range(0 if half != layer else 1, SIDE):
                        self.copy(src, mine, at, {"section": layer}, at + half * SIDE + k).wait_recv()

            @pl.when(self.s != layer)
            def _():
                beside.wait_send()

        return finish


class Feed:
    def __init__(self, st, layer, sources, piece, band):
        self.st, self.layer, self.sources, self.piece, self.band = st, layer, sources, piece, band
        steps = st.nz - 1
        self.across = st.take(2 * steps)
        self.sideways = st.take((SIDE - 1) * steps)
        self.passed = st.take(steps)
        self.own = st.take(2)

    def beside(self, h):
        b = self.band(self.st.z, h)
        return self.st.copy(b, b, self.own + h, self.st.peer("s", 0))

    def send(self, h, k, src):
        st = self.st
        dst = self.piece(st.z, h, (st.x, st.y)[h])
        return st.copy(dst if src is None else src, dst, self.across + 2 * (k - 1) + h, st.peer("z", k, h))

    def start(self):
        st = self.st

        @pl.when(st.s == self.layer)
        def _():
            for k in ORDER:
                for h in range(2):
                    for needed, src in self.sources(h, (st.x, st.y)[h], st.along("z", k)):
                        if needed is None:
                            self.send(h, k, src).start()
                        else:
                            pl.when(needed)(self.send(h, k, src).start)
            for h in range(2):
                self.beside(h).start()

    def relay(self, k):
        st = self.st
        p = self.piece(st.along("z", -k), st.s, st.quarter())
        st.copy(p, p, self.across + 2 * (k - 1) + st.s, st.peer("s", 0)).wait_recv()
        at = self.sideways + (SIDE - 1) * (k - 1) - 1
        st.begin([st.copy(p, p, at + j, st.aside(j)) for j in range(1, SIDE)])

    def collect(self, k):
        st = self.st
        z = st.along("z", -k)
        at = self.sideways + (SIDE - 1) * (k - 1) - 1
        for j in range(1, SIDE):
            p = self.piece(z, st.s, lax.rem(st.quarter() + SIDE - j, SIDE))
            st.copy(p, p, at + j, st.aside(j)).wait_recv()
        b = self.band(z, st.s)
        st.begin([st.copy(b, b, self.passed + k - 1, st.peer("s", 0))])

    def finish(self):
        st = self.st
        for k in ORDER:
            b = self.band(st.along("z", -k), 1 - st.s)
            st.copy(b, b, self.passed + k - 1, st.peer("s", 0)).wait_recv()

        @pl.when(st.s == self.layer)
        def _():
            for h in range(2):
                for k in ORDER:
                    self.send(h, k, None).wait_send()
                self.beside(h).wait_send()

        @pl.when(st.s != self.layer)
        def _():
            for h in range(2):
                self.beside(h).wait_recv()


class FeedDown:
    def __init__(self, st, layer, src, dst):
        self.st, self.layer = st, layer
        share = src.shape[1]
        spare = WIN - share
        odd = lax.rem(st.z, 2)
        place = dst.at[pl.ds(pl.multiple_of(odd * spare, UNIT), share), :]
        dst[pl.ds(pl.multiple_of((1 - odd) * share, UNIT), spare), :] = jnp.zeros((spare, D), BF16)
        self.local = pltpu.make_async_copy(src.at[0], place, st.lsem.at[st.local_used])
        st.local_used += 1
        self.remote = st.copy(src.at[0], place, st.take(1), st.peer("s", 0))

    def start(self):
        @pl.when(self.st.s == self.layer)
        def _():
            self.local.start()
            self.remote.start()

    def finish(self):
        @pl.when(self.st.s == self.layer)
        def _():
            self.local.wait()
            self.remote.wait_send()

        @pl.when(self.st.s != self.layer)
        def _():
            self.remote.wait_recv()


class Local:
    def __init__(self, st, layer, pairs):
        self.st, self.layer = st, layer
        self.copies = [pltpu.make_async_copy(a, b, st.lsem.at[st.local_used + i]) for i, (a, b) in enumerate(pairs)]
        st.local_used += len(pairs)

        @pl.when(st.s == layer)
        def _():
            for c in self.copies:
                c.start()

    def wait(self):
        @pl.when(self.st.s == self.layer)
        def _():
            for c in self.copies:
                c.wait()


def half_rows(z, h, share):
    return pl.ds(pl.multiple_of(z * share + h * (share // 2), UNIT), share // 2)


def feed_attention(st, layer, qkv, out, dst):
    share = qkv.shape[1]
    rows = st.block(st.z, share)
    local = Local(st, layer, [(qkv.at[0], dst.at[rows, :QKV]), (out.at[0], dst.at[rows, QKV:])])
    width = (QKV + D) // SIDE

    def piece(z, h, q):
        return dst.at[half_rows(z, h, share), pl.ds(pl.multiple_of(q * width, LANES), width)]

    def band(z, h):
        return dst.at[half_rows(z, h, share), :]

    return local, Feed(st, layer, lambda h, q, z_to: [(None, None)], piece, band)


def feed_windows(st, layer, gate, up, dst):
    share = gate.shape[1]
    pace = FF // st.nz // (LANES // 2)
    width = WIN // 2

    def window(z):
        return pl.multiple_of(z * pace // 2 * LANES, LANES)

    rows = st.block(st.z, share)
    local = Local(st, layer, [(w.at[0, :, pl.ds(window(st.z), WIN)], dst.at[i, rows, :]) for i, w in enumerate((gate, up))])

    def sources(h, q, z_to):
        at = pl.multiple_of(window(z_to) + lax.rem(q, 2) * width, LANES)
        part = slice(h * (share // 2), (h + 1) * (share // 2))
        return [(q < 2, gate.at[0, part, pl.ds(at, width)]), (q >= 2, up.at[0, part, pl.ds(at, width)])]

    def piece(z, h, q):
        return dst.at[q // 2, half_rows(z, h, share), pl.ds(pl.multiple_of(lax.rem(q, 2) * width, LANES), width)]

    def band(z, h):
        return dst.at[:, half_rows(z, h, share), :]

    return local, Feed(st, layer, sources, piece, band)


def arrived(copies):
    for c in copies:
        c.wait_recv()


def add_into(dst, parts):
    def one(i, c):
        total = parts[0][i].astype(F32)
        for p in parts[1:]:
            total = total + p[i].astype(F32)
        dst[i] = total.astype(dst.dtype)
        return c

    lax.fori_loop(0, dst.shape[0], one, 0)


def add_rows(dst, parts):
    total = parts[0][...].astype(F32)
    for p in parts[1:]:
        total = total + p[...].astype(F32)
    dst[...] = total.astype(dst.dtype)


def swapped_sum(st, copies, given, land):
    arrived(copies)
    for i in range(SIDE):
        add_into(land.at[i], [given.at[st.s, i], land.at[i]])


def sides(tile, chosen):
    half = HEAD_DIM
    low, high = tile[:half], tile[half:]
    zero = jnp.zeros_like(low)
    below = jnp.concatenate([jnp.where(chosen, low, zero), jnp.where(chosen, zero, high)], 1)
    return jnp.concatenate([jnp.concatenate([zero, low], 1), below], 0).astype(BF16)


def sides_t(tile_t, chosen):
    lane = lax.broadcasted_iota(jnp.int32, tile_t.shape, 1) < HEAD_DIM
    upper = jnp.where(jnp.logical_or(lane, jnp.logical_not(chosen)), 0.0, pltpu.roll(tile_t, HEAD_DIM, 1))
    lower = jnp.where(jnp.logical_or(lane, jnp.logical_not(chosen)), tile_t, 0.0)
    return jnp.concatenate([upper, lower], 0).astype(BF16)


def own_sides(tile):
    low, high = tile[:HEAD_DIM], tile[HEAD_DIM:]
    zero = jnp.zeros_like(low)
    rows = [[zero, low], [low, zero], [zero, high]]
    return jnp.concatenate([jnp.concatenate(p, 1) for p in rows], 0).astype(BF16)


def own_bias(width):
    key = lax.broadcasted_iota(jnp.int32, (HEAD_DIM, width), 0)
    query = lax.rem(lax.broadcasted_iota(jnp.int32, (HEAD_DIM, width), 1), HEAD_DIM)
    return jnp.where(key <= query, 0.0, NEG)


def earlier(pairs_ref, src, me, width):
    return pairs_ref[src, 0:1, :width] < pairs_ref[me, 0:1, :width]


def col_max(a):
    return jnp.max(a, 0, keepdims=True)


def col_sum(a):
    return jnp.sum(a, 0, keepdims=True)


def attn_fwd_kernel(layer, r):
    st = Stages(r)
    n, me = st.nc, st.c
    st.hail(st.beside() + st.upright(True), ring=True)
    first = layer == 0
    r.load()
    if first:
        wa_local, wa = feed_attention(st, layer, r.wqkv_shard, r.wout_shard, r.wa)
    gu_local, gu = feed_windows(st, layer, r.gate_shard, r.up_shard, r.gu)
    down = FeedDown(st, layer, r.down_shard, r.down)
    r.need("x")
    x = r.x[...]
    r1 = lax.rsqrt(jnp.mean(x * x, -1, keepdims=True) + EPS)
    unit = x * r1
    if first:
        r.need("pair", "small_own", "inverse")
        r.pairs[me] = jnp.broadcast_to(r.pair[...], r.pairs.shape[1:])
        r.parts[st.s, st.z] = r.small_own[...]
        wa_local.wait()
    gu_local.wait()
    st.met()
    if first:
        wa.start()
        at = st.take(2 * st.nz)
        mine = r.parts.at[st.s, st.z]
        st.begin(
            [st.copy(mine, mine, at + k, st.peer("z", k, st.s), at + st.s * st.nz + k) for k in range(1, st.nz)]
            + [st.copy(mine, mine, at + st.nz + k, st.peer("z", k, 1 - st.s), at + st.s * st.nz + k) for k in range(1, st.nz)]
            + [st.copy(mine, mine, at, st.peer("s", 0), at + st.s * st.nz)]
        )

        def tell(k, c):
            p = r.pairs.at[me]
            push(p, p, r.psem.at[k], r.psem2.at[k], "ctx", lax.rem(me + k, n)).start()
            return c

        lax.fori_loop(1, n, tell, 0)
        block = LANES // 2
        i = lax.broadcasted_iota(jnp.int32, (LANES, LANES), 0)
        pair = r.pairs[me, 0:1, :LANES]
        pos = jnp.where(i < block, pair * block + i, (2 * n - 1 - pair) * block + i - block)
        angle = pos.astype(F32) * r.inverse[...]
        lane = lax.rem(lax.broadcasted_iota(jnp.int32, (LANES, LANES), 1), HEAD_DIM)
        sine = jnp.sin(angle)
        r.cos[...] = jnp.cos(angle)
        r.sa[...] = jnp.where(lane < HEAD_DIM // 2, -sine, 0.0)
        r.sb[...] = jnp.where(lane < HEAD_DIM // 2, 0.0, sine)
        r.flush("cos", "sa", "sb")
        for h in (st.s, 1 - st.s):
            for k in range(st.nz):
                if h is st.s and k == 0:
                    continue
                st.copy(mine, mine, at, st.peer("s", 0), at + h * st.nz + k).wait_recv()
        for h in range(2):
            total = r.parts[h, 0]
            for k in range(1, st.nz):
                total = total + r.parts[h, k]
            r.small[h] = total
        r.flush("small")
        for k in ORDER:
            wa.relay(k)
    gu.start()
    down.start()
    if first:
        for k in ORDER:
            wa.collect(k)
    else:
        r.need("small", "pairs", "cos", "sa", "sb")
    small = r.small[layer]
    n1_f = unit * small[:, :D]
    n1 = n1_f.astype(BF16)
    bias = small[:, 2 * D :]
    if first:
        wa.finish()
        r.flush("wa")
    else:
        r.need("wa")
    cos, sa, sb = r.cos[...], r.sa[...], r.sb[...]
    lin = mm(n1, r.wa[:, D:QKV]) + bias[:, D:]
    r.kv[me] = jnp.concatenate([rope(lin[:, :LANES], cos, sa, sb), lin[:, LANES:]], 1).astype(BF16)

    def keys_copy(k, src):
        return push(r.kv.at[src], r.kv.at[src], r.csem.at[k], r.csem2.at[k], "ctx", lax.rem(me + k, n))

    def start(k, c):
        keys_copy(k, me).start()
        return c

    lax.fori_loop(1, n, start, 0)
    linq = mm(n1, r.wa[:, :D]) + bias[:, :D]
    for t in range(TILES):
        tile = slice(t * LANES, (t + 1) * LANES)
        q = rope(linq[:, tile], cos, sa, sb) * HEAD_DIM ** (-0.5)
        spread(r.qst, t, q.T)
        r.n1t[tile, :] = n1_f[:, tile].T.astype(BF16)
    r.flush("qst", "n1t")
    for k in ORDER[:2]:
        gu.relay(k)
    half = HEAD_DIM
    own_k = own_sides(r.kv[me, :, :LANES].astype(F32))
    own_vt = own_sides(r.kv[me, :, LANES:].astype(F32)).astype(F32).T.astype(BF16)
    for cols in GROUPS:
        width = cols.stop - cols.start
        bias = own_bias(width)
        sc = mm(own_k, r.qst[:, cols])
        s_a, s_l, s_h = sc[:half], sc[half : 2 * half] + bias, sc[2 * half :] + bias
        m_lo = col_max(s_l)
        m_hi = jnp.maximum(col_max(s_a), col_max(s_h))
        p_a, p_l, p_h = jnp.exp(s_a - m_hi), jnp.exp(s_l - m_lo), jnp.exp(s_h - m_hi)
        r.m_s[0:1, cols], r.m_s[1:2, cols] = m_lo, m_hi
        r.l_s[0:1, cols], r.l_s[1:2, cols] = col_sum(p_l), col_sum(p_a) + col_sum(p_h)
        r.acc_s[:, cols] = mm(own_vt, jnp.concatenate([p_a, p_l, p_h], 0).astype(BF16))

    def step(i, c):
        kx, vt, sel = [], [], []
        for j in range(BATCH):
            k = i * BATCH + 1 + j
            src = lax.rem(me + n - k, n)
            keys_copy(k, src).wait_recv()
            if first:
                p = r.pairs.at[src]
                push(p, p, r.psem.at[k], r.psem2.at[k], "ctx", lax.rem(me + k, n)).wait_recv()
            sel.append(src)
            chosen = earlier(r.pairs, src, me, LANES)
            kx.append(sides(r.kv[src, :, :LANES].astype(F32), chosen))
            vt.append(sides_t(r.kv[src, :, LANES:].astype(F32).T, chosen))
        kx = jnp.concatenate(kx, 0)
        vt = jnp.concatenate(vt, 1)
        for cols in GROUPS:
            width = cols.stop - cols.start
            sc = mm(kx, r.qst[:, cols])
            m_lo, m_hi = r.m_s[0:1, cols], r.m_s[1:2, cols]
            n_lo, n_hi = m_lo, m_hi
            chosen = [earlier(r.pairs, src, me, width) for src in sel]
            for j in range(BATCH):
                top = col_max(sc[(2 * j + 1) * half : (2 * j + 2) * half])
                n_hi = jnp.maximum(n_hi, col_max(sc[2 * j * half : (2 * j + 1) * half]))
                n_hi = jnp.where(chosen[j], n_hi, jnp.maximum(n_hi, top))
                n_lo = jnp.where(chosen[j], jnp.maximum(n_lo, top), n_lo)
            a_lo, a_hi = jnp.exp(m_lo - n_lo), jnp.exp(m_hi - n_hi)
            l_lo, l_hi = r.l_s[0:1, cols] * a_lo, r.l_s[1:2, cols] * a_hi
            ps = []
            for j in range(BATCH):
                p_a = jnp.exp(sc[2 * j * half : (2 * j + 1) * half] - n_hi)
                p_s = jnp.exp(sc[(2 * j + 1) * half : (2 * j + 2) * half] - jnp.where(chosen[j], n_lo, n_hi))
                total = col_sum(p_s)
                l_hi = l_hi + col_sum(p_a) + jnp.where(chosen[j], 0.0, total)
                l_lo = l_lo + jnp.where(chosen[j], total, 0.0)
                ps += [p_a.astype(BF16), p_s.astype(BF16)]
            r.m_s[0:1, cols], r.m_s[1:2, cols] = n_lo, n_hi
            r.l_s[0:1, cols], r.l_s[1:2, cols] = l_lo, l_hi
            new = mm(vt, jnp.concatenate(ps, 0))
            r.acc_s[:LANES, cols] = r.acc_s[:LANES, cols] * a_lo + new[:LANES]
            r.acc_s[LANES:, cols] = r.acc_s[LANES:, cols] * a_hi + new[LANES:]
        return c

    lax.fori_loop(0, 1, step, 0)
    gu.relay(2)
    lax.fori_loop(1, 3, step, 0)
    for k in ORDER[:2]:
        gu.collect(k)
    lax.fori_loop(3, (n - 1) // BATCH, step, 0)
    gu.collect(2)
    r.flush("kv")
    if first:
        r.flush("pairs")
    r.lse[...] = r.m_s[...] + jnp.log(r.l_s[...])
    for t in range(TILES):
        cols = slice(t * LANES, (t + 1) * LANES)
        wide = jnp.concatenate([r.acc_s[:LANES, cols] / r.l_s[0:1, cols], r.acc_s[LANES:, cols] / r.l_s[1:2, cols]], 0)
        tile_t = gathered_tile(wide, t)
        r.attt[cols, :] = tile_t.astype(BF16)
        r.att_s[:, cols] = tile_t.T.astype(BF16)
    r.flush("lse", "attt")
    mid = x + mm(r.att_s[...], r.wa[:, QKV:])
    r.mid[...] = mid
    r2 = lax.rsqrt(jnp.mean(mid * mid, -1, keepdims=True) + EPS)
    r.n2[...] = (mid * r2 * small[:, D : 2 * D]).astype(BF16)
    r.flush("mid", "n2")
    gu.finish()
    down.finish()
    r.flush("gu", "down")
    st.drain()

    def done(k, c):
        keys_copy(k, me).wait_send()
        if first:
            p = r.pairs.at[me]
            push(p, p, r.psem.at[k], r.psem2.at[k], "ctx", lax.rem(me + k, n)).wait_send()
        return c

    lax.fori_loop(1, n, done, 0)
    r.close()


class Attention:
    def __init__(self, st):
        self.st = st

    def columns(self, src, dst):
        st = self.st
        share = dst.shape[0]
        at = st.take(st.nz - 1)
        mine = dst.at[:, pl.ds(pl.multiple_of(st.z * LANES, LANES), LANES)]
        moving = st.begin(
            [
                st.copy(src.at[st.block(st.along("z", k), share), :], mine, at + k - 1, st.peer("z", k))
                for k in range(1, st.nz)
            ]
        )
        mine[...] = src[st.block(st.z, share), :]
        return moving

    def whole(self, dst):
        st = self.st
        rows = dst.shape[0] // st.nz
        at = st.take(st.nz - 1)
        mine = dst.at[pl.ds(pl.multiple_of(st.z * rows, UNIT), rows), :]
        return st.begin([st.copy(mine, mine, at + k - 1, st.peer("z", k)) for k in range(1, st.nz)])

    def begin(self, glin, small, all_glin, all_small):
        st = self.st
        tok = glin.shape[0]
        all_glin[st.block(st.z, tok), :] = glin[...]
        all_small[st.block(st.z, 2 * UNIT), :] = small[...]
        return self.whole(all_glin) + self.whole(all_small)

    def swap(self, moving, n1z, all_glin, all_small, dout, made, land):
        st = self.st
        arrived(moving)
        share = n1z.shape[0]
        per = 8
        for j in range(0, QKV // LANES, 2):
            cols = slice(j * LANES, min(j + 2, QKV // LANES) * LANES)
            d = mm(n1z[...], all_glin[:, cols]).astype(BF16)
            for t in range(j, min(j + 2, QKV // LANES)):
                made[t // per, (t % per) * share : (t % per + 1) * share, :] = d[:, (t - j) * LANES : (t - j + 1) * LANES]
        made[1, share : 8 * share, :] = dout[...]
        small = jnp.zeros((2 * UNIT, LANES), F32)
        for i in range(st.nz):
            small = small + all_small[i * 2 * UNIT : (i + 1) * 2 * UNIT, :]
        made[0, 8 * share : 8 * share + 2 * UNIT, :] = small.astype(BF16)
        made[0, 8 * share + 2 * UNIT :, :] = jnp.zeros((Q_ROWS - 8 * share - 2 * UNIT, LANES), BF16)
        made[1, 8 * share :, :] = jnp.zeros((Q_ROWS - 8 * share, LANES), BF16)
        return st.swap(made, land)

    def fold(self, moving, made, land, out):
        st = self.st
        arrived(moving)
        rows = Q_ROWS // 2 // 16
        for h in range(2):
            for i in range(16):
                at = slice((h * 16 + i) * rows, (h * 16 + i + 1) * rows)
                total = made[st.s, at, :].astype(F32) + land[at, :].astype(F32)
                out[h][i // SIDE, i % SIDE] = total.astype(BF16)


def attn_bwd_kernel(layer, r):
    st = Stages(r)
    n, me = st.nc, st.c
    last = layer == 0
    st.hail(st.upright() + (st.beside() if last else []), ring=True)
    r.load()
    half = HEAD_DIM
    r.need("gm")
    gm = r.gm[...]
    gmb = gm.astype(BF16)
    tok = gm.shape[0]
    r.all_gm[st.block(st.z, tok), :] = gmb
    sl, l1, t1 = (r.sla, r.slb), (r.l1a, r.l1b), (r.t1a, r.t1b)
    r.need("sla", "slb", "attt", "n1t")
    st.met()
    r1 = [st.scatter(AXES[h][0], sl[h], l1[h]) for h in range(2)]
    attention = Attention(st)
    out_factors = attention.whole(r.all_gm) + attention.columns(r.attt, r.attz)
    qkv_factor = attention.columns(r.n1t, r.n1z)
    if last:
        r.need("glin1", "gsmall1", "n1z1", "dout1")
        before = attention.begin(r.glin1, r.gsmall1, r.all_glin, r.all_small)
    r.need("wa", "qst", "lse", "kv", "pairs")
    ga = mm_nt(gmb, r.wa[:, QKV:])
    for t in range(TILES):
        tile = slice(t * LANES, (t + 1) * LANES)
        ga_t = ga[:, tile].T
        spread(r.gst_s, t, ga_t)
        prod = ga_t * r.attt[tile, :].astype(F32)
        low, high = halves(col_sum(prod[:half]), col_sum(prod[half:]))
        r.delta_s[0:1, tile], r.delta_s[1:2, tile] = low, high

    def own_block():
        keys, vals = r.kv[me, :, :LANES].astype(F32), r.kv[me, :, LANES:].astype(F32)
        kx, vx = own_sides(keys), own_sides(vals)
        kt = kx.astype(F32).T.astype(BF16)
        rows = slice(0, 3 * half)
        for cols in GROUPS:
            bias = own_bias(cols.stop - cols.start)
            sc = mm(kx, r.qst[:, cols])
            dp = mm(vx, r.gst_s[:, cols])
            lo, hi = (r.lse[0:1, cols], r.delta_s[0:1, cols]), (r.lse[1:2, cols], r.delta_s[1:2, cols])
            parts = [(sc[:half], hi), (sc[half : 2 * half] + bias, lo), (sc[2 * half :] + bias, hi)]
            for i, (part, (lse, delta)) in enumerate(parts):
                p = jnp.exp(part - lse)
                at = slice(i * half, (i + 1) * half)
                r.p_s[at, cols] = p.astype(BF16)
                r.ds_s[at, cols] = (p * (dp[at] - delta)).astype(BF16)
            r.gq_s[:, cols] = mm(kt, r.ds_s[rows, cols])
        made = []
        for w, q in ((r.ds_s, r.qst), (r.p_s, r.gst_s)):
            e = mm_nt(w[rows, :], q[...])
            low = e[:half, LANES:] + e[half : 2 * half, :LANES]
            made.append(jnp.concatenate([low, e[2 * half :, LANES:]], 0))
        return jnp.concatenate(made, 1)

    def sum_copy(k):
        return push(r.send_s.at[k], r.land_s.at[k], r.csem.at[k], r.csem2.at[k], "ctx", lax.rem(me + k, n))

    def step(i, c):
        kx, vx, kt, sel = [], [], [], []
        for j in range(BATCH):
            src = lax.rem(me + i * BATCH + 1 + j, n)
            sel.append(src)
            chosen = earlier(r.pairs, src, me, LANES)
            keys = r.kv[src, :, :LANES].astype(F32)
            kx.append(sides(keys, chosen))
            vx.append(sides(r.kv[src, :, LANES:].astype(F32), chosen))
            kt.append(sides_t(keys.T, chosen))
        kx, vx, kt = jnp.concatenate(kx, 0), jnp.concatenate(vx, 0), jnp.concatenate(kt, 1)
        rows = slice(0, 2 * BATCH * half)
        for cols in GROUPS:
            width = cols.stop - cols.start
            sc = mm(kx, r.qst[:, cols])
            dp = mm(vx, r.gst_s[:, cols])
            for j in range(BATCH):
                chosen = earlier(r.pairs, sel[j], me, width)
                for part in range(2):
                    lse, delta = r.lse[1:2, cols], r.delta_s[1:2, cols]
                    if part:
                        lse = jnp.where(chosen, r.lse[0:1, cols], lse)
                        delta = jnp.where(chosen, r.delta_s[0:1, cols], delta)
                    at = slice((2 * j + part) * half, (2 * j + part + 1) * half)
                    p = jnp.exp(sc[at] - lse)
                    r.p_s[at, cols] = p.astype(BF16)
                    r.ds_s[at, cols] = (p * (dp[at] - delta)).astype(BF16)
            r.gq_s[:, cols] += mm(kt, r.ds_s[rows, cols])
        ek = mm_nt(r.ds_s[rows, :], r.qst[...])
        ev = mm_nt(r.p_s[rows, :], r.gst_s[...])
        for j in range(BATCH):
            chosen = earlier(r.pairs, sel[j], me, LANES)
            k = i * BATCH + 1 + j
            for e, lanes in ((ek, slice(0, LANES)), (ev, slice(LANES, 2 * LANES))):
                top = e[2 * j * half : (2 * j + 1) * half]
                low = e[(2 * j + 1) * half : (2 * j + 2) * half]
                r.send_s[k, :half, lanes] = (top[:, LANES:] + jnp.where(chosen, low[:, :LANES], 0.0)).astype(BF16)
                r.send_s[k, half:, lanes] = jnp.where(chosen, 0.0, low[:, LANES:]).astype(BF16)
            sum_copy(k).start()
        return c

    own = own_block()
    lax.fori_loop(0, 3, step, 0)
    arrived(out_factors)
    share = D // st.nz
    for j in range(0, TILES, 2):
        cols = slice(j * LANES, min(j + 2, TILES) * LANES)
        d = mm(r.attz[...], r.all_gm[:, cols]).astype(BF16)
        for t in range(j, min(j + 2, TILES)):
            r.dout[t * share : (t + 1) * share, :] = d[:, (t - j) * LANES : (t - j + 1) * LANES]
    r.flush("dout")
    if last:
        qswap = attention.swap(before, r.n1z1, r.all_glin, r.all_small, r.dout1, r.qv, r.ql)
    lax.fori_loop(3, (n - 1) // BATCH, step, 0)
    if last:
        attention.fold(qswap, r.qv, r.ql, (r.qpa, r.qpb))
        r.flush("qpa", "qpb")
    arrived(qkv_factor)
    r.flush("n1z")

    def take(k, total):
        sum_copy(k).wait_recv()
        return total + r.land_s[k].astype(F32)

    own = lax.fori_loop(1, n, take, own)
    r.need("cos", "sa", "sb", "x", "small", "dg2")
    cos, sa, sb = r.cos[...], r.sa[...], r.sb[...]
    for t in range(TILES):
        gq = gathered_tile(r.gq_s[:, t * LANES : (t + 1) * LANES], t).T * HEAD_DIM ** (-0.5)
        r.glin[:, t * LANES : (t + 1) * LANES] = unrope(gq, cos, sa, sb).astype(BF16)
    r.glin[:, D : D + LANES] = unrope(own[:, :LANES], cos, sa, sb).astype(BF16)
    r.glin[:, D + LANES :] = own[:, LANES:].astype(BF16)
    r.flush("glin")
    gn1 = mm_nt(r.glin[...], r.wa[:, :QKV])
    x = r.x[...]
    r1_ = lax.rsqrt(jnp.mean(x * x, -1, keepdims=True) + EPS)
    unit = x * r1_
    dz = gn1 * r.small[layer][:, :D]
    r.gx[...] = gm + r1_ * (dz - unit * jnp.mean(dz * unit, -1, keepdims=True))
    r.flush("gx")
    dg1 = col_sum(gn1 * unit)
    dbias = col_sum(r.glin[...].astype(F32))
    r.gsmall[...] = jnp.zeros(r.gsmall.shape, F32)
    row = 0
    for part in (dg1, r.dg2[...], dbias):
        for t in range(part.shape[1] // LANES):
            r.gsmall[row : row + 1, :] = part[:, t * LANES : (t + 1) * LANES]
            row += 1
    r.flush("gsmall")
    for h in range(2):
        arrived(r1[h])
        mine = sl[h].at[st.along(AXES[h][0], 0)]
        add_into(t1[h], [mine] + [l1[h].at[k] for k in range(SIDE - 1)])
    r.flush("t1a", "t1b")
    st.drain()

    def done(k, c):
        sum_copy(k).wait_send()
        return c

    lax.fori_loop(1, n, done, 0)
    r.close()


def ffn_fwd_kernel(layer, r):
    st = Stages(r)
    n, me = st.nz, st.z
    carry = layer == 0
    st.hail(st.upright(carry) + (st.beside() + st.flat() if carry else []))
    r.load()
    if carry:
        wa_local, wa = feed_attention(st, 1, r.wqkv_shard, r.wout_shard, r.wa)
    r.need("n2")
    r.all[me] = r.n2[...]
    st.met()
    at = st.take(2 * n)

    def first(k):
        return st.copy(r.all.at[me], r.all.at[me], at + k, st.peer("z", k))

    def second(k):
        return st.copy(r.send_s.at[k], r.land_s.at[k], at + n + k, st.peer("z", -k))

    for k in ORDER:
        first(k).start()
    if carry:
        wa_local.wait()
        wa.start()
    r.need("gu", "down", "mid")

    def block(src):
        a = r.all[src]
        gate = mm(a, r.gu[0])
        up = mm(a, r.gu[1])
        r.gate[src] = gate
        r.up[src] = up
        hidden = (gate * jax.nn.sigmoid(gate) * up).astype(BF16)
        return mm(hidden, r.down[...])

    r.y[...] = r.mid[...] + block(me)
    for k in ORDER:
        first(k).wait_recv()
        r.send_s[k] = block(st.along("z", -k)).astype(BF16)
        second(k).start()
        if carry and k == 3:
            wa.relay(1)
            wa.relay(3)
    r.flush("all", "gate", "up")
    if carry:
        wa.relay(2)
        for k in ORDER:
            wa.collect(k)
    for k in ORDER:
        second(k).wait_recv()
        r.y[...] += r.land_s[k].astype(F32)
    r.flush("y")
    for k in ORDER:
        first(k).wait_send()
        second(k).wait_send()
    if carry:
        wa.finish()
        r.flush("wa")
    st.drain()
    r.close()


def ffn_bwd_kernel(layer, r):
    st = Stages(r)
    n, me = st.nz, st.z
    carry = layer == 0
    st.hail(st.upright() + st.beside() + (st.flat(True) if carry else []))
    r.load()
    tok = r.gy.shape[0]

    def rows_of(i):
        return pl.ds(pl.multiple_of(i * tok, tok), tok)

    r.need("gy")
    r.all_s[rows_of(me), :] = r.gy[...].astype(BF16)
    st.met()
    at = st.take(2 * n)

    def first(k):
        mine = r.all_s.at[rows_of(me), :]
        return st.copy(mine, mine, at + k, st.peer("z", k))

    def second(k):
        return st.copy(r.send_s.at[k], r.land_s.at[k], at + n + k, st.peer("z", -k))

    for k in ORDER:
        first(k).start()
    if carry:
        r.need("t1a", "t1b")
        rest = Rest(st, (r.t1a, r.t1b), (r.l2a, r.l2b), (r.t2a, r.t2b), (r.g1a, r.g1b), (r.ga, r.gb), 1)
    r.need("down", "gate", "up", "gu")

    def block(src):
        rows = rows_of(src)
        gh = mm_nt(r.all_s[rows, :], r.down[...])
        gate, up = r.gate[src], r.up[src]
        sg = jax.nn.sigmoid(gate)
        act = gate * sg
        r.hid_s[rows, :] = (act * up).astype(BF16)
        ggate = (gh * up * sg * (1.0 + gate * (1.0 - sg))).astype(BF16)
        gup = (gh * act).astype(BF16)
        r.g_s[0, rows, :] = ggate
        r.g_s[1, rows, :] = gup
        return mm_nt(ggate, r.gu[0]) + mm_nt(gup, r.gu[1])

    r.own_s[...] = block(me)
    for k in ORDER:
        if carry:
            rest.advance()
        first(k).wait_recv()
        r.send_s[k] = block(st.along("z", -k)).astype(BF16)
        second(k).start()

    refs = (r.fa, r.fb)
    share = D // n
    for j in range(WIN // (2 * LANES)):
        cols = slice(2 * j * LANES, 2 * (j + 1) * LANES)
        r.down_s[cols, :] = mm_tn(r.hid_s[:, cols], r.all_s[...]).astype(BF16)
    pad = (WIN - FF // n) * lax.rem(me, 2)
    half = FF // n // 2
    base = [n * per * UNIT for per in GATE_PER]
    for section in range(2):
        rows = r.down_s[pl.ds(pl.multiple_of(pad + section * half, UNIT), half), :]
        for t in range(TILES):
            put_units(refs, section, base, DOWN_PER, t * (half // UNIT), rows[:, t * LANES : (t + 1) * LANES])
        used = TILES * (half // UNIT)
        extra = 16 * sum(DOWN_PER) - used
        put_units(refs, section, base, DOWN_PER, used, jnp.zeros((extra * UNIT, LANES), BF16))
    r.need("n2_all")
    normed = jnp.concatenate([r.n2_all[i] for i in range(n)], 0)

    def product(section):
        for j in range(WIN // (2 * LANES)):
            d = mm_tn(normed, r.g_s[section, :, 2 * j * LANES : 2 * (j + 1) * LANES]).astype(BF16)
            for t in (2 * j, 2 * j + 1):
                tile = d[:, (t % 2) * LANES : (t % 2 + 1) * LANES]
                for i in range(n):
                    base = [i * per * UNIT for per in GATE_PER]
                    put_units(refs, section, base, GATE_PER, t * (share // UNIT), tile[i * share : (i + 1) * share, :])
        used = WIN // LANES * (share // UNIT)
        extra = 16 * sum(GATE_PER) - used
        for i in range(n):
            base = [i * per * UNIT for per in GATE_PER]
            put_units(refs, section, base, GATE_PER, used, jnp.zeros((extra * UNIT, LANES), BF16))

    product(1 - st.s)
    swaps = [st.swap(refs[h], (r.sla, r.slb)[h]) for h in range(2)]
    product(st.s)
    for k in ORDER:
        second(k).wait_recv()
        r.own_s[...] += r.land_s[k].astype(F32)
    gn2 = r.own_s[...]
    r.need("mid", "small")
    mid = r.mid[...]
    r2 = lax.rsqrt(jnp.mean(mid * mid, -1, keepdims=True) + EPS)
    unit = mid * r2
    r.dg2[...] = col_sum(gn2 * unit)
    dz = gn2 * r.small[layer][:, D : 2 * D]
    r.gm[...] = r.gy[...] + r2 * (dz - unit * jnp.mean(dz * unit, -1, keepdims=True))
    r.flush("dg2", "gm")
    for h in range(2):
        swapped_sum(st, swaps[h], refs[h], (r.sla, r.slb)[h])
    r.flush("sla", "slb")
    for k in ORDER:
        first(k).wait_send()
        second(k).wait_send()
    if carry:
        rest.finish()
    st.drain()
    r.close()


class Rest:
    def __init__(self, st, t1, l2, t2, g1, out, layer):
        self.st, self.t1, self.l2, self.t2, self.g1, self.out, self.layer = st, t1, l2, t2, g1, out, layer
        self.stage = 0
        self.moving = [st.scatter(AXES[h][1], t1[h], l2[h]) for h in range(2)]

    def advance(self):
        st = self.st
        for h in range(2):
            second = AXES[h][1]
            arrived(self.moving[h])
            mine = self.g1[h].at[st.along(second, 0)]
            if self.stage == 0:
                t2 = self.t2[h]
                add_rows(t2, [self.t1[h].at[st.along(second, 0)]] + [self.l2[h].at[k] for k in range(SIDE - 1)])
                per = GATE_PER[h] * UNIT
                self.moving[h] = st.deal(t2, mine, per)
                mine[st.block(st.z, per), :] = t2[st.block(st.z, per), :]
                mine[st.nz * per :, :] = t2[st.nz * per :, :]
            elif self.stage == 1:
                self.moving[h] = st.gather(second, self.g1[h])
            else:
                self.moving[h] = st.hand_over(AXES[h][0], self.g1[h], self.out[h], self.layer)
        self.stage += 1

    def finish(self):
        for h in range(2):
            self.moving[h]()


def reduce_kernel(layer, r):
    st = Stages(r)
    st.hail(st.beside() + st.upright() + st.flat(True))
    r.load()
    r.need("t1a", "t1b", "q1a", "q1b", "glin", "gsmall")
    qp = {1: (r.q1a, r.q1b), 0: (r.qpa, r.qpb)}
    land = {1: (r.m1a, r.m1b), 0: (r.m0a, r.m0b)}
    land2 = {1: (r.w1a, r.w1b), 0: (r.w0a, r.w0b)}
    part = {1: (r.e1a, r.e1b), 0: (r.e0a, r.e0b)}
    wide = {1: (r.h1a, r.h1b), 0: (r.h0a, r.h0b)}
    out = (r.qa, r.qb)
    moving = {}

    def along_first(l):
        moving[l] = [st.scatter(AXES[h][0], qp[l][h], land[l][h]) for h in range(2)]

    def along_second(l):
        for h in range(2):
            arrived(moving[l][h])
            own = qp[l][h].at[st.along(AXES[h][0], 0)]
            add_into(part[l][h], [own] + [land[l][h].at[k] for k in range(SIDE - 1)])
            moving[l][h] = st.scatter(AXES[h][1], part[l][h], land2[l][h])

    def back_second(l):
        for h in range(2):
            arrived(moving[l][h])
            i = st.along(AXES[h][1], 0)
            add_rows(wide[l][h].at[i], [part[l][h].at[i]] + [land2[l][h].at[k] for k in range(SIDE - 1)])
            moving[l][h] = st.gather(AXES[h][1], wide[l][h])

    def back_first(l):
        for h in range(2):
            arrived(moving[l][h])
            moving[l][h] = st.hand_over(AXES[h][0], wide[l][h], out[h], l)

    st.met()
    attention = Attention(st)
    factors = attention.begin(r.glin, r.gsmall, r.all_glin, r.all_small)
    rest = Rest(st, (r.t1a, r.t1b), (r.l2a, r.l2b), (r.t2a, r.t2b), (r.g1a, r.g1b), (r.ga, r.gb), 0)
    along_first(1)
    rest.advance()
    along_second(1)
    rest.advance()
    back_second(1)
    rest.advance()
    r.need("n1z", "dout")
    qswap = attention.swap(factors, r.n1z, r.all_glin, r.all_small, r.dout, r.qv, r.ql)
    attention.fold(qswap, r.qv, r.ql, qp[0])
    along_first(0)
    back_first(1)
    along_second(0)
    back_second(0)
    back_first(0)
    rest.finish()
    for l in (1, 0):
        for h in range(2):
            moving[l][h]()
    st.drain()
    r.close()


class Refs(types.SimpleNamespace):
    def load(self):
        for c in self.coming.values():
            c.start()

    def need(self, *names):
        for k in names:
            if k not in self.here:
                self.coming[k].wait()
                self.here.add(k)

    def flush(self, *names):
        for k in names:
            self.going[k].start()
            self.gone.add(k)

    def close(self):
        self.need(*self.coming)
        self.flush(*[k for k in self.going if k not in self.gone])
        for c in self.going.values():
            c.wait()


def call(kernel, layer, cid, name, ins, outs, scratch, sems, hbm=(), flops=10**10):
    staged = [k for k in ins if k not in hbm]
    made = [k for k in outs if k not in hbm]
    dma = pltpu.SemaphoreType.DMA
    counts = dict(ssem=sems, rsem=sems, lsem=12, csem=16, csem2=16, psem=16, psem2=16, isem=len(staged), osem=len(made))
    places = [pltpu.VMEM(ins[k].shape, ins[k].dtype) for k in staged] + [pltpu.VMEM(*outs[k]) for k in made]
    names = ["in_" + k for k in ins] + ["out_" + k for k in outs] + staged + made + list(scratch) + list(counts)

    def body(*refs):
        r = Refs(**dict(zip(names, refs)))
        for k in hbm:
            if k in ins or k in outs:
                setattr(r, k, getattr(r, ("in_" if k in ins else "out_") + k))
        r.here, r.gone = set(), set()
        r.coming = {
            k: pltpu.make_async_copy(getattr(r, "in_" + k), getattr(r, k), r.isem.at[i]) for i, k in enumerate(staged)
        }
        r.going = {
            k: pltpu.make_async_copy(getattr(r, k), getattr(r, "out_" + k), r.osem.at[i]) for i, k in enumerate(made)
        }
        kernel(layer, r)

    anywhere = pl.BlockSpec(memory_space=pl.ANY)
    got = pl.pallas_call(
        body,
        out_shape=[jax.ShapeDtypeStruct(s, t) for s, t in outs.values()],
        in_specs=[anywhere] * len(ins),
        out_specs=[anywhere] * len(outs),
        scratch_shapes=places + [pltpu.VMEM(s, t) for s, t in scratch.values()] + [dma((k,)) for k in counts.values()],
        compiler_params=pltpu.CompilerParams(
            collective_id=cid, has_side_effects=True, vmem_limit_bytes=VMEM_LIMIT
        ),
        cost_estimate=pl.CostEstimate(flops=flops, bytes_accessed=20 * 2**20, transcendentals=0),
        name=name,
    )(*ins.values())
    return dict(zip(outs, got))


FA_ROWS = tuple((4 * g + d) * UNIT for g, d in zip(GATE_PER, DOWN_PER))
RQ = Q_ROWS // 2 // 16
SIDES = (SIDE, SIDE)
WIDE = HEADS * HEAD_DIM


def bf(*shape):
    return (shape, BF16)


def f4(*shape):
    return (shape, F32)


def rest_scratch():
    made = {}
    for h, rows in zip("ab", FA_ROWS):
        made["l2" + h] = bf(SIDE - 1, rows, LANES)
        made["t2" + h] = bf(rows, LANES)
        made["g1" + h] = bf(SIDE, rows, LANES)
    return made


def rest_outs():
    return {"g" + h: bf(2, *SIDES, rows, LANES) for h, rows in zip("ab", FA_ROWS)}


def assemble_kernel(nz, *refs):
    given, results, held, outs, sem, osem = (refs[:2], refs[2:4]), refs[6:12], refs[12:14] + refs[4:6], refs[14:20], refs[20], refs[21]
    s = lax.axis_index("section")
    copies = [pltpu.make_async_copy(a, b, osem.at[i]) for i, (a, b) in enumerate(zip(outs, results))]
    for layer in range(2):
        @pl.when(s == layer)
        def _():
            moving = [pltpu.make_async_copy(a, b, sem.at[i]) for i, (a, b) in enumerate(zip(given[layer], held))]
            for c in moving:
                c.start()
            for c in moving:
                c.wait()

    gate_ref, up_ref, down_ref, qkv_ref, out_ref, small_ref = outs
    share = D // nz
    starts = window_starts(nz)

    def units(refs, section, base, per, first, count):
        rows = []
        for part, piece, slot, _, m in unit_runs(first, count, per):
            at = base[part] + slot * UNIT
            rows.append(refs[part][section, piece // SIDE, piece % SIDE, at : at + m * UNIT, :].astype(F32))
        return jnp.concatenate(rows, 0) if len(rows) > 1 else rows[0]

    for section, ref in ((0, gate_ref), (1, up_ref)):
        tiles = {}
        for w, a in enumerate(starts):
            for t in range(WIN // LANES):
                tiles.setdefault(a // LANES + t, []).append((w, t))
        for col, sources in tiles.items():
            total = None
            for w, t in sources:
                base = [w * per * UNIT for per in GATE_PER]
                got = units(held[:2], section, base, GATE_PER, t * (share // UNIT), share // UNIT)
                total = got if total is None else total + got
            ref[:, col * LANES : (col + 1) * LANES] = total
        copies[section].start()
    base = [nz * per * UNIT for per in GATE_PER]
    half = FF // nz // 2
    for section in range(2):
        for t in range(TILES):
            got = units(held[:2], section, base, DOWN_PER, t * (half // UNIT), half // UNIT)
            down_ref[section * half : (section + 1) * half, t * LANES : (t + 1) * LANES] = got
    copies[2].start()
    for t in range(QKV // LANES + TILES):
        got = units(held[2:], t // 8, (0, 0), Q_PER, (t % 8) * (share // UNIT), share // UNIT)
        if t < QKV // LANES:
            qkv_ref[:, t * LANES : (t + 1) * LANES] = got
        else:
            u = t - QKV // LANES
            out_ref[:, u * LANES : (u + 1) * LANES] = got
    small_ref[...] = units(held[2:], 0, (0, 0), Q_PER, 8 * (share // UNIT), 2)
    for c in copies[3:]:
        c.start()
    for c in copies:
        c.wait()


def assemble(zero, one, attn):
    nz = lax.axis_size("fsdp")
    vm = pl.BlockSpec(memory_space=pltpu.VMEM)
    anywhere = pl.BlockSpec(memory_space=pl.ANY)
    share = D // nz
    shapes = [(share, FF), (share, FF), (FF // nz, D), (share, QKV), (share, D), (2 * UNIT, LANES)]
    return pl.pallas_call(
        functools.partial(assemble_kernel, nz),
        out_shape=[jax.ShapeDtypeStruct(a, F32) for a in shapes],
        in_specs=[anywhere] * 4 + [vm] * 2,
        out_specs=[anywhere] * len(shapes),
        scratch_shapes=[pltpu.VMEM(a.shape, a.dtype) for a in zero]
        + [pltpu.VMEM(a, F32) for a in shapes]
        + [pltpu.SemaphoreType.DMA((2,)), pltpu.SemaphoreType.DMA((len(shapes),))],
        compiler_params=pltpu.CompilerParams(vmem_limit_bytes=VMEM_LIMIT),
        name="assemble",
    )(*zero, *one, *attn)


def window_starts(n):
    share = FF // n
    return [(i * share // LANES) * LANES for i in range(n)]


def attn_fwd(layer, x, shards, small, pair, pairs, tabs, wa):
    n, nz = lax.axis_size("ctx"), lax.axis_size("fsdp")
    tok = x.shape[0]
    ins = dict(x=x)
    outs = dict(
        mid=f4(tok, D), n2=bf(tok, D), n1t=bf(D, tok), qst=bf(2 * LANES, WIDE), kv=bf(n, tok, 2 * LANES), lse=f4(2, WIDE),
        attt=bf(D, tok), gu=bf(2, D, WIN), down=bf(WIN, D),
    )
    scratch = dict(m_s=f4(2, WIDE), l_s=f4(2, WIDE), acc_s=f4(2 * LANES, WIDE), att_s=bf(tok, D))
    if layer == 0:
        freq = jnp.arange(HEAD_DIM // 2, dtype=F32)
        inverse = jnp.tile(THETA ** (-2.0 * freq / HEAD_DIM), 4)[None, :]
        ins.update(small_own=small, pair=pair, inverse=inverse, wqkv_shard=shards["qkv"], wout_shard=shards["out"])
        outs.update(
            wa=bf(D, QKV + D), small=f4(2, 1, SMALL), pairs=((n, 8, 2 * LANES), jnp.int32),
            cos=f4(tok, LANES), sa=f4(tok, LANES), sb=f4(tok, LANES),
        )
        scratch.update(parts=f4(2, nz, 1, SMALL))
    else:
        ins.update(small=small, cos=tabs[0], sa=tabs[1], sb=tabs[2], wa=wa, pairs=pairs)
    ins.update(gate_shard=shards["gate"], up_shard=shards["up"], down_shard=shards["down"])
    hbm = ("wout_shard", "gate_shard", "up_shard", "down_shard", "wqkv_shard")
    return call(attn_fwd_kernel, layer, 1 + layer, f"attn_fwd_{layer}", ins, outs, scratch, 64, hbm)


def ffn_fwd(layer, a, shards):
    n = lax.axis_size("fsdp")
    tok = a["n2"].shape[0]
    ins = {k: a[k] for k in ("n2", "gu", "down", "mid")}
    outs = dict(y=f4(tok, D), all=bf(n, tok, D), gate=f4(n, tok, WIN), up=f4(n, tok, WIN))
    if layer == 0:
        ins.update(wqkv_shard=shards["qkv"], wout_shard=shards["out"])
        outs.update(wa=bf(D, QKV + D))
    scratch = dict(send_s=bf(n, tok, D), land_s=bf(n, tok, D))
    return call(ffn_fwd_kernel, layer, 3 + layer, f"ffn_fwd_{layer}", ins, outs, scratch, 32, ("wqkv_shard", "wout_shard"))


def ffn_bwd(layer, gy, a, f, small, before):
    n = lax.axis_size("fsdp")
    tok = gy.shape[0]
    ins = dict(gy=gy)
    outs = dict(gm=f4(tok, D), dg2=f4(1, D))
    scratch = dict(
        all_s=bf(n * tok, D), hid_s=bf(n * tok, WIN), g_s=bf(2, n * tok, WIN), down_s=bf(WIN, D),
        own_s=f4(tok, D), send_s=bf(n, tok, D), land_s=bf(n, tok, D),
    )
    for h, rows in zip("ab", FA_ROWS):
        scratch["f" + h] = bf(2, *SIDES, rows, LANES)
        outs["sl" + h] = bf(*SIDES, rows, LANES)
    if layer == 0:
        ins.update(t1a=before["t1a"], t1b=before["t1b"])
        outs.update(rest_outs())
        scratch.update(rest_scratch())
    ins.update(down=a["down"], gate=f["gate"], up=f["up"], gu=a["gu"], n2_all=f["all"], mid=a["mid"], small=small)
    return call(ffn_bwd_kernel, layer, 5 + layer, f"ffn_bwd_{layer}", ins, outs, scratch, 64, ("ga", "gb"), 2 * 10**10)


def attn_bwd(layer, x, a, b, wa, small, pairs, tabs, before):
    n, nz = lax.axis_size("ctx"), lax.axis_size("fsdp")
    tok = x.shape[0]
    share = D // nz
    ins = dict(gm=b["gm"], sla=b["sla"], slb=b["slb"])
    ins.update({k: a[k] for k in ("attt", "n1t")})
    if layer == 0:
        ins.update(glin1=before["glin"], gsmall1=before["gsmall"], n1z1=before["n1z"], dout1=before["dout"])
    ins.update({k: a[k] for k in ("qst", "lse", "kv")})
    ins.update(wa=wa, pairs=pairs, cos=tabs[0], sa=tabs[1], sb=tabs[2], x=x, small=small, dg2=b["dg2"])
    outs = dict(
        gx=f4(tok, D), glin=bf(tok, QKV), gsmall=f4(2 * UNIT, LANES), n1z=bf(share, nz * tok), dout=bf(TILES * share, LANES)
    )
    scratch = dict(
        gst_s=bf(2 * LANES, WIDE), delta_s=f4(2, WIDE), gq_s=f4(2 * LANES, WIDE), all_gm=bf(nz * tok, D), attz=bf(share, nz * tok),
        p_s=bf(2 * BATCH * HEAD_DIM, WIDE), ds_s=bf(2 * BATCH * HEAD_DIM, WIDE),
        send_s=bf(n, tok, 2 * LANES), land_s=bf(n, tok, 2 * LANES),
    )
    for h, rows in zip("ab", FA_ROWS):
        outs["t1" + h] = bf(SIDE, rows, LANES)
        scratch["l1" + h] = bf(SIDE - 1, SIDE, rows, LANES)
    if layer == 0:
        scratch.update(attention_scratch(tok))
        outs.update(qpa=bf(*SIDES, RQ, LANES), qpb=bf(*SIDES, RQ, LANES))
    return call(attn_bwd_kernel, layer, 7 + layer, f"attn_bwd_{layer}", ins, outs, scratch, 48, flops=2 * 10**10)


def attention_scratch(tok):
    nz = lax.axis_size("fsdp")
    return dict(all_glin=bf(nz * tok, QKV), all_small=f4(nz * 2 * UNIT, LANES), qv=bf(2, Q_ROWS, LANES), ql=bf(Q_ROWS, LANES))


def reduce_rest(last):
    ins = dict(glin=last["glin"], gsmall=last["gsmall"], t1a=last["t1a"], t1b=last["t1b"], q1a=last["qpa"], q1b=last["qpb"])
    ins.update(n1z=last["n1z"], dout=last["dout"])
    outs = rest_outs()
    scratch = rest_scratch()
    scratch.update(attention_scratch(last["glin"].shape[0]))
    scratch.update(qpa=bf(*SIDES, RQ, LANES), qpb=bf(*SIDES, RQ, LANES))
    for h in "ab":
        outs["q" + h] = bf(2, *SIDES, RQ, LANES)
        for l in "01":
            scratch["m" + l + h] = bf(SIDE - 1, SIDE, RQ, LANES)
            scratch["w" + l + h] = bf(SIDE - 1, RQ, LANES)
            scratch["e" + l + h] = bf(SIDE, RQ, LANES)
            scratch["h" + l + h] = bf(SIDE, RQ, LANES)
    return call(reduce_kernel, 0, 9, "reduce", ins, outs, scratch, 128, ("ga", "gb", "qa", "qb"))


def local(
    tokens, cotangent, pair_of, attn_gain, ffn_gain, qkv_weight, qkv_bias, out_weight, gate_weight, up_weight, down_weight,
):
    s = lax.axis_index("section")
    z = lax.axis_index("fsdp")
    nz = lax.axis_size("fsdp")
    qd = D // nz
    shards = dict(qkv=qkv_weight, out=out_weight, gate=gate_weight, up=up_weight, down=down_weight)

    def placed(part, size):
        whole = jnp.zeros((1, size), F32)
        return lax.dynamic_update_slice(whole, part.astype(F32), (0, z * part.shape[1]))

    small_own = jnp.concatenate([placed(attn_gain, D), placed(ffn_gain, D), placed(qkv_bias, QKV)], 1)
    pair = jnp.broadcast_to(pair_of.reshape(1, 1), (8, 2 * LANES))
    x0 = jnp.where(s == 0, tokens[0, 0], tokens[1, 0])
    a0 = attn_fwd(0, x0, shards, small_own, pair, None, None, None)
    small, pairs, tabs = a0["small"], a0["pairs"], (a0["cos"], a0["sa"], a0["sb"])
    f0 = ffn_fwd(0, a0, shards)
    x1 = f0["y"].astype(BF16).astype(F32)
    a1 = attn_fwd(1, x1, shards, small, None, pairs, tabs, f0["wa"])
    f1 = ffn_fwd(1, a1, None)

    gy = jnp.where(s == 0, cotangent[0, 0], cotangent[1, 0])
    b1 = ffn_bwd(1, gy, a1, f1, small, None)
    c1 = attn_bwd(1, x1, a1, b1, f0["wa"], small, pairs, tabs, None)
    gy = c1["gx"].astype(BF16).astype(F32)
    b0 = ffn_bwd(0, gy, a0, f0, small, c1)
    c0 = attn_bwd(0, x0, a0, b0, a0["wa"], small, pairs, tabs, c1)
    t = reduce_rest(c0)
    dgate, dup, ddown, dqkv, dout, small_grad = assemble((t["ga"], t["gb"]), (b0["ga"], b0["gb"]), (t["qa"], t["qb"]))
    small_grad = small_grad.reshape(-1)

    def mine(first, size):
        return lax.dynamic_slice_in_dim(small_grad, first + z * size, size, 0)[None]

    def by_layer(pair):
        theirs = jnp.where(s == 0, pair[1], pair[0])
        mine = jnp.where(s == 0, pair[0], pair[1])
        got = lax.ppermute(theirs, "section", [(0, 1), (1, 0)])
        return jnp.where(s == 0, jnp.stack([mine, got]), jnp.stack([got, mine]))[None, :, None]

    return (
        by_layer((f0["y"], f1["y"])),
        by_layer((c0["gx"], c1["gx"])),
        mine(0, qd),
        mine(D, qd),
        dqkv[None],
        mine(2 * D, QKV // nz),
        dout[None],
        dgate[None],
        dup[None],
        ddown[None],
    )


def solution(mesh):
    return jax.shard_map(
        local,
        mesh=mesh,
        in_specs=(
            P(None, "fsdp", "ctx", None),
            P(None, "fsdp", "ctx", None),
            P("ctx"),
            P("section", "fsdp"),
            P("section", "fsdp"),
            P("section", "fsdp", None),
            P("section", "fsdp"),
            P("section", "fsdp", None),
            P("section", "fsdp", None),
            P("section", "fsdp", None),
            P("section", "fsdp", None),
        ),
        out_specs=(
            P("section", None, "fsdp", "ctx", None),
            P("section", None, "fsdp", "ctx", None),
            P("section", "fsdp"),
            P("section", "fsdp"),
            P("section", "fsdp", None),
            P("section", "fsdp"),
            P("section", "fsdp", None),
            P("section", "fsdp", None),
            P("section", "fsdp", None),
            P("section", "fsdp", None),
        ),
        check_vma=False,
    )
```

```python
import functools
import types

import jax
import jax.numpy as jnp
from jax import lax
from jax.experimental import pallas as pl
from jax.experimental.pallas import tpu as pltpu
from jax.sharding import PartitionSpec as P

D = 896
HEADS = 14
KV_HEADS = 2
HEAD_DIM = 64
GROUP = HEADS // KV_HEADS
FF = 4864
QKV = 1152
EPS = 1e-06
THETA = 1000000.0
LANES = 128
TILES = D // LANES
WIN = 1280
NEG = -1e30
F32 = jnp.float32
BF16 = jnp.bfloat16
MESH = pl.DeviceIdType.MESH
VMEM_LIMIT = 60 * 2**20
UNIT = 16
SIDE = 4
GATE_PER = (5, 4)
DOWN_PER = (8, 9)
Q_PER = (4, 4)
Q_ROWS = 16 * sum(Q_PER) * UNIT


def mm(a, b):
    return jnp.dot(a, b, preferred_element_type=F32)


def mm_nt(a, b):
    return lax.dot_general(a, b, (((1,), (1,)), ((), ())), preferred_element_type=F32)


def mm_tn(a, b):
    return lax.dot_general(a, b, (((0,), (0,)), ((), ())), preferred_element_type=F32)


ORDER = (1, 3, 2)
SMALL = 2 * D + QKV
AXES = (("x", "y"), ("y", "x"))
BATCH = 3
GROUPS = tuple(slice(a, min(a + 2 * LANES, HEADS * HEAD_DIM)) for a in range(0, HEADS * HEAD_DIM, 2 * LANES))


def push(src, dst, ssem, rsem, axis, to):
    return pltpu.make_async_remote_copy(
        src_ref=src,
        dst_ref=dst,
        send_sem=ssem,
        recv_sem=rsem,
        device_id={axis: to},
        device_id_type=MESH,
    )


def rope(u, cos, sa, sb):
    return u * cos + pltpu.roll(u, 96, 1) * sa + pltpu.roll(u, 32, 1) * sb


def unrope(u, cos, sa, sb):
    return u * cos - pltpu.roll(u, 96, 1) * sa - pltpu.roll(u, 32, 1) * sb


def halves(a0, a1):
    lane = lax.broadcasted_iota(jnp.int32, a0.shape, 1) < HEAD_DIM
    low = jnp.where(lane, a0, pltpu.roll(a1, HEAD_DIM, 1))
    high = jnp.where(lane, pltpu.roll(a0, HEAD_DIM, 1), a1)
    return low, high


def spread(ref, t, tile_t):
    half = HEAD_DIM
    zero = jnp.zeros((half, LANES), F32)
    cols = slice(t * LANES, (t + 1) * LANES)
    for g in range(KV_HEADS):
        pair = [tile_t[j * half : (j + 1) * half, :] if (2 * t + j) // GROUP == g else zero for j in range(2)]
        for part, content in enumerate(halves(*pair)):
            ref[part * LANES + g * half : part * LANES + (g + 1) * half, cols] = content.astype(BF16)


def gathered_tile(wide, t):
    half = HEAD_DIM
    rows = []
    for j in range(2):
        g = (2 * t + j) // GROUP
        low = wide[g * half : (g + 1) * half, :]
        high = wide[LANES + g * half : LANES + (g + 1) * half, :]
        rows.append(halves(low, high)[j])
    return jnp.concatenate(rows, 0)


def dealt(a_per, b_per):
    where = [(0, u // a_per, u % a_per) for u in range(16 * a_per)]
    return where + [(1, v // b_per, v % b_per) for v in range(16 * b_per)]


def unit_runs(first, count, per):
    where = dealt(*per)
    found = []
    for i in range(count):
        part, piece, slot = where[first + i]
        if found and found[-1][0] == part and found[-1][1] == piece:
            found[-1][4] += 1
        else:
            found.append([part, piece, slot, i, 1])
    return found


def put_units(refs, section, base, per, first, rows):
    for part, piece, slot, i, m in unit_runs(first, rows.shape[0] // UNIT, per):
        at = base[part] + slot * UNIT
        refs[part][section, piece // SIDE, piece % SIDE, at : at + m * UNIT, :] = rows[i * UNIT : (i + m) * UNIT, :]


class Stages:
    def __init__(self, r):
        self.s = lax.axis_index("section")
        self.c = lax.axis_index("ctx")
        self.nc = lax.axis_size("ctx")
        self.x, self.y = self.c // SIDE, lax.rem(self.c, SIDE)
        self.z = lax.axis_index("fsdp")
        self.nz = lax.axis_size("fsdp")
        self.ssem, self.rsem, self.lsem = r.ssem, r.rsem, r.lsem
        self.used = 0
        self.local_used = 0
        self.sent = []

    def along(self, axis, k):
        own, n = {
            "x": (self.x, SIDE),
            "y": (self.y, SIDE),
            "z": (self.z, self.nz),
            "c": (self.c, self.nc),
        }[axis]
        return lax.rem(own + n + k, n)

    def peer(self, axis, k, section=None):
        if axis == "s":
            return {"section": 1 - self.s}
        if axis == "z":
            to = {"fsdp": self.along("z", k)}
        elif axis == "c":
            to = {"ctx": self.along("c", k)}
        elif axis == "x":
            to = {"ctx": self.along("x", k) * SIDE + self.y}
        else:
            to = {"ctx": self.x * SIDE + self.along("y", k)}
        if section is not None:
            to["section"] = section
        return to

    def hail(self, ids, ring=False):
        bar = pltpu.get_barrier_semaphore()
        for i in ids:
            pl.semaphore_signal(bar, inc=1, device_id=i, device_id_type=MESH)
        self.expected = len(ids)
        if ring:
            def one(k, c):
                pl.semaphore_signal(bar, inc=1, device_id=self.peer("c", k), device_id_type=MESH)
                return c

            lax.fori_loop(1, self.nc, one, 0)
            self.expected += self.nc - 1
        self.bar = bar

    def met(self):
        pl.semaphore_wait(self.bar, self.expected)

    def beside(self):
        return [self.peer("s", 0)]

    def upright(self, both=False):
        ids = [self.peer("z", k) for k in range(1, self.nz)]
        return ids + ([self.peer("z", k, 1 - self.s) for k in range(1, self.nz)] if both else [])

    def flat(self, both=False):
        ids = [self.peer(a, k) for a in "xy" for k in range(1, SIDE)]
        return ids + ([self.peer(a, k, 1 - self.s) for a in "xy" for k in range(1, SIDE)] if both else [])

    def take(self, count):
        self.used += count
        return self.used - count

    def copy(self, src, dst, at, to, recv_at=None):
        return pltpu.make_async_remote_copy(
            src_ref=src,
            dst_ref=dst,
            send_sem=self.ssem.at[at],
            recv_sem=self.rsem.at[at if recv_at is None else recv_at],
            device_id=to,
            device_id_type=MESH,
        )

    def begin(self, copies):
        for c in copies:
            c.start()
        self.sent += copies
        return copies

    def drain(self):
        for c in self.sent:
            c.wait_send()

    def swap(self, src, land):
        return self.begin([self.copy(src.at[1 - self.s], land, self.take(1), self.peer("s", 0))])

    def scatter(self, axis, src, land):
        n = self.nz if axis == "z" else SIDE
        at = self.take(n - 1)
        return self.begin(
            [self.copy(src.at[self.along(axis, k)], land.at[k - 1], at + k - 1, self.peer(axis, k)) for k in range(1, n)]
        )

    def gather(self, axis, ref):
        at = self.take(SIDE - 1)
        mine = ref.at[self.along(axis, 0)]
        return self.begin([self.copy(mine, mine, at + k - 1, self.peer(axis, k)) for k in range(1, SIDE)])

    def deal(self, src, dst, rows):
        at = self.take(self.nz - 1)
        mine = dst.at[self.block(self.z, rows), :]
        return self.begin(
            [
                self.copy(src.at[self.block(self.along("z", k), rows), :], mine, at + k - 1, self.peer("z", k))
                for k in range(1, self.nz)
            ]
        )

    def block(self, i, rows):
        return pl.ds(pl.multiple_of(i * rows, UNIT), rows)

    def aside(self, j):
        x = lax.rem(self.x + (1 - self.s) * j, SIDE)
        y = lax.rem(self.y + self.s * j, SIDE)
        return {"ctx": x * SIDE + y}

    def quarter(self):
        return self.x * (1 - self.s) + self.y * self.s

    def hand_over(self, axis, src, dst, layer):
        at = self.take(2 * SIDE)
        mine = dst.at[self.s, self.along(axis, 0)]
        self.begin(
            [
                self.copy(src, mine, at + k, self.peer(axis, k, layer), at + self.s * SIDE + k)
                for k in range(1, SIDE)
            ]
        )
        beside = self.copy(src, mine, at, {"section": layer}, at + self.s * SIDE)
        within = pltpu.make_async_copy(src, mine, self.lsem.at[self.local_used])
        self.local_used += 1

        @pl.when(self.s != layer)
        def _():
            beside.start()

        @pl.when(self.s == layer)
        def _():
            within.start()

        def finish():
            @pl.when(self.s == layer)
            def _():
                within.wait()
                for half in range(2):
                    for k in range(0 if half != layer else 1, SIDE):
                        self.copy(src, mine, at, {"section": layer}, at + half * SIDE + k).wait_recv()

            @pl.when(self.s != layer)
            def _():
                beside.wait_send()

        return finish


class Feed:
    def __init__(self, st, layer, sources, piece, band):
        self.st, self.layer, self.sources, self.piece, self.band = st, layer, sources, piece, band
        steps = st.nz - 1
        self.across = st.take(2 * steps)
        self.sideways = st.take((SIDE - 1) * steps)
        self.passed = st.take(steps)
        self.own = st.take(2)

    def beside(self, h):
        b = self.band(self.st.z, h)
        return self.st.copy(b, b, self.own + h, self.st.peer("s", 0))

    def send(self, h, k, src):
        st = self.st
        dst = self.piece(st.z, h, (st.x, st.y)[h])
        return st.copy(dst if src is None else src, dst, self.across + 2 * (k - 1) + h, st.peer("z", k, h))

    def start(self):
        st = self.st

        @pl.when(st.s == self.layer)
        def _():
            for k in ORDER:
                for h in range(2):
                    for needed, src in self.sources(h, (st.x, st.y)[h], st.along("z", k)):
                        if needed is None:
                            self.send(h, k, src).start()
                        else:
                            pl.when(needed)(self.send(h, k, src).start)
            for h in range(2):
                self.beside(h).start()

    def relay(self, k):
        st = self.st
        p = self.piece(st.along("z", -k), st.s, st.quarter())
        st.copy(p, p, self.across + 2 * (k - 1) + st.s, st.peer("s", 0)).wait_recv()
        at = self.sideways + (SIDE - 1) * (k - 1) - 1
        st.begin([st.copy(p, p, at + j, st.aside(j)) for j in range(1, SIDE)])

    def collect(self, k):
        st = self.st
        z = st.along("z", -k)
        at = self.sideways + (SIDE - 1) * (k - 1) - 1
        for j in range(1, SIDE):
            p = self.piece(z, st.s, lax.rem(st.quarter() + SIDE - j, SIDE))
            st.copy(p, p, at + j, st.aside(j)).wait_recv()
        b = self.band(z, st.s)
        st.begin([st.copy(b, b, self.passed + k - 1, st.peer("s", 0))])

    def finish(self):
        st = self.st
        for k in ORDER:
            b = self.band(st.along("z", -k), 1 - st.s)
            st.copy(b, b, self.passed + k - 1, st.peer("s", 0)).wait_recv()

        @pl.when(st.s == self.layer)
        def _():
            for h in range(2):
                for k in ORDER:
                    self.send(h, k, None).wait_send()
                self.beside(h).wait_send()

        @pl.when(st.s != self.layer)
        def _():
            for h in range(2):
                self.beside(h).wait_recv()


class FeedDown:
    def __init__(self, st, layer, src, dst):
        self.st, self.layer = st, layer
        share = src.shape[1]
        spare = WIN - share
        odd = lax.rem(st.z, 2)
        place = dst.at[pl.ds(pl.multiple_of(odd * spare, UNIT), share), :]
        dst[pl.ds(pl.multiple_of((1 - odd) * share, UNIT), spare), :] = jnp.zeros((spare, D), BF16)
        self.local = pltpu.make_async_copy(src.at[0], place, st.lsem.at[st.local_used])
        st.local_used += 1
        self.remote = st.copy(src.at[0], place, st.take(1), st.peer("s", 0))

    def start(self):
        @pl.when(self.st.s == self.layer)
        def _():
            self.local.start()
            self.remote.start()

    def finish(self):
        @pl.when(self.st.s == self.layer)
        def _():
            self.local.wait()
            self.remote.wait_send()

        @pl.when(self.st.s != self.layer)
        def _():
            self.remote.wait_recv()


class Local:
    def __init__(self, st, layer, pairs):
        self.st, self.layer = st, layer
        self.copies = [pltpu.make_async_copy(a, b, st.lsem.at[st.local_used + i]) for i, (a, b) in enumerate(pairs)]
        st.local_used += len(pairs)

        @pl.when(st.s == layer)
        def _():
            for c in self.copies:
                c.start()

    def wait(self):
        @pl.when(self.st.s == self.layer)
        def _():
            for c in self.copies:
                c.wait()


def half_rows(z, h, share):
    return pl.ds(pl.multiple_of(z * share + h * (share // 2), UNIT), share // 2)


def feed_attention(st, layer, qkv, out, dst):
    share = qkv.shape[1]
    rows = st.block(st.z, share)
    local = Local(st, layer, [(qkv.at[0], dst.at[rows, :QKV]), (out.at[0], dst.at[rows, QKV:])])
    width = (QKV + D) // SIDE

    def piece(z, h, q):
        return dst.at[half_rows(z, h, share), pl.ds(pl.multiple_of(q * width, LANES), width)]

    def band(z, h):
        return dst.at[half_rows(z, h, share), :]

    return local, Feed(st, layer, lambda h, q, z_to: [(None, None)], piece, band)


def feed_windows(st, layer, gate, up, dst):
    share = gate.shape[1]
    pace = FF // st.nz // (LANES // 2)
    width = WIN // 2

    def window(z):
        return pl.multiple_of(z * pace // 2 * LANES, LANES)

    rows = st.block(st.z, share)
    local = Local(st, layer, [(w.at[0, :, pl.ds(window(st.z), WIN)], dst.at[i, rows, :]) for i, w in enumerate((gate, up))])

    def sources(h, q, z_to):
        at = pl.multiple_of(window(z_to) + lax.rem(q, 2) * width, LANES)
        part = slice(h * (share // 2), (h + 1) * (share // 2))
        return [(q < 2, gate.at[0, part, pl.ds(at, width)]), (q >= 2, up.at[0, part, pl.ds(at, width)])]

    def piece(z, h, q):
        return dst.at[q // 2, half_rows(z, h, share), pl.ds(pl.multiple_of(lax.rem(q, 2) * width, LANES), width)]

    def band(z, h):
        return dst.at[:, half_rows(z, h, share), :]

    return local, Feed(st, layer, sources, piece, band)


def arrived(copies):
    for c in copies:
        c.wait_recv()


def add_into(dst, parts):
    def one(i, c):
        total = parts[0][i].astype(F32)
        for p in parts[1:]:
            total = total + p[i].astype(F32)
        dst[i] = total.astype(dst.dtype)
        return c

    lax.fori_loop(0, dst.shape[0], one, 0)


def add_rows(dst, parts):
    total = parts[0][...].astype(F32)
    for p in parts[1:]:
        total = total + p[...].astype(F32)
    dst[...] = total.astype(dst.dtype)


def swapped_sum(st, copies, given, land):
    arrived(copies)
    for i in range(SIDE):
        add_into(land.at[i], [given.at[st.s, i], land.at[i]])


def sides(tile, chosen):
    half = HEAD_DIM
    low, high = tile[:half], tile[half:]
    zero = jnp.zeros_like(low)
    below = jnp.concatenate([jnp.where(chosen, low, zero), jnp.where(chosen, zero, high)], 1)
    return jnp.concatenate([jnp.concatenate([zero, low], 1), below], 0).astype(BF16)


def sides_t(tile_t, chosen):
    lane = lax.broadcasted_iota(jnp.int32, tile_t.shape, 1) < HEAD_DIM
    upper = jnp.where(jnp.logical_or(lane, jnp.logical_not(chosen)), 0.0, pltpu.roll(tile_t, HEAD_DIM, 1))
    lower = jnp.where(jnp.logical_or(lane, jnp.logical_not(chosen)), tile_t, 0.0)
    return jnp.concatenate([upper, lower], 0).astype(BF16)


def own_sides(tile):
    low, high = tile[:HEAD_DIM], tile[HEAD_DIM:]
    zero = jnp.zeros_like(low)
    rows = [[zero, low], [low, zero], [zero, high]]
    return jnp.concatenate([jnp.concatenate(p, 1) for p in rows], 0).astype(BF16)


def own_bias(width):
    key = lax.broadcasted_iota(jnp.int32, (HEAD_DIM, width), 0)
    query = lax.rem(lax.broadcasted_iota(jnp.int32, (HEAD_DIM, width), 1), HEAD_DIM)
    return jnp.where(key <= query, 0.0, NEG)


def earlier(pairs_ref, src, me, width):
    return pairs_ref[src, 0:1, :width] < pairs_ref[me, 0:1, :width]


def col_max(a):
    return jnp.max(a, 0, keepdims=True)


def col_sum(a):
    return jnp.sum(a, 0, keepdims=True)


class View:
    def __init__(self, r, layer):
        self.r, self.layer = r, layer

    def named(self, k):
        own = k + str(self.layer)
        return own if hasattr(self.r, own) else k

    def __getattr__(self, k):
        return getattr(self.r, self.named(k))

    def need(self, *names):
        self.r.need(*[self.named(k) for k in names])

    def flush(self, *names):
        self.r.flush(*[self.named(k) for k in names])


def forward_kernel(_, r):
    st = Stages(r)
    n, me = st.nc, st.c
    st.hail(st.beside() + st.upright(True), ring=True)
    r.load()
    wa, gu, down = [None, None], [None, None], [None, None]
    for l in range(2):
        v = View(r, l)
        wa[l] = feed_attention(st, l, r.qkv_shard, r.out_shard, v.wa)
        gu[l] = feed_windows(st, l, r.gate_shard, r.up_shard, v.gu)
        down[l] = FeedDown(st, l, r.down_shard, v.down)
    r.need("pair", "small_own", "inverse", "x0")
    r.pairs[me] = jnp.broadcast_to(r.pair[...], r.pairs.shape[1:])
    r.parts[st.s, st.z] = r.small_own[...]
    wa[0][0].wait()
    st.met()
    wa[0][1].start()
    at = st.take(2 * st.nz)
    mine = r.parts.at[st.s, st.z]
    st.begin(
        [st.copy(mine, mine, at + k, st.peer("z", k, st.s), at + st.s * st.nz + k) for k in range(1, st.nz)]
        + [st.copy(mine, mine, at + st.nz + k, st.peer("z", k, 1 - st.s), at + st.s * st.nz + k) for k in range(1, st.nz)]
        + [st.copy(mine, mine, at, st.peer("s", 0), at + st.s * st.nz)]
    )

    def tell(k, c):
        p = r.pairs.at[me]
        push(p, p, r.psem.at[k], r.psem2.at[k], "ctx", lax.rem(me + k, n)).start()
        return c

    lax.fori_loop(1, n, tell, 0)
    block = LANES // 2
    i = lax.broadcasted_iota(jnp.int32, (LANES, LANES), 0)
    pair = r.pairs[me, 0:1, :LANES]
    pos = jnp.where(i < block, pair * block + i, (2 * n - 1 - pair) * block + i - block)
    angle = pos.astype(F32) * r.inverse[...]
    lane = lax.rem(lax.broadcasted_iota(jnp.int32, (LANES, LANES), 1), HEAD_DIM)
    sine = jnp.sin(angle)
    r.cos[...] = jnp.cos(angle)
    r.sa[...] = jnp.where(lane < HEAD_DIM // 2, -sine, 0.0)
    r.sb[...] = jnp.where(lane < HEAD_DIM // 2, 0.0, sine)
    r.flush("cos", "sa", "sb")
    for h in (st.s, 1 - st.s):
        for k in range(st.nz):
            if h is st.s and k == 0:
                continue
            st.copy(mine, mine, at, st.peer("s", 0), at + h * st.nz + k).wait_recv()
    for h in range(2):
        total = r.parts[h, 0]
        for k in range(1, st.nz):
            total = total + r.parts[h, k]
        r.small[h] = total
    r.flush("small")
    for k in ORDER:
        wa[0][1].relay(k)
    gu[0][0].wait()
    gu[0][1].start()
    down[0].start()
    for k in ORDER:
        wa[0][1].collect(k)

    def begin_next():
        wa[1][0].wait()
        wa[1][1].start()
        gu[1][0].wait()
        gu[1][1].start()
        down[1].start()

    def relays(*steps):
        def go():
            for feed, name, k in steps:
                getattr(feed, name)(k)

        return go

    g0, w1, g1 = gu[0][1], wa[1][1], gu[1][1]
    wa[0][1].finish()
    v = View(r, 0)
    v.flush("wa")
    attention_forward(
        st, v, 0,
        (
            relays((g0, "relay", 1), (g0, "relay", 3)),
            relays((g0, "relay", 2)),
            begin_next,
            relays((g0, "collect", 1), (g0, "collect", 3)),
            relays((g0, "collect", 2)),
        ),
    )

    def ready_0():
        g0.finish()
        down[0].finish()
        v.flush("gu", "down")

    ffn_forward(
        st, v, ready_0,
        (
            relays((w1, "relay", 1), (w1, "relay", 3)),
            relays((w1, "relay", 2), (g1, "relay", 1)),
            relays((g1, "relay", 3), (g1, "relay", 2), (w1, "collect", 1), (w1, "collect", 3)),
            relays((w1, "collect", 2), (g1, "collect", 1), (g1, "collect", 3), (g1, "collect", 2)),
        ),
    )
    r.x1[...] = r.y0[...].astype(BF16).astype(F32)
    r.flush("y0", "x1")
    r.need("gy")
    tok = r.gy.shape[0]
    rows = st.block(st.z, tok)
    r.gy_all[rows, :] = r.gy[...].astype(BF16)
    at = st.take(st.nz - 1)
    mine_gy = r.gy_all.at[rows, :]
    gy_moving = st.begin([st.copy(mine_gy, mine_gy, at + k - 1, st.peer("z", k)) for k in range(1, st.nz)])
    w1.finish()
    v = View(r, 1)
    v.flush("wa")
    nothing = lambda: None
    attention_forward(st, v, 1, (nothing,) * 5)

    def ready_1():
        g1.finish()
        down[1].finish()
        v.flush("gu", "down")

    ffn_forward(st, v, ready_1, (nothing,) * 4)
    r.flush("y1")
    arrived(gy_moving)
    r.flush("gy_all")
    st.drain()

    def done(k, c):
        p = r.pairs.at[me]
        push(p, p, r.psem.at[k], r.psem2.at[k], "ctx", lax.rem(me + k, n)).wait_send()
        return c

    lax.fori_loop(1, n, done, 0)
    r.close()


def attention_forward(st, r, layer, between):
    n, me = st.nc, st.c
    x = r.x[...]
    r1 = lax.rsqrt(jnp.mean(x * x, -1, keepdims=True) + EPS)
    small = r.small[layer]
    n1_f = x * r1 * small[:, :D]
    n1 = n1_f.astype(BF16)
    bias = small[:, 2 * D :]
    cos, sa, sb = r.cos[...], r.sa[...], r.sb[...]
    lin = mm(n1, r.wa[:, D:QKV]) + bias[:, D:]
    r.kv[me] = jnp.concatenate([rope(lin[:, :LANES], cos, sa, sb), lin[:, LANES:]], 1).astype(BF16)

    def keys_copy(k, src):
        return push(r.kv.at[src], r.kv.at[src], r.csem.at[k], r.csem2.at[k], "ctx", lax.rem(me + k, n))

    def start(k, c):
        keys_copy(k, me).start()
        return c

    lax.fori_loop(1, n, start, 0)
    linq = mm(n1, r.wa[:, :D]) + bias[:, :D]
    for t in range(TILES):
        tile = slice(t * LANES, (t + 1) * LANES)
        q = rope(linq[:, tile], cos, sa, sb) * HEAD_DIM ** (-0.5)
        spread(r.qst, t, q.T)
        r.n1t[tile, :] = n1_f[:, tile].T.astype(BF16)
    r.flush("qst", "n1t")
    between[0]()
    half = HEAD_DIM
    own_k = own_sides(r.kv[me, :, :LANES].astype(F32))
    own_vt = own_sides(r.kv[me, :, LANES:].astype(F32)).astype(F32).T.astype(BF16)
    for cols in GROUPS:
        width = cols.stop - cols.start
        bias = own_bias(width)
        sc = mm(own_k, r.qst[:, cols])
        s_a, s_l, s_h = sc[:half], sc[half : 2 * half] + bias, sc[2 * half :] + bias
        m_lo = col_max(s_l)
        m_hi = jnp.maximum(col_max(s_a), col_max(s_h))
        p_a, p_l, p_h = jnp.exp(s_a - m_hi), jnp.exp(s_l - m_lo), jnp.exp(s_h - m_hi)
        r.m_s[0:1, cols], r.m_s[1:2, cols] = m_lo, m_hi
        r.l_s[0:1, cols], r.l_s[1:2, cols] = col_sum(p_l), col_sum(p_a) + col_sum(p_h)
        r.acc_s[:, cols] = mm(own_vt, jnp.concatenate([p_a, p_l, p_h], 0).astype(BF16))

    def step(i, c):
        kx, vt, sel = [], [], []
        for j in range(BATCH):
            k = i * BATCH + 1 + j
            src = lax.rem(me + n - k, n)
            keys_copy(k, src).wait_recv()
            if layer == 0:
                p = r.pairs.at[src]
                push(p, p, r.psem.at[k], r.psem2.at[k], "ctx", lax.rem(me + k, n)).wait_recv()
            sel.append(src)
            chosen = earlier(r.pairs, src, me, LANES)
            kx.append(sides(r.kv[src, :, :LANES].astype(F32), chosen))
            vt.append(sides_t(r.kv[src, :, LANES:].astype(F32).T, chosen))
        kx = jnp.concatenate(kx, 0)
        vt = jnp.concatenate(vt, 1)
        for cols in GROUPS:
            width = cols.stop - cols.start
            sc = mm(kx, r.qst[:, cols])
            m_lo, m_hi = r.m_s[0:1, cols], r.m_s[1:2, cols]
            n_lo, n_hi = m_lo, m_hi
            chosen = [earlier(r.pairs, src, me, width) for src in sel]
            for j in range(BATCH):
                top = col_max(sc[(2 * j + 1) * half : (2 * j + 2) * half])
                n_hi = jnp.maximum(n_hi, col_max(sc[2 * j * half : (2 * j + 1) * half]))
                n_hi = jnp.where(chosen[j], n_hi, jnp.maximum(n_hi, top))
                n_lo = jnp.where(chosen[j], jnp.maximum(n_lo, top), n_lo)
            a_lo, a_hi = jnp.exp(m_lo - n_lo), jnp.exp(m_hi - n_hi)
            l_lo, l_hi = r.l_s[0:1, cols] * a_lo, r.l_s[1:2, cols] * a_hi
            ps = []
            for j in range(BATCH):
                p_a = jnp.exp(sc[2 * j * half : (2 * j + 1) * half] - n_hi)
                p_s = jnp.exp(sc[(2 * j + 1) * half : (2 * j + 2) * half] - jnp.where(chosen[j], n_lo, n_hi))
                total = col_sum(p_s)
                l_hi = l_hi + col_sum(p_a) + jnp.where(chosen[j], 0.0, total)
                l_lo = l_lo + jnp.where(chosen[j], total, 0.0)
                ps += [p_a.astype(BF16), p_s.astype(BF16)]
            r.m_s[0:1, cols], r.m_s[1:2, cols] = n_lo, n_hi
            r.l_s[0:1, cols], r.l_s[1:2, cols] = l_lo, l_hi
            new = mm(vt, jnp.concatenate(ps, 0))
            r.acc_s[:LANES, cols] = r.acc_s[:LANES, cols] * a_lo + new[:LANES]
            r.acc_s[LANES:, cols] = r.acc_s[LANES:, cols] * a_hi + new[LANES:]
        return c

    lax.fori_loop(0, 1, step, 0)
    between[1]()
    lax.fori_loop(1, 2, step, 0)
    between[2]()
    lax.fori_loop(2, 4, step, 0)
    between[3]()
    lax.fori_loop(4, (n - 1) // BATCH, step, 0)
    between[4]()
    r.flush("kv")
    if layer == 0:
        r.flush("pairs")
    r.lse[...] = r.m_s[...] + jnp.log(r.l_s[...])
    for t in range(TILES):
        cols = slice(t * LANES, (t + 1) * LANES)
        wide = jnp.concatenate([r.acc_s[:LANES, cols] / r.l_s[0:1, cols], r.acc_s[LANES:, cols] / r.l_s[1:2, cols]], 0)
        tile_t = gathered_tile(wide, t)
        r.attt[cols, :] = tile_t.astype(BF16)
        r.att_s[:, cols] = tile_t.T.astype(BF16)
    r.flush("lse", "attt")
    mid = x + mm(r.att_s[...], r.wa[:, QKV:])
    r.mid[...] = mid
    r2 = lax.rsqrt(jnp.mean(mid * mid, -1, keepdims=True) + EPS)
    r.all[st.z] = (mid * r2 * small[:, D : 2 * D]).astype(BF16)
    r.flush("mid")

    def done(k, c):
        keys_copy(k, me).wait_send()
        return c

    lax.fori_loop(1, n, done, 0)


def ffn_forward(st, r, ready, between):
    n, me = st.nz, st.z
    at = st.take(2 * n)

    def first(k):
        return st.copy(r.all.at[me], r.all.at[me], at + k, st.peer("z", k))

    def second(k):
        return st.copy(r.send_s.at[k], r.land_s.at[k], at + n + k, st.peer("z", -k))

    for k in ORDER:
        first(k).start()
    ready()

    def block(src):
        a = r.all[src]
        gate = mm(a, r.gu[0])
        up = mm(a, r.gu[1])
        r.gate[src] = gate.astype(BF16)
        r.up[src] = up.astype(BF16)
        hidden = (gate * jax.nn.sigmoid(gate) * up).astype(BF16)
        return mm(hidden, r.down[...])

    r.y[...] = r.mid[...] + block(me)
    for i, k in enumerate(ORDER):
        between[i]()
        first(k).wait_recv()
        r.send_s[k] = block(st.along("z", -k)).astype(BF16)
        second(k).start()
    r.flush("all", "gate", "up")
    between[3]()
    for k in ORDER:
        second(k).wait_recv()
        r.y[...] += r.land_s[k].astype(F32)
    for k in ORDER:
        first(k).wait_send()
        second(k).wait_send()


class Attention:
    def __init__(self, st):
        self.st = st

    def columns(self, src, dst):
        st = self.st
        share = dst.shape[0]
        at = st.take(st.nz - 1)
        mine = dst.at[:, pl.ds(pl.multiple_of(st.z * LANES, LANES), LANES)]
        moving = st.begin(
            [
                st.copy(src.at[st.block(st.along("z", k), share), :], mine, at + k - 1, st.peer("z", k))
                for k in range(1, st.nz)
            ]
        )
        mine[...] = src[st.block(st.z, share), :]
        return moving

    def whole(self, dst):
        st = self.st
        rows = dst.shape[0] // st.nz
        at = st.take(st.nz - 1)
        mine = dst.at[pl.ds(pl.multiple_of(st.z * rows, UNIT), rows), :]
        return st.begin([st.copy(mine, mine, at + k - 1, st.peer("z", k)) for k in range(1, st.nz)])

    def begin(self, glin, small, all_glin, all_small):
        st = self.st
        tok = glin.shape[0]
        all_glin[st.block(st.z, tok), :] = glin[...]
        all_small[st.block(st.z, 2 * UNIT), :] = small[...]
        return self.whole(all_glin) + self.whole(all_small)

    def swap(self, moving, n1z, all_glin, all_small, dout, made, land):
        st = self.st
        arrived(moving)
        share = n1z.shape[0]
        per = 8
        for j in range(0, QKV // LANES, 2):
            cols = slice(j * LANES, min(j + 2, QKV // LANES) * LANES)
            d = mm(n1z[...], all_glin[:, cols]).astype(BF16)
            for t in range(j, min(j + 2, QKV // LANES)):
                made[t // per, (t % per) * share : (t % per + 1) * share, :] = d[:, (t - j) * LANES : (t - j + 1) * LANES]
        made[1, share : 8 * share, :] = dout[...]
        small = jnp.zeros((2 * UNIT, LANES), F32)
        for i in range(st.nz):
            small = small + all_small[i * 2 * UNIT : (i + 1) * 2 * UNIT, :]
        made[0, 8 * share : 8 * share + 2 * UNIT, :] = small.astype(BF16)
        made[0, 8 * share + 2 * UNIT :, :] = jnp.zeros((Q_ROWS - 8 * share - 2 * UNIT, LANES), BF16)
        made[1, 8 * share :, :] = jnp.zeros((Q_ROWS - 8 * share, LANES), BF16)
        return st.swap(made, land)

    def fold(self, moving, made, land, out):
        st = self.st
        arrived(moving)
        rows = Q_ROWS // 2 // 16
        for h in range(2):
            for i in range(16):
                at = slice((h * 16 + i) * rows, (h * 16 + i + 1) * rows)
                total = made[st.s, at, :].astype(F32) + land[at, :].astype(F32)
                out[h][i // SIDE, i % SIDE] = total.astype(BF16)


class Rest:
    def __init__(self, st, t1, l2, t2, g1, out, layer):
        self.st, self.t1, self.l2, self.t2, self.g1, self.out, self.layer = st, t1, l2, t2, g1, out, layer
        self.stage = 0
        self.moving = [st.scatter(AXES[h][1], t1[h], l2[h]) for h in range(2)]

    def advance(self):
        st = self.st
        for h in range(2):
            second = AXES[h][1]
            arrived(self.moving[h])
            mine = self.g1[h].at[st.along(second, 0)]
            if self.stage == 0:
                t2 = self.t2[h]
                add_rows(t2, [self.t1[h].at[st.along(second, 0)]] + [self.l2[h].at[k] for k in range(SIDE - 1)])
                per = GATE_PER[h] * UNIT
                self.moving[h] = st.deal(t2, mine, per)
                mine[st.block(st.z, per), :] = t2[st.block(st.z, per), :]
                mine[st.nz * per :, :] = t2[st.nz * per :, :]
            elif self.stage == 1:
                self.moving[h] = st.gather(second, self.g1[h])
            else:
                self.moving[h] = st.hand_over(AXES[h][0], self.g1[h], self.out[h], self.layer)
        self.stage += 1

    def landed(self):
        for h in range(2):
            arrived(self.moving[h])

    def finish(self):
        for h in range(2):
            self.moving[h]()


class Few:
    def __init__(self, st, r, tag):
        self.st = st

        def both(name):
            return tuple(getattr(r, name + tag + h) for h in "ab")

        self.qp, self.land, self.part, self.land2, self.wide = both("qp"), both("qm"), both("qe"), both("qw"), both("qh")
        self.moving = [st.scatter(AXES[h][0], self.qp[h], self.land[h]) for h in range(2)]

    def second_sum(self):
        st = self.st
        for h in range(2):
            arrived(self.moving[h])
            own = self.qp[h].at[st.along(AXES[h][0], 0)]
            add_into(self.part[h], [own] + [self.land[h].at[k] for k in range(SIDE - 1)])
            self.moving[h] = st.scatter(AXES[h][1], self.part[h], self.land2[h])

    def first_gather(self):
        st = self.st
        for h in range(2):
            arrived(self.moving[h])
            i = st.along(AXES[h][1], 0)
            add_rows(self.wide[h].at[i], [self.part[h].at[i]] + [self.land2[h].at[k] for k in range(SIDE - 1)])
            self.moving[h] = st.gather(AXES[h][1], self.wide[h])

    def landed(self):
        for h in range(2):
            arrived(self.moving[h])


def backward_kernel(layer, r):
    st = Stages(r)
    n, me = st.nz, st.z
    carry = layer == 0
    ids = st.upright() + st.beside()
    if carry:
        ids += [st.peer(a, k, 1 - st.s) for a in "xy" for k in range(1, SIDE)]
    st.hail(ids, ring=True)
    r.load()
    tok = r.gy.shape[0]

    def rows_of(i):
        return pl.ds(pl.multiple_of(i * tok, tok), tok)

    r.need("gy")
    gyb = r.gy[...].astype(BF16)
    gy = gyb.astype(F32) if carry else r.gy[...]
    if carry:
        r.all_s[rows_of(me), :] = gyb
    else:
        r.need("all_s")
    st.met()
    at = st.take(2 * n)

    def first(k):
        mine = r.all_s.at[rows_of(me), :]
        return st.copy(mine, mine, at + k, st.peer("z", k))

    def second(k):
        return st.copy(r.send_s.at[k], r.land_s.at[k], at + n + k, st.peer("z", -k))

    if carry:
        for k in ORDER:
            first(k).start()
        r.need("p1a", "p1b")
        rest = Rest(st, (r.p1a, r.p1b), (r.l2a, r.l2b), (r.t2a, r.t2b), (r.g1a, r.g1b), (r.ga, r.gb), 1)
    r.need("down", "gate", "up", "gu")

    def block(src):
        rows = rows_of(src)
        gh = mm_nt(r.all_s[rows, :], r.down[...])
        gate, up = r.gate[src].astype(F32), r.up[src].astype(F32)
        sg = jax.nn.sigmoid(gate)
        act = gate * sg
        r.hid_s[rows, :] = (act * up).astype(BF16)
        ggate = (gh * up * sg * (1.0 + gate * (1.0 - sg))).astype(BF16)
        gup = (gh * act).astype(BF16)
        r.g_s[0, rows, :] = ggate
        r.g_s[1, rows, :] = gup
        return mm_nt(ggate, r.gu[0]) + mm_nt(gup, r.gu[1])

    r.own_s[...] = block(me)
    for k in ORDER:
        if carry:
            rest.advance()
            first(k).wait_recv()
        r.send_s[k] = block(st.along("z", -k)).astype(BF16)
        second(k).start()

    refs = (r.fa, r.fb)
    share = D // n
    for j in range(WIN // (2 * LANES)):
        cols = slice(2 * j * LANES, 2 * (j + 1) * LANES)
        r.down_s[cols, :] = mm_tn(r.hid_s[:, cols], r.all_s[...]).astype(BF16)
    pad = (WIN - FF // n) * lax.rem(me, 2)
    half = FF // n // 2
    base = [n * per * UNIT for per in GATE_PER]
    for section in range(2):
        rows = r.down_s[pl.ds(pl.multiple_of(pad + section * half, UNIT), half), :]
        for t in range(TILES):
            put_units(refs, section, base, DOWN_PER, t * (half // UNIT), rows[:, t * LANES : (t + 1) * LANES])
        used = TILES * (half // UNIT)
        extra = 16 * sum(DOWN_PER) - used
        put_units(refs, section, base, DOWN_PER, used, jnp.zeros((extra * UNIT, LANES), BF16))
    r.need("n2_all")
    normed = jnp.concatenate([r.n2_all[i] for i in range(n)], 0)

    def product(section):
        for j in range(WIN // (2 * LANES)):
            d = mm_tn(normed, r.g_s[section, :, 2 * j * LANES : 2 * (j + 1) * LANES]).astype(BF16)
            for t in (2 * j, 2 * j + 1):
                tile = d[:, (t % 2) * LANES : (t % 2 + 1) * LANES]
                for i in range(n):
                    base = [i * per * UNIT for per in GATE_PER]
                    put_units(refs, section, base, GATE_PER, t * (share // UNIT), tile[i * share : (i + 1) * share, :])
        used = WIN // LANES * (share // UNIT)
        extra = 16 * sum(GATE_PER) - used
        for i in range(n):
            base = [i * per * UNIT for per in GATE_PER]
            put_units(refs, section, base, GATE_PER, used, jnp.zeros((extra * UNIT, LANES), BF16))

    product(1 - st.s)
    swaps = [st.swap(refs[h], (r.sla, r.slb)[h]) for h in range(2)]
    product(st.s)
    for k in ORDER:
        second(k).wait_recv()
        r.own_s[...] += r.land_s[k].astype(F32)
    gn2 = r.own_s[...]
    r.need("mid", "small")
    mid = r.mid[...]
    r2 = lax.rsqrt(jnp.mean(mid * mid, -1, keepdims=True) + EPS)
    unit = mid * r2
    dg2 = col_sum(gn2 * unit)
    dz = gn2 * r.small[layer][:, D : 2 * D]
    gm = gy + r2 * (dz - unit * jnp.mean(dz * unit, -1, keepdims=True))
    r.gm_s[...] = gm
    for k in ORDER:
        if carry:
            first(k).wait_send()
        second(k).wait_send()
    attention_backward(st, r, layer, gm, dg2, refs, swaps, rest if carry else None)


def attention_backward(st, r, layer, gm, dg2, refs, swaps, rest):
    n, me = st.nc, st.c
    last = layer == 0
    half = HEAD_DIM
    gmb = gm.astype(BF16)
    tok = gm.shape[0]
    r.all_gm[st.block(st.z, tok), :] = gmb
    sl, l1, t1 = (r.sla, r.slb), (r.l1a, r.l1b), (r.t1a, r.t1b)
    r.need("attt", "n1t")
    attention = Attention(st)
    size = 2 * BATCH * half
    pr, ds, gst = r.g_s.at[0, :size, :WIDE], r.g_s.at[1, :size, :WIDE], r.hid_s.at[: 2 * LANES, :WIDE]
    out_factors = attention.whole(r.all_gm) + attention.columns(r.attt, r.attz)
    qkv_factor = attention.columns(r.n1t, r.n1z)
    if last:
        r.need("glin1", "gsmall1", "n1z1", "dout1")
        before = attention.begin(r.glin1, r.gsmall1, r.all_glin, r.all_small)
    r1 = []
    for h in range(2):
        swapped_sum(st, swaps[h], refs[h], sl[h])
        r1.append(st.scatter(AXES[h][0], sl[h], l1[h]))
    r.need("wa", "qst", "lse", "kv", "pairs")
    ga = mm_nt(gmb, r.wa[:, QKV:])
    for t in range(TILES):
        tile = slice(t * LANES, (t + 1) * LANES)
        ga_t = ga[:, tile].T
        spread(gst, t, ga_t)
        prod = ga_t * r.attt[tile, :].astype(F32)
        low, high = halves(col_sum(prod[:half]), col_sum(prod[half:]))
        r.delta_s[0:1, tile], r.delta_s[1:2, tile] = low, high

    def own_block():
        keys, vals = r.kv[me, :, :LANES].astype(F32), r.kv[me, :, LANES:].astype(F32)
        kx, vx = own_sides(keys), own_sides(vals)
        kt = kx.astype(F32).T.astype(BF16)
        rows = slice(0, 3 * half)
        for cols in GROUPS:
            bias = own_bias(cols.stop - cols.start)
            sc = mm(kx, r.qst[:, cols])
            dp = mm(vx, gst[:, cols])
            lo, hi = (r.lse[0:1, cols], r.delta_s[0:1, cols]), (r.lse[1:2, cols], r.delta_s[1:2, cols])
            parts = [(sc[:half], hi), (sc[half : 2 * half] + bias, lo), (sc[2 * half :] + bias, hi)]
            for i, (part, (lse, delta)) in enumerate(parts):
                p = jnp.exp(part - lse)
                at = slice(i * half, (i + 1) * half)
                pr[at, cols] = p.astype(BF16)
                ds[at, cols] = (p * (dp[at] - delta)).astype(BF16)
            r.gq_s[:, cols] = mm(kt, ds[rows, cols])
        made = []
        for w, q in ((ds, r.qst), (pr, gst)):
            e = mm_nt(w[rows, :], q[...])
            low = e[:half, LANES:] + e[half : 2 * half, :LANES]
            made.append(jnp.concatenate([low, e[2 * half :, LANES:]], 0))
        return jnp.concatenate(made, 1)

    def sum_copy(k):
        return push(r.send_k.at[k], r.land_k.at[k], r.csem.at[k], r.csem2.at[k], "ctx", lax.rem(me + k, n))

    def step(i):
        kx, vx, kt, sel = [], [], [], []
        for j in range(BATCH):
            src = lax.rem(me + i * BATCH + 1 + j, n)
            sel.append(src)
            chosen = earlier(r.pairs, src, me, LANES)
            keys = r.kv[src, :, :LANES].astype(F32)
            kx.append(sides(keys, chosen))
            vx.append(sides(r.kv[src, :, LANES:].astype(F32), chosen))
            kt.append(sides_t(keys.T, chosen))
        kx, vx, kt = jnp.concatenate(kx, 0), jnp.concatenate(vx, 0), jnp.concatenate(kt, 1)
        rows = slice(0, 2 * BATCH * half)
        for cols in GROUPS:
            width = cols.stop - cols.start
            sc = mm(kx, r.qst[:, cols])
            dp = mm(vx, gst[:, cols])
            for j in range(BATCH):
                chosen = earlier(r.pairs, sel[j], me, width)
                for part in range(2):
                    lse, delta = r.lse[1:2, cols], r.delta_s[1:2, cols]
                    if part:
                        lse = jnp.where(chosen, r.lse[0:1, cols], lse)
                        delta = jnp.where(chosen, r.delta_s[0:1, cols], delta)
                    at = slice((2 * j + part) * half, (2 * j + part + 1) * half)
                    p = jnp.exp(sc[at] - lse)
                    pr[at, cols] = p.astype(BF16)
                    ds[at, cols] = (p * (dp[at] - delta)).astype(BF16)
            r.gq_s[:, cols] += mm(kt, ds[rows, cols])
        ek = mm_nt(ds[rows, :], r.qst[...])
        ev = mm_nt(pr[rows, :], gst[...])
        for j in range(BATCH):
            chosen = earlier(r.pairs, sel[j], me, LANES)
            k = i * BATCH + 1 + j
            for e, lanes in ((ek, slice(0, LANES)), (ev, slice(LANES, 2 * LANES))):
                top = e[2 * j * half : (2 * j + 1) * half]
                low = e[(2 * j + 1) * half : (2 * j + 2) * half]
                r.send_k[k, :half, lanes] = (top[:, LANES:] + jnp.where(chosen, low[:, :LANES], 0.0)).astype(BF16)
                r.send_k[k, half:, lanes] = jnp.where(chosen, 0.0, low[:, LANES:]).astype(BF16)
            sum_copy(k).start()

    own = own_block()
    for i in range(3):
        step(i)
    arrived(out_factors)
    share = D // st.nz
    for j in range(0, TILES, 2):
        cols = slice(j * LANES, min(j + 2, TILES) * LANES)
        d = mm(r.attz[...], r.all_gm[:, cols]).astype(BF16)
        for t in range(j, min(j + 2, TILES)):
            r.dout[t * share : (t + 1) * share, :] = d[:, (t - j) * LANES : (t - j + 1) * LANES]
    r.flush("dout")
    if last:
        rest.finish()
        qswap = attention.swap(before, r.n1z1, r.all_glin, r.all_small, r.dout1, r.qv, r.ql)
    for i in range(3, (n - 1) // BATCH):
        step(i)
    arrived(qkv_factor)
    r.flush("n1z")
    if last:
        attention.fold(qswap, r.qv, r.ql, (r.qpa, r.qpb))
        few = Few(st, r, "")
        for h in range(2):
            arrived(r1[h])
            mine = sl[h].at[st.along(AXES[h][0], 0)]
            add_into(t1[h], [mine] + [l1[h].at[k] for k in range(SIDE - 1)])
        own_rest = Rest(st, t1, (r.l2c, r.l2d), (r.t2c, r.t2d), (r.g1c, r.g1d), None, 0)

    def take(k, total):
        sum_copy(k).wait_recv()
        return total + r.land_k[k].astype(F32)

    own = lax.fori_loop(1, n, take, own)
    if last:
        few.second_sum()
        own_rest.advance()
    r.need("cos", "sa", "sb", "x", "small")
    cos, sa, sb = r.cos[...], r.sa[...], r.sb[...]
    for t in range(TILES):
        gq = gathered_tile(r.gq_s[:, t * LANES : (t + 1) * LANES], t).T * HEAD_DIM ** (-0.5)
        r.glin[:, t * LANES : (t + 1) * LANES] = unrope(gq, cos, sa, sb).astype(BF16)
    r.glin[:, D : D + LANES] = unrope(own[:, :LANES], cos, sa, sb).astype(BF16)
    r.glin[:, D + LANES :] = own[:, LANES:].astype(BF16)
    r.flush("glin")
    gn1 = mm_nt(r.glin[...], r.wa[:, :QKV])
    x = r.x[...]
    r1_ = lax.rsqrt(jnp.mean(x * x, -1, keepdims=True) + EPS)
    unit = x * r1_
    dz = gn1 * r.small[layer][:, :D]
    r.gx[...] = r.gm_s[...] + r1_ * (dz - unit * jnp.mean(dz * unit, -1, keepdims=True))
    r.flush("gx")
    dg1 = col_sum(gn1 * unit)
    dbias = col_sum(r.glin[...].astype(F32))
    r.gsmall[...] = jnp.zeros(r.gsmall.shape, F32)
    row = 0
    for part in (dg1, dg2, dbias):
        for t in range(part.shape[1] // LANES):
            r.gsmall[row : row + 1, :] = part[:, t * LANES : (t + 1) * LANES]
            row += 1
    r.flush("gsmall")
    if last:
        few.first_gather()
        own_rest.advance()
        own_rest.landed()
        few.landed()
    else:
        for h in range(2):
            arrived(r1[h])
            mine = sl[h].at[st.along(AXES[h][0], 0)]
            add_into(t1[h], [mine] + [l1[h].at[k] for k in range(SIDE - 1)])
    st.drain()

    def done(k, c):
        sum_copy(k).wait_send()
        return c

    lax.fori_loop(1, n, done, 0)
    r.close()


def reduce_kernel(_, r):
    st = Stages(r)
    st.hail(st.beside() + st.upright() + st.flat(True))
    r.load()
    r.need("glin", "gsmall")
    attention = Attention(st)
    st.met()
    factors = attention.begin(r.glin, r.gsmall, r.all_glin, r.all_small)
    r.need("g1a", "g1b", "h1a", "h1b")
    last = []
    for h in range(2):
        last.append(st.hand_over(AXES[h][0], (r.g1a, r.g1b)[h], (r.ga, r.gb)[h], 0))
    for h in range(2):
        last.append(st.hand_over(AXES[h][0], (r.h1a, r.h1b)[h], (r.qa, r.qb)[h], 1))
    r.need("n1z", "dout")
    qswap = attention.swap(factors, r.n1z, r.all_glin, r.all_small, r.dout, r.qv, r.ql)
    attention.fold(qswap, r.qv, r.ql, (r.qpa, r.qpb))
    few = Few(st, r, "")
    few.second_sum()
    few.first_gather()
    for h in range(2):
        arrived(few.moving[h])
        last.append(st.hand_over(AXES[h][0], few.wide[h], (r.qa, r.qb)[h], 0))
    for finish in last:
        finish()
    st.drain()
    r.close()


class Refs(types.SimpleNamespace):
    def load(self):
        for c in self.coming.values():
            c.start()

    def need(self, *names):
        for k in names:
            if k not in self.here:
                self.coming[k].wait()
                self.here.add(k)

    def flush(self, *names):
        for k in names:
            self.going[k].start()
            self.gone.add(k)

    def close(self):
        self.need(*self.coming)
        self.flush(*[k for k in self.going if k not in self.gone])
        for c in self.going.values():
            c.wait()


def call(kernel, layer, cid, name, ins, outs, scratch, sems, hbm=(), flops=10**10):
    staged = [k for k in ins if k not in hbm]
    made = [k for k in outs if k not in hbm]
    dma = pltpu.SemaphoreType.DMA
    counts = dict(ssem=sems, rsem=sems, lsem=16, csem=16, csem2=16, psem=16, psem2=16, isem=len(staged), osem=len(made))
    if name == "forward":
        counts.update(csem1=16, csem21=16)
    places = [pltpu.VMEM(ins[k].shape, ins[k].dtype) for k in staged] + [pltpu.VMEM(*outs[k]) for k in made]
    names = ["in_" + k for k in ins] + ["out_" + k for k in outs] + staged + made + list(scratch) + list(counts)

    def body(*refs):
        r = Refs(**dict(zip(names, refs)))
        for k in hbm:
            if k in ins or k in outs:
                setattr(r, k, getattr(r, ("in_" if k in ins else "out_") + k))
        r.here, r.gone = set(), set()
        r.coming = {
            k: pltpu.make_async_copy(getattr(r, "in_" + k), getattr(r, k), r.isem.at[i]) for i, k in enumerate(staged)
        }
        r.going = {
            k: pltpu.make_async_copy(getattr(r, k), getattr(r, "out_" + k), r.osem.at[i]) for i, k in enumerate(made)
        }
        kernel(layer, r)

    anywhere = pl.BlockSpec(memory_space=pl.ANY)
    got = pl.pallas_call(
        body,
        out_shape=[jax.ShapeDtypeStruct(s, t) for s, t in outs.values()],
        in_specs=[anywhere] * len(ins),
        out_specs=[anywhere] * len(outs),
        scratch_shapes=places + [pltpu.VMEM(s, t) for s, t in scratch.values()] + [dma((k,)) for k in counts.values()],
        compiler_params=pltpu.CompilerParams(
            collective_id=cid, has_side_effects=True, vmem_limit_bytes=VMEM_LIMIT
        ),
        cost_estimate=pl.CostEstimate(flops=flops, bytes_accessed=20 * 2**20, transcendentals=0),
        name=name,
    )(*ins.values())
    return dict(zip(outs, got))


FA_ROWS = tuple((4 * g + d) * UNIT for g, d in zip(GATE_PER, DOWN_PER))
RQ = Q_ROWS // 2 // 16
SIDES = (SIDE, SIDE)
WIDE = HEADS * HEAD_DIM


def bf(*shape):
    return (shape, BF16)


def f4(*shape):
    return (shape, F32)


def rest_scratch():
    made = {}
    for h, rows in zip("ab", FA_ROWS):
        made["l2" + h] = bf(SIDE - 1, rows, LANES)
        made["t2" + h] = bf(rows, LANES)
        made["g1" + h] = bf(SIDE, rows, LANES)
    return made


def rest_outs():
    return {"g" + h: bf(2, *SIDES, rows, LANES) for h, rows in zip("ab", FA_ROWS)}


def assemble_kernel(nz, *refs):
    given, results, held, outs, sem, osem = (refs[:2], refs[2:4]), refs[6:12], refs[12:14] + refs[4:6], refs[14:20], refs[20], refs[21]
    s = lax.axis_index("section")
    copies = [pltpu.make_async_copy(a, b, osem.at[i]) for i, (a, b) in enumerate(zip(outs, results))]
    for layer in range(2):
        @pl.when(s == layer)
        def _():
            moving = [pltpu.make_async_copy(a, b, sem.at[i]) for i, (a, b) in enumerate(zip(given[layer], held))]
            for c in moving:
                c.start()
            for c in moving:
                c.wait()

    gate_ref, up_ref, down_ref, qkv_ref, out_ref, small_ref = outs
    share = D // nz
    starts = window_starts(nz)

    def units(refs, section, base, per, first, count):
        rows = []
        for part, piece, slot, _, m in unit_runs(first, count, per):
            at = base[part] + slot * UNIT
            rows.append(refs[part][section, piece // SIDE, piece % SIDE, at : at + m * UNIT, :].astype(F32))
        return jnp.concatenate(rows, 0) if len(rows) > 1 else rows[0]

    for section, ref in ((0, gate_ref), (1, up_ref)):
        tiles = {}
        for w, a in enumerate(starts):
            for t in range(WIN // LANES):
                tiles.setdefault(a // LANES + t, []).append((w, t))
        for col, sources in tiles.items():
            total = None
            for w, t in sources:
                base = [w * per * UNIT for per in GATE_PER]
                got = units(held[:2], section, base, GATE_PER, t * (share // UNIT), share // UNIT)
                total = got if total is None else total + got
            ref[:, col * LANES : (col + 1) * LANES] = total
        copies[section].start()
    base = [nz * per * UNIT for per in GATE_PER]
    half = FF // nz // 2
    for section in range(2):
        for t in range(TILES):
            got = units(held[:2], section, base, DOWN_PER, t * (half // UNIT), half // UNIT)
            down_ref[section * half : (section + 1) * half, t * LANES : (t + 1) * LANES] = got
    copies[2].start()
    for t in range(QKV // LANES + TILES):
        got = units(held[2:], t // 8, (0, 0), Q_PER, (t % 8) * (share // UNIT), share // UNIT)
        if t < QKV // LANES:
            qkv_ref[:, t * LANES : (t + 1) * LANES] = got
        else:
            u = t - QKV // LANES
            out_ref[:, u * LANES : (u + 1) * LANES] = got
    small_ref[...] = units(held[2:], 0, (0, 0), Q_PER, 8 * (share // UNIT), 2)
    for c in copies[3:]:
        c.start()
    for c in copies:
        c.wait()


def assemble(zero, one, attn):
    nz = lax.axis_size("fsdp")
    vm = pl.BlockSpec(memory_space=pltpu.VMEM)
    anywhere = pl.BlockSpec(memory_space=pl.ANY)
    share = D // nz
    shapes = [(share, FF), (share, FF), (FF // nz, D), (share, QKV), (share, D), (2 * UNIT, LANES)]
    return pl.pallas_call(
        functools.partial(assemble_kernel, nz),
        out_shape=[jax.ShapeDtypeStruct(a, F32) for a in shapes],
        in_specs=[anywhere] * 4 + [vm] * 2,
        out_specs=[anywhere] * len(shapes),
        scratch_shapes=[pltpu.VMEM(a.shape, a.dtype) for a in zero]
        + [pltpu.VMEM(a, F32) for a in shapes]
        + [pltpu.SemaphoreType.DMA((2,)), pltpu.SemaphoreType.DMA((len(shapes),))],
        compiler_params=pltpu.CompilerParams(vmem_limit_bytes=VMEM_LIMIT),
        name="assemble",
    )(*zero, *one, *attn)


def window_starts(n):
    share = FF // n
    return [(i * share // LANES) * LANES for i in range(n)]


def forward(x, gy, shards, small, pair):
    n, nz = lax.axis_size("ctx"), lax.axis_size("fsdp")
    tok = x.shape[0]
    freq = jnp.arange(HEAD_DIM // 2, dtype=F32)
    inverse = jnp.tile(THETA ** (-2.0 * freq / HEAD_DIM), 4)[None, :]
    ins = dict(small_own=small, pair=pair, inverse=inverse, x0=x, gy=gy)
    hbm = {k + "_shard": v for k, v in shards.items()}
    ins.update(hbm)
    outs = dict(
        small=f4(2, 1, SMALL), pairs=((n, 8, 2 * LANES), jnp.int32), cos=f4(tok, LANES), sa=f4(tok, LANES), sb=f4(tok, LANES),
        x1=f4(tok, D), gy_all=bf(nz * tok, D),
    )
    scratch = dict(m_s=f4(2, WIDE), l_s=f4(2, WIDE), acc_s=f4(2 * LANES, WIDE), att_s=bf(tok, D), parts=f4(2, nz, 1, SMALL))
    for l in "01":
        each = dict(
            mid=f4(tok, D), n1t=bf(D, tok), qst=bf(2 * LANES, WIDE), kv=bf(n, tok, 2 * LANES), lse=f4(2, WIDE),
            attt=bf(D, tok), gu=bf(2, D, WIN), down=bf(WIN, D), wa=bf(D, QKV + D),
            y=f4(tok, D), all=bf(nz, tok, D), gate=bf(nz, tok, WIN), up=bf(nz, tok, WIN),
        )
        outs.update({k + l: v for k, v in each.items()})
        scratch.update({"send_s" + l: bf(nz, tok, D), "land_s" + l: bf(nz, tok, D)})
    return call(forward_kernel, 0, 1, "forward", ins, outs, scratch, 160, tuple(hbm))


def backward(layer, gy, f, before):
    n, nz = lax.axis_size("ctx"), lax.axis_size("fsdp")
    tok = gy.shape[0]
    share = D // nz
    own = {k: f[k + str(layer)] for k in ("down", "gate", "up", "gu", "all", "mid", "attt", "n1t", "qst", "lse", "kv", "wa")}
    ins = dict(gy=gy)
    outs = dict(
        gx=f4(tok, D), glin=bf(tok, QKV), gsmall=f4(2 * UNIT, LANES), n1z=bf(share, nz * tok), dout=bf(TILES * share, LANES)
    )
    scratch = dict(
        hid_s=bf(nz * tok, WIN), g_s=bf(2, nz * tok, WIN), down_s=bf(WIN, D), gm_s=f4(tok, D),
        own_s=f4(tok, D), send_s=bf(nz, tok, D), land_s=bf(nz, tok, D),
        delta_s=f4(2, WIDE), gq_s=f4(2 * LANES, WIDE), all_gm=bf(nz * tok, D), attz=bf(share, nz * tok),
        send_k=bf(n, tok, 2 * LANES), land_k=bf(n, tok, 2 * LANES),
    )
    for h, rows in zip("ab", FA_ROWS):
        scratch["f" + h] = bf(2, *SIDES, rows, LANES)
        scratch["sl" + h] = bf(*SIDES, rows, LANES)
        scratch["l1" + h] = bf(SIDE - 1, SIDE, rows, LANES)
    if layer == 0:
        scratch["all_s"] = bf(nz * tok, D)
        ins.update(p1a=before["t1a"], p1b=before["t1b"])
        scratch.update(rest_scratch())
        outs.update(rest_outs())
    else:
        ins["all_s"] = f["gy_all"]
    ins.update(down=own["down"], gate=own["gate"], up=own["up"], gu=own["gu"], n2_all=own["all"], mid=own["mid"])
    ins["small"] = f["small"]
    ins.update({k: own[k] for k in ("attt", "n1t")})
    if layer == 0:
        ins.update(glin1=before["glin"], gsmall1=before["gsmall"], n1z1=before["n1z"], dout1=before["dout"])
        scratch.update(attention_scratch(tok))
        scratch.update(few_scratch())
        scratch.update(t1a=bf(SIDE, FA_ROWS[0], LANES), t1b=bf(SIDE, FA_ROWS[1], LANES))
        for h, rows in zip("cd", FA_ROWS):
            scratch["l2" + h] = bf(SIDE - 1, rows, LANES)
            scratch["t2" + h] = bf(rows, LANES)
            outs["g1" + h] = bf(SIDE, rows, LANES)
        for h in "ab":
            outs["qh" + h] = bf(SIDE, RQ, LANES)
    else:
        outs.update(t1a=bf(SIDE, FA_ROWS[0], LANES), t1b=bf(SIDE, FA_ROWS[1], LANES))
    ins.update({k: own[k] for k in ("qst", "lse", "kv", "wa")})
    ins.update({k: f[k] for k in ("pairs", "cos", "sa", "sb")})
    ins["x"] = f["x" + str(layer)] if layer else before["x0"]
    return call(backward_kernel, layer, 2 + layer, f"backward_{layer}", ins, outs, scratch, 112, ("ga", "gb"), 3 * 10**10)


def attention_scratch(tok):
    nz = lax.axis_size("fsdp")
    return dict(
        all_glin=bf(nz * tok, QKV), all_small=f4(nz * 2 * UNIT, LANES), qv=bf(2, Q_ROWS, LANES), ql=bf(Q_ROWS, LANES),
        qpa=bf(*SIDES, RQ, LANES), qpb=bf(*SIDES, RQ, LANES),
    )


def few_scratch():
    made = {}
    for h in "ab":
        made["qm" + h] = bf(SIDE - 1, SIDE, RQ, LANES)
        made["qw" + h] = bf(SIDE - 1, RQ, LANES)
        made["qe" + h] = bf(SIDE, RQ, LANES)
    return made


def reduce_rest(last):
    ins = dict(glin=last["glin"], gsmall=last["gsmall"], g1a=last["g1c"], g1b=last["g1d"], h1a=last["qha"], h1b=last["qhb"])
    ins.update(n1z=last["n1z"], dout=last["dout"])
    outs = rest_outs()
    scratch = attention_scratch(last["glin"].shape[0])
    scratch.update(few_scratch())
    for h in "ab":
        outs["q" + h] = bf(2, *SIDES, RQ, LANES)
        scratch["qh" + h] = bf(SIDE, RQ, LANES)
    return call(reduce_kernel, 0, 9, "reduce", ins, outs, scratch, 96, ("ga", "gb", "qa", "qb"))


def local(
    tokens, cotangent, pair_of, attn_gain, ffn_gain, qkv_weight, qkv_bias, out_weight, gate_weight, up_weight, down_weight,
):
    s = lax.axis_index("section")
    z = lax.axis_index("fsdp")
    nz = lax.axis_size("fsdp")
    qd = D // nz
    shards = dict(qkv=qkv_weight, out=out_weight, gate=gate_weight, up=up_weight, down=down_weight)

    def placed(part, size):
        whole = jnp.zeros((1, size), F32)
        return lax.dynamic_update_slice(whole, part.astype(F32), (0, z * part.shape[1]))

    small_own = jnp.concatenate([placed(attn_gain, D), placed(ffn_gain, D), placed(qkv_bias, QKV)], 1)
    pair = jnp.broadcast_to(pair_of.reshape(1, 1), (8, 2 * LANES))
    x0 = jnp.where(s == 0, tokens[0, 0], tokens[1, 0])
    gy = jnp.where(s == 0, cotangent[0, 0], cotangent[1, 0])
    f = forward(x0, gy, shards, small_own, pair)
    c1 = backward(1, gy, f, None)
    c0 = backward(0, c1["gx"], f, dict(c1, x0=x0))
    t = reduce_rest(c0)
    dgate, dup, ddown, dqkv, dout, small_grad = assemble((t["ga"], t["gb"]), (c0["ga"], c0["gb"]), (t["qa"], t["qb"]))
    small_grad = small_grad.reshape(-1)

    def mine(first, size):
        return lax.dynamic_slice_in_dim(small_grad, first + z * size, size, 0)[None]

    def by_layer(pair):
        theirs = jnp.where(s == 0, pair[1], pair[0])
        mine = jnp.where(s == 0, pair[0], pair[1])
        got = lax.ppermute(theirs, "section", [(0, 1), (1, 0)])
        return jnp.where(s == 0, jnp.stack([mine, got]), jnp.stack([got, mine]))[None, :, None]

    return (
        by_layer((f["y0"], f["y1"])),
        by_layer((c0["gx"], c1["gx"])),
        mine(0, qd),
        mine(D, qd),
        dqkv[None],
        mine(2 * D, QKV // nz),
        dout[None],
        dgate[None],
        dup[None],
        ddown[None],
    )


def solution(mesh):
    return jax.shard_map(
        local,
        mesh=mesh,
        in_specs=(
            P(None, "fsdp", "ctx", None),
            P(None, "fsdp", "ctx", None),
            P("ctx"),
            P("section", "fsdp"),
            P("section", "fsdp"),
            P("section", "fsdp", None),
            P("section", "fsdp"),
            P("section", "fsdp", None),
            P("section", "fsdp", None),
            P("section", "fsdp", None),
            P("section", "fsdp", None),
        ),
        out_specs=(
            P("section", None, "fsdp", "ctx", None),
            P("section", None, "fsdp", "ctx", None),
            P("section", "fsdp"),
            P("section", "fsdp"),
            P("section", "fsdp", None),
            P("section", "fsdp"),
            P("section", "fsdp", None),
            P("section", "fsdp", None),
            P("section", "fsdp", None),
            P("section", "fsdp", None),
        ),
        check_vma=False,
    )
```

```python
import functools
import types

import jax
import jax.numpy as jnp
import numpy as np
from jax import lax
from jax.experimental import pallas as pl
from jax.experimental.pallas import tpu as pltpu
from jax.sharding import PartitionSpec as P

D = 896
HEADS = 14
KV_HEADS = 2
HEAD_DIM = 64
GROUP = HEADS // KV_HEADS
FF = 4864
QKV = 1152
EPS = 1e-06
THETA = 1000000.0
LANES = 128
TILES = D // LANES
WIN = 1280
NEG = -1e30
F32 = jnp.float32
BF16 = jnp.bfloat16
MESH = pl.DeviceIdType.MESH
VMEM_LIMIT = 60 * 2**20
UNIT = 16
SIDE = 4
GATE_PER = (5, 4)
DOWN_PER = (8, 9)
Q_PER = (4, 4)
Q_ROWS = 16 * sum(Q_PER) * UNIT


def mm(a, b):
    return jnp.dot(a, b, preferred_element_type=F32)


def mm_nt(a, b):
    return lax.dot_general(a, b, (((1,), (1,)), ((), ())), preferred_element_type=F32)


def mm_tn(a, b):
    return lax.dot_general(a, b, (((0,), (0,)), ((), ())), preferred_element_type=F32)


ORDER = (1, 3, 2)
SMALL = 2 * D + QKV
AXES = (("x", "y"), ("y", "x"))
BATCH = 3
GROUPS = tuple(slice(a, min(a + 2 * LANES, HEADS * HEAD_DIM)) for a in range(0, HEADS * HEAD_DIM, 2 * LANES))


def push(src, dst, ssem, rsem, axis, to):
    return pltpu.make_async_remote_copy(
        src_ref=src,
        dst_ref=dst,
        send_sem=ssem,
        recv_sem=rsem,
        device_id={axis: to},
        device_id_type=MESH,
    )


def rope(u, cos, sa, sb):
    return u * cos + pltpu.roll(u, 96, 1) * sa + pltpu.roll(u, 32, 1) * sb


def unrope(u, cos, sa, sb):
    return u * cos - pltpu.roll(u, 96, 1) * sa - pltpu.roll(u, 32, 1) * sb


def halves(a0, a1):
    lane = lax.broadcasted_iota(jnp.int32, a0.shape, 1) < HEAD_DIM
    low = jnp.where(lane, a0, pltpu.roll(a1, HEAD_DIM, 1))
    high = jnp.where(lane, pltpu.roll(a0, HEAD_DIM, 1), a1)
    return low, high


def spread(ref, t, tile_t):
    half = HEAD_DIM
    zero = jnp.zeros((half, LANES), F32)
    cols = slice(t * LANES, (t + 1) * LANES)
    for g in range(KV_HEADS):
        pair = [tile_t[j * half : (j + 1) * half, :] if (2 * t + j) // GROUP == g else zero for j in range(2)]
        for part, content in enumerate(halves(*pair)):
            ref[part * LANES + g * half : part * LANES + (g + 1) * half, cols] = content.astype(BF16)


def gathered_tile(wide, t):
    half = HEAD_DIM
    rows = []
    for j in range(2):
        g = (2 * t + j) // GROUP
        low = wide[g * half : (g + 1) * half, :]
        high = wide[LANES + g * half : LANES + (g + 1) * half, :]
        rows.append(halves(low, high)[j])
    return jnp.concatenate(rows, 0)


def dealt(a_per, b_per):
    where = [(0, u // a_per, u % a_per) for u in range(16 * a_per)]
    return where + [(1, v // b_per, v % b_per) for v in range(16 * b_per)]


def unit_runs(first, count, per):
    where = dealt(*per)
    found = []
    for i in range(count):
        part, piece, slot = where[first + i]
        if found and found[-1][0] == part and found[-1][1] == piece:
            found[-1][4] += 1
        else:
            found.append([part, piece, slot, i, 1])
    return found


def put_units(refs, section, base, per, first, rows):
    for part, piece, slot, i, m in unit_runs(first, rows.shape[0] // UNIT, per):
        at = base[part] + slot * UNIT
        refs[part][section, piece // SIDE, piece % SIDE, at : at + m * UNIT, :] = rows[i * UNIT : (i + m) * UNIT, :]


class Stages:
    def __init__(self, r):
        self.s = lax.axis_index("section")
        self.c = lax.axis_index("ctx")
        self.nc = lax.axis_size("ctx")
        self.x, self.y = self.c // SIDE, lax.rem(self.c, SIDE)
        self.z = lax.axis_index("fsdp")
        self.nz = lax.axis_size("fsdp")
        self.ssem, self.rsem, self.lsem = r.ssem, r.rsem, r.lsem
        self.used = 0
        self.local_used = 0
        self.sent = []

    def along(self, axis, k):
        own, n = {
            "x": (self.x, SIDE),
            "y": (self.y, SIDE),
            "z": (self.z, self.nz),
            "c": (self.c, self.nc),
        }[axis]
        return lax.rem(own + n + k, n)

    def peer(self, axis, k, section=None):
        if axis == "s":
            return {"section": 1 - self.s}
        if axis == "z":
            to = {"fsdp": self.along("z", k)}
        elif axis == "c":
            to = {"ctx": self.along("c", k)}
        elif axis == "x":
            to = {"ctx": self.along("x", k) * SIDE + self.y}
        else:
            to = {"ctx": self.x * SIDE + self.along("y", k)}
        if section is not None:
            to["section"] = section
        return to

    def hail(self, ids, ring=False):
        bar = pltpu.get_barrier_semaphore()
        for i in ids:
            pl.semaphore_signal(bar, inc=1, device_id=i, device_id_type=MESH)
        self.expected = len(ids)
        if ring:
            def one(k, c):
                pl.semaphore_signal(bar, inc=1, device_id=self.peer("c", k), device_id_type=MESH)
                return c

            lax.fori_loop(1, self.nc, one, 0)
            self.expected += self.nc - 1
        self.bar = bar

    def met(self):
        pl.semaphore_wait(self.bar, self.expected)

    def beside(self):
        return [self.peer("s", 0)]

    def upright(self, both=False):
        ids = [self.peer("z", k) for k in range(1, self.nz)]
        return ids + ([self.peer("z", k, 1 - self.s) for k in range(1, self.nz)] if both else [])

    def flat(self, both=False):
        ids = [self.peer(a, k) for a in "xy" for k in range(1, SIDE)]
        return ids + ([self.peer(a, k, 1 - self.s) for a in "xy" for k in range(1, SIDE)] if both else [])

    def take(self, count):
        self.used += count
        return self.used - count

    def copy(self, src, dst, at, to, recv_at=None):
        return pltpu.make_async_remote_copy(
            src_ref=src,
            dst_ref=dst,
            send_sem=self.ssem.at[at],
            recv_sem=self.rsem.at[at if recv_at is None else recv_at],
            device_id=to,
            device_id_type=MESH,
        )

    def begin(self, copies):
        for c in copies:
            c.start()
        self.sent += copies
        return copies

    def drain(self):
        for c in self.sent:
            c.wait_send()

    def swap(self, src, land):
        return self.begin([self.copy(src.at[1 - self.s], land, self.take(1), self.peer("s", 0))])

    def scatter(self, axis, src, land):
        n = self.nz if axis == "z" else SIDE
        at = self.take(n - 1)
        return self.begin(
            [self.copy(src.at[self.along(axis, k)], land.at[k - 1], at + k - 1, self.peer(axis, k)) for k in range(1, n)]
        )

    def gather(self, axis, ref):
        at = self.take(SIDE - 1)
        mine = ref.at[self.along(axis, 0)]
        return self.begin([self.copy(mine, mine, at + k - 1, self.peer(axis, k)) for k in range(1, SIDE)])

    def deal(self, src, dst, rows):
        at = self.take(self.nz - 1)
        mine = dst.at[self.block(self.z, rows), :]
        return self.begin(
            [
                self.copy(src.at[self.block(self.along("z", k), rows), :], mine, at + k - 1, self.peer("z", k))
                for k in range(1, self.nz)
            ]
        )

    def block(self, i, rows):
        return pl.ds(pl.multiple_of(i * rows, UNIT), rows)

    def aside(self, j):
        x = lax.rem(self.x + (1 - self.s) * j, SIDE)
        y = lax.rem(self.y + self.s * j, SIDE)
        return {"ctx": x * SIDE + y}

    def quarter(self):
        return self.x * (1 - self.s) + self.y * self.s

    def hand_over(self, axis, src, dst, layer, part=None):
        at = self.take(2 * SIDE)
        mine = dst.at[self.s, self.along(axis, 0)]
        if part is not None:
            src, mine = src.at[part], mine.at[part]
        self.begin(
            [
                self.copy(src, mine, at + k, self.peer(axis, k, layer), at + self.s * SIDE + k)
                for k in range(1, SIDE)
            ]
        )
        beside = self.copy(src, mine, at, {"section": layer}, at + self.s * SIDE)
        within = pltpu.make_async_copy(src, mine, self.lsem.at[self.local_used])
        self.local_used += 1

        @pl.when(self.s != layer)
        def _():
            beside.start()

        @pl.when(self.s == layer)
        def _():
            within.start()

        def finish():
            @pl.when(self.s == layer)
            def _():
                within.wait()
                for half in range(2):
                    for k in range(0 if half != layer else 1, SIDE):
                        self.copy(src, mine, at, {"section": layer}, at + half * SIDE + k).wait_recv()

            @pl.when(self.s != layer)
            def _():
                beside.wait_send()

        return finish


class Feed:
    def __init__(self, st, layer, sources, piece, band):
        self.st, self.layer, self.sources, self.piece, self.band = st, layer, sources, piece, band
        steps = st.nz - 1
        self.across = st.take(2 * steps)
        self.sideways = st.take((SIDE - 1) * steps)
        self.passed = st.take(steps)
        self.own = st.take(2)

    def beside(self, h):
        b = self.band(self.st.z, h)
        return self.st.copy(b, b, self.own + h, self.st.peer("s", 0))

    def send(self, h, k, src):
        st = self.st
        dst = self.piece(st.z, h, (st.x, st.y)[h])
        return st.copy(dst if src is None else src, dst, self.across + 2 * (k - 1) + h, st.peer("z", k, h))

    def start(self):
        st = self.st

        @pl.when(st.s == self.layer)
        def _():
            for k in ORDER:
                for h in range(2):
                    for needed, src in self.sources(h, (st.x, st.y)[h], st.along("z", k)):
                        if needed is None:
                            self.send(h, k, src).start()
                        else:
                            pl.when(needed)(self.send(h, k, src).start)
            for h in range(2):
                self.beside(h).start()

    def relay(self, k):
        st = self.st
        p = self.piece(st.along("z", -k), st.s, st.quarter())
        st.copy(p, p, self.across + 2 * (k - 1) + st.s, st.peer("s", 0)).wait_recv()
        at = self.sideways + (SIDE - 1) * (k - 1) - 1
        st.begin([st.copy(p, p, at + j, st.aside(j)) for j in range(1, SIDE)])

    def collect(self, k):
        st = self.st
        z = st.along("z", -k)
        at = self.sideways + (SIDE - 1) * (k - 1) - 1
        for j in range(1, SIDE):
            p = self.piece(z, st.s, lax.rem(st.quarter() + SIDE - j, SIDE))
            st.copy(p, p, at + j, st.aside(j)).wait_recv()
        b = self.band(z, st.s)
        st.begin([st.copy(b, b, self.passed + k - 1, st.peer("s", 0))])

    def finish(self):
        st = self.st
        for k in ORDER:
            b = self.band(st.along("z", -k), 1 - st.s)
            st.copy(b, b, self.passed + k - 1, st.peer("s", 0)).wait_recv()

        @pl.when(st.s == self.layer)
        def _():
            for h in range(2):
                for k in ORDER:
                    self.send(h, k, None).wait_send()
                self.beside(h).wait_send()

        @pl.when(st.s != self.layer)
        def _():
            for h in range(2):
                self.beside(h).wait_recv()


class FeedDown:
    def __init__(self, st, layer, src, dst):
        self.st, self.layer = st, layer
        share = src.shape[1]
        spare = WIN - share
        odd = lax.rem(st.z, 2)
        place = dst.at[pl.ds(pl.multiple_of(odd * spare, UNIT), share), :]
        dst[pl.ds(pl.multiple_of((1 - odd) * share, UNIT), spare), :] = jnp.zeros((spare, D), BF16)
        self.local = pltpu.make_async_copy(src.at[0], place, st.lsem.at[st.local_used])
        st.local_used += 1
        self.remote = st.copy(src.at[0], place, st.take(1), st.peer("s", 0))

    def start(self):
        @pl.when(self.st.s == self.layer)
        def _():
            self.local.start()
            self.remote.start()

    def finish(self):
        @pl.when(self.st.s == self.layer)
        def _():
            self.local.wait()
            self.remote.wait_send()

        @pl.when(self.st.s != self.layer)
        def _():
            self.remote.wait_recv()


class Delivery:
    def __init__(self, st, layer, src, out):
        self.st, self.layer = st, layer
        mine = out.at[st.s]
        self.within = pltpu.make_async_copy(src, mine, st.lsem.at[st.local_used])
        st.local_used += 1
        self.over = st.copy(src, mine, st.take(1), st.peer("s", 0))
        pl.when(st.s == layer)(self.within.start)
        pl.when(st.s != layer)(self.over.start)

    def finish(self):
        @pl.when(self.st.s == self.layer)
        def _():
            self.within.wait()
            self.over.wait_recv()

        pl.when(self.st.s != self.layer)(self.over.wait_send)


class Local:
    def __init__(self, st, layer, pairs):
        self.st, self.layer = st, layer
        self.copies = [pltpu.make_async_copy(a, b, st.lsem.at[st.local_used + i]) for i, (a, b) in enumerate(pairs)]
        st.local_used += len(pairs)

        @pl.when(st.s == layer)
        def _():
            for c in self.copies:
                c.start()

    def wait(self):
        @pl.when(self.st.s == self.layer)
        def _():
            for c in self.copies:
                c.wait()


def half_rows(z, h, share):
    return pl.ds(pl.multiple_of(z * share + h * (share // 2), UNIT), share // 2)


def feed_attention(st, layer, qkv, out, dst):
    share = qkv.shape[1]
    rows = st.block(st.z, share)
    local = Local(st, layer, [(qkv.at[0], dst.at[rows, :QKV]), (out.at[0], dst.at[rows, QKV:])])
    width = (QKV + D) // SIDE

    def piece(z, h, q):
        return dst.at[half_rows(z, h, share), pl.ds(pl.multiple_of(q * width, LANES), width)]

    def band(z, h):
        return dst.at[half_rows(z, h, share), :]

    return local, Feed(st, layer, lambda h, q, z_to: [(None, None)], piece, band)


def feed_windows(st, layer, gate, up, dst):
    share = gate.shape[1]
    pace = FF // st.nz // (LANES // 2)
    width = WIN // 2

    def window(z):
        return pl.multiple_of(z * pace // 2 * LANES, LANES)

    rows = st.block(st.z, share)
    local = Local(st, layer, [(w.at[0, :, pl.ds(window(st.z), WIN)], dst.at[i, rows, :]) for i, w in enumerate((gate, up))])

    def sources(h, q, z_to):
        at = pl.multiple_of(window(z_to) + lax.rem(q, 2) * width, LANES)
        part = slice(h * (share // 2), (h + 1) * (share // 2))
        return [(q < 2, gate.at[0, part, pl.ds(at, width)]), (q >= 2, up.at[0, part, pl.ds(at, width)])]

    def piece(z, h, q):
        return dst.at[q // 2, half_rows(z, h, share), pl.ds(pl.multiple_of(lax.rem(q, 2) * width, LANES), width)]

    def band(z, h):
        return dst.at[:, half_rows(z, h, share), :]

    return local, Feed(st, layer, sources, piece, band)


def arrived(copies):
    for c in copies:
        c.wait_recv()


def add_into(dst, parts):
    def one(i, c):
        total = parts[0][i].astype(F32)
        for p in parts[1:]:
            total = total + p[i].astype(F32)
        dst[i] = total.astype(dst.dtype)
        return c

    lax.fori_loop(0, dst.shape[0], one, 0)


def add_rows(dst, parts):
    total = parts[0][...].astype(F32)
    for p in parts[1:]:
        total = total + p[...].astype(F32)
    dst[...] = total.astype(dst.dtype)


def swapped_sum(st, copies, given, land):
    arrived(copies)
    for i in range(SIDE):
        add_into(land.at[i], [given.at[st.s, i], land.at[i]])


def sides(tile, chosen):
    half = HEAD_DIM
    low, high = tile[:half], tile[half:]
    zero = jnp.zeros_like(low)
    below = jnp.concatenate([jnp.where(chosen, low, zero), jnp.where(chosen, zero, high)], 1)
    return jnp.concatenate([jnp.concatenate([zero, low], 1), below], 0).astype(BF16)


def sides_t(tile_t, chosen):
    lane = lax.broadcasted_iota(jnp.int32, tile_t.shape, 1) < HEAD_DIM
    upper = jnp.where(jnp.logical_or(lane, jnp.logical_not(chosen)), 0.0, pltpu.roll(tile_t, HEAD_DIM, 1))
    lower = jnp.where(jnp.logical_or(lane, jnp.logical_not(chosen)), tile_t, 0.0)
    return jnp.concatenate([upper, lower], 0).astype(BF16)


def own_sides(tile):
    low, high = tile[:HEAD_DIM], tile[HEAD_DIM:]
    zero = jnp.zeros_like(low)
    rows = [[zero, low], [low, zero], [zero, high]]
    return jnp.concatenate([jnp.concatenate(p, 1) for p in rows], 0).astype(BF16)


def own_bias(width):
    key = lax.broadcasted_iota(jnp.int32, (HEAD_DIM, width), 0)
    query = lax.rem(lax.broadcasted_iota(jnp.int32, (HEAD_DIM, width), 1), HEAD_DIM)
    return jnp.where(key <= query, 0.0, NEG)


def earlier(pairs_ref, src, me, width):
    return pairs_ref[src, 0:1, :width] < pairs_ref[me, 0:1, :width]


def col_max(a):
    return jnp.max(a, 0, keepdims=True)


def col_sum(a):
    return jnp.sum(a, 0, keepdims=True)


class View:
    def __init__(self, r, layer):
        self.r, self.layer = r, layer

    def named(self, k):
        own = k + str(self.layer)
        return own if hasattr(self.r, own) else k

    def __getattr__(self, k):
        return getattr(self.r, self.named(k))

    def need(self, *names):
        self.r.need(*[self.named(k) for k in names])

    def flush(self, *names):
        self.r.flush(*[self.named(k) for k in names])


def forward_kernel(_, r):
    st = Stages(r)
    n, me = st.nc, st.c
    st.hail(st.beside() + st.upright(True), ring=True)
    r.load()
    wa, gu, down = [None, None], [None, None], [None, None]
    for l in range(2):
        v = View(r, l)
        wa[l] = feed_attention(st, l, r.qkv_shard, r.out_shard, v.wa)
        gu[l] = feed_windows(st, l, r.gate_shard, r.up_shard, v.gu)
        down[l] = FeedDown(st, l, r.down_shard, v.down)
    r.need("inverse", "x0")
    r.pairs[me] = jnp.full(r.pairs.shape[1:], r.pair[0], jnp.int32)
    at = 0
    for part, size in ((r.attn_gain, D), (r.ffn_gain, D), (r.qkv_bias, QKV)):
        share = part.shape[1]
        line = jnp.concatenate([part[...].astype(F32), jnp.zeros((1, size - share), F32)], 1)
        line = pltpu.roll(jnp.broadcast_to(line, (8, size)), st.z * share, 1)
        r.parts[st.s, st.z, :, at : at + size] = line[:1]
        at += size
    wa[0][0].wait()
    st.met()
    wa[0][1].start()
    at = st.take(2 * st.nz)
    mine = r.parts.at[st.s, st.z]
    st.begin(
        [st.copy(mine, mine, at + k, st.peer("z", k, st.s), at + st.s * st.nz + k) for k in range(1, st.nz)]
        + [st.copy(mine, mine, at + st.nz + k, st.peer("z", k, 1 - st.s), at + st.s * st.nz + k) for k in range(1, st.nz)]
        + [st.copy(mine, mine, at, st.peer("s", 0), at + st.s * st.nz)]
    )

    def tell(k, c):
        p = r.pairs.at[me]
        push(p, p, r.psem.at[k], r.psem2.at[k], "ctx", lax.rem(me + k, n)).start()
        return c

    lax.fori_loop(1, n, tell, 0)
    block = LANES // 2
    i = lax.broadcasted_iota(jnp.int32, (LANES, LANES), 0)
    pair = r.pairs[me, 0:1, :LANES]
    pos = jnp.where(i < block, pair * block + i, (2 * n - 1 - pair) * block + i - block)
    angle = pos.astype(F32) * r.inverse[...]
    lane = lax.rem(lax.broadcasted_iota(jnp.int32, (LANES, LANES), 1), HEAD_DIM)
    sine = jnp.sin(angle)
    r.cos[...] = jnp.cos(angle)
    r.sa[...] = jnp.where(lane < HEAD_DIM // 2, -sine, 0.0)
    r.sb[...] = jnp.where(lane < HEAD_DIM // 2, 0.0, sine)
    r.flush("cos", "sa", "sb")
    for h in (st.s, 1 - st.s):
        for k in range(st.nz):
            if h is st.s and k == 0:
                continue
            st.copy(mine, mine, at, st.peer("s", 0), at + h * st.nz + k).wait_recv()
    for h in range(2):
        total = r.parts[h, 0]
        for k in range(1, st.nz):
            total = total + r.parts[h, k]
        r.small[h] = total
    r.flush("small")
    for k in ORDER:
        wa[0][1].relay(k)
    gu[0][0].wait()
    gu[0][1].start()
    down[0].start()
    for k in ORDER:
        wa[0][1].collect(k)

    def begin_next():
        wa[1][0].wait()
        wa[1][1].start()
        gu[1][0].wait()
        gu[1][1].start()
        down[1].start()

    def relays(*steps):
        def go():
            for feed, name, k in steps:
                getattr(feed, name)(k)

        return go

    g0, w1, g1 = gu[0][1], wa[1][1], gu[1][1]
    wa[0][1].finish()
    v = View(r, 0)
    v.flush("wa")
    attention_forward(
        st, v, 0,
        (
            relays((g0, "relay", 1), (g0, "relay", 3)),
            relays((g0, "relay", 2)),
            begin_next,
            relays((g0, "collect", 1), (g0, "collect", 3)),
            relays((g0, "collect", 2)),
        ),
    )

    def ready_0():
        g0.finish()
        down[0].finish()
        v.flush("gu", "down")

    ffn_forward(
        st, v, ready_0,
        (
            relays((w1, "relay", 1), (w1, "relay", 3)),
            relays((w1, "relay", 2), (g1, "relay", 1)),
            relays((g1, "relay", 3), (g1, "relay", 2), (w1, "collect", 1), (w1, "collect", 3)),
            relays((w1, "collect", 2), (g1, "collect", 1), (g1, "collect", 3), (g1, "collect", 2)),
        ),
    )
    r.x1[...] = r.y0[...].astype(BF16).astype(F32)
    r.flush("x1")
    done_0 = Delivery(st, 0, r.y0, r.layer_out)
    r.need("gy")
    tok = r.gy.shape[0]
    rows = st.block(st.z, tok)
    r.gy_all[rows, :] = r.gy[...].astype(BF16)
    at = st.take(st.nz - 1)
    mine_gy = r.gy_all.at[rows, :]
    gy_moving = st.begin([st.copy(mine_gy, mine_gy, at + k - 1, st.peer("z", k)) for k in range(1, st.nz)])
    w1.finish()
    v = View(r, 1)
    v.flush("wa")
    nothing = lambda: None
    attention_forward(st, v, 1, (nothing,) * 5)

    def ready_1():
        g1.finish()
        down[1].finish()
        v.flush("gu", "down")

    ffn_forward(st, v, ready_1, (nothing,) * 4)
    done_1 = Delivery(st, 1, r.y1, r.layer_out)
    arrived(gy_moving)
    r.flush("gy_all")
    done_0.finish()
    done_1.finish()
    st.drain()

    def done(k, c):
        p = r.pairs.at[me]
        push(p, p, r.psem.at[k], r.psem2.at[k], "ctx", lax.rem(me + k, n)).wait_send()
        return c

    lax.fori_loop(1, n, done, 0)
    r.close()


def attention_forward(st, r, layer, between):
    n, me = st.nc, st.c
    x = r.x[...]
    r1 = lax.rsqrt(jnp.mean(x * x, -1, keepdims=True) + EPS)
    small = r.small[layer]
    n1_f = x * r1 * small[:, :D]
    n1 = n1_f.astype(BF16)
    bias = small[:, 2 * D :]
    cos, sa, sb = r.cos[...], r.sa[...], r.sb[...]
    lin = mm(n1, r.wa[:, D:QKV]) + bias[:, D:]
    r.kv[me] = jnp.concatenate([rope(lin[:, :LANES], cos, sa, sb), lin[:, LANES:]], 1).astype(BF16)

    def keys_copy(k, src):
        return push(r.kv.at[src], r.kv.at[src], r.csem.at[k], r.csem2.at[k], "ctx", lax.rem(me + k, n))

    def start(k, c):
        keys_copy(k, me).start()
        return c

    lax.fori_loop(1, n, start, 0)
    linq = mm(n1, r.wa[:, :D]) + bias[:, :D]
    for t in range(TILES):
        tile = slice(t * LANES, (t + 1) * LANES)
        q = rope(linq[:, tile], cos, sa, sb) * HEAD_DIM ** (-0.5)
        spread(r.qst, t, q.T)
        r.n1t[tile, :] = n1_f[:, tile].T.astype(BF16)
    r.flush("qst", "n1t")
    between[0]()
    half = HEAD_DIM
    own_k = own_sides(r.kv[me, :, :LANES].astype(F32))
    own_vt = own_sides(r.kv[me, :, LANES:].astype(F32)).astype(F32).T.astype(BF16)
    for cols in GROUPS:
        width = cols.stop - cols.start
        bias = own_bias(width)
        sc = mm(own_k, r.qst[:, cols])
        s_a, s_l, s_h = sc[:half], sc[half : 2 * half] + bias, sc[2 * half :] + bias
        m_lo = col_max(s_l)
        m_hi = jnp.maximum(col_max(s_a), col_max(s_h))
        p_a, p_l, p_h = jnp.exp(s_a - m_hi), jnp.exp(s_l - m_lo), jnp.exp(s_h - m_hi)
        r.m_s[0:1, cols], r.m_s[1:2, cols] = m_lo, m_hi
        r.l_s[0:1, cols], r.l_s[1:2, cols] = col_sum(p_l), col_sum(p_a) + col_sum(p_h)
        r.acc_s[:, cols] = mm(own_vt, jnp.concatenate([p_a, p_l, p_h], 0).astype(BF16))

    def step(i, c):
        kx, vt, sel = [], [], []
        for j in range(BATCH):
            k = i * BATCH + 1 + j
            src = lax.rem(me + n - k, n)
            keys_copy(k, src).wait_recv()
            if layer == 0:
                p = r.pairs.at[src]
                push(p, p, r.psem.at[k], r.psem2.at[k], "ctx", lax.rem(me + k, n)).wait_recv()
            sel.append(src)
            chosen = earlier(r.pairs, src, me, LANES)
            kx.append(sides(r.kv[src, :, :LANES].astype(F32), chosen))
            vt.append(sides_t(r.kv[src, :, LANES:].astype(F32).T, chosen))
        kx = jnp.concatenate(kx, 0)
        vt = jnp.concatenate(vt, 1)
        for cols in GROUPS:
            width = cols.stop - cols.start
            sc = mm(kx, r.qst[:, cols])
            m_lo, m_hi = r.m_s[0:1, cols], r.m_s[1:2, cols]
            n_lo, n_hi = m_lo, m_hi
            chosen = [earlier(r.pairs, src, me, width) for src in sel]
            for j in range(BATCH):
                top = col_max(sc[(2 * j + 1) * half : (2 * j + 2) * half])
                n_hi = jnp.maximum(n_hi, col_max(sc[2 * j * half : (2 * j + 1) * half]))
                n_hi = jnp.where(chosen[j], n_hi, jnp.maximum(n_hi, top))
                n_lo = jnp.where(chosen[j], jnp.maximum(n_lo, top), n_lo)
            a_lo, a_hi = jnp.exp(m_lo - n_lo), jnp.exp(m_hi - n_hi)
            l_lo, l_hi = r.l_s[0:1, cols] * a_lo, r.l_s[1:2, cols] * a_hi
            ps = []
            for j in range(BATCH):
                p_a = jnp.exp(sc[2 * j * half : (2 * j + 1) * half] - n_hi)
                p_s = jnp.exp(sc[(2 * j + 1) * half : (2 * j + 2) * half] - jnp.where(chosen[j], n_lo, n_hi))
                total = col_sum(p_s)
                l_hi = l_hi + col_sum(p_a) + jnp.where(chosen[j], 0.0, total)
                l_lo = l_lo + jnp.where(chosen[j], total, 0.0)
                ps += [p_a.astype(BF16), p_s.astype(BF16)]
            r.m_s[0:1, cols], r.m_s[1:2, cols] = n_lo, n_hi
            r.l_s[0:1, cols], r.l_s[1:2, cols] = l_lo, l_hi
            new = mm(vt, jnp.concatenate(ps, 0))
            r.acc_s[:LANES, cols] = r.acc_s[:LANES, cols] * a_lo + new[:LANES]
            r.acc_s[LANES:, cols] = r.acc_s[LANES:, cols] * a_hi + new[LANES:]
        return c

    lax.fori_loop(0, 1, step, 0)
    between[1]()
    lax.fori_loop(1, 2, step, 0)
    between[2]()
    lax.fori_loop(2, 4, step, 0)
    between[3]()
    lax.fori_loop(4, (n - 1) // BATCH, step, 0)
    between[4]()
    r.flush("kv")
    if layer == 0:
        r.flush("pairs")
    r.lse[...] = r.m_s[...] + jnp.log(r.l_s[...])
    for t in range(TILES):
        cols = slice(t * LANES, (t + 1) * LANES)
        wide = jnp.concatenate([r.acc_s[:LANES, cols] / r.l_s[0:1, cols], r.acc_s[LANES:, cols] / r.l_s[1:2, cols]], 0)
        tile_t = gathered_tile(wide, t)
        r.attt[cols, :] = tile_t.astype(BF16)
        r.att_s[:, cols] = tile_t.T.astype(BF16)
    r.flush("lse", "attt")
    mid = x + mm(r.att_s[...], r.wa[:, QKV:])
    r.mid[...] = mid
    r2 = lax.rsqrt(jnp.mean(mid * mid, -1, keepdims=True) + EPS)
    r.all[st.z] = (mid * r2 * small[:, D : 2 * D]).astype(BF16)
    r.flush("mid")

    def done(k, c):
        keys_copy(k, me).wait_send()
        return c

    lax.fori_loop(1, n, done, 0)


def ffn_forward(st, r, ready, between):
    n, me = st.nz, st.z
    at = st.take(2 * n)

    def first(k):
        return st.copy(r.all.at[me], r.all.at[me], at + k, st.peer("z", k))

    def second(k):
        return st.copy(r.send_s.at[k], r.land_s.at[k], at + n + k, st.peer("z", -k))

    for k in ORDER:
        first(k).start()
    ready()

    tok = r.mid.shape[0]

    def block(sources):
        a = jnp.concatenate([r.all[i] for i in sources], 0) if len(sources) > 1 else r.all[sources[0]]
        gate = mm(a, r.gu[0])
        up = mm(a, r.gu[1])
        for j, i in enumerate(sources):
            r.gate[i] = gate[j * tok : (j + 1) * tok].astype(BF16)
            r.up[i] = up[j * tok : (j + 1) * tok].astype(BF16)
        hidden = (gate * jax.nn.sigmoid(gate) * up).astype(BF16)
        return mm(hidden, r.down[...])

    r.y[...] = r.mid[...] + block([me])
    between[0]()
    first(1).wait_recv()
    first(3).wait_recv()
    both = block([st.along("z", -1), st.along("z", -3)]).astype(BF16)
    for i, k in enumerate((1, 3)):
        r.send_s[k] = both[i * tok : (i + 1) * tok]
        second(k).start()
    between[1]()
    first(2).wait_recv()
    r.send_s[2] = block([st.along("z", -2)]).astype(BF16)
    second(2).start()
    between[2]()
    r.flush("all", "gate", "up")
    between[3]()
    for k in ORDER:
        second(k).wait_recv()
        r.y[...] += r.land_s[k].astype(F32)
    for k in ORDER:
        first(k).wait_send()
        second(k).wait_send()


class Attention:
    def __init__(self, st):
        self.st = st

    def columns(self, src, dst):
        st = self.st
        share = dst.shape[0]
        at = st.take(st.nz - 1)
        mine = dst.at[:, pl.ds(pl.multiple_of(st.z * LANES, LANES), LANES)]
        moving = st.begin(
            [
                st.copy(src.at[st.block(st.along("z", k), share), :], mine, at + k - 1, st.peer("z", k))
                for k in range(1, st.nz)
            ]
        )
        mine[...] = src[st.block(st.z, share), :]
        return moving

    def whole(self, dst, cols=slice(None)):
        st = self.st
        rows = dst.shape[0] // st.nz
        at = st.take(st.nz - 1)
        mine = dst.at[pl.ds(pl.multiple_of(st.z * rows, UNIT), rows), cols]
        return st.begin([st.copy(mine, mine, at + k - 1, st.peer("z", k)) for k in range(1, st.nz)])

    def begin(self, glin, small, all_glin, all_small):
        st = self.st
        tok = glin.shape[0]
        all_glin[st.block(st.z, tok), :] = glin[...]
        all_small[st.block(st.z, 2 * UNIT), :] = small[...]
        return self.whole(all_glin) + self.whole(all_small)

    def swap(self, moving, n1z, all_glin, all_small, dout, made, land):
        st = self.st
        arrived(moving)
        share = n1z.shape[0]
        per = 8
        for j in range(0, QKV // LANES, 2):
            cols = slice(j * LANES, min(j + 2, QKV // LANES) * LANES)
            d = mm(n1z[...], all_glin[:, cols]).astype(BF16)
            for t in range(j, min(j + 2, QKV // LANES)):
                made[t // per, (t % per) * share : (t % per + 1) * share, :] = d[:, (t - j) * LANES : (t - j + 1) * LANES]
        made[1, share : 8 * share, :] = dout[...]
        small = jnp.zeros((2 * UNIT, LANES), F32)
        for i in range(st.nz):
            small = small + all_small[i * 2 * UNIT : (i + 1) * 2 * UNIT, :]
        made[0, 8 * share : 8 * share + 2 * UNIT, :] = small.astype(BF16)
        made[0, 8 * share + 2 * UNIT :, :] = jnp.zeros((Q_ROWS - 8 * share - 2 * UNIT, LANES), BF16)
        made[1, 8 * share :, :] = jnp.zeros((Q_ROWS - 8 * share, LANES), BF16)
        return st.swap(made, land)

    def fold(self, moving, made, land, out):
        st = self.st
        arrived(moving)
        rows = Q_ROWS // 2 // 16
        for h in range(2):
            for i in range(16):
                at = slice((h * 16 + i) * rows, (h * 16 + i + 1) * rows)
                total = made[st.s, at, :].astype(F32) + land[at, :].astype(F32)
                out[h][i // SIDE, i % SIDE] = total.astype(BF16)


class Rest:
    def __init__(self, st, t1, l2, t2, g1, out, layer):
        self.st, self.t1, self.l2, self.t2, self.g1, self.out, self.layer = st, t1, l2, t2, g1, out, layer
        self.stage = 0
        self.moving = [st.scatter(AXES[h][1], t1[h], l2[h]) for h in range(2)]

    def advance(self):
        st = self.st
        for h in range(2):
            second = AXES[h][1]
            arrived(self.moving[h])
            mine = self.g1[h].at[st.along(second, 0)]
            if self.stage == 0:
                t2 = self.t2[h]
                add_rows(t2, [self.t1[h].at[st.along(second, 0)]] + [self.l2[h].at[k] for k in range(SIDE - 1)])
                per = GATE_PER[h] * UNIT
                self.moving[h] = st.deal(t2, mine, per)
                mine[st.block(st.z, per), :] = t2[st.block(st.z, per), :]
                mine[st.nz * per :, :] = t2[st.nz * per :, :]
            elif self.stage == 1:
                self.moving[h] = st.gather(second, self.g1[h])
            else:
                self.moving[h] = st.hand_over(AXES[h][0], self.g1[h], self.out[h], self.layer, slice(0, SIDE // 2))
        self.stage += 1

    def second_half(self):
        self.ends = self.moving + [
            self.st.hand_over(AXES[h][0], self.g1[h], self.out[h], self.layer, slice(SIDE // 2, SIDE)) for h in range(2)
        ]

    def finish(self):
        for end in self.ends:
            end()


class Few:
    def __init__(self, st, r, tag):
        self.st = st

        def both(name):
            return tuple(getattr(r, name + tag + h) for h in "ab")

        self.qp, self.land, self.part, self.land2, self.wide = both("qp"), both("qm"), both("qe"), both("qw"), both("qh")
        self.moving = [st.scatter(AXES[h][0], self.qp[h], self.land[h]) for h in range(2)]

    def second_sum(self):
        st = self.st
        for h in range(2):
            arrived(self.moving[h])
            own = self.qp[h].at[st.along(AXES[h][0], 0)]
            add_into(self.part[h], [own] + [self.land[h].at[k] for k in range(SIDE - 1)])
            self.moving[h] = st.scatter(AXES[h][1], self.part[h], self.land2[h])

    def first_gather(self):
        st = self.st
        for h in range(2):
            arrived(self.moving[h])
            i = st.along(AXES[h][1], 0)
            add_rows(self.wide[h].at[i], [self.part[h].at[i]] + [self.land2[h].at[k] for k in range(SIDE - 1)])
            self.moving[h] = st.gather(AXES[h][1], self.wide[h])

    def hand_over(self, out, layer):
        for h in range(2):
            arrived(self.moving[h])
        return [self.st.hand_over(AXES[h][0], self.wide[h], out[h], layer) for h in range(2)]


def backward_kernel(layer, r):
    st = Stages(r)
    n, me = st.nz, st.z
    carry = layer == 0
    ids = st.upright() + st.beside()
    if carry:
        ids += [st.peer(a, k, 1 - st.s) for a in "xy" for k in range(1, SIDE)]
    st.hail(ids, ring=True)
    r.load()
    tok = r.gy.shape[0]

    def rows_of(i):
        return pl.ds(pl.multiple_of(i * tok, tok), tok)

    r.need("gy")
    gyb = r.gy[...].astype(BF16)
    gy = gyb.astype(F32) if carry else r.gy[...]
    above = None
    if carry:
        r.all_s[rows_of(me), :] = gyb
    else:
        r.need("all_s")
    st.met()
    at = st.take(2 * n)

    def first(k):
        mine = r.all_s.at[rows_of(me), :]
        return st.copy(mine, mine, at + k, st.peer("z", k))

    def second(k):
        return st.copy(r.send_s.at[k], r.land_s.at[k], at + n + k, st.peer("z", -k))

    if carry:
        for k in ORDER:
            first(k).start()
        above = Delivery(st, 1, r.gy, r.input_grad)
        r.need("p1a", "p1b")
        rest = Rest(st, (r.p1a, r.p1b), (r.l2a, r.l2b), (r.t2a, r.t2b), (r.g1a, r.g1b), (r.ga, r.gb), 1)
    r.need("down", "gate", "up", "gu")

    def block(sources):
        def stacked(ref):
            parts = [ref[rows_of(i), :] for i in sources]
            return jnp.concatenate(parts, 0) if len(parts) > 1 else parts[0]

        def picked(ref):
            parts = [ref[i].astype(F32) for i in sources]
            return jnp.concatenate(parts, 0) if len(parts) > 1 else parts[0]

        def keep(ref, value):
            for j, i in enumerate(sources):
                ref[rows_of(i), :] = value[j * tok : (j + 1) * tok]

        gh = mm_nt(stacked(r.all_s), r.down[...])
        gate, up = picked(r.gate), picked(r.up)
        sg = jax.nn.sigmoid(gate)
        act = gate * sg
        keep(r.hid_s, (act * up).astype(BF16))
        ggate = (gh * up * sg * (1.0 + gate * (1.0 - sg))).astype(BF16)
        gup = (gh * act).astype(BF16)
        keep(r.g_s.at[0], ggate)
        keep(r.g_s.at[1], gup)
        return mm_nt(ggate, r.gu[0]) + mm_nt(gup, r.gu[1])

    r.own_s[...] = block([me])
    if carry:
        rest.advance()
        first(1).wait_recv()
        first(3).wait_recv()
    both = block([st.along("z", -1), st.along("z", -3)]).astype(BF16)
    for i, k in enumerate((1, 3)):
        r.send_s[k] = both[i * tok : (i + 1) * tok]
        second(k).start()
    if carry:
        rest.advance()
        first(2).wait_recv()
    r.send_s[2] = block([st.along("z", -2)]).astype(BF16)
    second(2).start()
    if carry:
        rest.advance()

    late = [
        pltpu.make_async_copy(r.wa.at[:, :QKV], r.gu.at[0, :, :QKV], st.lsem.at[st.local_used]),
        pltpu.make_async_copy(r.wa.at[:, QKV:], r.gu.at[1, :, :D], st.lsem.at[st.local_used + 1]),
    ]
    st.local_used += 2
    for c in late:
        c.start()
    refs = (r.fa, r.fb)
    share = D // n
    for j in range(WIN // (2 * LANES)):
        cols = slice(2 * j * LANES, 2 * (j + 1) * LANES)
        r.down[cols, :] = mm_tn(r.hid_s[:, cols], r.all_s[...]).astype(BF16)
    pad = (WIN - FF // n) * lax.rem(me, 2)
    half = FF // n // 2
    base = [n * per * UNIT for per in GATE_PER]
    for section in range(2):
        rows = r.down[pl.ds(pl.multiple_of(pad + section * half, UNIT), half), :]
        for t in range(TILES):
            put_units(refs, section, base, DOWN_PER, t * (half // UNIT), rows[:, t * LANES : (t + 1) * LANES])
        used = TILES * (half // UNIT)
        extra = 16 * sum(DOWN_PER) - used
        put_units(refs, section, base, DOWN_PER, used, jnp.zeros((extra * UNIT, LANES), BF16))
    r.need("n2_all")
    normed = jnp.concatenate([r.n2_all[i] for i in range(n)], 0)

    def product(section):
        for j in range(WIN // (2 * LANES)):
            d = mm_tn(normed, r.g_s[section, :, 2 * j * LANES : 2 * (j + 1) * LANES]).astype(BF16)
            for t in (2 * j, 2 * j + 1):
                tile = d[:, (t % 2) * LANES : (t % 2 + 1) * LANES]
                for i in range(n):
                    base = [i * per * UNIT for per in GATE_PER]
                    put_units(refs, section, base, GATE_PER, t * (share // UNIT), tile[i * share : (i + 1) * share, :])
        used = WIN // LANES * (share // UNIT)
        extra = 16 * sum(GATE_PER) - used
        for i in range(n):
            base = [i * per * UNIT for per in GATE_PER]
            put_units(refs, section, base, GATE_PER, used, jnp.zeros((extra * UNIT, LANES), BF16))

    product(1 - st.s)
    if carry:
        rest.second_half()
    swaps = [st.swap(refs[h], (r.sla, r.slb)[h]) for h in range(2)]
    product(st.s)
    for k in ORDER:
        second(k).wait_recv()
        r.own_s[...] += r.land_s[k].astype(F32)
    gn2 = r.own_s[...]
    r.need("mid", "small")
    mid = r.mid[...]
    r2 = lax.rsqrt(jnp.mean(mid * mid, -1, keepdims=True) + EPS)
    unit = mid * r2
    dg2 = col_sum(gn2 * unit)
    dz = gn2 * r.small[layer][:, D : 2 * D]
    gm = gy + r2 * (dz - unit * jnp.mean(dz * unit, -1, keepdims=True))
    r.gm_s[...] = gm
    for k in ORDER:
        if carry:
            first(k).wait_send()
        second(k).wait_send()
    attention_backward(st, r, layer, gm, dg2, refs, swaps, rest if carry else None, above, late)


def attention_backward(st, r, layer, gm, dg2, refs, swaps, rest, above, late):
    n, me = st.nc, st.c
    last = layer == 0
    half = HEAD_DIM
    gmb = gm.astype(BF16)
    tok = gm.shape[0]
    r.all_gm[st.block(st.z, tok), :] = gmb
    sl, l1, t1 = (r.sla, r.slb), (r.l1a, r.l1b), (r.t1a, r.t1b)
    r.need("attt", "n1t")
    attention = Attention(st)
    size = 2 * BATCH * half
    pr, ds, gst = r.g_s.at[0, :size, :WIDE], r.g_s.at[1, :size, :WIDE], r.hid_s.at[: 2 * LANES, :WIDE]
    out_factors = attention.whole(r.all_gm) + attention.columns(r.attt, r.attz)
    qkv_factor = attention.columns(r.n1t, r.n1z)
    if last:
        r.need("glin1", "gsmall1", "n1z1", "dout1")
        before = attention.begin(r.glin1, r.gsmall1, r.all_glin, r.all_small)
    r1 = []
    for h in range(2):
        swapped_sum(st, swaps[h], refs[h], sl[h])
        r1.append(st.scatter(AXES[h][0], sl[h], l1[h]))
    r.need("qst", "lse", "kv", "pairs")
    for c in late:
        c.wait()
    ga = mm_nt(gmb, r.gu[1, :, :D])
    for t in range(TILES):
        tile = slice(t * LANES, (t + 1) * LANES)
        ga_t = ga[:, tile].T
        spread(gst, t, ga_t)
        prod = ga_t * r.attt[tile, :].astype(F32)
        low, high = halves(col_sum(prod[:half]), col_sum(prod[half:]))
        r.delta_s[0:1, tile], r.delta_s[1:2, tile] = low, high

    def own_block():
        keys, vals = r.kv[me, :, :LANES].astype(F32), r.kv[me, :, LANES:].astype(F32)
        kx, vx = own_sides(keys), own_sides(vals)
        kt = kx.astype(F32).T.astype(BF16)
        rows = slice(0, 3 * half)
        for cols in GROUPS:
            bias = own_bias(cols.stop - cols.start)
            sc = mm(kx, r.qst[:, cols])
            dp = mm(vx, gst[:, cols])
            lo, hi = (r.lse[0:1, cols], r.delta_s[0:1, cols]), (r.lse[1:2, cols], r.delta_s[1:2, cols])
            parts = [(sc[:half], hi), (sc[half : 2 * half] + bias, lo), (sc[2 * half :] + bias, hi)]
            for i, (part, (lse, delta)) in enumerate(parts):
                p = jnp.exp(part - lse)
                at = slice(i * half, (i + 1) * half)
                pr[at, cols] = p.astype(BF16)
                ds[at, cols] = (p * (dp[at] - delta)).astype(BF16)
            r.gq_s[:, cols] = mm(kt, ds[rows, cols])
        made = []
        for w, q in ((ds, r.qst), (pr, gst)):
            e = mm_nt(w[rows, :], q[...])
            low = e[:half, LANES:] + e[half : 2 * half, :LANES]
            made.append(jnp.concatenate([low, e[2 * half :, LANES:]], 0))
        return jnp.concatenate(made, 1)

    def sum_copy(k):
        return push(r.send_k.at[k], r.land_k.at[k], r.csem.at[k], r.csem2.at[k], "ctx", lax.rem(me + k, n))

    def step(i):
        kx, vx, kt, sel = [], [], [], []
        for j in range(BATCH):
            src = lax.rem(me + i * BATCH + 1 + j, n)
            sel.append(src)
            chosen = earlier(r.pairs, src, me, LANES)
            keys = r.kv[src, :, :LANES].astype(F32)
            kx.append(sides(keys, chosen))
            vx.append(sides(r.kv[src, :, LANES:].astype(F32), chosen))
            kt.append(sides_t(keys.T, chosen))
        kx, vx, kt = jnp.concatenate(kx, 0), jnp.concatenate(vx, 0), jnp.concatenate(kt, 1)
        rows = slice(0, 2 * BATCH * half)
        for cols in GROUPS:
            width = cols.stop - cols.start
            sc = mm(kx, r.qst[:, cols])
            dp = mm(vx, gst[:, cols])
            for j in range(BATCH):
                chosen = earlier(r.pairs, sel[j], me, width)
                for part in range(2):
                    lse, delta = r.lse[1:2, cols], r.delta_s[1:2, cols]
                    if part:
                        lse = jnp.where(chosen, r.lse[0:1, cols], lse)
                        delta = jnp.where(chosen, r.delta_s[0:1, cols], delta)
                    at = slice((2 * j + part) * half, (2 * j + part + 1) * half)
                    p = jnp.exp(sc[at] - lse)
                    pr[at, cols] = p.astype(BF16)
                    ds[at, cols] = (p * (dp[at] - delta)).astype(BF16)
            r.gq_s[:, cols] += mm(kt, ds[rows, cols])
        ek = mm_nt(ds[rows, :], r.qst[...])
        ev = mm_nt(pr[rows, :], gst[...])
        for j in range(BATCH):
            chosen = earlier(r.pairs, sel[j], me, LANES)
            k = i * BATCH + 1 + j
            for e, lanes in ((ek, slice(0, LANES)), (ev, slice(LANES, 2 * LANES))):
                top = e[2 * j * half : (2 * j + 1) * half]
                low = e[(2 * j + 1) * half : (2 * j + 2) * half]
                r.send_k[k, :half, lanes] = (top[:, LANES:] + jnp.where(chosen, low[:, :LANES], 0.0)).astype(BF16)
                r.send_k[k, half:, lanes] = jnp.where(chosen, 0.0, low[:, LANES:]).astype(BF16)
            sum_copy(k).start()

    own = own_block()
    for i in range(3):
        step(i)
    arrived(out_factors)
    share = D // st.nz
    for j in range(0, TILES, 2):
        cols = slice(j * LANES, min(j + 2, TILES) * LANES)
        d = mm(r.attz[...], r.all_gm[:, cols]).astype(BF16)
        for t in range(j, min(j + 2, TILES)):
            r.dout[t * share : (t + 1) * share, :] = d[:, (t - j) * LANES : (t - j + 1) * LANES]
    if not last:
        r.flush("dout")
    if last:
        qswap = attention.swap(before, r.n1z1, r.all_glin, r.all_small, r.dout1, r.qv, r.ql)
    for i in range(3, (n - 1) // BATCH):
        step(i)
    arrived(qkv_factor)
    if last:
        rest.finish()
        attention.fold(qswap, r.qv, r.ql, (r.qpa, r.qpb))
        few = Few(st, r, "")
        for h in range(2):
            arrived(r1[h])
            mine = sl[h].at[st.along(AXES[h][0], 0)]
            add_into(t1[h], [mine] + [l1[h].at[k] for k in range(SIDE - 1)])
        own_rest = Rest(st, t1, (r.l2c, r.l2d), (r.t2c, r.t2d), (r.g1c, r.g1d), (r.ha, r.hb), 0)
        glin = r.zglin.at[st.block(st.z, tok), :]
    else:
        r.flush("n1z")
        glin = r.glin
    r.need("cos", "sa", "sb", "x", "small")
    cos, sa, sb = r.cos[...], r.sa[...], r.sb[...]
    for t in range(TILES):
        gq = gathered_tile(r.gq_s[:, t * LANES : (t + 1) * LANES], t).T * HEAD_DIM ** (-0.5)
        glin[:, t * LANES : (t + 1) * LANES] = unrope(gq, cos, sa, sb).astype(BF16)
    if last:
        factors = attention.whole(r.zglin, slice(0, D))
        few.second_sum()
        own_rest.advance()

    def take(k, total):
        sum_copy(k).wait_recv()
        return total + r.land_k[k].astype(F32)

    own = lax.fori_loop(1, n, take, own)
    glin[:, D : D + LANES] = unrope(own[:, :LANES], cos, sa, sb).astype(BF16)
    glin[:, D + LANES :] = own[:, LANES:].astype(BF16)
    if last:
        factors += attention.whole(r.zglin, slice(D, QKV))
    else:
        r.flush("glin")
    gn1 = mm_nt(glin[...], r.gu[0, :, :QKV])
    x = r.x[...]
    r1_ = lax.rsqrt(jnp.mean(x * x, -1, keepdims=True) + EPS)
    unit = x * r1_
    dg1 = col_sum(gn1 * unit)
    dbias = col_sum(glin[...].astype(F32))
    gsmall = r.zsmall.at[st.block(st.z, 2 * UNIT), :] if last else r.gsmall
    gsmall[...] = jnp.zeros(gsmall.shape, F32)
    row = 0
    for part in (dg1, dg2, dbias):
        for t in range(part.shape[1] // LANES):
            gsmall[row : row + 1, :] = part[:, t * LANES : (t + 1) * LANES]
            row += 1
    if last:
        factors += attention.whole(r.zsmall)
        own_rest.advance()
        few.first_gather()
    else:
        r.flush("gsmall")
    dz = gn1 * r.small[layer][:, :D]
    r.gx[...] = r.gm_s[...] + r1_ * (dz - unit * jnp.mean(dz * unit, -1, keepdims=True))
    if last:
        below = Delivery(st, 0, r.gx, r.input_grad)
        out = (r.qa, r.qb)
        zswap = attention.swap(factors, r.n1z, r.zglin, r.zsmall, r.dout, r.zv, r.zl)
        own_rest.advance()
        ends = few.hand_over(out, 1)
        attention.fold(zswap, r.zv, r.zl, (r.qp0a, r.qp0b))
        few = Few(st, r, "0")
        few.second_sum()
        own_rest.second_half()
        few.first_gather()
        ends += few.hand_over(out, 0)
        own_rest.finish()
        for end in ends:
            end()
        above.finish()
        below.finish()
    else:
        for h in range(2):
            arrived(r1[h])
            mine = sl[h].at[st.along(AXES[h][0], 0)]
            add_into(t1[h], [mine] + [l1[h].at[k] for k in range(SIDE - 1)])
    st.drain()

    def done(k, c):
        sum_copy(k).wait_send()
        return c

    lax.fori_loop(1, n, done, 0)
    r.close()


class Refs(types.SimpleNamespace):
    def load(self):
        for c in self.coming.values():
            c.start()

    def need(self, *names):
        for k in names:
            if k not in self.here:
                self.coming[k].wait()
                self.here.add(k)

    def flush(self, *names):
        for k in names:
            self.going[k].start()
            self.gone.add(k)

    def close(self):
        self.need(*self.coming)
        self.flush(*[k for k in self.going if k not in self.gone])
        for c in self.going.values():
            c.wait()


def call(kernel, layer, cid, name, ins, outs, scratch, sems, hbm=(), flops=10**10, picked=(), whole=(), scalars=()):
    staged = [k for k in ins if k not in hbm + whole + scalars]
    made = [k for k in outs if k not in hbm]
    dma = pltpu.SemaphoreType.DMA
    counts = dict(ssem=sems, rsem=sems, lsem=20, csem=16, csem2=16, psem=16, psem2=16, isem=len(staged), osem=len(made))
    if name == "forward":
        counts.update(csem1=16, csem21=16)
    places = [pltpu.VMEM(ins[k].shape[2 if k in picked else 0 :], ins[k].dtype) for k in staged] + [pltpu.VMEM(*outs[k]) for k in made]
    names = ["in_" + k for k in ins] + ["out_" + k for k in outs] + staged + made + list(scratch) + list(counts)

    def body(*refs):
        r = Refs(**dict(zip(names, refs)))
        for k in hbm + whole + scalars:
            if k in ins or k in outs:
                setattr(r, k, getattr(r, ("in_" if k in ins else "out_") + k))
        r.here, r.gone = set(), set()
        def source(k):
            ref = getattr(r, "in_" + k)
            return ref.at[lax.axis_index("section"), 0] if k in picked else ref

        r.coming = {k: pltpu.make_async_copy(source(k), getattr(r, k), r.isem.at[i]) for i, k in enumerate(staged)}
        r.going = {
            k: pltpu.make_async_copy(getattr(r, k), getattr(r, "out_" + k), r.osem.at[i]) for i, k in enumerate(made)
        }
        kernel(layer, r)

    anywhere = pl.BlockSpec(memory_space=pl.ANY)
    places_in = {k: pl.BlockSpec(memory_space=pltpu.VMEM) for k in whole}
    places_in.update({k: pl.BlockSpec(memory_space=pltpu.SMEM) for k in scalars})
    got = pl.pallas_call(
        body,
        out_shape=[jax.ShapeDtypeStruct(s, t) for s, t in outs.values()],
        in_specs=[places_in.get(k, anywhere) for k in ins],
        out_specs=[anywhere] * len(outs),
        scratch_shapes=places + [pltpu.VMEM(s, t) for s, t in scratch.values()] + [dma((k,)) for k in counts.values()],
        compiler_params=pltpu.CompilerParams(
            collective_id=cid, has_side_effects=True, vmem_limit_bytes=VMEM_LIMIT
        ),
        cost_estimate=pl.CostEstimate(flops=flops, bytes_accessed=20 * 2**20, transcendentals=0),
        name=name,
    )(*ins.values())
    return dict(zip(outs, got))


FAR = ("ga", "gb", "ha", "hb", "qa", "qb", "input_grad", "wa")
FA_ROWS = tuple((4 * g + d) * UNIT for g, d in zip(GATE_PER, DOWN_PER))
RQ = Q_ROWS // 2 // 16
SIDES = (SIDE, SIDE)
WIDE = HEADS * HEAD_DIM


def bf(*shape):
    return (shape, BF16)


def f4(*shape):
    return (shape, F32)


def rest_scratch():
    made = {}
    for h, rows in zip("ab", FA_ROWS):
        made["l2" + h] = bf(SIDE - 1, rows, LANES)
        made["t2" + h] = bf(rows, LANES)
        made["g1" + h] = bf(SIDE, rows, LANES)
    return made


def rest_outs():
    return {"g" + h: bf(2, *SIDES, rows, LANES) for h, rows in zip("ab", FA_ROWS)}


def assemble_kernel(nz, *refs):
    given, results, held, outs, sem, osem = (refs[:2], refs[2:4]), refs[6:14], refs[14:16] + refs[4:6], refs[16:24], refs[24], refs[25]
    s = lax.axis_index("section")
    copies = [pltpu.make_async_copy(a, b, osem.at[i]) for i, (a, b) in enumerate(zip(outs, results))]
    for layer in range(2):
        @pl.when(s == layer)
        def _():
            moving = [pltpu.make_async_copy(a, b, sem.at[i]) for i, (a, b) in enumerate(zip(given[layer], held))]
            for c in moving:
                c.start()
            for c in moving:
                c.wait()

    gate_ref, up_ref, down_ref, qkv_ref, out_ref = outs[:5]
    share = D // nz
    starts = window_starts(nz)

    def units(refs, section, base, per, first, count):
        rows = []
        for part, piece, slot, _, m in unit_runs(first, count, per):
            at = base[part] + slot * UNIT
            rows.append(refs[part][section, piece // SIDE, piece % SIDE, at : at + m * UNIT, :].astype(F32))
        return jnp.concatenate(rows, 0) if len(rows) > 1 else rows[0]

    for section, ref in ((0, gate_ref), (1, up_ref)):
        tiles = {}
        for w, a in enumerate(starts):
            for t in range(WIN // LANES):
                tiles.setdefault(a // LANES + t, []).append((w, t))
        for col, sources in tiles.items():
            total = None
            for w, t in sources:
                base = [w * per * UNIT for per in GATE_PER]
                got = units(held[:2], section, base, GATE_PER, t * (share // UNIT), share // UNIT)
                total = got if total is None else total + got
            ref[:, col * LANES : (col + 1) * LANES] = total
        copies[section].start()
    base = [nz * per * UNIT for per in GATE_PER]
    half = FF // nz // 2
    for section in range(2):
        for t in range(TILES):
            got = units(held[:2], section, base, DOWN_PER, t * (half // UNIT), half // UNIT)
            down_ref[section * half : (section + 1) * half, t * LANES : (t + 1) * LANES] = got
    copies[2].start()
    for t in range(QKV // LANES + TILES):
        got = units(held[2:], t // 8, (0, 0), Q_PER, (t % 8) * (share // UNIT), share // UNIT)
        if t < QKV // LANES:
            qkv_ref[:, t * LANES : (t + 1) * LANES] = got
        else:
            u = t - QKV // LANES
            out_ref[:, u * LANES : (u + 1) * LANES] = got
    small = units(held[2:], 0, (0, 0), Q_PER, 8 * (share // UNIT), 2)
    z = lax.axis_index("fsdp")
    row = 0
    for ref, size in zip(outs[5:], (D, D, QKV)):
        tiles = size // LANES
        line = jnp.concatenate([small[row + t : row + t + 1, :] for t in range(tiles)], 1)
        part = size // nz
        ref[...] = pltpu.roll(jnp.broadcast_to(line, (8, size)), lax.rem(size - z * part, size), 1)[:1, :part]
        row += tiles
    for c in copies[3:]:
        c.start()
    for c in copies:
        c.wait()


def assemble(zero, one, attn):
    nz = lax.axis_size("fsdp")
    vm = pl.BlockSpec(memory_space=pltpu.VMEM)
    anywhere = pl.BlockSpec(memory_space=pl.ANY)
    share = D // nz
    shapes = [(share, FF), (share, FF), (FF // nz, D), (share, QKV), (share, D), (1, share), (1, share), (1, QKV // nz)]
    return pl.pallas_call(
        functools.partial(assemble_kernel, nz),
        out_shape=[jax.ShapeDtypeStruct(a, F32) for a in shapes],
        in_specs=[anywhere] * 4 + [vm] * 2,
        out_specs=[anywhere] * len(shapes),
        scratch_shapes=[pltpu.VMEM(a.shape, a.dtype) for a in zero]
        + [pltpu.VMEM(a, F32) for a in shapes]
        + [pltpu.SemaphoreType.DMA((2,)), pltpu.SemaphoreType.DMA((len(shapes),))],
        compiler_params=pltpu.CompilerParams(vmem_limit_bytes=VMEM_LIMIT),
        name="assemble",
    )(*zero, *one, *attn)


def window_starts(n):
    share = FF // n
    return [(i * share // LANES) * LANES for i in range(n)]


def forward(tokens, cotangent, shards, gains, pair_of):
    n, nz = lax.axis_size("ctx"), lax.axis_size("fsdp")
    tok = tokens.shape[2]
    freq = np.arange(HEAD_DIM // 2, dtype=np.float64)
    inverse = jnp.asarray(np.tile(THETA ** (-2.0 * freq / HEAD_DIM), 4)[None, :].astype(np.float32))
    ins = dict(gains, pair=pair_of, inverse=inverse, x0=tokens, gy=cotangent)
    hbm = {k + "_shard": v for k, v in shards.items()}
    ins.update(hbm)
    outs = dict(
        small=f4(2, 1, SMALL), pairs=((n, 8, 2 * LANES), jnp.int32), cos=f4(tok, LANES), sa=f4(tok, LANES), sb=f4(tok, LANES),
        x1=f4(tok, D), gy_all=bf(nz * tok, D), layer_out=f4(2, tok, D),
    )
    scratch = dict(m_s=f4(2, WIDE), l_s=f4(2, WIDE), acc_s=f4(2 * LANES, WIDE), att_s=bf(tok, D), parts=f4(2, nz, 1, SMALL))
    for l in "01":
        each = dict(
            mid=f4(tok, D), n1t=bf(D, tok), qst=bf(2 * LANES, WIDE), kv=bf(n, tok, 2 * LANES), lse=f4(2, WIDE),
            attt=bf(D, tok), gu=bf(2, D, WIN), down=bf(WIN, D), wa=bf(D, QKV + D),
            all=bf(nz, tok, D), gate=bf(nz, tok, WIN), up=bf(nz, tok, WIN),
        )
        outs.update({k + l: v for k, v in each.items()})
        scratch.update({"y" + l: f4(tok, D), "send_s" + l: bf(nz, tok, D), "land_s" + l: bf(nz, tok, D)})
    return call(forward_kernel, 0, 1, "forward", ins, outs, scratch, 160, tuple(hbm) + ("layer_out",), picked=("x0", "gy"), whole=tuple(gains), scalars=("pair",))


def backward(layer, gy, f, before):
    n, nz = lax.axis_size("ctx"), lax.axis_size("fsdp")
    tok = gy.shape[-2]
    share = D // nz
    own = {k: f[k + str(layer)] for k in ("down", "gate", "up", "gu", "all", "mid", "attt", "n1t", "qst", "lse", "kv", "wa")}
    ins = dict(gy=gy)
    outs = {}
    factors = dict(n1z=bf(share, nz * tok), dout=bf(TILES * share, LANES))
    scratch = dict(
        hid_s=bf(nz * tok, WIN), g_s=bf(2, nz * tok, WIN), gm_s=f4(tok, D),
        own_s=f4(tok, D), send_s=bf(nz, tok, D), land_s=bf(nz, tok, D),
        delta_s=f4(2, WIDE), gq_s=f4(2 * LANES, WIDE), all_gm=bf(nz * tok, D), attz=bf(share, nz * tok),
        send_k=bf(n, tok, 2 * LANES), land_k=bf(n, tok, 2 * LANES),
    )
    for h, rows in zip("ab", FA_ROWS):
        scratch["f" + h] = bf(2, *SIDES, rows, LANES)
        scratch["sl" + h] = bf(*SIDES, rows, LANES)
        scratch["l1" + h] = bf(SIDE - 1, SIDE, rows, LANES)
    if layer == 0:
        scratch["gx"] = f4(tok, D)
        outs["input_grad"] = f4(2, tok, D)
        scratch["all_s"] = bf(nz * tok, D)
        ins.update(p1a=before["t1a"], p1b=before["t1b"])
        scratch.update(rest_scratch())
        outs.update(rest_outs())
    else:
        ins["all_s"] = f["gy_all"]
        outs["gx"] = f4(tok, D)
    ins.update(down=own["down"], gate=own["gate"], up=own["up"], gu=own["gu"], n2_all=own["all"], mid=own["mid"])
    ins["small"] = f["small"]
    ins.update({k: own[k] for k in ("attt", "n1t")})
    if layer == 0:
        ins.update(glin1=before["glin"], gsmall1=before["gsmall"], n1z1=before["n1z"], dout1=before["dout"])
        scratch.update(factors)
        scratch.update(all_glin=bf(nz * tok, QKV), all_small=f4(nz * 2 * UNIT, LANES), qv=bf(2, Q_ROWS, LANES), ql=bf(Q_ROWS, LANES))
        scratch.update(zglin=bf(nz * tok, QKV), zsmall=f4(nz * 2 * UNIT, LANES), zv=bf(2, Q_ROWS, LANES), zl=bf(Q_ROWS, LANES))
        scratch.update(t1a=bf(SIDE, FA_ROWS[0], LANES), t1b=bf(SIDE, FA_ROWS[1], LANES))
        for g, h, rows in zip("ab", "cd", FA_ROWS):
            scratch["l2" + h] = bf(SIDE - 1, rows, LANES)
            scratch["t2" + h] = bf(rows, LANES)
            scratch["g1" + h] = bf(SIDE, rows, LANES)
            outs["h" + g] = bf(2, *SIDES, rows, LANES)
            outs["q" + g] = bf(2, *SIDES, RQ, LANES)
            for tag in ("", "0"):
                scratch["qp" + tag + g] = bf(*SIDES, RQ, LANES)
                scratch["qm" + tag + g] = bf(SIDE - 1, SIDE, RQ, LANES)
                scratch["qw" + tag + g] = bf(SIDE - 1, RQ, LANES)
                scratch["qe" + tag + g] = bf(SIDE, RQ, LANES)
                scratch["qh" + tag + g] = bf(SIDE, RQ, LANES)
    else:
        outs.update(factors)
        outs.update(glin=bf(tok, QKV), gsmall=f4(2 * UNIT, LANES), t1a=bf(SIDE, FA_ROWS[0], LANES), t1b=bf(SIDE, FA_ROWS[1], LANES))
    ins.update({k: own[k] for k in ("qst", "lse", "kv", "wa")})
    ins.update({k: f[k] for k in ("pairs", "cos", "sa", "sb")})
    ins["x"] = f["x" + str(layer)] if layer else before["x0"]
    return call(backward_kernel, layer, 2 + layer, f"backward_{layer}", ins, outs, scratch, 240, FAR, 3 * 10**10, ("x",) if layer == 0 else ("gy",))


def local(
    tokens, cotangent, pair_of, attn_gain, ffn_gain, qkv_weight, qkv_bias, out_weight, gate_weight, up_weight, down_weight,
):
    shards = dict(qkv=qkv_weight, out=out_weight, gate=gate_weight, up=up_weight, down=down_weight)

    gains = dict(attn_gain=attn_gain, ffn_gain=ffn_gain, qkv_bias=qkv_bias)
    f = forward(tokens, cotangent, shards, gains, pair_of)
    c1 = backward(1, cotangent, f, None)
    c0 = backward(0, c1["gx"], f, dict(c1, x0=tokens))
    dgate, dup, ddown, dqkv, dout, dg1, dg2, dbias = assemble((c0["ha"], c0["hb"]), (c0["ga"], c0["gb"]), (c0["qa"], c0["qb"]))
    return (
        f["layer_out"][None, :, None],
        c0["input_grad"][None, :, None],
        dg1,
        dg2,
        dqkv[None],
        dbias,
        dout[None],
        dgate[None],
        dup[None],
        ddown[None],
    )


def solution(mesh):
    return jax.shard_map(
        local,
        mesh=mesh,
        in_specs=(
            P(None, "fsdp", "ctx", None),
            P(None, "fsdp", "ctx", None),
            P("ctx"),
            P("section", "fsdp"),
            P("section", "fsdp"),
            P("section", "fsdp", None),
            P("section", "fsdp"),
            P("section", "fsdp", None),
            P("section", "fsdp", None),
            P("section", "fsdp", None),
            P("section", "fsdp", None),
        ),
        out_specs=(
            P("section", None, "fsdp", "ctx", None),
            P("section", None, "fsdp", "ctx", None),
            P("section", "fsdp"),
            P("section", "fsdp"),
            P("section", "fsdp", None),
            P("section", "fsdp"),
            P("section", "fsdp", None),
            P("section", "fsdp", None),
            P("section", "fsdp", None),
            P("section", "fsdp", None),
        ),
        check_vma=False,
    )
```

```python
import functools
import types

import jax
import jax.numpy as jnp
import numpy as np
from jax import lax
from jax.experimental import pallas as pl
from jax.experimental.pallas import tpu as pltpu
from jax.sharding import PartitionSpec as P

D = 896
HEADS = 14
KV_HEADS = 2
HEAD_DIM = 64
GROUP = HEADS // KV_HEADS
FF = 4864
QKV = 1152
EPS = 1e-06
THETA = 1000000.0
LANES = 128
TILES = D // LANES
WIN = 1280
NEG = -1e30
F32 = jnp.float32
BF16 = jnp.bfloat16
MESH = pl.DeviceIdType.MESH
VMEM_LIMIT = 60 * 2**20
UNIT = 16
SIDE = 4
GATE_PER = (5, 4)
DOWN_PER = (8, 9)
Q_PER = (4, 4)
Q_ROWS = 16 * sum(Q_PER) * UNIT


def mm(a, b):
    return jnp.dot(a, b, preferred_element_type=F32)


def mm_nt(a, b):
    return lax.dot_general(a, b, (((1,), (1,)), ((), ())), preferred_element_type=F32)


def mm_tn(a, b):
    return lax.dot_general(a, b, (((0,), (0,)), ((), ())), preferred_element_type=F32)


ORDER = (1, 3, 2)
SMALL = 2 * D + QKV
AXES = (("x", "y"), ("y", "x"))
BATCH = 3
GROUPS = tuple(slice(a, min(a + 2 * LANES, HEADS * HEAD_DIM)) for a in range(0, HEADS * HEAD_DIM, 2 * LANES))


def push(src, dst, ssem, rsem, axis, to):
    return pltpu.make_async_remote_copy(
        src_ref=src,
        dst_ref=dst,
        send_sem=ssem,
        recv_sem=rsem,
        device_id={axis: to},
        device_id_type=MESH,
    )


def rope(u, cos, sa, sb):
    return u * cos + pltpu.roll(u, 96, 1) * sa + pltpu.roll(u, 32, 1) * sb


def unrope(u, cos, sa, sb):
    return u * cos - pltpu.roll(u, 96, 1) * sa - pltpu.roll(u, 32, 1) * sb


def halves(a0, a1):
    lane = lax.broadcasted_iota(jnp.int32, a0.shape, 1) < HEAD_DIM
    low = jnp.where(lane, a0, pltpu.roll(a1, HEAD_DIM, 1))
    high = jnp.where(lane, pltpu.roll(a0, HEAD_DIM, 1), a1)
    return low, high


def spread(ref, t, tile_t):
    half = HEAD_DIM
    zero = jnp.zeros((half, LANES), F32)
    cols = slice(t * LANES, (t + 1) * LANES)
    for g in range(KV_HEADS):
        pair = [tile_t[j * half : (j + 1) * half, :] if (2 * t + j) // GROUP == g else zero for j in range(2)]
        for part, content in enumerate(halves(*pair)):
            ref[part * LANES + g * half : part * LANES + (g + 1) * half, cols] = content.astype(BF16)


def gathered_tile(wide, t):
    half = HEAD_DIM
    rows = []
    for j in range(2):
        g = (2 * t + j) // GROUP
        low = wide[g * half : (g + 1) * half, :]
        high = wide[LANES + g * half : LANES + (g + 1) * half, :]
        rows.append(halves(low, high)[j])
    return jnp.concatenate(rows, 0)


def dealt(a_per, b_per):
    where = [(0, u // a_per, u % a_per) for u in range(16 * a_per)]
    return where + [(1, v // b_per, v % b_per) for v in range(16 * b_per)]


def unit_runs(first, count, per):
    where = dealt(*per)
    found = []
    for i in range(count):
        part, piece, slot = where[first + i]
        if found and found[-1][0] == part and found[-1][1] == piece:
            found[-1][4] += 1
        else:
            found.append([part, piece, slot, i, 1])
    return found


def put_units(refs, section, base, per, first, rows):
    for part, piece, slot, i, m in unit_runs(first, rows.shape[0] // UNIT, per):
        at = base[part] + slot * UNIT
        refs[part][section, piece // SIDE, piece % SIDE, at : at + m * UNIT, :] = rows[i * UNIT : (i + m) * UNIT, :]


class Stages:
    def __init__(self, r):
        self.s = lax.axis_index("section")
        self.c = lax.axis_index("ctx")
        self.nc = lax.axis_size("ctx")
        self.x, self.y = self.c // SIDE, lax.rem(self.c, SIDE)
        self.z = lax.axis_index("fsdp")
        self.nz = lax.axis_size("fsdp")
        self.ssem, self.rsem, self.lsem = r.ssem, r.rsem, r.lsem
        self.used = 0
        self.local_used = 0
        self.sent = []

    def along(self, axis, k):
        own, n = {
            "x": (self.x, SIDE),
            "y": (self.y, SIDE),
            "z": (self.z, self.nz),
            "c": (self.c, self.nc),
        }[axis]
        return lax.rem(own + n + k, n)

    def peer(self, axis, k, section=None):
        if axis == "s":
            return {"section": 1 - self.s}
        if axis == "z":
            to = {"fsdp": self.along("z", k)}
        elif axis == "c":
            to = {"ctx": self.along("c", k)}
        elif axis == "x":
            to = {"ctx": self.along("x", k) * SIDE + self.y}
        else:
            to = {"ctx": self.x * SIDE + self.along("y", k)}
        if section is not None:
            to["section"] = section
        return to

    def hail(self, ids, ring=False):
        bar = pltpu.get_barrier_semaphore()
        for i in ids:
            pl.semaphore_signal(bar, inc=1, device_id=i, device_id_type=MESH)
        self.expected = len(ids)
        if ring:
            def one(k, c):
                pl.semaphore_signal(bar, inc=1, device_id=self.peer("c", k), device_id_type=MESH)
                return c

            lax.fori_loop(1, self.nc, one, 0)
            self.expected += self.nc - 1
        self.bar = bar

    def met(self):
        pl.semaphore_wait(self.bar, self.expected)

    def beside(self):
        return [self.peer("s", 0)]

    def upright(self, both=False):
        ids = [self.peer("z", k) for k in range(1, self.nz)]
        return ids + ([self.peer("z", k, 1 - self.s) for k in range(1, self.nz)] if both else [])

    def flat(self, both=False):
        ids = [self.peer(a, k) for a in "xy" for k in range(1, SIDE)]
        return ids + ([self.peer(a, k, 1 - self.s) for a in "xy" for k in range(1, SIDE)] if both else [])

    def take(self, count):
        self.used += count
        return self.used - count

    def copy(self, src, dst, at, to, recv_at=None):
        return pltpu.make_async_remote_copy(
            src_ref=src,
            dst_ref=dst,
            send_sem=self.ssem.at[at],
            recv_sem=self.rsem.at[at if recv_at is None else recv_at],
            device_id=to,
            device_id_type=MESH,
        )

    def begin(self, copies):
        for c in copies:
            c.start()
        self.sent += copies
        return copies

    def drain(self):
        for c in self.sent:
            c.wait_send()

    def swap(self, src, land):
        return self.begin([self.copy(src.at[1 - self.s], land, self.take(1), self.peer("s", 0))])

    def scatter(self, axis, src, land):
        n = self.nz if axis == "z" else SIDE
        at = self.take(n - 1)
        return self.begin(
            [self.copy(src.at[self.along(axis, k)], land.at[k - 1], at + k - 1, self.peer(axis, k)) for k in range(1, n)]
        )

    def gather(self, axis, ref):
        at = self.take(SIDE - 1)
        mine = ref.at[self.along(axis, 0)]
        return self.begin([self.copy(mine, mine, at + k - 1, self.peer(axis, k)) for k in range(1, SIDE)])

    def deal(self, src, dst, rows):
        at = self.take(self.nz - 1)
        mine = dst.at[self.block(self.z, rows), :]
        return self.begin(
            [
                self.copy(src.at[self.block(self.along("z", k), rows), :], mine, at + k - 1, self.peer("z", k))
                for k in range(1, self.nz)
            ]
        )

    def block(self, i, rows):
        return pl.ds(pl.multiple_of(i * rows, UNIT), rows)

    def aside(self, j):
        x = lax.rem(self.x + (1 - self.s) * j, SIDE)
        y = lax.rem(self.y + self.s * j, SIDE)
        return {"ctx": x * SIDE + y}

    def quarter(self):
        return self.x * (1 - self.s) + self.y * self.s

    def hand_over(self, axis, src, dst, layer, part=None):
        return Handover(self, axis, src, dst, layer, part)


class Handover:
    def __init__(self, st, axis, src, dst, layer, part=None):
        self.st, self.axis, self.layer = st, axis, layer
        self.at = st.take(2 * SIDE)
        mine = dst.at[st.s, st.along(axis, 0)]
        if part is not None:
            src, mine = src.at[part], mine.at[part]
        self.src, self.mine, self.dst, self.part = src, mine, dst, part
        st.begin(
            [st.copy(src, mine, self.at + k, st.peer(axis, k, layer), self.at + st.s * SIDE + k) for k in (1, SIDE - 1)]
        )
        self.beside = st.copy(src, mine, self.at, {"section": layer}, self.at + st.s * SIDE)
        self.within = pltpu.make_async_copy(src, mine, st.lsem.at[st.local_used])
        st.local_used += 1
        pl.when(st.s != layer)(self.beside.start)
        pl.when(st.s == layer)(self.within.start)

    def arrival(self, half, k):
        return self.st.copy(self.src, self.mine, self.at, {"section": self.layer}, self.at + half * SIDE + k)

    def passing(self, half):
        st = self.st
        way = 1 - 2 * half
        p = self.dst.at[half, st.along(self.axis, -way)]
        if self.part is not None:
            p = p.at[self.part]
        at = self.at + half * SIDE + 2
        return st.copy(p, p, at, st.peer(self.axis, way), at)

    def relay(self):
        @pl.when(self.st.s == self.layer)
        def _():
            for half, k in ((0, 1), (1, SIDE - 1)):
                self.arrival(half, k).wait_recv()
                self.passing(half).start()

    def finish(self):
        @pl.when(self.st.s == self.layer)
        def _():
            self.within.wait()
            for half, k in ((0, SIDE - 1), (1, 1), (0, 2), (1, 2), (1 - self.layer, 0)):
                self.arrival(half, k).wait_recv()
            for half in range(2):
                self.passing(half).wait_send()

        pl.when(self.st.s != self.layer)(self.beside.wait_send)


class Scatter:
    def __init__(self, st, axis, src, land):
        self.st, self.axis, self.src, self.land = st, axis, src, land
        self.at = st.take(6)
        low, high = slice(0, SIDE // 2), slice(SIDE // 2, SIDE)
        far = src.at[st.along(axis, 2)]
        self.through = [
            self.send(far.at[low], land.at[2, low], 0, 1),
            self.send(far.at[high], land.at[2, high], 1, -1),
        ]
        self.straight = [
            self.send(src.at[st.along(axis, 1), high], land.at[0, high], 2, 1),
            self.send(src.at[st.along(axis, -1), low], land.at[1, low], 3, -1),
        ]
        st.begin(self.through + self.straight)

    def send(self, src, dst, i, way):
        return self.st.copy(src, dst, self.at + i, self.st.peer(self.axis, way))

    def pass_on(self):
        st = self.st
        low, high = slice(0, SIDE // 2), slice(SIDE // 2, SIDE)
        self.late = []
        for i, (part, way) in enumerate(((low, 1), (high, -1))):
            self.through[i].wait_recv()
            mine = self.src.at[st.along(self.axis, way), part]
            add_into(mine, [mine, self.land.at[2, part]])
            self.late.append(self.send(mine, self.land.at[i, part], 4 + i, way))
        st.begin(self.late)

    def sum_into(self, out):
        arrived(self.straight + self.late)
        add_into(out, [self.src.at[self.st.along(self.axis, 0)], self.land.at[0], self.land.at[1]])


class Feed:
    def __init__(self, st, layer, sources, piece, band):
        self.st, self.layer, self.sources, self.piece, self.band = st, layer, sources, piece, band
        steps = st.nz - 1
        self.across = st.take(2 * steps)
        self.sideways = st.take((SIDE - 1) * steps)
        self.passed = st.take(steps)
        self.own = st.take(2)

    def beside(self, h):
        b = self.band(self.st.z, h)
        return self.st.copy(b, b, self.own + h, self.st.peer("s", 0))

    def send(self, h, k, src):
        st = self.st
        dst = self.piece(st.z, h, (st.x, st.y)[h])
        return st.copy(dst if src is None else src, dst, self.across + 2 * (k - 1) + h, st.peer("z", k, h))

    def start(self):
        st = self.st

        @pl.when(st.s == self.layer)
        def _():
            for k in ORDER:
                for h in range(2):
                    for needed, src in self.sources(h, (st.x, st.y)[h], st.along("z", k)):
                        if needed is None:
                            self.send(h, k, src).start()
                        else:
                            pl.when(needed)(self.send(h, k, src).start)
            for h in range(2):
                self.beside(h).start()

    def relay(self, k):
        st = self.st
        p = self.piece(st.along("z", -k), st.s, st.quarter())
        st.copy(p, p, self.across + 2 * (k - 1) + st.s, st.peer("s", 0)).wait_recv()
        at = self.sideways + (SIDE - 1) * (k - 1) - 1
        st.begin([st.copy(p, p, at + j, st.aside(j)) for j in range(1, SIDE)])

    def collect(self, k):
        st = self.st
        z = st.along("z", -k)
        at = self.sideways + (SIDE - 1) * (k - 1) - 1
        for j in range(1, SIDE):
            p = self.piece(z, st.s, lax.rem(st.quarter() + SIDE - j, SIDE))
            st.copy(p, p, at + j, st.aside(j)).wait_recv()
        b = self.band(z, st.s)
        st.begin([st.copy(b, b, self.passed + k - 1, st.peer("s", 0))])

    def finish(self):
        st = self.st
        for k in ORDER:
            b = self.band(st.along("z", -k), 1 - st.s)
            st.copy(b, b, self.passed + k - 1, st.peer("s", 0)).wait_recv()

        @pl.when(st.s == self.layer)
        def _():
            for h in range(2):
                for k in ORDER:
                    self.send(h, k, None).wait_send()
                self.beside(h).wait_send()

        @pl.when(st.s != self.layer)
        def _():
            for h in range(2):
                self.beside(h).wait_recv()


class FeedDown:
    def __init__(self, st, layer, src, dst):
        self.st, self.layer = st, layer
        share = src.shape[1]
        spare = WIN - share
        odd = lax.rem(st.z, 2)
        place = dst.at[pl.ds(pl.multiple_of(odd * spare, UNIT), share), :]
        dst[pl.ds(pl.multiple_of((1 - odd) * share, UNIT), spare), :] = jnp.zeros((spare, D), BF16)
        self.local = pltpu.make_async_copy(src.at[0], place, st.lsem.at[st.local_used])
        st.local_used += 1
        self.remote = st.copy(src.at[0], place, st.take(1), st.peer("s", 0))

    def start(self):
        @pl.when(self.st.s == self.layer)
        def _():
            self.local.start()
            self.remote.start()

    def finish(self):
        @pl.when(self.st.s == self.layer)
        def _():
            self.local.wait()
            self.remote.wait_send()

        @pl.when(self.st.s != self.layer)
        def _():
            self.remote.wait_recv()


class Delivery:
    def __init__(self, st, layer, src, out):
        self.st, self.layer = st, layer
        mine = out.at[st.s]
        self.within = pltpu.make_async_copy(src, mine, st.lsem.at[st.local_used])
        st.local_used += 1
        self.over = st.copy(src, mine, st.take(1), st.peer("s", 0))
        pl.when(st.s == layer)(self.within.start)
        pl.when(st.s != layer)(self.over.start)

    def finish(self):
        @pl.when(self.st.s == self.layer)
        def _():
            self.within.wait()
            self.over.wait_recv()

        pl.when(self.st.s != self.layer)(self.over.wait_send)


class Local:
    def __init__(self, st, layer, pairs):
        self.st, self.layer = st, layer
        self.copies = [pltpu.make_async_copy(a, b, st.lsem.at[st.local_used + i]) for i, (a, b) in enumerate(pairs)]
        st.local_used += len(pairs)

        @pl.when(st.s == layer)
        def _():
            for c in self.copies:
                c.start()

    def wait(self):
        @pl.when(self.st.s == self.layer)
        def _():
            for c in self.copies:
                c.wait()


def half_rows(z, h, share):
    return pl.ds(pl.multiple_of(z * share + h * (share // 2), UNIT), share // 2)


def feed_attention(st, layer, qkv, out, dst):
    share = qkv.shape[1]
    rows = st.block(st.z, share)
    local = Local(st, layer, [(qkv.at[0], dst.at[rows, :QKV]), (out.at[0], dst.at[rows, QKV:])])
    width = (QKV + D) // SIDE

    def piece(z, h, q):
        return dst.at[half_rows(z, h, share), pl.ds(pl.multiple_of(q * width, LANES), width)]

    def band(z, h):
        return dst.at[half_rows(z, h, share), :]

    return local, Feed(st, layer, lambda h, q, z_to: [(None, None)], piece, band)


def feed_windows(st, layer, gate, up, dst):
    share = gate.shape[1]
    pace = FF // st.nz // (LANES // 2)
    width = WIN // 2

    def window(z):
        return pl.multiple_of(z * pace // 2 * LANES, LANES)

    rows = st.block(st.z, share)
    local = Local(st, layer, [(w.at[0, :, pl.ds(window(st.z), WIN)], dst.at[i, rows, :]) for i, w in enumerate((gate, up))])

    def sources(h, q, z_to):
        at = pl.multiple_of(window(z_to) + lax.rem(q, 2) * width, LANES)
        part = slice(h * (share // 2), (h + 1) * (share // 2))
        return [(q < 2, gate.at[0, part, pl.ds(at, width)]), (q >= 2, up.at[0, part, pl.ds(at, width)])]

    def piece(z, h, q):
        return dst.at[q // 2, half_rows(z, h, share), pl.ds(pl.multiple_of(lax.rem(q, 2) * width, LANES), width)]

    def band(z, h):
        return dst.at[:, half_rows(z, h, share), :]

    return local, Feed(st, layer, sources, piece, band)


def arrived(copies):
    for c in copies:
        c.wait_recv()


def add_into(dst, parts):
    def one(i, c):
        total = parts[0][i].astype(F32)
        for p in parts[1:]:
            total = total + p[i].astype(F32)
        dst[i] = total.astype(dst.dtype)
        return c

    lax.fori_loop(0, dst.shape[0], one, 0)


def add_rows(dst, parts):
    total = parts[0][...].astype(F32)
    for p in parts[1:]:
        total = total + p[...].astype(F32)
    dst[...] = total.astype(dst.dtype)


def swapped_sum(st, copies, given, land):
    arrived(copies)
    for i in range(SIDE):
        add_into(land.at[i], [given.at[st.s, i], land.at[i]])


def sides(tile, chosen):
    half = HEAD_DIM
    low, high = tile[:half], tile[half:]
    zero = jnp.zeros_like(low)
    below = jnp.concatenate([jnp.where(chosen, low, zero), jnp.where(chosen, zero, high)], 1)
    return jnp.concatenate([jnp.concatenate([zero, low], 1), below], 0).astype(BF16)


def sides_t(tile_t, chosen):
    lane = lax.broadcasted_iota(jnp.int32, tile_t.shape, 1) < HEAD_DIM
    upper = jnp.where(jnp.logical_or(lane, jnp.logical_not(chosen)), 0.0, pltpu.roll(tile_t, HEAD_DIM, 1))
    lower = jnp.where(jnp.logical_or(lane, jnp.logical_not(chosen)), tile_t, 0.0)
    return jnp.concatenate([upper, lower], 0).astype(BF16)


def own_sides(tile):
    low, high = tile[:HEAD_DIM], tile[HEAD_DIM:]
    zero = jnp.zeros_like(low)
    rows = [[zero, low], [low, zero], [zero, high]]
    return jnp.concatenate([jnp.concatenate(p, 1) for p in rows], 0).astype(BF16)


def own_bias(width):
    key = lax.broadcasted_iota(jnp.int32, (HEAD_DIM, width), 0)
    query = lax.rem(lax.broadcasted_iota(jnp.int32, (HEAD_DIM, width), 1), HEAD_DIM)
    return jnp.where(key <= query, 0.0, NEG)


def earlier(pairs_ref, src, me, width):
    return pairs_ref[src, 0:1, :width] < pairs_ref[me, 0:1, :width]


def col_max(a):
    return jnp.max(a, 0, keepdims=True)


def col_sum(a):
    return jnp.sum(a, 0, keepdims=True)


class View:
    def __init__(self, r, layer):
        self.r, self.layer = r, layer

    def named(self, k):
        own = k + str(self.layer)
        return own if hasattr(self.r, own) else k

    def __getattr__(self, k):
        return getattr(self.r, self.named(k))

    def need(self, *names):
        self.r.need(*[self.named(k) for k in names])

    def flush(self, *names):
        self.r.flush(*[self.named(k) for k in names])


def forward_kernel(_, r):
    st = Stages(r)
    n, me = st.nc, st.c
    st.hail(st.beside() + st.upright(True), ring=True)
    r.load()
    wa, gu, down = [None, None], [None, None], [None, None]
    for l in range(2):
        v = View(r, l)
        wa[l] = feed_attention(st, l, r.qkv_shard, r.out_shard, v.wa)
        gu[l] = feed_windows(st, l, r.gate_shard, r.up_shard, v.gu)
        down[l] = FeedDown(st, l, r.down_shard, v.down)
    r.need("inverse", "x0")
    r.pairs[me] = jnp.full(r.pairs.shape[1:], r.pair[0], jnp.int32)
    at = 0
    for part, size in ((r.attn_gain, D), (r.ffn_gain, D), (r.qkv_bias, QKV)):
        share = part.shape[1]
        line = jnp.concatenate([part[...].astype(F32), jnp.zeros((1, size - share), F32)], 1)
        line = pltpu.roll(jnp.broadcast_to(line, (8, size)), st.z * share, 1)
        r.parts[st.s, st.z, :, at : at + size] = line[:1]
        at += size
    wa[0][0].wait()
    st.met()
    wa[0][1].start()
    at = st.take(2 * st.nz)
    mine = r.parts.at[st.s, st.z]
    st.begin(
        [st.copy(mine, mine, at + k, st.peer("z", k, st.s), at + st.s * st.nz + k) for k in range(1, st.nz)]
        + [st.copy(mine, mine, at + st.nz + k, st.peer("z", k, 1 - st.s), at + st.s * st.nz + k) for k in range(1, st.nz)]
        + [st.copy(mine, mine, at, st.peer("s", 0), at + st.s * st.nz)]
    )

    def tell(k, c):
        p = r.pairs.at[me]
        push(p, p, r.psem.at[k], r.psem2.at[k], "ctx", lax.rem(me + k, n)).start()
        return c

    lax.fori_loop(1, n, tell, 0)
    block = LANES // 2
    i = lax.broadcasted_iota(jnp.int32, (LANES, LANES), 0)
    pair = r.pairs[me, 0:1, :LANES]
    pos = jnp.where(i < block, pair * block + i, (2 * n - 1 - pair) * block + i - block)
    angle = pos.astype(F32) * r.inverse[...]
    lane = lax.rem(lax.broadcasted_iota(jnp.int32, (LANES, LANES), 1), HEAD_DIM)
    sine = jnp.sin(angle)
    r.cos[...] = jnp.cos(angle)
    r.sa[...] = jnp.where(lane < HEAD_DIM // 2, -sine, 0.0)
    r.sb[...] = jnp.where(lane < HEAD_DIM // 2, 0.0, sine)
    r.flush("cos", "sa", "sb")
    for h in (st.s, 1 - st.s):
        for k in range(st.nz):
            if h is st.s and k == 0:
                continue
            st.copy(mine, mine, at, st.peer("s", 0), at + h * st.nz + k).wait_recv()
    for h in range(2):
        total = r.parts[h, 0]
        for k in range(1, st.nz):
            total = total + r.parts[h, k]
        r.small[h] = total
    r.flush("small")
    for k in ORDER:
        wa[0][1].relay(k)
    gu[0][0].wait()
    gu[0][1].start()
    down[0].start()
    for k in ORDER:
        wa[0][1].collect(k)

    def begin_next():
        wa[1][0].wait()
        wa[1][1].start()
        gu[1][0].wait()
        gu[1][1].start()
        down[1].start()

    def relays(*steps):
        def go():
            for feed, name, k in steps:
                getattr(feed, name)(k)

        return go

    g0, w1, g1 = gu[0][1], wa[1][1], gu[1][1]
    wa[0][1].finish()
    v = View(r, 0)
    v.flush("wa")
    attention_forward(
        st, v, 0,
        (
            relays((g0, "relay", 1), (g0, "relay", 3)),
            relays((g0, "relay", 2)),
            begin_next,
            relays((g0, "collect", 1), (g0, "collect", 3)),
            relays((g0, "collect", 2)),
        ),
    )

    def ready_0():
        g0.finish()
        down[0].finish()
        v.flush("gu", "down")

    ffn_forward(
        st, v, ready_0,
        (
            relays((w1, "relay", 1), (w1, "relay", 3)),
            relays((w1, "relay", 2), (g1, "relay", 1)),
            relays((g1, "relay", 3), (g1, "relay", 2), (w1, "collect", 1), (w1, "collect", 3)),
            relays((w1, "collect", 2), (g1, "collect", 1), (g1, "collect", 3), (g1, "collect", 2)),
        ),
    )
    r.x1[...] = r.y0[...].astype(BF16).astype(F32)
    r.flush("x1")
    done_0 = Delivery(st, 0, r.y0, r.layer_out)
    r.need("gy")
    tok = r.gy.shape[0]
    rows = st.block(st.z, tok)
    r.gy_all[rows, :] = r.gy[...].astype(BF16)
    at = st.take(st.nz - 1)
    mine_gy = r.gy_all.at[rows, :]
    gy_moving = st.begin([st.copy(mine_gy, mine_gy, at + k - 1, st.peer("z", k)) for k in range(1, st.nz)])
    w1.finish()
    v = View(r, 1)
    v.flush("wa")
    nothing = lambda: None
    attention_forward(st, v, 1, (nothing,) * 5)

    def ready_1():
        g1.finish()
        down[1].finish()
        v.flush("gu", "down")

    ffn_forward(st, v, ready_1, (nothing,) * 4)
    done_1 = Delivery(st, 1, r.y1, r.layer_out)
    arrived(gy_moving)
    r.flush("gy_all")
    done_0.finish()
    done_1.finish()
    st.drain()

    def done(k, c):
        p = r.pairs.at[me]
        push(p, p, r.psem.at[k], r.psem2.at[k], "ctx", lax.rem(me + k, n)).wait_send()
        return c

    lax.fori_loop(1, n, done, 0)
    r.close()


def attention_forward(st, r, layer, between):
    n, me = st.nc, st.c
    x = r.x[...]
    r1 = lax.rsqrt(jnp.mean(x * x, -1, keepdims=True) + EPS)
    small = r.small[layer]
    n1_f = x * r1 * small[:, :D]
    n1 = n1_f.astype(BF16)
    bias = small[:, 2 * D :]
    cos, sa, sb = r.cos[...], r.sa[...], r.sb[...]
    lin = mm(n1, r.wa[:, D:QKV]) + bias[:, D:]
    r.kv[me] = jnp.concatenate([rope(lin[:, :LANES], cos, sa, sb), lin[:, LANES:]], 1).astype(BF16)

    def keys_copy(k, src):
        return push(r.kv.at[src], r.kv.at[src], r.csem.at[k], r.csem2.at[k], "ctx", lax.rem(me + k, n))

    def start(k, c):
        keys_copy(k, me).start()
        return c

    lax.fori_loop(1, n, start, 0)
    linq = mm(n1, r.wa[:, :D]) + bias[:, :D]
    for t in range(TILES):
        tile = slice(t * LANES, (t + 1) * LANES)
        q = rope(linq[:, tile], cos, sa, sb) * HEAD_DIM ** (-0.5)
        spread(r.qst, t, q.T)
        r.n1t[tile, :] = n1_f[:, tile].T.astype(BF16)
    r.flush("qst", "n1t")
    between[0]()
    half = HEAD_DIM
    own_k = own_sides(r.kv[me, :, :LANES].astype(F32))
    own_vt = own_sides(r.kv[me, :, LANES:].astype(F32)).astype(F32).T.astype(BF16)
    for cols in GROUPS:
        width = cols.stop - cols.start
        bias = own_bias(width)
        sc = mm(own_k, r.qst[:, cols])
        s_a, s_l, s_h = sc[:half], sc[half : 2 * half] + bias, sc[2 * half :] + bias
        m_lo = col_max(s_l)
        m_hi = jnp.maximum(col_max(s_a), col_max(s_h))
        p_a, p_l, p_h = jnp.exp(s_a - m_hi), jnp.exp(s_l - m_lo), jnp.exp(s_h - m_hi)
        r.m_s[0:1, cols], r.m_s[1:2, cols] = m_lo, m_hi
        r.l_s[0:1, cols], r.l_s[1:2, cols] = col_sum(p_l), col_sum(p_a) + col_sum(p_h)
        r.acc_s[:, cols] = mm(own_vt, jnp.concatenate([p_a, p_l, p_h], 0).astype(BF16))

    def step(i, c):
        kx, vt, sel = [], [], []
        for j in range(BATCH):
            k = i * BATCH + 1 + j
            src = lax.rem(me + n - k, n)
            keys_copy(k, src).wait_recv()
            if layer == 0:
                p = r.pairs.at[src]
                push(p, p, r.psem.at[k], r.psem2.at[k], "ctx", lax.rem(me + k, n)).wait_recv()
            sel.append(src)
            chosen = earlier(r.pairs, src, me, LANES)
            kx.append(sides(r.kv[src, :, :LANES].astype(F32), chosen))
            vt.append(sides_t(r.kv[src, :, LANES:].astype(F32).T, chosen))
        kx = jnp.concatenate(kx, 0)
        vt = jnp.concatenate(vt, 1)
        for cols in GROUPS:
            width = cols.stop - cols.start
            sc = mm(kx, r.qst[:, cols])
            m_lo, m_hi = r.m_s[0:1, cols], r.m_s[1:2, cols]
            n_lo, n_hi = m_lo, m_hi
            chosen = [earlier(r.pairs, src, me, width) for src in sel]
            for j in range(BATCH):
                top = col_max(sc[(2 * j + 1) * half : (2 * j + 2) * half])
                n_hi = jnp.maximum(n_hi, col_max(sc[2 * j * half : (2 * j + 1) * half]))
                n_hi = jnp.where(chosen[j], n_hi, jnp.maximum(n_hi, top))
                n_lo = jnp.where(chosen[j], jnp.maximum(n_lo, top), n_lo)
            a_lo, a_hi = jnp.exp(m_lo - n_lo), jnp.exp(m_hi - n_hi)
            l_lo, l_hi = r.l_s[0:1, cols] * a_lo, r.l_s[1:2, cols] * a_hi
            ps = []
            for j in range(BATCH):
                p_a = jnp.exp(sc[2 * j * half : (2 * j + 1) * half] - n_hi)
                p_s = jnp.exp(sc[(2 * j + 1) * half : (2 * j + 2) * half] - jnp.where(chosen[j], n_lo, n_hi))
                total = col_sum(p_s)
                l_hi = l_hi + col_sum(p_a) + jnp.where(chosen[j], 0.0, total)
                l_lo = l_lo + jnp.where(chosen[j], total, 0.0)
                ps += [p_a.astype(BF16), p_s.astype(BF16)]
            r.m_s[0:1, cols], r.m_s[1:2, cols] = n_lo, n_hi
            r.l_s[0:1, cols], r.l_s[1:2, cols] = l_lo, l_hi
            new = mm(vt, jnp.concatenate(ps, 0))
            r.acc_s[:LANES, cols] = r.acc_s[:LANES, cols] * a_lo + new[:LANES]
            r.acc_s[LANES:, cols] = r.acc_s[LANES:, cols] * a_hi + new[LANES:]
        return c

    lax.fori_loop(0, 1, step, 0)
    between[1]()
    lax.fori_loop(1, 2, step, 0)
    between[2]()
    lax.fori_loop(2, 4, step, 0)
    between[3]()
    lax.fori_loop(4, (n - 1) // BATCH, step, 0)
    between[4]()
    r.flush("kv")
    if layer == 0:
        r.flush("pairs")
    r.lse[...] = r.m_s[...] + jnp.log(r.l_s[...])
    for t in range(TILES):
        cols = slice(t * LANES, (t + 1) * LANES)
        wide = jnp.concatenate([r.acc_s[:LANES, cols] / r.l_s[0:1, cols], r.acc_s[LANES:, cols] / r.l_s[1:2, cols]], 0)
        tile_t = gathered_tile(wide, t)
        r.attt[cols, :] = tile_t.astype(BF16)
        r.att_s[:, cols] = tile_t.T.astype(BF16)
    r.flush("lse", "attt")
    mid = x + mm(r.att_s[...], r.wa[:, QKV:])
    r.mid[...] = mid
    r2 = lax.rsqrt(jnp.mean(mid * mid, -1, keepdims=True) + EPS)
    r.all[st.z] = (mid * r2 * small[:, D : 2 * D]).astype(BF16)
    r.flush("mid")

    def done(k, c):
        keys_copy(k, me).wait_send()
        return c

    lax.fori_loop(1, n, done, 0)


def ffn_forward(st, r, ready, between):
    n, me = st.nz, st.z
    at = st.take(2 * n)

    def first(k):
        return st.copy(r.all.at[me], r.all.at[me], at + k, st.peer("z", k))

    def second(k):
        return st.copy(r.send_s.at[k], r.land_s.at[k], at + n + k, st.peer("z", -k))

    for k in ORDER:
        first(k).start()
    ready()

    tok = r.mid.shape[0]

    def block(sources):
        a = jnp.concatenate([r.all[i] for i in sources], 0) if len(sources) > 1 else r.all[sources[0]]
        gate = mm(a, r.gu[0])
        up = mm(a, r.gu[1])
        for j, i in enumerate(sources):
            r.gate[i] = gate[j * tok : (j + 1) * tok].astype(BF16)
            r.up[i] = up[j * tok : (j + 1) * tok].astype(BF16)
        hidden = (gate * jax.nn.sigmoid(gate) * up).astype(BF16)
        return mm(hidden, r.down[...])

    r.y[...] = r.mid[...] + block([me])
    between[0]()
    first(1).wait_recv()
    first(3).wait_recv()
    both = block([st.along("z", -1), st.along("z", -3)]).astype(BF16)
    for i, k in enumerate((1, 3)):
        r.send_s[k] = both[i * tok : (i + 1) * tok]
        second(k).start()
    between[1]()
    first(2).wait_recv()
    r.send_s[2] = block([st.along("z", -2)]).astype(BF16)
    second(2).start()
    between[2]()
    r.flush("all", "gate", "up")
    between[3]()
    for k in ORDER:
        second(k).wait_recv()
        r.y[...] += r.land_s[k].astype(F32)
    for k in ORDER:
        first(k).wait_send()
        second(k).wait_send()


class Attention:
    def __init__(self, st):
        self.st = st

    def columns(self, src, dst):
        st = self.st
        share = dst.shape[0]
        at = st.take(st.nz - 1)
        mine = dst.at[:, pl.ds(pl.multiple_of(st.z * LANES, LANES), LANES)]
        moving = st.begin(
            [
                st.copy(src.at[st.block(st.along("z", k), share), :], mine, at + k - 1, st.peer("z", k))
                for k in range(1, st.nz)
            ]
        )
        mine[...] = src[st.block(st.z, share), :]
        return moving

    def whole(self, dst, cols=slice(None)):
        st = self.st
        rows = dst.shape[0] // st.nz
        at = st.take(st.nz - 1)
        mine = dst.at[pl.ds(pl.multiple_of(st.z * rows, UNIT), rows), cols]
        return st.begin([st.copy(mine, mine, at + k - 1, st.peer("z", k)) for k in range(1, st.nz)])

    def begin(self, glin, small, all_glin, all_small):
        st = self.st
        tok = glin.shape[0]
        all_glin[st.block(st.z, tok), :] = glin[...]
        all_small[st.block(st.z, 2 * UNIT), :] = small[...]
        return self.whole(all_glin) + self.whole(all_small)

    def swap(self, moving, n1z, all_glin, all_small, dout, made, land):
        st = self.st
        arrived(moving)
        share = n1z.shape[0]
        per = 8
        for j in range(0, QKV // LANES, 2):
            cols = slice(j * LANES, min(j + 2, QKV // LANES) * LANES)
            d = mm(n1z[...], all_glin[:, cols]).astype(BF16)
            for t in range(j, min(j + 2, QKV // LANES)):
                made[t // per, (t % per) * share : (t % per + 1) * share, :] = d[:, (t - j) * LANES : (t - j + 1) * LANES]
        made[1, share : 8 * share, :] = dout[...]
        small = jnp.zeros((2 * UNIT, LANES), F32)
        for i in range(st.nz):
            small = small + all_small[i * 2 * UNIT : (i + 1) * 2 * UNIT, :]
        made[0, 8 * share : 8 * share + 2 * UNIT, :] = small.astype(BF16)
        made[0, 8 * share + 2 * UNIT :, :] = jnp.zeros((Q_ROWS - 8 * share - 2 * UNIT, LANES), BF16)
        made[1, 8 * share :, :] = jnp.zeros((Q_ROWS - 8 * share, LANES), BF16)
        return st.swap(made, land)

    def fold(self, moving, made, land, out):
        st = self.st
        arrived(moving)
        rows = Q_ROWS // 2 // 16
        for h in range(2):
            for i in range(16):
                at = slice((h * 16 + i) * rows, (h * 16 + i + 1) * rows)
                total = made[st.s, at, :].astype(F32) + land[at, :].astype(F32)
                out[h][i // SIDE, i % SIDE] = total.astype(BF16)


class Rest:
    def __init__(self, st, t1, l2, t2, g1, out, layer):
        self.st, self.t1, self.l2, self.t2, self.g1, self.out, self.layer = st, t1, l2, t2, g1, out, layer
        self.stage = 0
        self.moving = [st.scatter(AXES[h][1], t1[h], l2[h]) for h in range(2)]

    def advance(self):
        st = self.st
        for h in range(2):
            second = AXES[h][1]
            arrived(self.moving[h])
            mine = self.g1[h].at[st.along(second, 0)]
            if self.stage == 0:
                t2 = self.t2[h]
                add_rows(t2, [self.t1[h].at[st.along(second, 0)]] + [self.l2[h].at[k] for k in range(SIDE - 1)])
                per = GATE_PER[h] * UNIT
                self.moving[h] = st.deal(t2, mine, per)
                mine[st.block(st.z, per), :] = t2[st.block(st.z, per), :]
                mine[st.nz * per :, :] = t2[st.nz * per :, :]
            elif self.stage == 1:
                self.moving[h] = st.gather(second, self.g1[h])
        if self.stage == 2:
            self.ends = []
            self.open = []
            self.give(slice(0, SIDE // 2))
        self.stage += 1

    def give(self, part):
        made = [self.st.hand_over(AXES[h][0], self.g1[h], self.out[h], self.layer, part) for h in range(2)]
        self.ends += made
        self.open += made

    def relay(self):
        for one in self.open:
            one.relay()
        self.open = []

    def finish(self):
        for one in self.ends:
            one.finish()


class Few:
    def __init__(self, st, r, tag):
        self.st = st

        def both(name):
            return tuple(getattr(r, name + tag + h) for h in "ab")

        self.qp, self.land, self.part, self.land2, self.wide = both("qp"), both("qm"), both("qe"), both("qw"), both("qh")
        self.moving = [st.scatter(AXES[h][0], self.qp[h], self.land[h]) for h in range(2)]

    def second_sum(self):
        st = self.st
        for h in range(2):
            arrived(self.moving[h])
            own = self.qp[h].at[st.along(AXES[h][0], 0)]
            add_into(self.part[h], [own] + [self.land[h].at[k] for k in range(SIDE - 1)])
            self.moving[h] = st.scatter(AXES[h][1], self.part[h], self.land2[h])

    def first_gather(self):
        st = self.st
        for h in range(2):
            arrived(self.moving[h])
            i = st.along(AXES[h][1], 0)
            add_rows(self.wide[h].at[i], [self.part[h].at[i]] + [self.land2[h].at[k] for k in range(SIDE - 1)])
            self.moving[h] = st.gather(AXES[h][1], self.wide[h])

    def hand_over(self, out, layer):
        for h in range(2):
            arrived(self.moving[h])
        return [self.st.hand_over(AXES[h][0], self.wide[h], out[h], layer) for h in range(2)]


def backward_kernel(layer, r):
    st = Stages(r)
    n, me = st.nz, st.z
    carry = layer == 0
    ids = st.upright() + st.beside()
    if carry:
        ids += [st.peer(a, k, 1 - st.s) for a in "xy" for k in range(1, SIDE)]
    st.hail(ids, ring=True)
    r.load()
    tok = r.gy.shape[0]

    def rows_of(i):
        return pl.ds(pl.multiple_of(i * tok, tok), tok)

    r.need("gy")
    gyb = r.gy[...].astype(BF16)
    gy = gyb.astype(F32) if carry else r.gy[...]
    above = None
    if carry:
        r.all_s[rows_of(me), :] = gyb
    else:
        r.need("all_s")
    st.met()
    at = st.take(2 * n)

    def first(k):
        mine = r.all_s.at[rows_of(me), :]
        return st.copy(mine, mine, at + k, st.peer("z", k))

    def second(k):
        return st.copy(r.send_s.at[k], r.land_s.at[k], at + n + k, st.peer("z", -k))

    if carry:
        for k in ORDER:
            first(k).start()
        above = Delivery(st, 1, r.gy, r.input_grad)
        r.need("p1a", "p1b")
        rest = Rest(st, (r.p1a, r.p1b), (r.l2a, r.l2b), (r.t2a, r.t2b), (r.g1a, r.g1b), (r.ga, r.gb), 1)
    r.need("down", "gate", "up", "gu")

    def block(sources):
        def stacked(ref):
            parts = [ref[rows_of(i), :] for i in sources]
            return jnp.concatenate(parts, 0) if len(parts) > 1 else parts[0]

        def picked(ref):
            parts = [ref[i].astype(F32) for i in sources]
            return jnp.concatenate(parts, 0) if len(parts) > 1 else parts[0]

        def keep(ref, value):
            for j, i in enumerate(sources):
                ref[rows_of(i), :] = value[j * tok : (j + 1) * tok]

        gh = mm_nt(stacked(r.all_s), r.down[...])
        gate, up = picked(r.gate), picked(r.up)
        sg = jax.nn.sigmoid(gate)
        act = gate * sg
        keep(r.hid_s, (act * up).astype(BF16))
        ggate = (gh * up * sg * (1.0 + gate * (1.0 - sg))).astype(BF16)
        gup = (gh * act).astype(BF16)
        keep(r.g_s.at[0], ggate)
        keep(r.g_s.at[1], gup)
        return mm_nt(ggate, r.gu[0]) + mm_nt(gup, r.gu[1])

    r.own_s[...] = block([me])
    if carry:
        rest.advance()
        first(1).wait_recv()
        first(3).wait_recv()
    both = block([st.along("z", -1), st.along("z", -3)]).astype(BF16)
    for i, k in enumerate((1, 3)):
        r.send_s[k] = both[i * tok : (i + 1) * tok]
        second(k).start()
    if carry:
        rest.advance()
        first(2).wait_recv()
    r.send_s[2] = block([st.along("z", -2)]).astype(BF16)
    second(2).start()
    attention = Attention(st)
    before = None
    if carry:
        r.need("glin1", "gsmall1")
        before = attention.begin(r.glin1, r.gsmall1, r.all_glin, r.all_small)
        rest.advance()

    late = [
        pltpu.make_async_copy(r.wa.at[:, :QKV], r.gu.at[0, :, :QKV], st.lsem.at[st.local_used]),
        pltpu.make_async_copy(r.wa.at[:, QKV:], r.gu.at[1, :, :D], st.lsem.at[st.local_used + 1]),
    ]
    st.local_used += 2
    for c in late:
        c.start()
    refs = (r.fa, r.fb)
    share = D // n
    for j in range(WIN // (2 * LANES)):
        cols = slice(2 * j * LANES, 2 * (j + 1) * LANES)
        r.down[cols, :] = mm_tn(r.hid_s[:, cols], r.all_s[...]).astype(BF16)
    pad = (WIN - FF // n) * lax.rem(me, 2)
    half = FF // n // 2
    base = [n * per * UNIT for per in GATE_PER]
    for section in range(2):
        rows = r.down[pl.ds(pl.multiple_of(pad + section * half, UNIT), half), :]
        for t in range(TILES):
            put_units(refs, section, base, DOWN_PER, t * (half // UNIT), rows[:, t * LANES : (t + 1) * LANES])
        used = TILES * (half // UNIT)
        extra = 16 * sum(DOWN_PER) - used
        put_units(refs, section, base, DOWN_PER, used, jnp.zeros((extra * UNIT, LANES), BF16))
    r.need("n2_all")
    normed = jnp.concatenate([r.n2_all[i] for i in range(n)], 0)

    def product(section):
        for j in range(WIN // (2 * LANES)):
            d = mm_tn(normed, r.g_s[section, :, 2 * j * LANES : 2 * (j + 1) * LANES]).astype(BF16)
            for t in (2 * j, 2 * j + 1):
                tile = d[:, (t % 2) * LANES : (t % 2 + 1) * LANES]
                for i in range(n):
                    base = [i * per * UNIT for per in GATE_PER]
                    put_units(refs, section, base, GATE_PER, t * (share // UNIT), tile[i * share : (i + 1) * share, :])
        used = WIN // LANES * (share // UNIT)
        extra = 16 * sum(GATE_PER) - used
        for i in range(n):
            base = [i * per * UNIT for per in GATE_PER]
            put_units(refs, section, base, GATE_PER, used, jnp.zeros((extra * UNIT, LANES), BF16))

    product(1 - st.s)
    swaps = [st.swap(refs[h], (r.sla, r.slb)[h]) for h in range(2)]
    product(st.s)
    for k in ORDER:
        second(k).wait_recv()
        r.own_s[...] += r.land_s[k].astype(F32)
    gn2 = r.own_s[...]
    r.need("mid", "small")
    mid = r.mid[...]
    r2 = lax.rsqrt(jnp.mean(mid * mid, -1, keepdims=True) + EPS)
    unit = mid * r2
    dg2 = col_sum(gn2 * unit)
    dz = gn2 * r.small[layer][:, D : 2 * D]
    gm = gy + r2 * (dz - unit * jnp.mean(dz * unit, -1, keepdims=True))
    r.gm_s[...] = gm
    for k in ORDER:
        if carry:
            first(k).wait_send()
        second(k).wait_send()
    attention_backward(st, r, layer, gm, dg2, refs, swaps, rest if carry else None, above, late, attention, before)


def attention_backward(st, r, layer, gm, dg2, refs, swaps, rest, above, late, attention, before):
    n, me = st.nc, st.c
    last = layer == 0
    half = HEAD_DIM
    gmb = gm.astype(BF16)
    tok = gm.shape[0]
    r.all_gm[st.block(st.z, tok), :] = gmb
    sl, l1, t1 = (r.sla, r.slb), (r.l1a, r.l1b), (r.t1a, r.t1b)
    r.need("attt", "n1t")
    size = 2 * BATCH * half
    pr, ds, gst = r.g_s.at[0, :size, :WIDE], r.g_s.at[1, :size, :WIDE], r.hid_s.at[: 2 * LANES, :WIDE]
    out_factors = attention.whole(r.all_gm) + attention.columns(r.attt, r.attz)
    qkv_factor = attention.columns(r.n1t, r.n1z)
    r1 = []
    for h in range(2):
        swapped_sum(st, swaps[h], refs[h], sl[h])
        r1.append(Scatter(st, AXES[h][0], sl[h], l1[h]))
    r.need("qst", "lse", "kv", "pairs")
    for c in late:
        c.wait()
    ga = mm_nt(gmb, r.gu[1, :, :D])
    for t in range(TILES):
        tile = slice(t * LANES, (t + 1) * LANES)
        ga_t = ga[:, tile].T
        spread(gst, t, ga_t)
        prod = ga_t * r.attt[tile, :].astype(F32)
        low, high = halves(col_sum(prod[:half]), col_sum(prod[half:]))
        r.delta_s[0:1, tile], r.delta_s[1:2, tile] = low, high

    def own_block():
        keys, vals = r.kv[me, :, :LANES].astype(F32), r.kv[me, :, LANES:].astype(F32)
        kx, vx = own_sides(keys), own_sides(vals)
        kt = kx.astype(F32).T.astype(BF16)
        rows = slice(0, 3 * half)
        for cols in GROUPS:
            bias = own_bias(cols.stop - cols.start)
            sc = mm(kx, r.qst[:, cols])
            dp = mm(vx, gst[:, cols])
            lo, hi = (r.lse[0:1, cols], r.delta_s[0:1, cols]), (r.lse[1:2, cols], r.delta_s[1:2, cols])
            parts = [(sc[:half], hi), (sc[half : 2 * half] + bias, lo), (sc[2 * half :] + bias, hi)]
            for i, (part, (lse, delta)) in enumerate(parts):
                p = jnp.exp(part - lse)
                at = slice(i * half, (i + 1) * half)
                pr[at, cols] = p.astype(BF16)
                ds[at, cols] = (p * (dp[at] - delta)).astype(BF16)
            r.gq_s[:, cols] = mm(kt, ds[rows, cols])
        made = []
        for w, q in ((ds, r.qst), (pr, gst)):
            e = mm_nt(w[rows, :], q[...])
            low = e[:half, LANES:] + e[half : 2 * half, :LANES]
            made.append(jnp.concatenate([low, e[2 * half :, LANES:]], 0))
        return jnp.concatenate(made, 1)

    def sum_copy(k):
        return push(r.send_k.at[k], r.land_k.at[k], r.csem.at[k], r.csem2.at[k], "ctx", lax.rem(me + k, n))

    def step(i):
        kx, vx, kt, sel = [], [], [], []
        for j in range(BATCH):
            src = lax.rem(me + i * BATCH + 1 + j, n)
            sel.append(src)
            chosen = earlier(r.pairs, src, me, LANES)
            keys = r.kv[src, :, :LANES].astype(F32)
            kx.append(sides(keys, chosen))
            vx.append(sides(r.kv[src, :, LANES:].astype(F32), chosen))
            kt.append(sides_t(keys.T, chosen))
        kx, vx, kt = jnp.concatenate(kx, 0), jnp.concatenate(vx, 0), jnp.concatenate(kt, 1)
        rows = slice(0, 2 * BATCH * half)
        for cols in GROUPS:
            width = cols.stop - cols.start
            sc = mm(kx, r.qst[:, cols])
            dp = mm(vx, gst[:, cols])
            for j in range(BATCH):
                chosen = earlier(r.pairs, sel[j], me, width)
                for part in range(2):
                    lse, delta = r.lse[1:2, cols], r.delta_s[1:2, cols]
                    if part:
                        lse = jnp.where(chosen, r.lse[0:1, cols], lse)
                        delta = jnp.where(chosen, r.delta_s[0:1, cols], delta)
                    at = slice((2 * j + part) * half, (2 * j + part + 1) * half)
                    p = jnp.exp(sc[at] - lse)
                    pr[at, cols] = p.astype(BF16)
                    ds[at, cols] = (p * (dp[at] - delta)).astype(BF16)
            r.gq_s[:, cols] += mm(kt, ds[rows, cols])
        ek = mm_nt(ds[rows, :], r.qst[...])
        ev = mm_nt(pr[rows, :], gst[...])
        for j in range(BATCH):
            chosen = earlier(r.pairs, sel[j], me, LANES)
            k = i * BATCH + 1 + j
            for e, lanes in ((ek, slice(0, LANES)), (ev, slice(LANES, 2 * LANES))):
                top = e[2 * j * half : (2 * j + 1) * half]
                low = e[(2 * j + 1) * half : (2 * j + 2) * half]
                r.send_k[k, :half, lanes] = (top[:, LANES:] + jnp.where(chosen, low[:, :LANES], 0.0)).astype(BF16)
                r.send_k[k, half:, lanes] = jnp.where(chosen, 0.0, low[:, LANES:]).astype(BF16)
            sum_copy(k).start()

    own = own_block()
    for i in range((n - 1) // BATCH):
        step(i)
        if i == 0:
            for one in r1:
                one.pass_on()
        if i == 1 and last:
            rest.relay()

    def out_gradient():
        arrived(out_factors)
        share = D // st.nz
        for j in range(0, TILES, 2):
            cols = slice(j * LANES, min(j + 2, TILES) * LANES)
            d = mm(r.attz[...], r.all_gm[:, cols]).astype(BF16)
            for t in range(j, min(j + 2, TILES)):
                r.dout[t * share : (t + 1) * share, :] = d[:, (t - j) * LANES : (t - j + 1) * LANES]

    glin = r.zglin.at[st.block(st.z, tok), :] if last else r.glin
    r.need("cos", "sa", "sb", "x", "small")
    cos, sa, sb = r.cos[...], r.sa[...], r.sb[...]
    for t in range(TILES):
        gq = gathered_tile(r.gq_s[:, t * LANES : (t + 1) * LANES], t).T * HEAD_DIM ** (-0.5)
        glin[:, t * LANES : (t + 1) * LANES] = unrope(gq, cos, sa, sb).astype(BF16)
    if last:
        factors = attention.whole(r.zglin, slice(0, D))
        r.need("n1z1", "dout1")
        qswap = attention.swap(before, r.n1z1, r.all_glin, r.all_small, r.dout1, r.qv, r.ql)
        for h in range(2):
            r1[h].sum_into(t1[h])
        own_rest = Rest(st, t1, (r.l2c, r.l2d), (r.t2c, r.t2d), (r.g1c, r.g1d), (r.ha, r.hb), 0)
        rest.give(slice(2, 3))
        attention.fold(qswap, r.qv, r.ql, (r.qpa, r.qpb))
        few = Few(st, r, "")
    else:
        out_gradient()
        arrived(qkv_factor)
        r.flush("dout", "n1z")

    def take(k, total):
        sum_copy(k).wait_recv()
        return total + r.land_k[k].astype(F32)

    own = lax.fori_loop(1, n, take, own)
    glin[:, D : D + LANES] = unrope(own[:, :LANES], cos, sa, sb).astype(BF16)
    glin[:, D + LANES :] = own[:, LANES:].astype(BF16)
    if last:
        factors += attention.whole(r.zglin, slice(D, QKV))
        own_rest.advance()
        few.second_sum()
    else:
        r.flush("glin")
    gn1 = mm_nt(glin[...], r.gu[0, :, :QKV])
    x = r.x[...]
    r1_ = lax.rsqrt(jnp.mean(x * x, -1, keepdims=True) + EPS)
    unit = x * r1_
    dg1 = col_sum(gn1 * unit)
    dbias = col_sum(glin[...].astype(F32))
    gsmall = r.zsmall.at[st.block(st.z, 2 * UNIT), :] if last else r.gsmall
    gsmall[...] = jnp.zeros(gsmall.shape, F32)
    row = 0
    for part in (dg1, dg2, dbias):
        for t in range(part.shape[1] // LANES):
            gsmall[row : row + 1, :] = part[:, t * LANES : (t + 1) * LANES]
            row += 1
    if last:
        factors += attention.whole(r.zsmall)
        own_rest.advance()
        few.first_gather()
        rest.relay()
        rest.give(slice(3, 4))
    else:
        r.flush("gsmall")
    dz = gn1 * r.small[layer][:, :D]
    r.gx[...] = r.gm_s[...] + r1_ * (dz - unit * jnp.mean(dz * unit, -1, keepdims=True))
    if last:
        below = Delivery(st, 0, r.gx, r.input_grad)
        out = (r.qa, r.qb)
        out_gradient()
        arrived(qkv_factor)
        own_rest.advance()
        zswap = attention.swap(factors, r.n1z, r.zglin, r.zsmall, r.dout, r.zv, r.zl)
        attention.fold(zswap, r.zv, r.zl, (r.qp0a, r.qp0b))
        last_few = Few(st, r, "0")
        ends = few.hand_over(out, 1)
        rest.relay()
        own_rest.relay()
        last_few.second_sum()
        own_rest.give(slice(2, SIDE))
        for end in ends:
            end.relay()
        last_few.first_gather()
        own_rest.relay()
        final = last_few.hand_over(out, 0)
        rest.finish()
        for end in final:
            end.relay()
        for end in ends:
            end.finish()
        own_rest.finish()
        for end in final:
            end.finish()
        above.finish()
        below.finish()
    else:
        for h in range(2):
            r1[h].sum_into(t1[h])
    st.drain()

    def done(k, c):
        sum_copy(k).wait_send()
        return c

    lax.fori_loop(1, n, done, 0)
    r.close()


class Refs(types.SimpleNamespace):
    def load(self):
        for c in self.coming.values():
            c.start()

    def need(self, *names):
        for k in names:
            if k not in self.here:
                self.coming[k].wait()
                self.here.add(k)

    def flush(self, *names):
        for k in names:
            self.going[k].start()
            self.gone.add(k)

    def close(self):
        self.need(*self.coming)
        self.flush(*[k for k in self.going if k not in self.gone])
        for c in self.going.values():
            c.wait()


def call(kernel, layer, cid, name, ins, outs, scratch, sems, hbm=(), flops=10**10, picked=(), whole=(), scalars=()):
    staged = [k for k in ins if k not in hbm + whole + scalars]
    made = [k for k in outs if k not in hbm]
    dma = pltpu.SemaphoreType.DMA
    counts = dict(ssem=sems, rsem=sems, lsem=20, csem=16, csem2=16, psem=16, psem2=16, isem=len(staged), osem=len(made))
    if name == "forward":
        counts.update(csem1=16, csem21=16)
    places = [pltpu.VMEM(ins[k].shape[2 if k in picked else 0 :], ins[k].dtype) for k in staged] + [pltpu.VMEM(*outs[k]) for k in made]
    names = ["in_" + k for k in ins] + ["out_" + k for k in outs] + staged + made + list(scratch) + list(counts)

    def body(*refs):
        r = Refs(**dict(zip(names, refs)))
        for k in hbm + whole + scalars:
            if k in ins or k in outs:
                setattr(r, k, getattr(r, ("in_" if k in ins else "out_") + k))
        r.here, r.gone = set(), set()
        def source(k):
            ref = getattr(r, "in_" + k)
            return ref.at[lax.axis_index("section"), 0] if k in picked else ref

        r.coming = {k: pltpu.make_async_copy(source(k), getattr(r, k), r.isem.at[i]) for i, k in enumerate(staged)}
        r.going = {
            k: pltpu.make_async_copy(getattr(r, k), getattr(r, "out_" + k), r.osem.at[i]) for i, k in enumerate(made)
        }
        kernel(layer, r)

    anywhere = pl.BlockSpec(memory_space=pl.ANY)
    places_in = {k: pl.BlockSpec(memory_space=pltpu.VMEM) for k in whole}
    places_in.update({k: pl.BlockSpec(memory_space=pltpu.SMEM) for k in scalars})
    got = pl.pallas_call(
        body,
        out_shape=[jax.ShapeDtypeStruct(s, t) for s, t in outs.values()],
        in_specs=[places_in.get(k, anywhere) for k in ins],
        out_specs=[anywhere] * len(outs),
        scratch_shapes=places + [pltpu.VMEM(s, t) for s, t in scratch.values()] + [dma((k,)) for k in counts.values()],
        compiler_params=pltpu.CompilerParams(
            collective_id=cid, has_side_effects=True, vmem_limit_bytes=VMEM_LIMIT
        ),
        cost_estimate=pl.CostEstimate(flops=flops, bytes_accessed=20 * 2**20, transcendentals=0),
        name=name,
    )(*ins.values())
    return dict(zip(outs, got))


FAR = ("ga", "gb", "ha", "hb", "qa", "qb", "input_grad", "wa")
FA_ROWS = tuple((4 * g + d) * UNIT for g, d in zip(GATE_PER, DOWN_PER))
RQ = Q_ROWS // 2 // 16
SIDES = (SIDE, SIDE)
WIDE = HEADS * HEAD_DIM


def bf(*shape):
    return (shape, BF16)


def f4(*shape):
    return (shape, F32)


def rest_scratch():
    made = {}
    for h, rows in zip("ab", FA_ROWS):
        made["l2" + h] = bf(SIDE - 1, rows, LANES)
        made["t2" + h] = bf(rows, LANES)
        made["g1" + h] = bf(SIDE, rows, LANES)
    return made


def rest_outs():
    return {"g" + h: bf(2, *SIDES, rows, LANES) for h, rows in zip("ab", FA_ROWS)}


def assemble_kernel(nz, *refs):
    given, results, held, outs, sem, osem = (refs[:2], refs[2:4]), refs[6:14], refs[14:16] + refs[4:6], refs[16:24], refs[24], refs[25]
    s = lax.axis_index("section")
    copies = [pltpu.make_async_copy(a, b, osem.at[i]) for i, (a, b) in enumerate(zip(outs, results))]
    for layer in range(2):
        @pl.when(s == layer)
        def _():
            moving = [pltpu.make_async_copy(a, b, sem.at[i]) for i, (a, b) in enumerate(zip(given[layer], held))]
            for c in moving:
                c.start()
            for c in moving:
                c.wait()

    gate_ref, up_ref, down_ref, qkv_ref, out_ref = outs[:5]
    share = D // nz
    starts = window_starts(nz)

    def units(refs, section, base, per, first, count):
        rows = []
        for part, piece, slot, _, m in unit_runs(first, count, per):
            at = base[part] + slot * UNIT
            rows.append(refs[part][section, piece // SIDE, piece % SIDE, at : at + m * UNIT, :].astype(F32))
        return jnp.concatenate(rows, 0) if len(rows) > 1 else rows[0]

    for section, ref in ((0, gate_ref), (1, up_ref)):
        tiles = {}
        for w, a in enumerate(starts):
            for t in range(WIN // LANES):
                tiles.setdefault(a // LANES + t, []).append((w, t))
        for col, sources in tiles.items():
            total = None
            for w, t in sources:
                base = [w * per * UNIT for per in GATE_PER]
                got = units(held[:2], section, base, GATE_PER, t * (share // UNIT), share // UNIT)
                total = got if total is None else total + got
            ref[:, col * LANES : (col + 1) * LANES] = total
        copies[section].start()
    base = [nz * per * UNIT for per in GATE_PER]
    half = FF // nz // 2
    for section in range(2):
        for t in range(TILES):
            got = units(held[:2], section, base, DOWN_PER, t * (half // UNIT), half // UNIT)
            down_ref[section * half : (section + 1) * half, t * LANES : (t + 1) * LANES] = got
    copies[2].start()
    for t in range(QKV // LANES + TILES):
        got = units(held[2:], t // 8, (0, 0), Q_PER, (t % 8) * (share // UNIT), share // UNIT)
        if t < QKV // LANES:
            qkv_ref[:, t * LANES : (t + 1) * LANES] = got
        else:
            u = t - QKV // LANES
            out_ref[:, u * LANES : (u + 1) * LANES] = got
    small = units(held[2:], 0, (0, 0), Q_PER, 8 * (share // UNIT), 2)
    z = lax.axis_index("fsdp")
    row = 0
    for ref, size in zip(outs[5:], (D, D, QKV)):
        tiles = size // LANES
        line = jnp.concatenate([small[row + t : row + t + 1, :] for t in range(tiles)], 1)
        part = size // nz
        ref[...] = pltpu.roll(jnp.broadcast_to(line, (8, size)), lax.rem(size - z * part, size), 1)[:1, :part]
        row += tiles
    for c in copies[3:]:
        c.start()
    for c in copies:
        c.wait()


def assemble(zero, one, attn):
    nz = lax.axis_size("fsdp")
    vm = pl.BlockSpec(memory_space=pltpu.VMEM)
    anywhere = pl.BlockSpec(memory_space=pl.ANY)
    share = D // nz
    shapes = [(share, FF), (share, FF), (FF // nz, D), (share, QKV), (share, D), (1, share), (1, share), (1, QKV // nz)]
    return pl.pallas_call(
        functools.partial(assemble_kernel, nz),
        out_shape=[jax.ShapeDtypeStruct(a, F32) for a in shapes],
        in_specs=[anywhere] * 4 + [vm] * 2,
        out_specs=[anywhere] * len(shapes),
        scratch_shapes=[pltpu.VMEM(a.shape, a.dtype) for a in zero]
        + [pltpu.VMEM(a, F32) for a in shapes]
        + [pltpu.SemaphoreType.DMA((2,)), pltpu.SemaphoreType.DMA((len(shapes),))],
        compiler_params=pltpu.CompilerParams(vmem_limit_bytes=VMEM_LIMIT),
        name="assemble",
    )(*zero, *one, *attn)


def window_starts(n):
    share = FF // n
    return [(i * share // LANES) * LANES for i in range(n)]


def forward(tokens, cotangent, shards, gains, pair_of):
    n, nz = lax.axis_size("ctx"), lax.axis_size("fsdp")
    tok = tokens.shape[2]
    freq = np.arange(HEAD_DIM // 2, dtype=np.float64)
    inverse = jnp.asarray(np.tile(THETA ** (-2.0 * freq / HEAD_DIM), 4)[None, :].astype(np.float32))
    ins = dict(gains, pair=pair_of, inverse=inverse, x0=tokens, gy=cotangent)
    hbm = {k + "_shard": v for k, v in shards.items()}
    ins.update(hbm)
    outs = dict(
        small=f4(2, 1, SMALL), pairs=((n, 8, 2 * LANES), jnp.int32), cos=f4(tok, LANES), sa=f4(tok, LANES), sb=f4(tok, LANES),
        x1=f4(tok, D), gy_all=bf(nz * tok, D), layer_out=f4(2, tok, D),
    )
    scratch = dict(m_s=f4(2, WIDE), l_s=f4(2, WIDE), acc_s=f4(2 * LANES, WIDE), att_s=bf(tok, D), parts=f4(2, nz, 1, SMALL))
    for l in "01":
        each = dict(
            mid=f4(tok, D), n1t=bf(D, tok), qst=bf(2 * LANES, WIDE), kv=bf(n, tok, 2 * LANES), lse=f4(2, WIDE),
            attt=bf(D, tok), gu=bf(2, D, WIN), down=bf(WIN, D), wa=bf(D, QKV + D),
            all=bf(nz, tok, D), gate=bf(nz, tok, WIN), up=bf(nz, tok, WIN),
        )
        outs.update({k + l: v for k, v in each.items()})
        scratch.update({"y" + l: f4(tok, D), "send_s" + l: bf(nz, tok, D), "land_s" + l: bf(nz, tok, D)})
    return call(forward_kernel, 0, 1, "forward", ins, outs, scratch, 160, tuple(hbm) + ("layer_out",), picked=("x0", "gy"), whole=tuple(gains), scalars=("pair",))


def backward(layer, gy, f, before):
    n, nz = lax.axis_size("ctx"), lax.axis_size("fsdp")
    tok = gy.shape[-2]
    share = D // nz
    own = {k: f[k + str(layer)] for k in ("down", "gate", "up", "gu", "all", "mid", "attt", "n1t", "qst", "lse", "kv", "wa")}
    ins = dict(gy=gy)
    outs = {}
    factors = dict(n1z=bf(share, nz * tok), dout=bf(TILES * share, LANES))
    scratch = dict(
        hid_s=bf(nz * tok, WIN), g_s=bf(2, nz * tok, WIN), gm_s=f4(tok, D),
        own_s=f4(tok, D), send_s=bf(nz, tok, D), land_s=bf(nz, tok, D),
        delta_s=f4(2, WIDE), gq_s=f4(2 * LANES, WIDE), all_gm=bf(nz * tok, D), attz=bf(share, nz * tok),
        send_k=bf(n, tok, 2 * LANES), land_k=bf(n, tok, 2 * LANES),
    )
    for h, rows in zip("ab", FA_ROWS):
        scratch["f" + h] = bf(2, *SIDES, rows, LANES)
        scratch["sl" + h] = bf(*SIDES, rows, LANES)
        scratch["l1" + h] = bf(SIDE - 1, SIDE, rows, LANES)
    if layer == 0:
        scratch["gx"] = f4(tok, D)
        outs["input_grad"] = f4(2, tok, D)
        scratch["all_s"] = bf(nz * tok, D)
        ins.update(p1a=before["t1a"], p1b=before["t1b"])
        scratch.update(rest_scratch())
        outs.update(rest_outs())
    else:
        ins["all_s"] = f["gy_all"]
        outs["gx"] = f4(tok, D)
    ins.update(down=own["down"], gate=own["gate"], up=own["up"], gu=own["gu"], n2_all=own["all"], mid=own["mid"])
    ins["small"] = f["small"]
    ins.update({k: own[k] for k in ("attt", "n1t")})
    if layer == 0:
        ins.update(glin1=before["glin"], gsmall1=before["gsmall"], n1z1=before["n1z"], dout1=before["dout"])
        scratch.update(factors)
        scratch.update(all_glin=bf(nz * tok, QKV), all_small=f4(nz * 2 * UNIT, LANES), qv=bf(2, Q_ROWS, LANES), ql=bf(Q_ROWS, LANES))
        scratch.update(zglin=bf(nz * tok, QKV), zsmall=f4(nz * 2 * UNIT, LANES), zv=bf(2, Q_ROWS, LANES), zl=bf(Q_ROWS, LANES))
        scratch.update(t1a=bf(SIDE, FA_ROWS[0], LANES), t1b=bf(SIDE, FA_ROWS[1], LANES))
        for g, h, rows in zip("ab", "cd", FA_ROWS):
            scratch["l2" + h] = bf(SIDE - 1, rows, LANES)
            scratch["t2" + h] = bf(rows, LANES)
            scratch["g1" + h] = bf(SIDE, rows, LANES)
            outs["h" + g] = bf(2, *SIDES, rows, LANES)
            outs["q" + g] = bf(2, *SIDES, RQ, LANES)
            for tag in ("", "0"):
                scratch["qp" + tag + g] = bf(*SIDES, RQ, LANES)
                scratch["qm" + tag + g] = bf(SIDE - 1, SIDE, RQ, LANES)
                scratch["qw" + tag + g] = bf(SIDE - 1, RQ, LANES)
                scratch["qe" + tag + g] = bf(SIDE, RQ, LANES)
                scratch["qh" + tag + g] = bf(SIDE, RQ, LANES)
    else:
        outs.update(factors)
        outs.update(glin=bf(tok, QKV), gsmall=f4(2 * UNIT, LANES), t1a=bf(SIDE, FA_ROWS[0], LANES), t1b=bf(SIDE, FA_ROWS[1], LANES))
    ins.update({k: own[k] for k in ("qst", "lse", "kv", "wa")})
    ins.update({k: f[k] for k in ("pairs", "cos", "sa", "sb")})
    ins["x"] = f["x" + str(layer)] if layer else before["x0"]
    return call(backward_kernel, layer, 2 + layer, f"backward_{layer}", ins, outs, scratch, 256, FAR, 3 * 10**10, ("x",) if layer == 0 else ("gy",))


def local(
    tokens, cotangent, pair_of, attn_gain, ffn_gain, qkv_weight, qkv_bias, out_weight, gate_weight, up_weight, down_weight,
):
    shards = dict(qkv=qkv_weight, out=out_weight, gate=gate_weight, up=up_weight, down=down_weight)

    gains = dict(attn_gain=attn_gain, ffn_gain=ffn_gain, qkv_bias=qkv_bias)
    f = forward(tokens, cotangent, shards, gains, pair_of)
    c1 = backward(1, cotangent, f, None)
    c0 = backward(0, c1["gx"], f, dict(c1, x0=tokens))
    dgate, dup, ddown, dqkv, dout, dg1, dg2, dbias = assemble((c0["ha"], c0["hb"]), (c0["ga"], c0["gb"]), (c0["qa"], c0["qb"]))
    return (
        f["layer_out"][None, :, None],
        c0["input_grad"][None, :, None],
        dg1,
        dg2,
        dqkv[None],
        dbias,
        dout[None],
        dgate[None],
        dup[None],
        ddown[None],
    )


def solution(mesh):
    return jax.shard_map(
        local,
        mesh=mesh,
        in_specs=(
            P(None, "fsdp", "ctx", None),
            P(None, "fsdp", "ctx", None),
            P("ctx"),
            P("section", "fsdp"),
            P("section", "fsdp"),
            P("section", "fsdp", None),
            P("section", "fsdp"),
            P("section", "fsdp", None),
            P("section", "fsdp", None),
            P("section", "fsdp", None),
            P("section", "fsdp", None),
        ),
        out_specs=(
            P("section", None, "fsdp", "ctx", None),
            P("section", None, "fsdp", "ctx", None),
            P("section", "fsdp"),
            P("section", "fsdp"),
            P("section", "fsdp", None),
            P("section", "fsdp"),
            P("section", "fsdp", None),
            P("section", "fsdp", None),
            P("section", "fsdp", None),
            P("section", "fsdp", None),
        ),
        check_vma=False,
    )
```

```python
import functools
import types

import jax
import jax.numpy as jnp
import numpy as np
from jax import lax
from jax.experimental import pallas as pl
from jax.experimental.pallas import tpu as pltpu
from jax.sharding import PartitionSpec as P

D = 896
HEADS = 14
KV_HEADS = 2
HEAD_DIM = 64
GROUP = HEADS // KV_HEADS
FF = 4864
QKV = 1152
EPS = 1e-06
THETA = 1000000.0
LANES = 128
TILES = D // LANES
WIN = 1280
NEG = -1e30
F32 = jnp.float32
BF16 = jnp.bfloat16
MESH = pl.DeviceIdType.MESH
VMEM_LIMIT = 60 * 2**20
UNIT = 16
SIDE = 4
GATE_PER = (5, 4)
DOWN_PER = (8, 9)
Q_PER = (4, 4)
Q_ROWS = 16 * sum(Q_PER) * UNIT


def mm(a, b):
    return jnp.dot(a, b, preferred_element_type=F32)


def mm_nt(a, b):
    return lax.dot_general(a, b, (((1,), (1,)), ((), ())), preferred_element_type=F32)


def mm_tn(a, b):
    return lax.dot_general(a, b, (((0,), (0,)), ((), ())), preferred_element_type=F32)


ORDER = (1, 3, 2)
SMALL = 2 * D + QKV
AXES = (("x", "y"), ("y", "x"))
BATCH = 3
GROUPS = tuple(slice(a, min(a + 2 * LANES, HEADS * HEAD_DIM)) for a in range(0, HEADS * HEAD_DIM, 2 * LANES))


def push(src, dst, ssem, rsem, axis, to):
    return pltpu.make_async_remote_copy(
        src_ref=src,
        dst_ref=dst,
        send_sem=ssem,
        recv_sem=rsem,
        device_id={axis: to},
        device_id_type=MESH,
    )


def rope(u, cos, sa, sb):
    return u * cos + pltpu.roll(u, 96, 1) * sa + pltpu.roll(u, 32, 1) * sb


def unrope(u, cos, sa, sb):
    return u * cos - pltpu.roll(u, 96, 1) * sa - pltpu.roll(u, 32, 1) * sb


def halves(a0, a1):
    lane = lax.broadcasted_iota(jnp.int32, a0.shape, 1) < HEAD_DIM
    low = jnp.where(lane, a0, pltpu.roll(a1, HEAD_DIM, 1))
    high = jnp.where(lane, pltpu.roll(a0, HEAD_DIM, 1), a1)
    return low, high


def spread(ref, t, tile_t):
    half = HEAD_DIM
    zero = jnp.zeros((half, LANES), F32)
    cols = slice(t * LANES, (t + 1) * LANES)
    for g in range(KV_HEADS):
        pair = [tile_t[j * half : (j + 1) * half, :] if (2 * t + j) // GROUP == g else zero for j in range(2)]
        for part, content in enumerate(halves(*pair)):
            ref[part * LANES + g * half : part * LANES + (g + 1) * half, cols] = content.astype(BF16)


def gathered_tile(wide, t):
    half = HEAD_DIM
    rows = []
    for j in range(2):
        g = (2 * t + j) // GROUP
        low = wide[g * half : (g + 1) * half, :]
        high = wide[LANES + g * half : LANES + (g + 1) * half, :]
        rows.append(halves(low, high)[j])
    return jnp.concatenate(rows, 0)


def dealt(a_per, b_per):
    where = [(0, u // a_per, u % a_per) for u in range(16 * a_per)]
    return where + [(1, v // b_per, v % b_per) for v in range(16 * b_per)]


def unit_runs(first, count, per):
    where = dealt(*per)
    found = []
    for i in range(count):
        part, piece, slot = where[first + i]
        if found and found[-1][0] == part and found[-1][1] == piece:
            found[-1][4] += 1
        else:
            found.append([part, piece, slot, i, 1])
    return found


def put_units(refs, section, base, per, first, rows):
    for part, piece, slot, i, m in unit_runs(first, rows.shape[0] // UNIT, per):
        at = base[part] + slot * UNIT
        refs[part][section, piece // SIDE, piece % SIDE, at : at + m * UNIT, :] = rows[i * UNIT : (i + m) * UNIT, :]


class Stages:
    def __init__(self, r):
        self.s = lax.axis_index("section")
        self.c = lax.axis_index("ctx")
        self.nc = lax.axis_size("ctx")
        self.x, self.y = self.c // SIDE, lax.rem(self.c, SIDE)
        self.z = lax.axis_index("fsdp")
        self.nz = lax.axis_size("fsdp")
        self.ssem, self.rsem, self.lsem = r.ssem, r.rsem, r.lsem
        self.used = 0
        self.local_used = 0
        self.sent = []

    def along(self, axis, k):
        own, n = {
            "x": (self.x, SIDE),
            "y": (self.y, SIDE),
            "z": (self.z, self.nz),
            "c": (self.c, self.nc),
        }[axis]
        return lax.rem(own + n + k, n)

    def peer(self, axis, k, section=None):
        if axis == "s":
            return {"section": 1 - self.s}
        if axis == "z":
            to = {"fsdp": self.along("z", k)}
        elif axis == "c":
            to = {"ctx": self.along("c", k)}
        elif axis == "x":
            to = {"ctx": self.along("x", k) * SIDE + self.y}
        else:
            to = {"ctx": self.x * SIDE + self.along("y", k)}
        if section is not None:
            to["section"] = section
        return to

    def hail(self, ids, ring=False):
        bar = pltpu.get_barrier_semaphore()
        for i in ids:
            pl.semaphore_signal(bar, inc=1, device_id=i, device_id_type=MESH)
        self.expected = len(ids)
        if ring:
            def one(k, c):
                pl.semaphore_signal(bar, inc=1, device_id=self.peer("c", k), device_id_type=MESH)
                return c

            lax.fori_loop(1, self.nc, one, 0)
            self.expected += self.nc - 1
        self.bar = bar

    def met(self):
        pl.semaphore_wait(self.bar, self.expected)

    def beside(self):
        return [self.peer("s", 0)]

    def upright(self, both=False):
        ids = [self.peer("z", k) for k in range(1, self.nz)]
        return ids + ([self.peer("z", k, 1 - self.s) for k in range(1, self.nz)] if both else [])

    def flat(self, both=False):
        ids = [self.peer(a, k) for a in "xy" for k in range(1, SIDE)]
        return ids + ([self.peer(a, k, 1 - self.s) for a in "xy" for k in range(1, SIDE)] if both else [])

    def take(self, count):
        self.used += count
        return self.used - count

    def copy(self, src, dst, at, to, recv_at=None):
        return pltpu.make_async_remote_copy(
            src_ref=src,
            dst_ref=dst,
            send_sem=self.ssem.at[at],
            recv_sem=self.rsem.at[at if recv_at is None else recv_at],
            device_id=to,
            device_id_type=MESH,
        )

    def begin(self, copies):
        for c in copies:
            c.start()
        self.sent += copies
        return copies

    def drain(self):
        for c in self.sent:
            c.wait_send()

    def swap(self, src, land):
        return self.begin([self.copy(src.at[1 - self.s], land, self.take(1), self.peer("s", 0))])

    def scatter(self, axis, src, land):
        n = self.nz if axis == "z" else SIDE
        at = self.take(n - 1)
        return self.begin(
            [self.copy(src.at[self.along(axis, k)], land.at[k - 1], at + k - 1, self.peer(axis, k)) for k in range(1, n)]
        )

    def gather(self, axis, ref):
        at = self.take(SIDE - 1)
        mine = ref.at[self.along(axis, 0)]
        return self.begin([self.copy(mine, mine, at + k - 1, self.peer(axis, k)) for k in range(1, SIDE)])

    def deal(self, src, dst, rows):
        at = self.take(self.nz - 1)
        mine = dst.at[self.block(self.z, rows), :]
        return self.begin(
            [
                self.copy(src.at[self.block(self.along("z", k), rows), :], mine, at + k - 1, self.peer("z", k))
                for k in range(1, self.nz)
            ]
        )

    def block(self, i, rows):
        return pl.ds(pl.multiple_of(i * rows, UNIT), rows)

    def aside(self, j):
        x = lax.rem(self.x + (1 - self.s) * j, SIDE)
        y = lax.rem(self.y + self.s * j, SIDE)
        return {"ctx": x * SIDE + y}

    def quarter(self):
        return self.x * (1 - self.s) + self.y * self.s

    def hand_over(self, axis, src, dst, layer, part=None):
        return Handover(self, axis, src, dst, layer, part)


class Handover:
    def __init__(self, st, axis, src, dst, layer, part=None):
        self.st, self.axis, self.layer = st, axis, layer
        self.at = st.take(2 * SIDE)
        mine = dst.at[st.s, st.along(axis, 0)]
        if part is not None:
            src, mine = src.at[part], mine.at[part]
        self.src, self.mine, self.dst, self.part = src, mine, dst, part
        st.begin(
            [st.copy(src, mine, self.at + k, st.peer(axis, k, layer), self.at + st.s * SIDE + k) for k in (1, SIDE - 1)]
        )
        self.beside = st.copy(src, mine, self.at, {"section": layer}, self.at + st.s * SIDE)
        self.within = pltpu.make_async_copy(src, mine, st.lsem.at[st.local_used])
        st.local_used += 1
        pl.when(st.s != layer)(self.beside.start)
        pl.when(st.s == layer)(self.within.start)

    def arrival(self, half, k):
        return self.st.copy(self.src, self.mine, self.at, {"section": self.layer}, self.at + half * SIDE + k)

    def passing(self, half):
        st = self.st
        way = 1 - 2 * half
        p = self.dst.at[half, st.along(self.axis, -way)]
        if self.part is not None:
            p = p.at[self.part]
        at = self.at + half * SIDE + 2
        return st.copy(p, p, at, st.peer(self.axis, way), at)

    def relay(self):
        @pl.when(self.st.s == self.layer)
        def _():
            for half, k in ((0, 1), (1, SIDE - 1)):
                self.arrival(half, k).wait_recv()
                self.passing(half).start()

    def finish(self):
        @pl.when(self.st.s == self.layer)
        def _():
            self.within.wait()
            for half, k in ((0, SIDE - 1), (1, 1), (0, 2), (1, 2), (1 - self.layer, 0)):
                self.arrival(half, k).wait_recv()
            for half in range(2):
                self.passing(half).wait_send()

        pl.when(self.st.s != self.layer)(self.beside.wait_send)


class Scatter:
    def __init__(self, st, axis, src, land):
        self.st, self.axis, self.src, self.land = st, axis, src, land
        self.at = st.take(6)
        low, high = slice(0, SIDE // 2), slice(SIDE // 2, SIDE)
        far = src.at[st.along(axis, 2)]
        self.through = [
            self.send(far.at[low], land.at[2, low], 0, 1),
            self.send(far.at[high], land.at[2, high], 1, -1),
        ]
        self.straight = [
            self.send(src.at[st.along(axis, 1), high], land.at[0, high], 2, 1),
            self.send(src.at[st.along(axis, -1), low], land.at[1, low], 3, -1),
        ]
        st.begin(self.through + self.straight)

    def send(self, src, dst, i, way):
        return self.st.copy(src, dst, self.at + i, self.st.peer(self.axis, way))

    def pass_on(self):
        st = self.st
        low, high = slice(0, SIDE // 2), slice(SIDE // 2, SIDE)
        self.late = []
        for i, (part, way) in enumerate(((low, 1), (high, -1))):
            self.through[i].wait_recv()
            mine = self.src.at[st.along(self.axis, way), part]
            add_into(mine, [mine, self.land.at[2, part]])
            self.late.append(self.send(mine, self.land.at[i, part], 4 + i, way))
        st.begin(self.late)

    def sum_into(self, out):
        arrived(self.straight + self.late)
        add_into(out, [self.src.at[self.st.along(self.axis, 0)], self.land.at[0], self.land.at[1]])


class Feed:
    def __init__(self, st, layer, sources, piece, band):
        self.st, self.layer, self.sources, self.piece, self.band = st, layer, sources, piece, band
        steps = st.nz - 1
        self.across = st.take(2 * steps)
        self.sideways = st.take((SIDE - 1) * steps)
        self.passed = st.take(steps)
        self.own = st.take(2)

    def beside(self, h):
        b = self.band(self.st.z, h)
        return self.st.copy(b, b, self.own + h, self.st.peer("s", 0))

    def send(self, h, k, src):
        st = self.st
        dst = self.piece(st.z, h, (st.x, st.y)[h])
        return st.copy(dst if src is None else src, dst, self.across + 2 * (k - 1) + h, st.peer("z", k, h))

    def start_beside(self):
        @pl.when(self.st.s == self.layer)
        def _():
            for h in range(2):
                self.beside(h).start()

    def start(self):
        st = self.st

        @pl.when(st.s == self.layer)
        def _():
            for k in ORDER:
                for h in range(2):
                    for needed, src in self.sources(h, (st.x, st.y)[h], st.along("z", k)):
                        if needed is None:
                            self.send(h, k, src).start()
                        else:
                            pl.when(needed)(self.send(h, k, src).start)

    def relay(self, k):
        st = self.st
        p = self.piece(st.along("z", -k), st.s, st.quarter())
        st.copy(p, p, self.across + 2 * (k - 1) + st.s, st.peer("s", 0)).wait_recv()
        at = self.sideways + (SIDE - 1) * (k - 1) - 1
        st.begin([st.copy(p, p, at + j, st.aside(j)) for j in range(1, SIDE)])

    def collect(self, k):
        st = self.st
        z = st.along("z", -k)
        at = self.sideways + (SIDE - 1) * (k - 1) - 1
        for j in range(1, SIDE):
            p = self.piece(z, st.s, lax.rem(st.quarter() + SIDE - j, SIDE))
            st.copy(p, p, at + j, st.aside(j)).wait_recv()
        b = self.band(z, st.s)
        st.begin([st.copy(b, b, self.passed + k - 1, st.peer("s", 0))])

    def finish(self):
        st = self.st
        for k in ORDER:
            b = self.band(st.along("z", -k), 1 - st.s)
            st.copy(b, b, self.passed + k - 1, st.peer("s", 0)).wait_recv()

        @pl.when(st.s == self.layer)
        def _():
            for h in range(2):
                for k in ORDER:
                    self.send(h, k, None).wait_send()
                self.beside(h).wait_send()

        @pl.when(st.s != self.layer)
        def _():
            for h in range(2):
                self.beside(h).wait_recv()


class FeedDown:
    def __init__(self, st, layer, src, dst):
        self.st, self.layer = st, layer
        share = src.shape[1]
        spare = WIN - share
        odd = lax.rem(st.z, 2)
        place = dst.at[pl.ds(pl.multiple_of(odd * spare, UNIT), share), :]
        dst[pl.ds(pl.multiple_of((1 - odd) * share, UNIT), spare), :] = jnp.zeros((spare, D), BF16)
        self.local = pltpu.make_async_copy(src.at[0], place, st.lsem.at[st.local_used])
        st.local_used += 1
        self.remote = st.copy(src.at[0], place, st.take(1), st.peer("s", 0))

    def start(self):
        @pl.when(self.st.s == self.layer)
        def _():
            self.local.start()
            self.remote.start()

    def finish(self):
        @pl.when(self.st.s == self.layer)
        def _():
            self.local.wait()
            self.remote.wait_send()

        @pl.when(self.st.s != self.layer)
        def _():
            self.remote.wait_recv()


class Delivery:
    def __init__(self, st, layer, src, out):
        self.st, self.layer = st, layer
        mine = out.at[st.s]
        self.within = pltpu.make_async_copy(src, mine, st.lsem.at[st.local_used])
        st.local_used += 1
        self.over = st.copy(src, mine, st.take(1), st.peer("s", 0))
        pl.when(st.s == layer)(self.within.start)
        pl.when(st.s != layer)(self.over.start)

    def finish(self):
        @pl.when(self.st.s == self.layer)
        def _():
            self.within.wait()
            self.over.wait_recv()

        pl.when(self.st.s != self.layer)(self.over.wait_send)


class Local:
    def __init__(self, st, layer, pairs):
        self.st, self.layer = st, layer
        self.copies = [pltpu.make_async_copy(a, b, st.lsem.at[st.local_used + i]) for i, (a, b) in enumerate(pairs)]
        st.local_used += len(pairs)

        @pl.when(st.s == layer)
        def _():
            for c in self.copies:
                c.start()

    def wait(self):
        @pl.when(self.st.s == self.layer)
        def _():
            for c in self.copies:
                c.wait()


def half_rows(z, h, share):
    return pl.ds(pl.multiple_of(z * share + h * (share // 2), UNIT), share // 2)


def feed_attention(st, layer, qkv, out, dst):
    share = qkv.shape[1]
    rows = st.block(st.z, share)
    local = Local(st, layer, [(qkv.at[0], dst.at[rows, :QKV]), (out.at[0], dst.at[rows, QKV:])])
    whole = QKV + D
    split = whole // 4 * 3

    def feed(low, high):
        width = (high - low) // SIDE

        def piece(z, h, q):
            return dst.at[half_rows(z, h, share), pl.ds(pl.multiple_of(low + q * width, LANES), width)]

        def band(z, h):
            return dst.at[half_rows(z, h, share), low:high]

        return Feed(st, layer, lambda h, q, z_to: [(None, None)], piece, band)

    return local, feed(0, split), feed(split, whole)


def feed_windows(st, layer, gate, up, dst):
    share = gate.shape[1]
    pace = FF // st.nz // (LANES // 2)
    width = WIN // 2

    def window(z):
        return pl.multiple_of(z * pace // 2 * LANES, LANES)

    rows = st.block(st.z, share)
    local = Local(st, layer, [(w.at[0, :, pl.ds(window(st.z), WIN)], dst.at[i, rows, :]) for i, w in enumerate((gate, up))])

    def sources(h, q, z_to):
        at = pl.multiple_of(window(z_to) + lax.rem(q, 2) * width, LANES)
        part = slice(h * (share // 2), (h + 1) * (share // 2))
        return [(q < 2, gate.at[0, part, pl.ds(at, width)]), (q >= 2, up.at[0, part, pl.ds(at, width)])]

    def piece(z, h, q):
        return dst.at[q // 2, half_rows(z, h, share), pl.ds(pl.multiple_of(lax.rem(q, 2) * width, LANES), width)]

    def band(z, h):
        return dst.at[:, half_rows(z, h, share), :]

    return local, Feed(st, layer, sources, piece, band)


class Ring:
    def __init__(self, st, place, rows):
        self.st, self.place, self.rows = st, place, rows
        self.at = st.take(4)
        mine = place(st.z, 0, rows)
        self.near = st.begin([self.send(mine, i, way) for i, way in enumerate((1, -1))])

    def send(self, ref, i, way):
        return self.st.copy(ref, ref, self.at + i, self.st.peer("z", way))

    def pass_on(self):
        st, half = self.st, self.rows // 2
        arrived(self.near)
        self.far = st.begin(
            [
                self.send(self.place(st.along("z", -1), 0, half), 2, 1),
                self.send(self.place(st.along("z", 1), half, half), 3, -1),
            ]
        )

    def finish(self):
        arrived(self.far)


def arrived(copies):
    for c in copies:
        c.wait_recv()


def add_into(dst, parts):
    def one(i, c):
        total = parts[0][i].astype(F32)
        for p in parts[1:]:
            total = total + p[i].astype(F32)
        dst[i] = total.astype(dst.dtype)
        return c

    lax.fori_loop(0, dst.shape[0], one, 0)


def add_rows(dst, parts):
    total = parts[0][...].astype(F32)
    for p in parts[1:]:
        total = total + p[...].astype(F32)
    dst[...] = total.astype(dst.dtype)


def swapped_sum(st, copies, given, land):
    arrived(copies)
    for i in range(SIDE):
        add_into(land.at[i], [given.at[st.s, i], land.at[i]])


def sides(tile, chosen):
    half = HEAD_DIM
    low, high = tile[:half], tile[half:]
    zero = jnp.zeros_like(low)
    below = jnp.concatenate([jnp.where(chosen, low, zero), jnp.where(chosen, zero, high)], 1)
    return jnp.concatenate([jnp.concatenate([zero, low], 1), below], 0).astype(BF16)


def sides_t(tile_t, chosen):
    lane = lax.broadcasted_iota(jnp.int32, tile_t.shape, 1) < HEAD_DIM
    upper = jnp.where(jnp.logical_or(lane, jnp.logical_not(chosen)), 0.0, pltpu.roll(tile_t, HEAD_DIM, 1))
    lower = jnp.where(jnp.logical_or(lane, jnp.logical_not(chosen)), tile_t, 0.0)
    return jnp.concatenate([upper, lower], 0).astype(BF16)


def own_sides(tile):
    low, high = tile[:HEAD_DIM], tile[HEAD_DIM:]
    zero = jnp.zeros_like(low)
    rows = [[zero, low], [low, zero], [zero, high]]
    return jnp.concatenate([jnp.concatenate(p, 1) for p in rows], 0).astype(BF16)


def own_bias(width):
    key = lax.broadcasted_iota(jnp.int32, (HEAD_DIM, width), 0)
    query = lax.rem(lax.broadcasted_iota(jnp.int32, (HEAD_DIM, width), 1), HEAD_DIM)
    return jnp.where(key <= query, 0.0, NEG)


def earlier(pairs_ref, src, me, width):
    return pairs_ref[src, 0:1, :width] < pairs_ref[me, 0:1, :width]


def col_max(a):
    return jnp.max(a, 0, keepdims=True)


def col_sum(a):
    return jnp.sum(a, 0, keepdims=True)


class View:
    def __init__(self, r, layer):
        self.r, self.layer = r, layer

    def named(self, k):
        own = k + str(self.layer)
        return own if hasattr(self.r, own) else k

    def __getattr__(self, k):
        return getattr(self.r, self.named(k))

    def need(self, *names):
        self.r.need(*[self.named(k) for k in names])

    def flush(self, *names):
        self.r.flush(*[self.named(k) for k in names])


def forward_kernel(_, r):
    st = Stages(r)
    n, me = st.nc, st.c
    st.hail(st.beside() + st.upright(True), ring=True)
    r.load()
    wa, gu, down = [None, None], [None, None], [None, None]
    for l in range(2):
        v = View(r, l)
        wa[l] = feed_attention(st, l, r.qkv_shard, r.out_shard, v.wa)
        gu[l] = feed_windows(st, l, r.gate_shard, r.up_shard, v.gu)
        down[l] = FeedDown(st, l, r.down_shard, v.down)
    r.need("inverse", "x0")
    r.pairs[me] = jnp.full(r.pairs.shape[1:], r.pair[0], jnp.int32)
    at = 0
    for part, size in ((r.attn_gain, D), (r.ffn_gain, D), (r.qkv_bias, QKV)):
        share = part.shape[1]
        line = jnp.concatenate([part[...].astype(F32), jnp.zeros((1, size - share), F32)], 1)
        line = pltpu.roll(jnp.broadcast_to(line, (8, size)), st.z * share, 1)
        r.parts[st.s, st.z, :, at : at + size] = line[:1]
        at += size
    wa[0][0].wait()
    st.met()
    wa[0][1].start()
    wa[0][1].start_beside()
    at = st.take(2 * st.nz)
    mine = r.parts.at[st.s, st.z]
    st.begin(
        [st.copy(mine, mine, at + k, st.peer("z", k, st.s), at + st.s * st.nz + k) for k in range(1, st.nz)]
        + [st.copy(mine, mine, at + st.nz + k, st.peer("z", k, 1 - st.s), at + st.s * st.nz + k) for k in range(1, st.nz)]
        + [st.copy(mine, mine, at, st.peer("s", 0), at + st.s * st.nz)]
    )

    def tell(k, c):
        p = r.pairs.at[me]
        push(p, p, r.psem.at[k], r.psem2.at[k], "ctx", lax.rem(me + k, n)).start()
        return c

    lax.fori_loop(1, n, tell, 0)
    block = LANES // 2
    i = lax.broadcasted_iota(jnp.int32, (LANES, LANES), 0)
    pair = r.pairs[me, 0:1, :LANES]
    pos = jnp.where(i < block, pair * block + i, (2 * n - 1 - pair) * block + i - block)
    angle = pos.astype(F32) * r.inverse[...]
    lane = lax.rem(lax.broadcasted_iota(jnp.int32, (LANES, LANES), 1), HEAD_DIM)
    sine = jnp.sin(angle)
    r.cos[...] = jnp.cos(angle)
    r.sa[...] = jnp.where(lane < HEAD_DIM // 2, -sine, 0.0)
    r.sb[...] = jnp.where(lane < HEAD_DIM // 2, 0.0, sine)
    r.flush("cos", "sa", "sb")
    for h in (st.s, 1 - st.s):
        for k in range(st.nz):
            if h is st.s and k == 0:
                continue
            st.copy(mine, mine, at, st.peer("s", 0), at + h * st.nz + k).wait_recv()
    for h in range(2):
        total = r.parts[h, 0]
        for k in range(1, st.nz):
            total = total + r.parts[h, k]
        r.small[h] = total
    r.flush("small")
    for k in ORDER:
        wa[0][1].relay(k)
    wa[0][2].start()
    gu[0][0].wait()
    gu[0][1].start()
    for k in ORDER:
        wa[0][1].collect(k)
    wa[0][2].start_beside()
    gu[0][1].start_beside()
    down[0].start()

    def begin_next():
        wa[1][0].wait()
        gu[1][0].wait()
        for feed in (wa[1][1], wa[1][2], gu[1][1]):
            feed.start()
            feed.start_beside()
        down[1].start()

    def relays(*steps):
        def go():
            for feed, name, k in steps:
                getattr(feed, name)(k)

        return go

    g0, w0, w1, w2, g1 = gu[0][1], wa[0][2], wa[1][1], wa[1][2], gu[1][1]
    wa[0][1].finish()
    v = View(r, 0)

    def out_ready():
        g0.collect(2)
        w0.finish()
        v.flush("wa")

    attention_forward(
        st, v, 0,
        (
            relays((w0, "relay", 1), (w0, "relay", 3), (w0, "relay", 2), (g0, "relay", 1), (g0, "relay", 3)),
            relays((g0, "relay", 2), (w0, "collect", 1), (w0, "collect", 3), (w0, "collect", 2)),
            begin_next,
            relays((g0, "collect", 1), (g0, "collect", 3)),
            out_ready,
        ),
    )

    def ready_0():
        g0.finish()
        down[0].finish()
        v.flush("gu", "down")

    ffn_forward(
        st, v, ready_0,
        (
            relays((w1, "relay", 1), (w1, "relay", 3)),
            relays((w1, "relay", 2), (w2, "relay", 1), (w2, "relay", 3), (w2, "relay", 2), (g1, "relay", 1)),
            relays((g1, "relay", 3), (g1, "relay", 2), (w1, "collect", 1), (w1, "collect", 3)),
            relays(
                (w1, "collect", 2), (w2, "collect", 1), (w2, "collect", 3), (w2, "collect", 2),
                (g1, "collect", 1), (g1, "collect", 3), (g1, "collect", 2),
            ),
        ),
    )
    r.x1[...] = r.y0[...].astype(BF16).astype(F32)
    r.flush("x1")
    done_0 = Delivery(st, 0, r.y0, r.layer_out)
    r.need("gy")
    tok = r.gy.shape[0]
    rows = st.block(st.z, tok)
    r.gy_all[rows, :] = r.gy[...].astype(BF16)
    at = st.take(st.nz - 1)
    mine_gy = r.gy_all.at[rows, :]
    gy_moving = st.begin([st.copy(mine_gy, mine_gy, at + k - 1, st.peer("z", k)) for k in range(1, st.nz)])
    w1.finish()
    w2.finish()
    v = View(r, 1)
    v.flush("wa")
    nothing = lambda: None
    attention_forward(st, v, 1, (nothing,) * 5)

    def ready_1():
        g1.finish()
        down[1].finish()
        v.flush("gu", "down")

    ffn_forward(st, v, ready_1, (nothing,) * 4)
    done_1 = Delivery(st, 1, r.y1, r.layer_out)
    arrived(gy_moving)
    r.flush("gy_all")
    done_0.finish()
    done_1.finish()
    st.drain()

    def done(k, c):
        p = r.pairs.at[me]
        push(p, p, r.psem.at[k], r.psem2.at[k], "ctx", lax.rem(me + k, n)).wait_send()
        return c

    lax.fori_loop(1, n, done, 0)
    r.close()


def attention_forward(st, r, layer, between):
    n, me = st.nc, st.c
    x = r.x[...]
    r1 = lax.rsqrt(jnp.mean(x * x, -1, keepdims=True) + EPS)
    small = r.small[layer]
    n1_f = x * r1 * small[:, :D]
    n1 = n1_f.astype(BF16)
    bias = small[:, 2 * D :]
    cos, sa, sb = r.cos[...], r.sa[...], r.sb[...]
    lin = mm(n1, r.wa[:, D:QKV]) + bias[:, D:]
    r.kv[me] = jnp.concatenate([rope(lin[:, :LANES], cos, sa, sb), lin[:, LANES:]], 1).astype(BF16)

    def keys_copy(k, src):
        return push(r.kv.at[src], r.kv.at[src], r.csem.at[k], r.csem2.at[k], "ctx", lax.rem(me + k, n))

    def start(k, c):
        keys_copy(k, me).start()
        return c

    lax.fori_loop(1, n, start, 0)
    linq = mm(n1, r.wa[:, :D]) + bias[:, :D]
    for t in range(TILES):
        tile = slice(t * LANES, (t + 1) * LANES)
        q = rope(linq[:, tile], cos, sa, sb) * HEAD_DIM ** (-0.5)
        spread(r.qst, t, q.T)
        r.n1t[tile, :] = n1_f[:, tile].T.astype(BF16)
    r.flush("qst", "n1t")
    between[0]()
    half = HEAD_DIM
    own_k = own_sides(r.kv[me, :, :LANES].astype(F32))
    own_vt = own_sides(r.kv[me, :, LANES:].astype(F32)).astype(F32).T.astype(BF16)
    for cols in GROUPS:
        width = cols.stop - cols.start
        bias = own_bias(width)
        sc = mm(own_k, r.qst[:, cols])
        s_a, s_l, s_h = sc[:half], sc[half : 2 * half] + bias, sc[2 * half :] + bias
        m_lo = col_max(s_l)
        m_hi = jnp.maximum(col_max(s_a), col_max(s_h))
        p_a, p_l, p_h = jnp.exp(s_a - m_hi), jnp.exp(s_l - m_lo), jnp.exp(s_h - m_hi)
        r.m_s[0:1, cols], r.m_s[1:2, cols] = m_lo, m_hi
        r.l_s[0:1, cols], r.l_s[1:2, cols] = col_sum(p_l), col_sum(p_a) + col_sum(p_h)
        r.acc_s[:, cols] = mm(own_vt, jnp.concatenate([p_a, p_l, p_h], 0).astype(BF16))

    def step(i, c):
        kx, vt, sel = [], [], []
        for j in range(BATCH):
            k = i * BATCH + 1 + j
            src = lax.rem(me + n - k, n)
            keys_copy(k, src).wait_recv()
            if layer == 0:
                p = r.pairs.at[src]
                push(p, p, r.psem.at[k], r.psem2.at[k], "ctx", lax.rem(me + k, n)).wait_recv()
            sel.append(src)
            chosen = earlier(r.pairs, src, me, LANES)
            kx.append(sides(r.kv[src, :, :LANES].astype(F32), chosen))
            vt.append(sides_t(r.kv[src, :, LANES:].astype(F32).T, chosen))
        kx = jnp.concatenate(kx, 0)
        vt = jnp.concatenate(vt, 1)
        for cols in GROUPS:
            width = cols.stop - cols.start
            sc = mm(kx, r.qst[:, cols])
            m_lo, m_hi = r.m_s[0:1, cols], r.m_s[1:2, cols]
            n_lo, n_hi = m_lo, m_hi
            chosen = [earlier(r.pairs, src, me, width) for src in sel]
            for j in range(BATCH):
                top = col_max(sc[(2 * j + 1) * half : (2 * j + 2) * half])
                n_hi = jnp.maximum(n_hi, col_max(sc[2 * j * half : (2 * j + 1) * half]))
                n_hi = jnp.where(chosen[j], n_hi, jnp.maximum(n_hi, top))
                n_lo = jnp.where(chosen[j], jnp.maximum(n_lo, top), n_lo)
            a_lo, a_hi = jnp.exp(m_lo - n_lo), jnp.exp(m_hi - n_hi)
            l_lo, l_hi = r.l_s[0:1, cols] * a_lo, r.l_s[1:2, cols] * a_hi
            ps = []
            for j in range(BATCH):
                p_a = jnp.exp(sc[2 * j * half : (2 * j + 1) * half] - n_hi)
                p_s = jnp.exp(sc[(2 * j + 1) * half : (2 * j + 2) * half] - jnp.where(chosen[j], n_lo, n_hi))
                total = col_sum(p_s)
                l_hi = l_hi + col_sum(p_a) + jnp.where(chosen[j], 0.0, total)
                l_lo = l_lo + jnp.where(chosen[j], total, 0.0)
                ps += [p_a.astype(BF16), p_s.astype(BF16)]
            r.m_s[0:1, cols], r.m_s[1:2, cols] = n_lo, n_hi
            r.l_s[0:1, cols], r.l_s[1:2, cols] = l_lo, l_hi
            new = mm(vt, jnp.concatenate(ps, 0))
            r.acc_s[:LANES, cols] = r.acc_s[:LANES, cols] * a_lo + new[:LANES]
            r.acc_s[LANES:, cols] = r.acc_s[LANES:, cols] * a_hi + new[LANES:]
        return c

    lax.fori_loop(0, 1, step, 0)
    between[1]()
    lax.fori_loop(1, 2, step, 0)
    between[2]()
    lax.fori_loop(2, 4, step, 0)
    between[3]()
    lax.fori_loop(4, (n - 1) // BATCH, step, 0)
    between[4]()
    r.flush("kv")
    if layer == 0:
        r.flush("pairs")
    r.lse[...] = r.m_s[...] + jnp.log(r.l_s[...])
    for t in range(TILES):
        cols = slice(t * LANES, (t + 1) * LANES)
        wide = jnp.concatenate([r.acc_s[:LANES, cols] / r.l_s[0:1, cols], r.acc_s[LANES:, cols] / r.l_s[1:2, cols]], 0)
        tile_t = gathered_tile(wide, t)
        r.attt[cols, :] = tile_t.astype(BF16)
        r.att_s[:, cols] = tile_t.T.astype(BF16)
    r.flush("lse", "attt")
    mid = x + mm(r.att_s[...], r.wa[:, QKV:])
    r.mid[...] = mid
    r2 = lax.rsqrt(jnp.mean(mid * mid, -1, keepdims=True) + EPS)
    r.all[st.z] = (mid * r2 * small[:, D : 2 * D]).astype(BF16)
    r.flush("mid")

    def done(k, c):
        keys_copy(k, me).wait_send()
        return c

    lax.fori_loop(1, n, done, 0)


def ffn_forward(st, r, ready, between):
    n, me = st.nz, st.z
    tok = r.mid.shape[0]
    at = st.take(n)

    def second(k):
        return st.copy(r.send_s.at[k], r.land_s.at[k], at + k, st.peer("z", -k))

    ring = Ring(st, lambda z, row, rows: r.all.at[z, row : row + rows, :], tok)
    ready()

    def block(sources):
        a = jnp.concatenate([r.all[i] for i in sources], 0) if len(sources) > 1 else r.all[sources[0]]
        gate = mm(a, r.gu[0])
        up = mm(a, r.gu[1])
        for j, i in enumerate(sources):
            r.gate[i] = gate[j * tok : (j + 1) * tok].astype(BF16)
            r.up[i] = up[j * tok : (j + 1) * tok].astype(BF16)
        hidden = (gate * jax.nn.sigmoid(gate) * up).astype(BF16)
        return mm(hidden, r.down[...])

    r.y[...] = r.mid[...] + block([me])
    between[0]()
    ring.pass_on()
    both = block([st.along("z", -1), st.along("z", -3)]).astype(BF16)
    for i, k in enumerate((1, 3)):
        r.send_s[k] = both[i * tok : (i + 1) * tok]
        second(k).start()
    between[1]()
    ring.finish()
    r.send_s[2] = block([st.along("z", -2)]).astype(BF16)
    second(2).start()
    between[2]()
    r.flush("all", "gate", "up")
    between[3]()
    for k in ORDER:
        second(k).wait_recv()
        r.y[...] += r.land_s[k].astype(F32)
    for k in ORDER:
        second(k).wait_send()


class Attention:
    def __init__(self, st):
        self.st = st

    def columns(self, src, dst):
        st = self.st
        share = dst.shape[0]
        at = st.take(st.nz - 1)
        mine = dst.at[:, pl.ds(pl.multiple_of(st.z * LANES, LANES), LANES)]
        moving = st.begin(
            [
                st.copy(src.at[st.block(st.along("z", k), share), :], mine, at + k - 1, st.peer("z", k))
                for k in range(1, st.nz)
            ]
        )
        mine[...] = src[st.block(st.z, share), :]
        return moving

    def whole(self, dst, cols=slice(None)):
        st = self.st
        rows = dst.shape[0] // st.nz
        at = st.take(st.nz - 1)
        mine = dst.at[pl.ds(pl.multiple_of(st.z * rows, UNIT), rows), cols]
        return st.begin([st.copy(mine, mine, at + k - 1, st.peer("z", k)) for k in range(1, st.nz)])

    def begin(self, glin, small, all_glin, all_small):
        st = self.st
        tok = glin.shape[0]
        all_glin[st.block(st.z, tok), :] = glin[...]
        all_small[st.block(st.z, 2 * UNIT), :] = small[...]
        return self.whole(all_glin) + self.whole(all_small)

    def swap(self, moving, n1z, all_glin, all_small, dout, made, land):
        st = self.st
        arrived(moving)
        share = n1z.shape[0]
        per = 8
        for j in range(0, QKV // LANES, 2):
            cols = slice(j * LANES, min(j + 2, QKV // LANES) * LANES)
            d = mm(n1z[...], all_glin[:, cols]).astype(BF16)
            for t in range(j, min(j + 2, QKV // LANES)):
                made[t // per, (t % per) * share : (t % per + 1) * share, :] = d[:, (t - j) * LANES : (t - j + 1) * LANES]
        made[1, share : 8 * share, :] = dout[...]
        small = jnp.zeros((2 * UNIT, LANES), F32)
        for i in range(st.nz):
            small = small + all_small[i * 2 * UNIT : (i + 1) * 2 * UNIT, :]
        made[0, 8 * share : 8 * share + 2 * UNIT, :] = small.astype(BF16)
        made[0, 8 * share + 2 * UNIT :, :] = jnp.zeros((Q_ROWS - 8 * share - 2 * UNIT, LANES), BF16)
        made[1, 8 * share :, :] = jnp.zeros((Q_ROWS - 8 * share, LANES), BF16)
        return st.swap(made, land)

    def fold(self, moving, made, land, out):
        st = self.st
        arrived(moving)
        rows = Q_ROWS // 2 // 16
        for h in range(2):
            for i in range(16):
                at = slice((h * 16 + i) * rows, (h * 16 + i + 1) * rows)
                total = made[st.s, at, :].astype(F32) + land[at, :].astype(F32)
                out[h][i // SIDE, i % SIDE] = total.astype(BF16)


class Rest:
    def __init__(self, st, t1, l2, t2, g1, out, layer):
        self.st, self.t1, self.l2, self.t2, self.g1, self.out, self.layer = st, t1, l2, t2, g1, out, layer
        self.stage = 0
        self.moving = [st.scatter(AXES[h][1], t1[h], l2[h]) for h in range(2)]

    def advance(self):
        st = self.st
        for h in range(2):
            second = AXES[h][1]
            arrived(self.moving[h])
            mine = self.g1[h].at[st.along(second, 0)]
            if self.stage == 0:
                t2 = self.t2[h]
                add_rows(t2, [self.t1[h].at[st.along(second, 0)]] + [self.l2[h].at[k] for k in range(SIDE - 1)])
                per = GATE_PER[h] * UNIT
                self.moving[h] = st.deal(t2, mine, per)
                mine[st.block(st.z, per), :] = t2[st.block(st.z, per), :]
                mine[st.nz * per :, :] = t2[st.nz * per :, :]
            elif self.stage == 1:
                self.moving[h] = st.gather(second, self.g1[h])
        if self.stage == 2:
            self.ends = []
            self.open = []
            self.give(slice(0, SIDE // 2))
        self.stage += 1

    def give(self, part):
        made = [self.st.hand_over(AXES[h][0], self.g1[h], self.out[h], self.layer, part) for h in range(2)]
        self.ends += made
        self.open += made

    def relay(self):
        for one in self.open:
            one.relay()
        self.open = []

    def finish(self):
        for one in self.ends:
            one.finish()


class Few:
    def __init__(self, st, r, tag):
        self.st = st

        def both(name):
            return tuple(getattr(r, name + tag + h) for h in "ab")

        self.qp, self.land, self.part, self.land2, self.wide = both("qp"), both("qm"), both("qe"), both("qw"), both("qh")
        self.moving = [st.scatter(AXES[h][0], self.qp[h], self.land[h]) for h in range(2)]

    def second_sum(self):
        st = self.st
        for h in range(2):
            arrived(self.moving[h])
            own = self.qp[h].at[st.along(AXES[h][0], 0)]
            add_into(self.part[h], [own] + [self.land[h].at[k] for k in range(SIDE - 1)])
            self.moving[h] = st.scatter(AXES[h][1], self.part[h], self.land2[h])

    def first_gather(self):
        st = self.st
        for h in range(2):
            arrived(self.moving[h])
            i = st.along(AXES[h][1], 0)
            add_rows(self.wide[h].at[i], [self.part[h].at[i]] + [self.land2[h].at[k] for k in range(SIDE - 1)])
            self.moving[h] = st.gather(AXES[h][1], self.wide[h])

    def hand_over(self, out, layer):
        for h in range(2):
            arrived(self.moving[h])
        return [self.st.hand_over(AXES[h][0], self.wide[h], out[h], layer) for h in range(2)]


def backward_kernel(layer, r):
    st = Stages(r)
    n, me = st.nz, st.z
    carry = layer == 0
    ids = st.upright() + st.beside()
    if carry:
        ids += [st.peer(a, k, 1 - st.s) for a in "xy" for k in range(1, SIDE)]
    st.hail(ids, ring=True)
    r.load()
    tok = r.gy.shape[0]

    def rows_of(i):
        return pl.ds(pl.multiple_of(i * tok, tok), tok)

    r.need("gy")
    gyb = r.gy[...].astype(BF16)
    gy = gyb.astype(F32) if carry else r.gy[...]
    above = None
    if carry:
        r.all_s[rows_of(me), :] = gyb
    else:
        r.need("all_s")
    st.met()
    at = st.take(2 * n)

    def second(k):
        return st.copy(r.send_s.at[k], r.land_s.at[k], at + n + k, st.peer("z", -k))

    if carry:
        ring = Ring(st, lambda z, row, rows: r.all_s.at[pl.ds(pl.multiple_of(z * tok + row, UNIT), rows), :], tok)
        above = Delivery(st, 1, r.gy, r.input_grad)
        r.need("p1a", "p1b")
        rest = Rest(st, (r.p1a, r.p1b), (r.l2a, r.l2b), (r.t2a, r.t2b), (r.g1a, r.g1b), (r.ga, r.gb), 1)
    r.need("down", "gate", "up", "gu")

    def block(sources):
        def stacked(ref):
            parts = [ref[rows_of(i), :] for i in sources]
            return jnp.concatenate(parts, 0) if len(parts) > 1 else parts[0]

        def picked(ref):
            parts = [ref[i].astype(F32) for i in sources]
            return jnp.concatenate(parts, 0) if len(parts) > 1 else parts[0]

        def keep(ref, value):
            for j, i in enumerate(sources):
                ref[rows_of(i), :] = value[j * tok : (j + 1) * tok]

        gh = mm_nt(stacked(r.all_s), r.down[...])
        gate, up = picked(r.gate), picked(r.up)
        sg = jax.nn.sigmoid(gate)
        act = gate * sg
        keep(r.hid_s, (act * up).astype(BF16))
        ggate = (gh * up * sg * (1.0 + gate * (1.0 - sg))).astype(BF16)
        gup = (gh * act).astype(BF16)
        keep(r.g_s.at[0], ggate)
        keep(r.g_s.at[1], gup)
        return mm_nt(ggate, r.gu[0]) + mm_nt(gup, r.gu[1])

    r.own_s[...] = block([me])
    if carry:
        rest.advance()
        ring.pass_on()
    both = block([st.along("z", -1), st.along("z", -3)]).astype(BF16)
    for i, k in enumerate((1, 3)):
        r.send_s[k] = both[i * tok : (i + 1) * tok]
        second(k).start()
    if carry:
        rest.advance()
        ring.finish()
    r.send_s[2] = block([st.along("z", -2)]).astype(BF16)
    second(2).start()
    attention = Attention(st)
    before = None
    if carry:
        r.need("glin1", "gsmall1")
        before = attention.begin(r.glin1, r.gsmall1, r.all_glin, r.all_small)
        rest.advance()

    late = [
        pltpu.make_async_copy(r.wa.at[:, :QKV], r.gu.at[0, :, :QKV], st.lsem.at[st.local_used]),
        pltpu.make_async_copy(r.wa.at[:, QKV:], r.gu.at[1, :, :D], st.lsem.at[st.local_used + 1]),
    ]
    st.local_used += 2
    for c in late:
        c.start()
    refs = (r.fa, r.fb)
    share = D // n
    for j in range(WIN // (2 * LANES)):
        cols = slice(2 * j * LANES, 2 * (j + 1) * LANES)
        r.down[cols, :] = mm_tn(r.hid_s[:, cols], r.all_s[...]).astype(BF16)
    pad = (WIN - FF // n) * lax.rem(me, 2)
    half = FF // n // 2
    base = [n * per * UNIT for per in GATE_PER]
    for section in range(2):
        rows = r.down[pl.ds(pl.multiple_of(pad + section * half, UNIT), half), :]
        for t in range(TILES):
            put_units(refs, section, base, DOWN_PER, t * (half // UNIT), rows[:, t * LANES : (t + 1) * LANES])
        used = TILES * (half // UNIT)
        extra = 16 * sum(DOWN_PER) - used
        put_units(refs, section, base, DOWN_PER, used, jnp.zeros((extra * UNIT, LANES), BF16))
    r.need("n2_all")
    normed = jnp.concatenate([r.n2_all[i] for i in range(n)], 0)

    def product(section):
        for j in range(WIN // (2 * LANES)):
            d = mm_tn(normed, r.g_s[section, :, 2 * j * LANES : 2 * (j + 1) * LANES]).astype(BF16)
            for t in (2 * j, 2 * j + 1):
                tile = d[:, (t % 2) * LANES : (t % 2 + 1) * LANES]
                for i in range(n):
                    base = [i * per * UNIT for per in GATE_PER]
                    put_units(refs, section, base, GATE_PER, t * (share // UNIT), tile[i * share : (i + 1) * share, :])
        used = WIN // LANES * (share // UNIT)
        extra = 16 * sum(GATE_PER) - used
        for i in range(n):
            base = [i * per * UNIT for per in GATE_PER]
            put_units(refs, section, base, GATE_PER, used, jnp.zeros((extra * UNIT, LANES), BF16))

    product(1 - st.s)
    swaps = [st.swap(refs[h], (r.sla, r.slb)[h]) for h in range(2)]
    product(st.s)
    for k in ORDER:
        second(k).wait_recv()
        r.own_s[...] += r.land_s[k].astype(F32)
    gn2 = r.own_s[...]
    r.need("mid", "small")
    mid = r.mid[...]
    r2 = lax.rsqrt(jnp.mean(mid * mid, -1, keepdims=True) + EPS)
    unit = mid * r2
    dg2 = col_sum(gn2 * unit)
    dz = gn2 * r.small[layer][:, D : 2 * D]
    gm = gy + r2 * (dz - unit * jnp.mean(dz * unit, -1, keepdims=True))
    r.gm_s[...] = gm
    for k in ORDER:
        second(k).wait_send()
    attention_backward(st, r, layer, gm, dg2, refs, swaps, rest if carry else None, above, late, attention, before)


def attention_backward(st, r, layer, gm, dg2, refs, swaps, rest, above, late, attention, before):
    n, me = st.nc, st.c
    last = layer == 0
    half = HEAD_DIM
    gmb = gm.astype(BF16)
    tok = gm.shape[0]
    r.all_gm[st.block(st.z, tok), :] = gmb
    sl, l1, t1 = (r.sla, r.slb), (r.l1a, r.l1b), (r.t1a, r.t1b)
    r.need("attt", "n1t")
    size = 2 * BATCH * half
    pr, ds, gst = r.g_s.at[0, :size, :WIDE], r.g_s.at[1, :size, :WIDE], r.hid_s.at[: 2 * LANES, :WIDE]
    out_factors = attention.whole(r.all_gm) + attention.columns(r.attt, r.attz)
    qkv_factor = attention.columns(r.n1t, r.n1z)
    r1 = []
    for h in range(2):
        swapped_sum(st, swaps[h], refs[h], sl[h])
        r1.append(Scatter(st, AXES[h][0], sl[h], l1[h]))
    r.need("qst", "lse", "kv", "pairs")
    for c in late:
        c.wait()
    ga = mm_nt(gmb, r.gu[1, :, :D])
    for t in range(TILES):
        tile = slice(t * LANES, (t + 1) * LANES)
        ga_t = ga[:, tile].T
        spread(gst, t, ga_t)
        prod = ga_t * r.attt[tile, :].astype(F32)
        low, high = halves(col_sum(prod[:half]), col_sum(prod[half:]))
        r.delta_s[0:1, tile], r.delta_s[1:2, tile] = low, high

    def own_block():
        keys, vals = r.kv[me, :, :LANES].astype(F32), r.kv[me, :, LANES:].astype(F32)
        kx, vx = own_sides(keys), own_sides(vals)
        kt = kx.astype(F32).T.astype(BF16)
        rows = slice(0, 3 * half)
        for cols in GROUPS:
            bias = own_bias(cols.stop - cols.start)
            sc = mm(kx, r.qst[:, cols])
            dp = mm(vx, gst[:, cols])
            lo, hi = (r.lse[0:1, cols], r.delta_s[0:1, cols]), (r.lse[1:2, cols], r.delta_s[1:2, cols])
            parts = [(sc[:half], hi), (sc[half : 2 * half] + bias, lo), (sc[2 * half :] + bias, hi)]
            for i, (part, (lse, delta)) in enumerate(parts):
                p = jnp.exp(part - lse)
                at = slice(i * half, (i + 1) * half)
                pr[at, cols] = p.astype(BF16)
                ds[at, cols] = (p * (dp[at] - delta)).astype(BF16)
            r.gq_s[:, cols] = mm(kt, ds[rows, cols])
        made = []
        for w, q in ((ds, r.qst), (pr, gst)):
            e = mm_nt(w[rows, :], q[...])
            low = e[:half, LANES:] + e[half : 2 * half, :LANES]
            made.append(jnp.concatenate([low, e[2 * half :, LANES:]], 0))
        return jnp.concatenate(made, 1)

    def sum_copy(k):
        return push(r.send_k.at[k], r.land_k.at[k], r.csem.at[k], r.csem2.at[k], "ctx", lax.rem(me + k, n))

    def step(i):
        kx, vx, kt, sel = [], [], [], []
        for j in range(BATCH):
            src = lax.rem(me + i * BATCH + 1 + j, n)
            sel.append(src)
            chosen = earlier(r.pairs, src, me, LANES)
            keys = r.kv[src, :, :LANES].astype(F32)
            kx.append(sides(keys, chosen))
            vx.append(sides(r.kv[src, :, LANES:].astype(F32), chosen))
            kt.append(sides_t(keys.T, chosen))
        kx, vx, kt = jnp.concatenate(kx, 0), jnp.concatenate(vx, 0), jnp.concatenate(kt, 1)
        rows = slice(0, 2 * BATCH * half)
        for cols in GROUPS:
            width = cols.stop - cols.start
            sc = mm(kx, r.qst[:, cols])
            dp = mm(vx, gst[:, cols])
            for j in range(BATCH):
                chosen = earlier(r.pairs, sel[j], me, width)
                for part in range(2):
                    lse, delta = r.lse[1:2, cols], r.delta_s[1:2, cols]
                    if part:
                        lse = jnp.where(chosen, r.lse[0:1, cols], lse)
                        delta = jnp.where(chosen, r.delta_s[0:1, cols], delta)
                    at = slice((2 * j + part) * half, (2 * j + part + 1) * half)
                    p = jnp.exp(sc[at] - lse)
                    pr[at, cols] = p.astype(BF16)
                    ds[at, cols] = (p * (dp[at] - delta)).astype(BF16)
            r.gq_s[:, cols] += mm(kt, ds[rows, cols])
        ek = mm_nt(ds[rows, :], r.qst[...])
        ev = mm_nt(pr[rows, :], gst[...])
        for j in range(BATCH):
            chosen = earlier(r.pairs, sel[j], me, LANES)
            k = i * BATCH + 1 + j
            for e, lanes in ((ek, slice(0, LANES)), (ev, slice(LANES, 2 * LANES))):
                top = e[2 * j * half : (2 * j + 1) * half]
                low = e[(2 * j + 1) * half : (2 * j + 2) * half]
                r.send_k[k, :half, lanes] = (top[:, LANES:] + jnp.where(chosen, low[:, :LANES], 0.0)).astype(BF16)
                r.send_k[k, half:, lanes] = jnp.where(chosen, 0.0, low[:, LANES:]).astype(BF16)
            sum_copy(k).start()

    own = own_block()
    for i in range((n - 1) // BATCH):
        step(i)
        if i == 0:
            for one in r1:
                one.pass_on()
        if i == 1 and last:
            rest.relay()

    def out_gradient():
        arrived(out_factors)
        share = D // st.nz
        for j in range(0, TILES, 2):
            cols = slice(j * LANES, min(j + 2, TILES) * LANES)
            d = mm(r.attz[...], r.all_gm[:, cols]).astype(BF16)
            for t in range(j, min(j + 2, TILES)):
                r.dout[t * share : (t + 1) * share, :] = d[:, (t - j) * LANES : (t - j + 1) * LANES]

    glin = r.zglin.at[st.block(st.z, tok), :] if last else r.glin
    r.need("cos", "sa", "sb", "x", "small")
    cos, sa, sb = r.cos[...], r.sa[...], r.sb[...]
    for t in range(TILES):
        gq = gathered_tile(r.gq_s[:, t * LANES : (t + 1) * LANES], t).T * HEAD_DIM ** (-0.5)
        glin[:, t * LANES : (t + 1) * LANES] = unrope(gq, cos, sa, sb).astype(BF16)
    if last:
        factors = attention.whole(r.zglin, slice(0, D))
        r.need("n1z1", "dout1")
        qswap = attention.swap(before, r.n1z1, r.all_glin, r.all_small, r.dout1, r.qv, r.ql)
        for h in range(2):
            r1[h].sum_into(t1[h])
        own_rest = Rest(st, t1, (r.l2c, r.l2d), (r.t2c, r.t2d), (r.g1c, r.g1d), (r.ha, r.hb), 0)
        rest.give(slice(2, 3))
        attention.fold(qswap, r.qv, r.ql, (r.qpa, r.qpb))
        few = Few(st, r, "")
    else:
        out_gradient()
        arrived(qkv_factor)
        r.flush("dout", "n1z")

    def take(k, total):
        sum_copy(k).wait_recv()
        return total + r.land_k[k].astype(F32)

    own = lax.fori_loop(1, n, take, own)
    glin[:, D : D + LANES] = unrope(own[:, :LANES], cos, sa, sb).astype(BF16)
    glin[:, D + LANES :] = own[:, LANES:].astype(BF16)
    if last:
        factors += attention.whole(r.zglin, slice(D, QKV))
        own_rest.advance()
        few.second_sum()
    else:
        r.flush("glin")
    gn1 = mm_nt(glin[...], r.gu[0, :, :QKV])
    x = r.x[...]
    r1_ = lax.rsqrt(jnp.mean(x * x, -1, keepdims=True) + EPS)
    unit = x * r1_
    dg1 = col_sum(gn1 * unit)
    dbias = col_sum(glin[...].astype(F32))
    gsmall = r.zsmall.at[st.block(st.z, 2 * UNIT), :] if last else r.gsmall
    gsmall[...] = jnp.zeros(gsmall.shape, F32)
    row = 0
    for part in (dg1, dg2, dbias):
        for t in range(part.shape[1] // LANES):
            gsmall[row : row + 1, :] = part[:, t * LANES : (t + 1) * LANES]
            row += 1
    if last:
        factors += attention.whole(r.zsmall)
        own_rest.advance()
        few.first_gather()
        rest.relay()
        rest.give(slice(3, 4))
    else:
        r.flush("gsmall")
    dz = gn1 * r.small[layer][:, :D]
    r.gx[...] = r.gm_s[...] + r1_ * (dz - unit * jnp.mean(dz * unit, -1, keepdims=True))
    if last:
        below = Delivery(st, 0, r.gx, r.input_grad)
        out = (r.qa, r.qb)
        out_gradient()
        arrived(qkv_factor)
        own_rest.advance()
        zswap = attention.swap(factors, r.n1z, r.zglin, r.zsmall, r.dout, r.zv, r.zl)
        attention.fold(zswap, r.zv, r.zl, (r.qp0a, r.qp0b))
        last_few = Few(st, r, "0")
        ends = few.hand_over(out, 1)
        rest.relay()
        own_rest.relay()
        last_few.second_sum()
        own_rest.give(slice(2, SIDE))
        for end in ends:
            end.relay()
        last_few.first_gather()
        own_rest.relay()
        final = last_few.hand_over(out, 0)
        rest.finish()
        for end in final:
            end.relay()
        for end in ends:
            end.finish()
        own_rest.finish()
        for end in final:
            end.finish()
        above.finish()
        below.finish()
    else:
        for h in range(2):
            r1[h].sum_into(t1[h])
    st.drain()

    def done(k, c):
        sum_copy(k).wait_send()
        return c

    lax.fori_loop(1, n, done, 0)
    r.close()


class Refs(types.SimpleNamespace):
    def load(self):
        for c in self.coming.values():
            c.start()

    def need(self, *names):
        for k in names:
            if k not in self.here:
                self.coming[k].wait()
                self.here.add(k)

    def flush(self, *names):
        for k in names:
            self.going[k].start()
            self.gone.add(k)

    def close(self):
        self.need(*self.coming)
        self.flush(*[k for k in self.going if k not in self.gone])
        for c in self.going.values():
            c.wait()


def call(kernel, layer, cid, name, ins, outs, scratch, sems, hbm=(), flops=10**10, picked=(), whole=(), scalars=()):
    staged = [k for k in ins if k not in hbm + whole + scalars]
    made = [k for k in outs if k not in hbm]
    dma = pltpu.SemaphoreType.DMA
    counts = dict(ssem=sems, rsem=sems, lsem=20, csem=16, csem2=16, psem=16, psem2=16, isem=len(staged), osem=len(made))
    if name == "forward":
        counts.update(csem1=16, csem21=16)
    places = [pltpu.VMEM(ins[k].shape[2 if k in picked else 0 :], ins[k].dtype) for k in staged] + [pltpu.VMEM(*outs[k]) for k in made]
    names = ["in_" + k for k in ins] + ["out_" + k for k in outs] + staged + made + list(scratch) + list(counts)

    def body(*refs):
        r = Refs(**dict(zip(names, refs)))
        for k in hbm + whole + scalars:
            if k in ins or k in outs:
                setattr(r, k, getattr(r, ("in_" if k in ins else "out_") + k))
        r.here, r.gone = set(), set()
        def source(k):
            ref = getattr(r, "in_" + k)
            return ref.at[lax.axis_index("section"), 0] if k in picked else ref

        r.coming = {k: pltpu.make_async_copy(source(k), getattr(r, k), r.isem.at[i]) for i, k in enumerate(staged)}
        r.going = {
            k: pltpu.make_async_copy(getattr(r, k), getattr(r, "out_" + k), r.osem.at[i]) for i, k in enumerate(made)
        }
        kernel(layer, r)

    anywhere = pl.BlockSpec(memory_space=pl.ANY)
    places_in = {k: pl.BlockSpec(memory_space=pltpu.VMEM) for k in whole}
    places_in.update({k: pl.BlockSpec(memory_space=pltpu.SMEM) for k in scalars})
    got = pl.pallas_call(
        body,
        out_shape=[jax.ShapeDtypeStruct(s, t) for s, t in outs.values()],
        in_specs=[places_in.get(k, anywhere) for k in ins],
        out_specs=[anywhere] * len(outs),
        scratch_shapes=places + [pltpu.VMEM(s, t) for s, t in scratch.values()] + [dma((k,)) for k in counts.values()],
        compiler_params=pltpu.CompilerParams(
            collective_id=cid, has_side_effects=True, vmem_limit_bytes=VMEM_LIMIT
        ),
        cost_estimate=pl.CostEstimate(flops=flops, bytes_accessed=20 * 2**20, transcendentals=0),
        name=name,
    )(*ins.values())
    return dict(zip(outs, got))


FAR = ("ga", "gb", "ha", "hb", "qa", "qb", "input_grad", "wa")
FA_ROWS = tuple((4 * g + d) * UNIT for g, d in zip(GATE_PER, DOWN_PER))
RQ = Q_ROWS // 2 // 16
SIDES = (SIDE, SIDE)
WIDE = HEADS * HEAD_DIM


def bf(*shape):
    return (shape, BF16)


def f4(*shape):
    return (shape, F32)


def rest_scratch():
    made = {}
    for h, rows in zip("ab", FA_ROWS):
        made["l2" + h] = bf(SIDE - 1, rows, LANES)
        made["t2" + h] = bf(rows, LANES)
        made["g1" + h] = bf(SIDE, rows, LANES)
    return made


def rest_outs():
    return {"g" + h: bf(2, *SIDES, rows, LANES) for h, rows in zip("ab", FA_ROWS)}


def assemble_kernel(nz, *refs):
    given, results, held, outs, sem, osem = (refs[:2], refs[2:4]), refs[6:14], refs[14:16] + refs[4:6], refs[16:24], refs[24], refs[25]
    s = lax.axis_index("section")
    copies = [pltpu.make_async_copy(a, b, osem.at[i]) for i, (a, b) in enumerate(zip(outs, results))]
    for layer in range(2):
        @pl.when(s == layer)
        def _():
            moving = [pltpu.make_async_copy(a, b, sem.at[i]) for i, (a, b) in enumerate(zip(given[layer], held))]
            for c in moving:
                c.start()
            for c in moving:
                c.wait()

    gate_ref, up_ref, down_ref, qkv_ref, out_ref = outs[:5]
    share = D // nz
    starts = window_starts(nz)

    def units(refs, section, base, per, first, count):
        rows = []
        for part, piece, slot, _, m in unit_runs(first, count, per):
            at = base[part] + slot * UNIT
            rows.append(refs[part][section, piece // SIDE, piece % SIDE, at : at + m * UNIT, :].astype(F32))
        return jnp.concatenate(rows, 0) if len(rows) > 1 else rows[0]

    for section, ref in ((0, gate_ref), (1, up_ref)):
        tiles = {}
        for w, a in enumerate(starts):
            for t in range(WIN // LANES):
                tiles.setdefault(a // LANES + t, []).append((w, t))
        for col, sources in tiles.items():
            total = None
            for w, t in sources:
                base = [w * per * UNIT for per in GATE_PER]
                got = units(held[:2], section, base, GATE_PER, t * (share // UNIT), share // UNIT)
                total = got if total is None else total + got
            ref[:, col * LANES : (col + 1) * LANES] = total
        copies[section].start()
    base = [nz * per * UNIT for per in GATE_PER]
    half = FF // nz // 2
    for section in range(2):
        for t in range(TILES):
            got = units(held[:2], section, base, DOWN_PER, t * (half // UNIT), half // UNIT)
            down_ref[section * half : (section + 1) * half, t * LANES : (t + 1) * LANES] = got
    copies[2].start()
    for t in range(QKV // LANES + TILES):
        got = units(held[2:], t // 8, (0, 0), Q_PER, (t % 8) * (share // UNIT), share // UNIT)
        if t < QKV // LANES:
            qkv_ref[:, t * LANES : (t + 1) * LANES] = got
        else:
            u = t - QKV // LANES
            out_ref[:, u * LANES : (u + 1) * LANES] = got
    small = units(held[2:], 0, (0, 0), Q_PER, 8 * (share // UNIT), 2)
    z = lax.axis_index("fsdp")
    row = 0
    for ref, size in zip(outs[5:], (D, D, QKV)):
        tiles = size // LANES
        line = jnp.concatenate([small[row + t : row + t + 1, :] for t in range(tiles)], 1)
        part = size // nz
        ref[...] = pltpu.roll(jnp.broadcast_to(line, (8, size)), lax.rem(size - z * part, size), 1)[:1, :part]
        row += tiles
    for c in copies[3:]:
        c.start()
    for c in copies:
        c.wait()


def assemble(zero, one, attn):
    nz = lax.axis_size("fsdp")
    vm = pl.BlockSpec(memory_space=pltpu.VMEM)
    anywhere = pl.BlockSpec(memory_space=pl.ANY)
    share = D // nz
    shapes = [(share, FF), (share, FF), (FF // nz, D), (share, QKV), (share, D), (1, share), (1, share), (1, QKV // nz)]
    return pl.pallas_call(
        functools.partial(assemble_kernel, nz),
        out_shape=[jax.ShapeDtypeStruct(a, F32) for a in shapes],
        in_specs=[anywhere] * 4 + [vm] * 2,
        out_specs=[anywhere] * len(shapes),
        scratch_shapes=[pltpu.VMEM(a.shape, a.dtype) for a in zero]
        + [pltpu.VMEM(a, F32) for a in shapes]
        + [pltpu.SemaphoreType.DMA((2,)), pltpu.SemaphoreType.DMA((len(shapes),))],
        compiler_params=pltpu.CompilerParams(vmem_limit_bytes=VMEM_LIMIT),
        name="assemble",
    )(*zero, *one, *attn)


def window_starts(n):
    share = FF // n
    return [(i * share // LANES) * LANES for i in range(n)]


def forward(tokens, cotangent, shards, gains, pair_of):
    n, nz = lax.axis_size("ctx"), lax.axis_size("fsdp")
    tok = tokens.shape[2]
    freq = np.arange(HEAD_DIM // 2, dtype=np.float64)
    inverse = jnp.asarray(np.tile(THETA ** (-2.0 * freq / HEAD_DIM), 4)[None, :].astype(np.float32))
    ins = dict(gains, pair=pair_of, inverse=inverse, x0=tokens, gy=cotangent)
    hbm = {k + "_shard": v for k, v in shards.items()}
    ins.update(hbm)
    outs = dict(
        small=f4(2, 1, SMALL), pairs=((n, 8, 2 * LANES), jnp.int32), cos=f4(tok, LANES), sa=f4(tok, LANES), sb=f4(tok, LANES),
        x1=f4(tok, D), gy_all=bf(nz * tok, D), layer_out=f4(2, tok, D),
    )
    scratch = dict(m_s=f4(2, WIDE), l_s=f4(2, WIDE), acc_s=f4(2 * LANES, WIDE), att_s=bf(tok, D), parts=f4(2, nz, 1, SMALL))
    for l in "01":
        each = dict(
            mid=f4(tok, D), n1t=bf(D, tok), qst=bf(2 * LANES, WIDE), kv=bf(n, tok, 2 * LANES), lse=f4(2, WIDE),
            attt=bf(D, tok), gu=bf(2, D, WIN), down=bf(WIN, D), wa=bf(D, QKV + D),
            all=bf(nz, tok, D), gate=bf(nz, tok, WIN), up=bf(nz, tok, WIN),
        )
        outs.update({k + l: v for k, v in each.items()})
        scratch.update({"y" + l: f4(tok, D), "send_s" + l: bf(nz, tok, D), "land_s" + l: bf(nz, tok, D)})
    return call(forward_kernel, 0, 1, "forward", ins, outs, scratch, 200, tuple(hbm) + ("layer_out",), picked=("x0", "gy"), whole=tuple(gains), scalars=("pair",))


def backward(layer, gy, f, before):
    n, nz = lax.axis_size("ctx"), lax.axis_size("fsdp")
    tok = gy.shape[-2]
    share = D // nz
    own = {k: f[k + str(layer)] for k in ("down", "gate", "up", "gu", "all", "mid", "attt", "n1t", "qst", "lse", "kv", "wa")}
    ins = dict(gy=gy)
    outs = {}
    factors = dict(n1z=bf(share, nz * tok), dout=bf(TILES * share, LANES))
    scratch = dict(
        hid_s=bf(nz * tok, WIN), g_s=bf(2, nz * tok, WIN), gm_s=f4(tok, D),
        own_s=f4(tok, D), send_s=bf(nz, tok, D), land_s=bf(nz, tok, D),
        delta_s=f4(2, WIDE), gq_s=f4(2 * LANES, WIDE), all_gm=bf(nz * tok, D), attz=bf(share, nz * tok),
        send_k=bf(n, tok, 2 * LANES), land_k=bf(n, tok, 2 * LANES),
    )
    for h, rows in zip("ab", FA_ROWS):
        scratch["f" + h] = bf(2, *SIDES, rows, LANES)
        scratch["sl" + h] = bf(*SIDES, rows, LANES)
        scratch["l1" + h] = bf(SIDE - 1, SIDE, rows, LANES)
    if layer == 0:
        scratch["gx"] = f4(tok, D)
        outs["input_grad"] = f4(2, tok, D)
        scratch["all_s"] = bf(nz * tok, D)
        ins.update(p1a=before["t1a"], p1b=before["t1b"])
        scratch.update(rest_scratch())
        outs.update(rest_outs())
    else:
        ins["all_s"] = f["gy_all"]
        outs["gx"] = f4(tok, D)
    ins.update(down=own["down"], gate=own["gate"], up=own["up"], gu=own["gu"], n2_all=own["all"], mid=own["mid"])
    ins["small"] = f["small"]
    ins.update({k: own[k] for k in ("attt", "n1t")})
    if layer == 0:
        ins.update(glin1=before["glin"], gsmall1=before["gsmall"], n1z1=before["n1z"], dout1=before["dout"])
        scratch.update(factors)
        scratch.update(all_glin=bf(nz * tok, QKV), all_small=f4(nz * 2 * UNIT, LANES), qv=bf(2, Q_ROWS, LANES), ql=bf(Q_ROWS, LANES))
        scratch.update(zglin=bf(nz * tok, QKV), zsmall=f4(nz * 2 * UNIT, LANES), zv=bf(2, Q_ROWS, LANES), zl=bf(Q_ROWS, LANES))
        scratch.update(t1a=bf(SIDE, FA_ROWS[0], LANES), t1b=bf(SIDE, FA_ROWS[1], LANES))
        for g, h, rows in zip("ab", "cd", FA_ROWS):
            scratch["l2" + h] = bf(SIDE - 1, rows, LANES)
            scratch["t2" + h] = bf(rows, LANES)
            scratch["g1" + h] = bf(SIDE, rows, LANES)
            outs["h" + g] = bf(2, *SIDES, rows, LANES)
            outs["q" + g] = bf(2, *SIDES, RQ, LANES)
            for tag in ("", "0"):
                scratch["qp" + tag + g] = bf(*SIDES, RQ, LANES)
                scratch["qm" + tag + g] = bf(SIDE - 1, SIDE, RQ, LANES)
                scratch["qw" + tag + g] = bf(SIDE - 1, RQ, LANES)
                scratch["qe" + tag + g] = bf(SIDE, RQ, LANES)
                scratch["qh" + tag + g] = bf(SIDE, RQ, LANES)
    else:
        outs.update(factors)
        outs.update(glin=bf(tok, QKV), gsmall=f4(2 * UNIT, LANES), t1a=bf(SIDE, FA_ROWS[0], LANES), t1b=bf(SIDE, FA_ROWS[1], LANES))
    ins.update({k: own[k] for k in ("qst", "lse", "kv", "wa")})
    ins.update({k: f[k] for k in ("pairs", "cos", "sa", "sb")})
    ins["x"] = f["x" + str(layer)] if layer else before["x0"]
    return call(backward_kernel, layer, 2 + layer, f"backward_{layer}", ins, outs, scratch, 256, FAR, 3 * 10**10, ("x",) if layer == 0 else ("gy",))


def local(
    tokens, cotangent, pair_of, attn_gain, ffn_gain, qkv_weight, qkv_bias, out_weight, gate_weight, up_weight, down_weight,
):
    shards = dict(qkv=qkv_weight, out=out_weight, gate=gate_weight, up=up_weight, down=down_weight)

    gains = dict(attn_gain=attn_gain, ffn_gain=ffn_gain, qkv_bias=qkv_bias)
    f = forward(tokens, cotangent, shards, gains, pair_of)
    c1 = backward(1, cotangent, f, None)
    c0 = backward(0, c1["gx"], f, dict(c1, x0=tokens))
    dgate, dup, ddown, dqkv, dout, dg1, dg2, dbias = assemble((c0["ha"], c0["hb"]), (c0["ga"], c0["gb"]), (c0["qa"], c0["qb"]))
    return (
        f["layer_out"][None, :, None],
        c0["input_grad"][None, :, None],
        dg1,
        dg2,
        dqkv[None],
        dbias,
        dout[None],
        dgate[None],
        dup[None],
        ddown[None],
    )


def solution(mesh):
    return jax.shard_map(
        local,
        mesh=mesh,
        in_specs=(
            P(None, "fsdp", "ctx", None),
            P(None, "fsdp", "ctx", None),
            P("ctx"),
            P("section", "fsdp"),
            P("section", "fsdp"),
            P("section", "fsdp", None),
            P("section", "fsdp"),
            P("section", "fsdp", None),
            P("section", "fsdp", None),
            P("section", "fsdp", None),
            P("section", "fsdp", None),
        ),
        out_specs=(
            P("section", None, "fsdp", "ctx", None),
            P("section", None, "fsdp", "ctx", None),
            P("section", "fsdp"),
            P("section", "fsdp"),
            P("section", "fsdp", None),
            P("section", "fsdp"),
            P("section", "fsdp", None),
            P("section", "fsdp", None),
            P("section", "fsdp", None),
            P("section", "fsdp", None),
        ),
        check_vma=False,
    )
```

```python
import functools
import types

import jax
import jax.numpy as jnp
import numpy as np
from jax import lax
from jax.experimental import pallas as pl
from jax.experimental.pallas import tpu as pltpu
from jax.sharding import PartitionSpec as P

D = 896
HEADS = 14
KV_HEADS = 2
HEAD_DIM = 64
GROUP = HEADS // KV_HEADS
FF = 4864
QKV = 1152
EPS = 1e-06
THETA = 1000000.0
LANES = 128
TILES = D // LANES
WIN = 1280
NEG = -1e30
F32 = jnp.float32
BF16 = jnp.bfloat16
MESH = pl.DeviceIdType.MESH
VMEM_LIMIT = 60 * 2**20
UNIT = 16
SIDE = 4
GATE_PER = (5, 4)
DOWN_PER = (8, 9)
Q_PER = (4, 4)
Q_ROWS = 16 * sum(Q_PER) * UNIT


def mm(a, b):
    return jnp.dot(a, b, preferred_element_type=F32)


def mm_nt(a, b):
    return lax.dot_general(a, b, (((1,), (1,)), ((), ())), preferred_element_type=F32)


def mm_tn(a, b):
    return lax.dot_general(a, b, (((0,), (0,)), ((), ())), preferred_element_type=F32)


ORDER = (1, 3, 2)
SMALL = 2 * D + QKV
AXES = (("x", "y"), ("y", "x"))
BATCH = 3
GROUPS = tuple(slice(a, min(a + 2 * LANES, HEADS * HEAD_DIM)) for a in range(0, HEADS * HEAD_DIM, 2 * LANES))


def push(src, dst, ssem, rsem, axis, to):
    return pltpu.make_async_remote_copy(
        src_ref=src,
        dst_ref=dst,
        send_sem=ssem,
        recv_sem=rsem,
        device_id={axis: to},
        device_id_type=MESH,
    )


def rope(u, cos, sa, sb):
    return u * cos + pltpu.roll(u, 96, 1) * sa + pltpu.roll(u, 32, 1) * sb


def unrope(u, cos, sa, sb):
    return u * cos - pltpu.roll(u, 96, 1) * sa - pltpu.roll(u, 32, 1) * sb


def halves(a0, a1):
    lane = lax.broadcasted_iota(jnp.int32, a0.shape, 1) < HEAD_DIM
    low = jnp.where(lane, a0, pltpu.roll(a1, HEAD_DIM, 1))
    high = jnp.where(lane, pltpu.roll(a0, HEAD_DIM, 1), a1)
    return low, high


def spread(ref, t, tile_t):
    half = HEAD_DIM
    zero = jnp.zeros((half, LANES), F32)
    cols = slice(t * LANES, (t + 1) * LANES)
    for g in range(KV_HEADS):
        pair = [tile_t[j * half : (j + 1) * half, :] if (2 * t + j) // GROUP == g else zero for j in range(2)]
        for part, content in enumerate(halves(*pair)):
            ref[part * LANES + g * half : part * LANES + (g + 1) * half, cols] = content.astype(BF16)


def gathered_tile(wide, t):
    half = HEAD_DIM
    rows = []
    for j in range(2):
        g = (2 * t + j) // GROUP
        low = wide[g * half : (g + 1) * half, :]
        high = wide[LANES + g * half : LANES + (g + 1) * half, :]
        rows.append(halves(low, high)[j])
    return jnp.concatenate(rows, 0)


def dealt(a_per, b_per):
    where = [(0, u // a_per, u % a_per) for u in range(16 * a_per)]
    return where + [(1, v // b_per, v % b_per) for v in range(16 * b_per)]


def unit_runs(first, count, per):
    where = dealt(*per)
    found = []
    for i in range(count):
        part, piece, slot = where[first + i]
        if found and found[-1][0] == part and found[-1][1] == piece:
            found[-1][4] += 1
        else:
            found.append([part, piece, slot, i, 1])
    return found


def put_units(refs, section, base, per, first, rows):
    for part, piece, slot, i, m in unit_runs(first, rows.shape[0] // UNIT, per):
        at = base[part] + slot * UNIT
        refs[part][section, piece // SIDE, piece % SIDE, at : at + m * UNIT, :] = rows[i * UNIT : (i + m) * UNIT, :]


class Stages:
    def __init__(self, r):
        self.s = lax.axis_index("section")
        self.c = lax.axis_index("ctx")
        self.nc = lax.axis_size("ctx")
        self.x, self.y = self.c // SIDE, lax.rem(self.c, SIDE)
        self.z = lax.axis_index("fsdp")
        self.nz = lax.axis_size("fsdp")
        self.ssem, self.rsem, self.lsem = r.ssem, r.rsem, r.lsem
        self.used = 0
        self.local_used = 0
        self.sent = []

    def along(self, axis, k):
        own, n = {
            "x": (self.x, SIDE),
            "y": (self.y, SIDE),
            "z": (self.z, self.nz),
            "c": (self.c, self.nc),
        }[axis]
        return lax.rem(own + n + k, n)

    def peer(self, axis, k, section=None):
        if axis == "s":
            return {"section": 1 - self.s}
        if axis == "z":
            to = {"fsdp": self.along("z", k)}
        elif axis == "c":
            to = {"ctx": self.along("c", k)}
        elif axis == "x":
            to = {"ctx": self.along("x", k) * SIDE + self.y}
        else:
            to = {"ctx": self.x * SIDE + self.along("y", k)}
        if section is not None:
            to["section"] = section
        return to

    def hail(self, ids, ring=False):
        bar = pltpu.get_barrier_semaphore()
        for i in ids:
            pl.semaphore_signal(bar, inc=1, device_id=i, device_id_type=MESH)
        self.expected = len(ids)
        if ring:
            def one(k, c):
                pl.semaphore_signal(bar, inc=1, device_id=self.peer("c", k), device_id_type=MESH)
                return c

            lax.fori_loop(1, self.nc, one, 0)
            self.expected += self.nc - 1
        self.bar = bar

    def met(self):
        pl.semaphore_wait(self.bar, self.expected)

    def beside(self):
        return [self.peer("s", 0)]

    def upright(self, both=False):
        ids = [self.peer("z", k) for k in range(1, self.nz)]
        return ids + ([self.peer("z", k, 1 - self.s) for k in range(1, self.nz)] if both else [])

    def flat(self, both=False):
        ids = [self.peer(a, k) for a in "xy" for k in range(1, SIDE)]
        return ids + ([self.peer(a, k, 1 - self.s) for a in "xy" for k in range(1, SIDE)] if both else [])

    def take(self, count):
        self.used += count
        return self.used - count

    def copy(self, src, dst, at, to, recv_at=None):
        return pltpu.make_async_remote_copy(
            src_ref=src,
            dst_ref=dst,
            send_sem=self.ssem.at[at],
            recv_sem=self.rsem.at[at if recv_at is None else recv_at],
            device_id=to,
            device_id_type=MESH,
        )

    def begin(self, copies):
        for c in copies:
            c.start()
        self.sent += copies
        return copies

    def drain(self):
        for c in self.sent:
            c.wait_send()

    def swap(self, src, land):
        return self.begin([self.copy(src.at[1 - self.s], land, self.take(1), self.peer("s", 0))])

    def scatter(self, axis, src, land):
        n = self.nz if axis == "z" else SIDE
        at = self.take(n - 1)
        return self.begin(
            [self.copy(src.at[self.along(axis, k)], land.at[k - 1], at + k - 1, self.peer(axis, k)) for k in range(1, n)]
        )

    def gather(self, axis, ref):
        at = self.take(SIDE - 1)
        mine = ref.at[self.along(axis, 0)]
        return self.begin([self.copy(mine, mine, at + k - 1, self.peer(axis, k)) for k in range(1, SIDE)])

    def deal(self, src, dst, rows):
        at = self.take(self.nz - 1)
        mine = dst.at[self.block(self.z, rows), :]
        return self.begin(
            [
                self.copy(src.at[self.block(self.along("z", k), rows), :], mine, at + k - 1, self.peer("z", k))
                for k in range(1, self.nz)
            ]
        )

    def block(self, i, rows):
        return pl.ds(pl.multiple_of(i * rows, UNIT), rows)

    def aside(self, j):
        x = lax.rem(self.x + (1 - self.s) * j, SIDE)
        y = lax.rem(self.y + self.s * j, SIDE)
        return {"ctx": x * SIDE + y}

    def quarter(self):
        return self.x * (1 - self.s) + self.y * self.s

    def hand_over(self, axis, src, dst, layer, part=None):
        return Handover(self, axis, src, dst, layer, part)


class Handover:
    def __init__(self, st, axis, src, dst, layer, part=None):
        self.st, self.axis, self.layer = st, axis, layer
        self.at = st.take(2 * SIDE)
        mine = dst.at[st.s, st.along(axis, 0)]
        if part is not None:
            src, mine = src.at[part], mine.at[part]
        self.src, self.mine, self.dst, self.part = src, mine, dst, part
        st.begin(
            [st.copy(src, mine, self.at + k, st.peer(axis, k, layer), self.at + st.s * SIDE + k) for k in (1, SIDE - 1)]
        )
        self.beside = st.copy(src, mine, self.at, {"section": layer}, self.at + st.s * SIDE)
        self.within = pltpu.make_async_copy(src, mine, st.lsem.at[st.local_used])
        st.local_used += 1
        pl.when(st.s != layer)(self.beside.start)
        pl.when(st.s == layer)(self.within.start)

    def arrival(self, half, k):
        return self.st.copy(self.src, self.mine, self.at, {"section": self.layer}, self.at + half * SIDE + k)

    def passing(self, half):
        st = self.st
        way = 1 - 2 * half
        p = self.dst.at[half, st.along(self.axis, -way)]
        if self.part is not None:
            p = p.at[self.part]
        at = self.at + half * SIDE + 2
        return st.copy(p, p, at, st.peer(self.axis, way), at)

    def relay(self):
        @pl.when(self.st.s == self.layer)
        def _():
            for half, k in ((0, 1), (1, SIDE - 1)):
                self.arrival(half, k).wait_recv()
                self.passing(half).start()

    def finish(self):
        @pl.when(self.st.s == self.layer)
        def _():
            self.within.wait()
            for half, k in ((0, SIDE - 1), (1, 1), (0, 2), (1, 2), (1 - self.layer, 0)):
                self.arrival(half, k).wait_recv()
            for half in range(2):
                self.passing(half).wait_send()

        pl.when(self.st.s != self.layer)(self.beside.wait_send)


class Scatter:
    def __init__(self, st, axis, src, land):
        self.st, self.axis, self.src, self.land = st, axis, src, land
        self.at = st.take(6)
        low, high = slice(0, SIDE // 2), slice(SIDE // 2, SIDE)
        far = src.at[st.along(axis, 2)]
        self.through = [
            self.send(far.at[low], land.at[2, low], 0, 1),
            self.send(far.at[high], land.at[2, high], 1, -1),
        ]
        self.straight = [
            self.send(src.at[st.along(axis, 1), high], land.at[0, high], 2, 1),
            self.send(src.at[st.along(axis, -1), low], land.at[1, low], 3, -1),
        ]
        st.begin(self.through + self.straight)

    def send(self, src, dst, i, way):
        return self.st.copy(src, dst, self.at + i, self.st.peer(self.axis, way))

    def pass_on(self):
        st = self.st
        low, high = slice(0, SIDE // 2), slice(SIDE // 2, SIDE)
        self.late = []
        for i, (part, way) in enumerate(((low, 1), (high, -1))):
            self.through[i].wait_recv()
            mine = self.src.at[st.along(self.axis, way), part]
            add_into(mine, [mine, self.land.at[2, part]])
            self.late.append(self.send(mine, self.land.at[i, part], 4 + i, way))
        st.begin(self.late)

    def sum_into(self, out):
        arrived(self.straight + self.late)
        add_into(out, [self.src.at[self.st.along(self.axis, 0)], self.land.at[0], self.land.at[1]])


class Feed:
    def __init__(self, st, layer, sources, piece, band):
        self.st, self.layer, self.sources, self.piece, self.band = st, layer, sources, piece, band
        steps = st.nz - 1
        self.across = st.take(2 * steps)
        self.sideways = st.take((SIDE - 1) * steps)
        self.passed = st.take(steps)
        self.own = st.take(2)

    def beside(self, h):
        b = self.band(self.st.z, h)
        return self.st.copy(b, b, self.own + h, self.st.peer("s", 0))

    def send(self, h, k, src):
        st = self.st
        dst = self.piece(st.z, h, (st.x, st.y)[h])
        return st.copy(dst if src is None else src, dst, self.across + 2 * (k - 1) + h, st.peer("z", k, h))

    def start_beside(self):
        @pl.when(self.st.s == self.layer)
        def _():
            for h in range(2):
                self.beside(h).start()

    def start(self):
        st = self.st

        @pl.when(st.s == self.layer)
        def _():
            for k in ORDER:
                for h in range(2):
                    for needed, src in self.sources(h, (st.x, st.y)[h], st.along("z", k)):
                        if needed is None:
                            self.send(h, k, src).start()
                        else:
                            pl.when(needed)(self.send(h, k, src).start)

    def relay(self, k):
        st = self.st
        p = self.piece(st.along("z", -k), st.s, st.quarter())
        st.copy(p, p, self.across + 2 * (k - 1) + st.s, st.peer("s", 0)).wait_recv()
        at = self.sideways + (SIDE - 1) * (k - 1) - 1
        st.begin([st.copy(p, p, at + j, st.aside(j)) for j in range(1, SIDE)])

    def collect(self, k):
        st = self.st
        z = st.along("z", -k)
        at = self.sideways + (SIDE - 1) * (k - 1) - 1
        for j in range(1, SIDE):
            p = self.piece(z, st.s, lax.rem(st.quarter() + SIDE - j, SIDE))
            st.copy(p, p, at + j, st.aside(j)).wait_recv()
        b = self.band(z, st.s)
        st.begin([st.copy(b, b, self.passed + k - 1, st.peer("s", 0))])

    def finish(self):
        st = self.st
        for k in ORDER:
            b = self.band(st.along("z", -k), 1 - st.s)
            st.copy(b, b, self.passed + k - 1, st.peer("s", 0)).wait_recv()

        @pl.when(st.s == self.layer)
        def _():
            for h in range(2):
                for k in ORDER:
                    self.send(h, k, None).wait_send()
                self.beside(h).wait_send()

        @pl.when(st.s != self.layer)
        def _():
            for h in range(2):
                self.beside(h).wait_recv()


class FeedDown:
    def __init__(self, st, layer, src, dst):
        self.st, self.layer = st, layer
        share = src.shape[1]
        spare = WIN - share
        odd = lax.rem(st.z, 2)
        place = dst.at[pl.ds(pl.multiple_of(odd * spare, UNIT), share), :]
        dst[pl.ds(pl.multiple_of((1 - odd) * share, UNIT), spare), :] = jnp.zeros((spare, D), BF16)
        self.local = pltpu.make_async_copy(src.at[0], place, st.lsem.at[st.local_used])
        st.local_used += 1
        self.remote = st.copy(src.at[0], place, st.take(1), st.peer("s", 0))

    def start(self):
        @pl.when(self.st.s == self.layer)
        def _():
            self.local.start()
            self.remote.start()

    def finish(self):
        @pl.when(self.st.s == self.layer)
        def _():
            self.local.wait()
            self.remote.wait_send()

        @pl.when(self.st.s != self.layer)
        def _():
            self.remote.wait_recv()


class Delivery:
    def __init__(self, st, layer, src, out):
        self.st, self.layer = st, layer
        mine = out.at[st.s]
        self.within = pltpu.make_async_copy(src, mine, st.lsem.at[st.local_used])
        st.local_used += 1
        self.over = st.copy(src, mine, st.take(1), st.peer("s", 0))
        pl.when(st.s == layer)(self.within.start)
        pl.when(st.s != layer)(self.over.start)

    def finish(self):
        @pl.when(self.st.s == self.layer)
        def _():
            self.within.wait()
            self.over.wait_recv()

        pl.when(self.st.s != self.layer)(self.over.wait_send)


class Local:
    def __init__(self, st, layer, pairs):
        self.st, self.layer = st, layer
        self.copies = [pltpu.make_async_copy(a, b, st.lsem.at[st.local_used + i]) for i, (a, b) in enumerate(pairs)]
        st.local_used += len(pairs)

        @pl.when(st.s == layer)
        def _():
            for c in self.copies:
                c.start()

    def wait(self):
        @pl.when(self.st.s == self.layer)
        def _():
            for c in self.copies:
                c.wait()


def half_rows(z, h, share):
    return pl.ds(pl.multiple_of(z * share + h * (share // 2), UNIT), share // 2)


def feed_attention(st, layer, qkv, out, dst):
    share = qkv.shape[1]
    rows = st.block(st.z, share)
    local = Local(st, layer, [(qkv.at[0], dst.at[rows, :QKV]), (out.at[0], dst.at[rows, QKV:])])
    whole = QKV + D
    split = whole // 4 * 3

    def feed(low, high):
        width = (high - low) // SIDE

        def piece(z, h, q):
            return dst.at[half_rows(z, h, share), pl.ds(pl.multiple_of(low + q * width, LANES), width)]

        def band(z, h):
            return dst.at[half_rows(z, h, share), low:high]

        return Feed(st, layer, lambda h, q, z_to: [(None, None)], piece, band)

    return local, feed(0, split), feed(split, whole)


def feed_windows(st, layer, gate, up, dst):
    share = gate.shape[1]
    pace = FF // st.nz // (LANES // 2)
    width = WIN // 2

    def window(z):
        return pl.multiple_of(z * pace // 2 * LANES, LANES)

    rows = st.block(st.z, share)
    local = Local(st, layer, [(w.at[0, :, pl.ds(window(st.z), WIN)], dst.at[i, rows, :]) for i, w in enumerate((gate, up))])

    def sources(h, q, z_to):
        at = pl.multiple_of(window(z_to) + lax.rem(q, 2) * width, LANES)
        part = slice(h * (share // 2), (h + 1) * (share // 2))
        return [(q < 2, gate.at[0, part, pl.ds(at, width)]), (q >= 2, up.at[0, part, pl.ds(at, width)])]

    def piece(z, h, q):
        return dst.at[q // 2, half_rows(z, h, share), pl.ds(pl.multiple_of(lax.rem(q, 2) * width, LANES), width)]

    def band(z, h):
        return dst.at[:, half_rows(z, h, share), :]

    return local, Feed(st, layer, sources, piece, band)


class Ring:
    def __init__(self, st, place, rows):
        self.st, self.place, self.rows = st, place, rows
        self.at = st.take(4)
        mine = place(st.z, 0, rows)
        self.near = st.begin([self.send(mine, i, way) for i, way in enumerate((1, -1))])

    def send(self, ref, i, way):
        return self.st.copy(ref, ref, self.at + i, self.st.peer("z", way))

    def pass_on(self):
        st, half = self.st, self.rows // 2
        arrived(self.near)
        self.far = st.begin(
            [
                self.send(self.place(st.along("z", -1), 0, half), 2, 1),
                self.send(self.place(st.along("z", 1), half, half), 3, -1),
            ]
        )

    def finish(self):
        arrived(self.far)


def arrived(copies):
    for c in copies:
        c.wait_recv()


def add_into(dst, parts):
    def one(i, c):
        total = parts[0][i].astype(F32)
        for p in parts[1:]:
            total = total + p[i].astype(F32)
        dst[i] = total.astype(dst.dtype)
        return c

    lax.fori_loop(0, dst.shape[0], one, 0)


def add_rows(dst, parts):
    total = parts[0][...].astype(F32)
    for p in parts[1:]:
        total = total + p[...].astype(F32)
    dst[...] = total.astype(dst.dtype)


def swapped_sum(st, copies, given, land):
    arrived(copies)
    for i in range(SIDE):
        add_into(land.at[i], [given.at[st.s, i], land.at[i]])


def sides(tile, chosen):
    half = HEAD_DIM
    low, high = tile[:half], tile[half:]
    zero = jnp.zeros_like(low)
    below = jnp.concatenate([jnp.where(chosen, low, zero), jnp.where(chosen, zero, high)], 1)
    return jnp.concatenate([jnp.concatenate([zero, low], 1), below], 0).astype(BF16)


def sides_t(tile_t, chosen):
    lane = lax.broadcasted_iota(jnp.int32, tile_t.shape, 1) < HEAD_DIM
    upper = jnp.where(jnp.logical_or(lane, jnp.logical_not(chosen)), 0.0, pltpu.roll(tile_t, HEAD_DIM, 1))
    lower = jnp.where(jnp.logical_or(lane, jnp.logical_not(chosen)), tile_t, 0.0)
    return jnp.concatenate([upper, lower], 0).astype(BF16)


def own_sides(tile):
    low, high = tile[:HEAD_DIM], tile[HEAD_DIM:]
    zero = jnp.zeros_like(low)
    rows = [[zero, low], [low, zero], [zero, high]]
    return jnp.concatenate([jnp.concatenate(p, 1) for p in rows], 0).astype(BF16)


def own_bias(width):
    key = lax.broadcasted_iota(jnp.int32, (HEAD_DIM, width), 0)
    query = lax.rem(lax.broadcasted_iota(jnp.int32, (HEAD_DIM, width), 1), HEAD_DIM)
    return jnp.where(key <= query, 0.0, NEG)


def earlier(pairs_ref, src, me, width):
    return pairs_ref[src, 0:1, :width] < pairs_ref[me, 0:1, :width]


def col_max(a):
    return jnp.max(a, 0, keepdims=True)


def col_sum(a):
    return jnp.sum(a, 0, keepdims=True)


class View:
    def __init__(self, r, layer):
        self.r, self.layer = r, layer

    def named(self, k):
        own = k + str(self.layer)
        return own if hasattr(self.r, own) else k

    def __getattr__(self, k):
        return getattr(self.r, self.named(k))

    def need(self, *names):
        self.r.need(*[self.named(k) for k in names])

    def flush(self, *names):
        self.r.flush(*[self.named(k) for k in names])


def forward_kernel(_, r):
    st = Stages(r)
    n, me = st.nc, st.c
    st.hail(st.beside() + st.upright(True), ring=True)
    r.load()
    wa, gu, down = [None, None], [None, None], [None, None]
    for l in range(2):
        v = View(r, l)
        wa[l] = feed_attention(st, l, r.qkv_shard, r.out_shard, v.wa)
        gu[l] = feed_windows(st, l, r.gate_shard, r.up_shard, v.gu)
        down[l] = FeedDown(st, l, r.down_shard, v.down)
    r.need("inverse", "x0")
    r.pairs[me] = jnp.full(r.pairs.shape[1:], r.pair[0], jnp.int32)
    at = 0
    for part, size in ((r.attn_gain, D), (r.ffn_gain, D), (r.qkv_bias, QKV)):
        share = part.shape[1]
        line = jnp.concatenate([part[...].astype(F32), jnp.zeros((1, size - share), F32)], 1)
        line = pltpu.roll(jnp.broadcast_to(line, (8, size)), st.z * share, 1)
        r.parts[st.s, st.z, :, at : at + size] = line[:1]
        at += size
    wa[0][0].wait()
    st.met()
    wa[0][1].start()
    wa[0][1].start_beside()
    at = st.take(2 * st.nz)
    mine = r.parts.at[st.s, st.z]
    st.begin(
        [st.copy(mine, mine, at + k, st.peer("z", k, st.s), at + st.s * st.nz + k) for k in range(1, st.nz)]
        + [st.copy(mine, mine, at + st.nz + k, st.peer("z", k, 1 - st.s), at + st.s * st.nz + k) for k in range(1, st.nz)]
        + [st.copy(mine, mine, at, st.peer("s", 0), at + st.s * st.nz)]
    )

    def tell(k, c):
        p = r.pairs.at[me]
        push(p, p, r.psem.at[k], r.psem2.at[k], "ctx", lax.rem(me + k, n)).start()
        return c

    lax.fori_loop(1, n, tell, 0)
    block = LANES // 2
    i = lax.broadcasted_iota(jnp.int32, (LANES, LANES), 0)
    pair = r.pairs[me, 0:1, :LANES]
    pos = jnp.where(i < block, pair * block + i, (2 * n - 1 - pair) * block + i - block)
    angle = pos.astype(F32) * r.inverse[...]
    lane = lax.rem(lax.broadcasted_iota(jnp.int32, (LANES, LANES), 1), HEAD_DIM)
    sine = jnp.sin(angle)
    r.cos[...] = jnp.cos(angle)
    r.sa[...] = jnp.where(lane < HEAD_DIM // 2, -sine, 0.0)
    r.sb[...] = jnp.where(lane < HEAD_DIM // 2, 0.0, sine)
    r.flush("cos", "sa", "sb")
    for h in (st.s, 1 - st.s):
        for k in range(st.nz):
            if h is st.s and k == 0:
                continue
            st.copy(mine, mine, at, st.peer("s", 0), at + h * st.nz + k).wait_recv()
    for h in range(2):
        total = r.parts[h, 0]
        for k in range(1, st.nz):
            total = total + r.parts[h, k]
        r.small[h] = total
    r.flush("small")
    for k in ORDER:
        wa[0][1].relay(k)
    wa[0][2].start()
    gu[0][0].wait()
    gu[0][1].start()
    for k in ORDER:
        wa[0][1].collect(k)
    wa[0][2].start_beside()
    gu[0][1].start_beside()
    down[0].start()

    def begin_next():
        wa[1][0].wait()
        gu[1][0].wait()
        for feed in (wa[1][1], wa[1][2], gu[1][1]):
            feed.start()

    def besides_next():
        for feed in (wa[1][1], wa[1][2], gu[1][1]):
            feed.start_beside()
        down[1].start()

    def relays(*steps):
        def go():
            for feed, name, k in steps:
                getattr(feed, name)(k)

        return go

    g0, w0, w1, w2, g1 = gu[0][1], wa[0][2], wa[1][1], wa[1][2], gu[1][1]
    wa[0][1].finish()
    v = View(r, 0)

    def out_ready():
        w0.finish()
        v.flush("wa")

    nothing = lambda: None
    ahead = relays((w0, "relay", 1), (w0, "relay", 3), (w0, "relay", 2), (g0, "relay", 1), (g0, "relay", 3))
    attention_forward(
        st, v, 0,
        (
            lambda: (ahead(), begin_next()),
            relays((g0, "relay", 2), (w0, "collect", 1), (w0, "collect", 3), (w0, "collect", 2)),
            nothing,
            nothing,
            out_ready,
        ),
    )

    def ready_0():
        relays((g0, "collect", 1), (g0, "collect", 3), (g0, "collect", 2))()
        g0.finish()
        down[0].finish()
        v.flush("gu", "down")

    first = relays((w1, "relay", 1), (w1, "relay", 3), (w1, "relay", 2))
    ffn_forward(
        st, v, ready_0,
        (
            lambda: (besides_next(), first()),
            relays((w2, "relay", 1), (w2, "relay", 3), (w2, "relay", 2), (g1, "relay", 1), (g1, "relay", 3)),
            relays((g1, "relay", 2), (w1, "collect", 1), (w1, "collect", 3), (w1, "collect", 2)),
            relays((w2, "collect", 1), (w2, "collect", 3), (w2, "collect", 2)),
        ),
    )
    r.x1[...] = r.y0[...].astype(BF16).astype(F32)
    r.flush("x1")
    done_0 = Delivery(st, 0, r.y0, r.layer_out)
    r.need("gy")
    tok = r.gy.shape[0]
    rows = st.block(st.z, tok)
    r.gy_all[rows, :] = r.gy[...].astype(BF16)
    at = st.take(st.nz - 1)
    mine_gy = r.gy_all.at[rows, :]
    gy_moving = st.begin([st.copy(mine_gy, mine_gy, at + k - 1, st.peer("z", k)) for k in range(1, st.nz)])
    w1.finish()
    w2.finish()
    v = View(r, 1)
    v.flush("wa")
    attention_forward(
        st, v, 1,
        (nothing, relays((g1, "collect", 1)), relays((g1, "collect", 3)), relays((g1, "collect", 2)), nothing),
    )

    def ready_1():
        g1.finish()
        down[1].finish()
        v.flush("gu", "down")

    ffn_forward(st, v, ready_1, (nothing,) * 4)
    done_1 = Delivery(st, 1, r.y1, r.layer_out)
    arrived(gy_moving)
    r.flush("gy_all")
    done_0.finish()
    done_1.finish()
    st.drain()

    def done(k, c):
        p = r.pairs.at[me]
        push(p, p, r.psem.at[k], r.psem2.at[k], "ctx", lax.rem(me + k, n)).wait_send()
        return c

    lax.fori_loop(1, n, done, 0)
    r.close()


def attention_forward(st, r, layer, between):
    n, me = st.nc, st.c
    x = r.x[...]
    r1 = lax.rsqrt(jnp.mean(x * x, -1, keepdims=True) + EPS)
    small = r.small[layer]
    n1_f = x * r1 * small[:, :D]
    n1 = n1_f.astype(BF16)
    bias = small[:, 2 * D :]
    cos, sa, sb = r.cos[...], r.sa[...], r.sb[...]
    lin = mm(n1, r.wa[:, D:QKV]) + bias[:, D:]
    r.kv[me] = jnp.concatenate([rope(lin[:, :LANES], cos, sa, sb), lin[:, LANES:]], 1).astype(BF16)

    def keys_copy(k, src):
        return push(r.kv.at[src], r.kv.at[src], r.csem.at[k], r.csem2.at[k], "ctx", lax.rem(me + k, n))

    def start(k, c):
        keys_copy(k, me).start()
        return c

    lax.fori_loop(1, n, start, 0)
    linq = mm(n1, r.wa[:, :D]) + bias[:, :D]
    for t in range(TILES):
        tile = slice(t * LANES, (t + 1) * LANES)
        q = rope(linq[:, tile], cos, sa, sb) * HEAD_DIM ** (-0.5)
        spread(r.qst, t, q.T)
        r.n1t[tile, :] = n1_f[:, tile].T.astype(BF16)
    r.flush("qst", "n1t")
    between[0]()
    half = HEAD_DIM
    own_k = own_sides(r.kv[me, :, :LANES].astype(F32))
    own_vt = own_sides(r.kv[me, :, LANES:].astype(F32)).astype(F32).T.astype(BF16)
    for cols in GROUPS:
        width = cols.stop - cols.start
        bias = own_bias(width)
        sc = mm(own_k, r.qst[:, cols])
        s_a, s_l, s_h = sc[:half], sc[half : 2 * half] + bias, sc[2 * half :] + bias
        m_lo = col_max(s_l)
        m_hi = jnp.maximum(col_max(s_a), col_max(s_h))
        p_a, p_l, p_h = jnp.exp(s_a - m_hi), jnp.exp(s_l - m_lo), jnp.exp(s_h - m_hi)
        r.m_s[0:1, cols], r.m_s[1:2, cols] = m_lo, m_hi
        r.l_s[0:1, cols], r.l_s[1:2, cols] = col_sum(p_l), col_sum(p_a) + col_sum(p_h)
        r.acc_s[:, cols] = mm(own_vt, jnp.concatenate([p_a, p_l, p_h], 0).astype(BF16))

    def step(i, c):
        kx, vt, sel = [], [], []
        for j in range(BATCH):
            k = i * BATCH + 1 + j
            src = lax.rem(me + n - k, n)
            keys_copy(k, src).wait_recv()
            if layer == 0:
                p = r.pairs.at[src]
                push(p, p, r.psem.at[k], r.psem2.at[k], "ctx", lax.rem(me + k, n)).wait_recv()
            sel.append(src)
            chosen = earlier(r.pairs, src, me, LANES)
            kx.append(sides(r.kv[src, :, :LANES].astype(F32), chosen))
            vt.append(sides_t(r.kv[src, :, LANES:].astype(F32).T, chosen))
        kx = jnp.concatenate(kx, 0)
        vt = jnp.concatenate(vt, 1)
        for cols in GROUPS:
            width = cols.stop - cols.start
            sc = mm(kx, r.qst[:, cols])
            m_lo, m_hi = r.m_s[0:1, cols], r.m_s[1:2, cols]
            n_lo, n_hi = m_lo, m_hi
            chosen = [earlier(r.pairs, src, me, width) for src in sel]
            for j in range(BATCH):
                top = col_max(sc[(2 * j + 1) * half : (2 * j + 2) * half])
                n_hi = jnp.maximum(n_hi, col_max(sc[2 * j * half : (2 * j + 1) * half]))
                n_hi = jnp.where(chosen[j], n_hi, jnp.maximum(n_hi, top))
                n_lo = jnp.where(chosen[j], jnp.maximum(n_lo, top), n_lo)
            a_lo, a_hi = jnp.exp(m_lo - n_lo), jnp.exp(m_hi - n_hi)
            l_lo, l_hi = r.l_s[0:1, cols] * a_lo, r.l_s[1:2, cols] * a_hi
            ps = []
            for j in range(BATCH):
                p_a = jnp.exp(sc[2 * j * half : (2 * j + 1) * half] - n_hi)
                p_s = jnp.exp(sc[(2 * j + 1) * half : (2 * j + 2) * half] - jnp.where(chosen[j], n_lo, n_hi))
                total = col_sum(p_s)
                l_hi = l_hi + col_sum(p_a) + jnp.where(chosen[j], 0.0, total)
                l_lo = l_lo + jnp.where(chosen[j], total, 0.0)
                ps += [p_a.astype(BF16), p_s.astype(BF16)]
            r.m_s[0:1, cols], r.m_s[1:2, cols] = n_lo, n_hi
            r.l_s[0:1, cols], r.l_s[1:2, cols] = l_lo, l_hi
            new = mm(vt, jnp.concatenate(ps, 0))
            r.acc_s[:LANES, cols] = r.acc_s[:LANES, cols] * a_lo + new[:LANES]
            r.acc_s[LANES:, cols] = r.acc_s[LANES:, cols] * a_hi + new[LANES:]
        return c

    lax.fori_loop(0, 1, step, 0)
    between[1]()
    lax.fori_loop(1, 2, step, 0)
    between[2]()
    lax.fori_loop(2, 4, step, 0)
    between[3]()
    lax.fori_loop(4, (n - 1) // BATCH, step, 0)
    between[4]()
    r.flush("kv")
    if layer == 0:
        r.flush("pairs")
    r.lse[...] = r.m_s[...] + jnp.log(r.l_s[...])
    for t in range(TILES):
        cols = slice(t * LANES, (t + 1) * LANES)
        wide = jnp.concatenate([r.acc_s[:LANES, cols] / r.l_s[0:1, cols], r.acc_s[LANES:, cols] / r.l_s[1:2, cols]], 0)
        tile_t = gathered_tile(wide, t)
        r.attt[cols, :] = tile_t.astype(BF16)
        r.att_s[:, cols] = tile_t.T.astype(BF16)
    r.flush("lse", "attt")
    mid = x + mm(r.att_s[...], r.wa[:, QKV:])
    r.mid[...] = mid
    r2 = lax.rsqrt(jnp.mean(mid * mid, -1, keepdims=True) + EPS)
    r.all[st.z] = (mid * r2 * small[:, D : 2 * D]).astype(BF16)
    r.flush("mid")

    def done(k, c):
        keys_copy(k, me).wait_send()
        return c

    lax.fori_loop(1, n, done, 0)


def ffn_forward(st, r, ready, between):
    n, me = st.nz, st.z
    tok = r.mid.shape[0]
    at = st.take(n)

    def second(k):
        return st.copy(r.send_s.at[k], r.land_s.at[k], at + k, st.peer("z", -k))

    ring = Ring(st, lambda z, row, rows: r.all.at[z, row : row + rows, :], tok)
    ready()

    def block(sources):
        a = jnp.concatenate([r.all[i] for i in sources], 0) if len(sources) > 1 else r.all[sources[0]]
        gate = mm(a, r.gu[0])
        up = mm(a, r.gu[1])
        for j, i in enumerate(sources):
            r.gate[i] = gate[j * tok : (j + 1) * tok].astype(BF16)
            r.up[i] = up[j * tok : (j + 1) * tok].astype(BF16)
        hidden = (gate * jax.nn.sigmoid(gate) * up).astype(BF16)
        return mm(hidden, r.down[...])

    r.y[...] = r.mid[...] + block([me])
    between[0]()
    ring.pass_on()
    both = block([st.along("z", -1), st.along("z", -3)]).astype(BF16)
    for i, k in enumerate((1, 3)):
        r.send_s[k] = both[i * tok : (i + 1) * tok]
        second(k).start()
    between[1]()
    ring.finish()
    r.send_s[2] = block([st.along("z", -2)]).astype(BF16)
    second(2).start()
    between[2]()
    r.flush("all", "gate", "up")
    between[3]()
    for k in ORDER:
        second(k).wait_recv()
        r.y[...] += r.land_s[k].astype(F32)
    for k in ORDER:
        second(k).wait_send()


class Attention:
    def __init__(self, st):
        self.st = st

    def columns(self, src, dst):
        st = self.st
        share = dst.shape[0]
        at = st.take(st.nz - 1)
        mine = dst.at[:, pl.ds(pl.multiple_of(st.z * LANES, LANES), LANES)]
        moving = st.begin(
            [
                st.copy(src.at[st.block(st.along("z", k), share), :], mine, at + k - 1, st.peer("z", k))
                for k in range(1, st.nz)
            ]
        )
        mine[...] = src[st.block(st.z, share), :]
        return moving

    def whole(self, dst, cols=slice(None)):
        st = self.st
        rows = dst.shape[0] // st.nz
        at = st.take(st.nz - 1)
        mine = dst.at[pl.ds(pl.multiple_of(st.z * rows, UNIT), rows), cols]
        return st.begin([st.copy(mine, mine, at + k - 1, st.peer("z", k)) for k in range(1, st.nz)])

    def begin(self, glin, small, all_glin, all_small):
        st = self.st
        tok = glin.shape[0]
        all_glin[st.block(st.z, tok), :] = glin[...]
        all_small[st.block(st.z, 2 * UNIT), :] = small[...]
        return self.whole(all_glin) + self.whole(all_small)

    def swap(self, moving, n1z, all_glin, all_small, dout, made, land):
        st = self.st
        arrived(moving)
        share = n1z.shape[0]
        per = 8
        for j in range(0, QKV // LANES, 2):
            cols = slice(j * LANES, min(j + 2, QKV // LANES) * LANES)
            d = mm(n1z[...], all_glin[:, cols]).astype(BF16)
            for t in range(j, min(j + 2, QKV // LANES)):
                made[t // per, (t % per) * share : (t % per + 1) * share, :] = d[:, (t - j) * LANES : (t - j + 1) * LANES]
        made[1, share : 8 * share, :] = dout[...]
        small = jnp.zeros((2 * UNIT, LANES), F32)
        for i in range(st.nz):
            small = small + all_small[i * 2 * UNIT : (i + 1) * 2 * UNIT, :]
        made[0, 8 * share : 8 * share + 2 * UNIT, :] = small.astype(BF16)
        made[0, 8 * share + 2 * UNIT :, :] = jnp.zeros((Q_ROWS - 8 * share - 2 * UNIT, LANES), BF16)
        made[1, 8 * share :, :] = jnp.zeros((Q_ROWS - 8 * share, LANES), BF16)
        return st.swap(made, land)

    def fold(self, moving, made, land, out):
        st = self.st
        arrived(moving)
        rows = Q_ROWS // 2 // 16
        for h in range(2):
            for i in range(16):
                at = slice((h * 16 + i) * rows, (h * 16 + i + 1) * rows)
                total = made[st.s, at, :].astype(F32) + land[at, :].astype(F32)
                out[h][i // SIDE, i % SIDE] = total.astype(BF16)


class Rest:
    def __init__(self, st, t1, l2, t2, g1, out, layer):
        self.st, self.t1, self.l2, self.t2, self.g1, self.out, self.layer = st, t1, l2, t2, g1, out, layer
        self.stage = 0
        self.moving = [st.scatter(AXES[h][1], t1[h], l2[h]) for h in range(2)]

    def advance(self):
        st = self.st
        for h in range(2):
            second = AXES[h][1]
            arrived(self.moving[h])
            mine = self.g1[h].at[st.along(second, 0)]
            if self.stage == 0:
                t2 = self.t2[h]
                add_rows(t2, [self.t1[h].at[st.along(second, 0)]] + [self.l2[h].at[k] for k in range(SIDE - 1)])
                per = GATE_PER[h] * UNIT
                self.moving[h] = st.deal(t2, mine, per)
                mine[st.block(st.z, per), :] = t2[st.block(st.z, per), :]
                mine[st.nz * per :, :] = t2[st.nz * per :, :]
            elif self.stage == 1:
                self.moving[h] = st.gather(second, self.g1[h])
        if self.stage == 2:
            self.ends = []
            self.open = []
            self.give(slice(0, SIDE // 2))
        self.stage += 1

    def give(self, part):
        made = [self.st.hand_over(AXES[h][0], self.g1[h], self.out[h], self.layer, part) for h in range(2)]
        self.ends += made
        self.open += made

    def relay(self, count=None):
        for one in self.open[:count]:
            one.relay()
        self.open = self.open[count:] if count else []

    def finish(self):
        for one in self.ends:
            one.finish()


class Few:
    def __init__(self, st, r, tag):
        self.st = st

        def both(name):
            return tuple(getattr(r, name + tag + h) for h in "ab")

        self.qp, self.land, self.part, self.land2, self.wide = both("qp"), both("qm"), both("qe"), both("qw"), both("qh")
        self.moving = [st.scatter(AXES[h][0], self.qp[h], self.land[h]) for h in range(2)]

    def second_sum(self):
        st = self.st
        for h in range(2):
            arrived(self.moving[h])
            own = self.qp[h].at[st.along(AXES[h][0], 0)]
            add_into(self.part[h], [own] + [self.land[h].at[k] for k in range(SIDE - 1)])
            self.moving[h] = st.scatter(AXES[h][1], self.part[h], self.land2[h])

    def first_gather(self):
        st = self.st
        for h in range(2):
            arrived(self.moving[h])
            i = st.along(AXES[h][1], 0)
            add_rows(self.wide[h].at[i], [self.part[h].at[i]] + [self.land2[h].at[k] for k in range(SIDE - 1)])
            self.moving[h] = st.gather(AXES[h][1], self.wide[h])

    def hand_over(self, out, layer):
        for h in range(2):
            arrived(self.moving[h])
        return [self.st.hand_over(AXES[h][0], self.wide[h], out[h], layer) for h in range(2)]


def backward_kernel(layer, r):
    st = Stages(r)
    n, me = st.nz, st.z
    carry = layer == 0
    ids = st.upright() + st.beside()
    if carry:
        ids += [st.peer(a, k, 1 - st.s) for a in "xy" for k in range(1, SIDE)]
    st.hail(ids, ring=True)
    r.load()
    tok = r.gy.shape[0]

    def rows_of(i):
        return pl.ds(pl.multiple_of(i * tok, tok), tok)

    r.need("gy")
    gyb = r.gy[...].astype(BF16)
    gy = gyb.astype(F32) if carry else r.gy[...]
    above = None
    if carry:
        r.all_s[rows_of(me), :] = gyb
    else:
        r.need("all_s")
    st.met()
    at = st.take(2 * n)

    def second(k):
        return st.copy(r.send_s.at[k], r.land_s.at[k], at + n + k, st.peer("z", -k))

    if carry:
        ring = Ring(st, lambda z, row, rows: r.all_s.at[pl.ds(pl.multiple_of(z * tok + row, UNIT), rows), :], tok)
        above = Delivery(st, 1, r.gy, r.input_grad)
        r.need("p1a", "p1b")
        rest = Rest(st, (r.p1a, r.p1b), (r.l2a, r.l2b), (r.t2a, r.t2b), (r.g1a, r.g1b), (r.ga, r.gb), 1)
    r.need("down", "gate", "up", "gu")

    def block(sources):
        def stacked(ref):
            parts = [ref[rows_of(i), :] for i in sources]
            return jnp.concatenate(parts, 0) if len(parts) > 1 else parts[0]

        def picked(ref):
            parts = [ref[i].astype(F32) for i in sources]
            return jnp.concatenate(parts, 0) if len(parts) > 1 else parts[0]

        def keep(ref, value):
            for j, i in enumerate(sources):
                ref[rows_of(i), :] = value[j * tok : (j + 1) * tok]

        gh = mm_nt(stacked(r.all_s), r.down[...])
        gate, up = picked(r.gate), picked(r.up)
        sg = jax.nn.sigmoid(gate)
        act = gate * sg
        keep(r.hid_s, (act * up).astype(BF16))
        ggate = (gh * up * sg * (1.0 + gate * (1.0 - sg))).astype(BF16)
        gup = (gh * act).astype(BF16)
        keep(r.g_s.at[0], ggate)
        keep(r.g_s.at[1], gup)
        return mm_nt(ggate, r.gu[0]) + mm_nt(gup, r.gu[1])

    r.own_s[...] = block([me])
    if carry:
        rest.advance()
        ring.pass_on()
    both = block([st.along("z", -1), st.along("z", -3)]).astype(BF16)
    for i, k in enumerate((1, 3)):
        r.send_s[k] = both[i * tok : (i + 1) * tok]
        second(k).start()
    if carry:
        rest.advance()
        ring.finish()
    r.send_s[2] = block([st.along("z", -2)]).astype(BF16)
    second(2).start()
    attention = Attention(st)
    before = None
    if carry:
        r.need("glin1", "gsmall1")
        before = attention.begin(r.glin1, r.gsmall1, r.all_glin, r.all_small)
        rest.advance()

    late = [
        pltpu.make_async_copy(r.wa.at[:, :QKV], r.gu.at[0, :, :QKV], st.lsem.at[st.local_used]),
        pltpu.make_async_copy(r.wa.at[:, QKV:], r.gu.at[1, :, :D], st.lsem.at[st.local_used + 1]),
    ]
    st.local_used += 2
    for c in late:
        c.start()
    refs = (r.fa, r.fb)
    share = D // n
    for j in range(WIN // (2 * LANES)):
        cols = slice(2 * j * LANES, 2 * (j + 1) * LANES)
        r.down[cols, :] = mm_tn(r.hid_s[:, cols], r.all_s[...]).astype(BF16)
    pad = (WIN - FF // n) * lax.rem(me, 2)
    half = FF // n // 2
    base = [n * per * UNIT for per in GATE_PER]
    for section in range(2):
        rows = r.down[pl.ds(pl.multiple_of(pad + section * half, UNIT), half), :]
        for t in range(TILES):
            put_units(refs, section, base, DOWN_PER, t * (half // UNIT), rows[:, t * LANES : (t + 1) * LANES])
        used = TILES * (half // UNIT)
        extra = 16 * sum(DOWN_PER) - used
        put_units(refs, section, base, DOWN_PER, used, jnp.zeros((extra * UNIT, LANES), BF16))
    if carry:
        rest.give(slice(SIDE // 2, SIDE))
    r.need("n2_all")
    normed = jnp.concatenate([r.n2_all[i] for i in range(n)], 0)

    def product(section):
        for j in range(WIN // (2 * LANES)):
            d = mm_tn(normed, r.g_s[section, :, 2 * j * LANES : 2 * (j + 1) * LANES]).astype(BF16)
            for t in (2 * j, 2 * j + 1):
                tile = d[:, (t % 2) * LANES : (t % 2 + 1) * LANES]
                for i in range(n):
                    base = [i * per * UNIT for per in GATE_PER]
                    put_units(refs, section, base, GATE_PER, t * (share // UNIT), tile[i * share : (i + 1) * share, :])
        used = WIN // LANES * (share // UNIT)
        extra = 16 * sum(GATE_PER) - used
        for i in range(n):
            base = [i * per * UNIT for per in GATE_PER]
            put_units(refs, section, base, GATE_PER, used, jnp.zeros((extra * UNIT, LANES), BF16))

    product(1 - st.s)
    if carry:
        rest.relay(2)
    swaps = [st.swap(refs[h], (r.sla, r.slb)[h]) for h in range(2)]
    product(st.s)
    for k in ORDER:
        second(k).wait_recv()
        r.own_s[...] += r.land_s[k].astype(F32)
    gn2 = r.own_s[...]
    r.need("mid", "small")
    mid = r.mid[...]
    r2 = lax.rsqrt(jnp.mean(mid * mid, -1, keepdims=True) + EPS)
    unit = mid * r2
    dg2 = col_sum(gn2 * unit)
    dz = gn2 * r.small[layer][:, D : 2 * D]
    gm = gy + r2 * (dz - unit * jnp.mean(dz * unit, -1, keepdims=True))
    r.gm_s[...] = gm
    for k in ORDER:
        second(k).wait_send()
    attention_backward(st, r, layer, gm, dg2, refs, swaps, rest if carry else None, above, late, attention, before)


def attention_backward(st, r, layer, gm, dg2, refs, swaps, rest, above, late, attention, before):
    n, me = st.nc, st.c
    last = layer == 0
    half = HEAD_DIM
    gmb = gm.astype(BF16)
    tok = gm.shape[0]
    r.all_gm[st.block(st.z, tok), :] = gmb
    sl, l1, t1 = (r.sla, r.slb), (r.l1a, r.l1b), (r.t1a, r.t1b)
    r.need("attt", "n1t")
    size = 2 * BATCH * half
    pr, ds, gst = r.g_s.at[0, :size, :WIDE], r.g_s.at[1, :size, :WIDE], r.hid_s.at[: 2 * LANES, :WIDE]
    out_factors = attention.whole(r.all_gm) + attention.columns(r.attt, r.attz)
    qkv_factor = attention.columns(r.n1t, r.n1z)
    r1 = []
    for h in range(2):
        swapped_sum(st, swaps[h], refs[h], sl[h])
        r1.append(Scatter(st, AXES[h][0], sl[h], l1[h]))
    r.need("qst", "lse", "kv", "pairs")
    for c in late:
        c.wait()
    ga = mm_nt(gmb, r.gu[1, :, :D])
    for t in range(TILES):
        tile = slice(t * LANES, (t + 1) * LANES)
        ga_t = ga[:, tile].T
        spread(gst, t, ga_t)
        prod = ga_t * r.attt[tile, :].astype(F32)
        low, high = halves(col_sum(prod[:half]), col_sum(prod[half:]))
        r.delta_s[0:1, tile], r.delta_s[1:2, tile] = low, high

    def own_block():
        keys, vals = r.kv[me, :, :LANES].astype(F32), r.kv[me, :, LANES:].astype(F32)
        kx, vx = own_sides(keys), own_sides(vals)
        kt = kx.astype(F32).T.astype(BF16)
        rows = slice(0, 3 * half)
        for cols in GROUPS:
            bias = own_bias(cols.stop - cols.start)
            sc = mm(kx, r.qst[:, cols])
            dp = mm(vx, gst[:, cols])
            lo, hi = (r.lse[0:1, cols], r.delta_s[0:1, cols]), (r.lse[1:2, cols], r.delta_s[1:2, cols])
            parts = [(sc[:half], hi), (sc[half : 2 * half] + bias, lo), (sc[2 * half :] + bias, hi)]
            for i, (part, (lse, delta)) in enumerate(parts):
                p = jnp.exp(part - lse)
                at = slice(i * half, (i + 1) * half)
                pr[at, cols] = p.astype(BF16)
                ds[at, cols] = (p * (dp[at] - delta)).astype(BF16)
            r.gq_s[:, cols] = mm(kt, ds[rows, cols])
        made = []
        for w, q in ((ds, r.qst), (pr, gst)):
            e = mm_nt(w[rows, :], q[...])
            low = e[:half, LANES:] + e[half : 2 * half, :LANES]
            made.append(jnp.concatenate([low, e[2 * half :, LANES:]], 0))
        return jnp.concatenate(made, 1)

    def sum_copy(k):
        return push(r.send_k.at[k], r.land_k.at[k], r.csem.at[k], r.csem2.at[k], "ctx", lax.rem(me + k, n))

    def step(i):
        kx, vx, kt, sel = [], [], [], []
        for j in range(BATCH):
            src = lax.rem(me + i * BATCH + 1 + j, n)
            sel.append(src)
            chosen = earlier(r.pairs, src, me, LANES)
            keys = r.kv[src, :, :LANES].astype(F32)
            kx.append(sides(keys, chosen))
            vx.append(sides(r.kv[src, :, LANES:].astype(F32), chosen))
            kt.append(sides_t(keys.T, chosen))
        kx, vx, kt = jnp.concatenate(kx, 0), jnp.concatenate(vx, 0), jnp.concatenate(kt, 1)
        rows = slice(0, 2 * BATCH * half)
        for cols in GROUPS:
            width = cols.stop - cols.start
            sc = mm(kx, r.qst[:, cols])
            dp = mm(vx, gst[:, cols])
            for j in range(BATCH):
                chosen = earlier(r.pairs, sel[j], me, width)
                for part in range(2):
                    lse, delta = r.lse[1:2, cols], r.delta_s[1:2, cols]
                    if part:
                        lse = jnp.where(chosen, r.lse[0:1, cols], lse)
                        delta = jnp.where(chosen, r.delta_s[0:1, cols], delta)
                    at = slice((2 * j + part) * half, (2 * j + part + 1) * half)
                    p = jnp.exp(sc[at] - lse)
                    pr[at, cols] = p.astype(BF16)
                    ds[at, cols] = (p * (dp[at] - delta)).astype(BF16)
            r.gq_s[:, cols] += mm(kt, ds[rows, cols])
        ek = mm_nt(ds[rows, :], r.qst[...])
        ev = mm_nt(pr[rows, :], gst[...])
        for j in range(BATCH):
            chosen = earlier(r.pairs, sel[j], me, LANES)
            k = i * BATCH + 1 + j
            for e, lanes in ((ek, slice(0, LANES)), (ev, slice(LANES, 2 * LANES))):
                top = e[2 * j * half : (2 * j + 1) * half]
                low = e[(2 * j + 1) * half : (2 * j + 2) * half]
                r.send_k[k, :half, lanes] = (top[:, LANES:] + jnp.where(chosen, low[:, :LANES], 0.0)).astype(BF16)
                r.send_k[k, half:, lanes] = jnp.where(chosen, 0.0, low[:, LANES:]).astype(BF16)
            sum_copy(k).start()

    own = own_block()
    for i in range((n - 1) // BATCH):
        step(i)
        if i == 0:
            for one in r1:
                one.pass_on()
            if last:
                rest.relay()

    def out_gradient():
        arrived(out_factors)
        share = D // st.nz
        for j in range(0, TILES, 2):
            cols = slice(j * LANES, min(j + 2, TILES) * LANES)
            d = mm(r.attz[...], r.all_gm[:, cols]).astype(BF16)
            for t in range(j, min(j + 2, TILES)):
                r.dout[t * share : (t + 1) * share, :] = d[:, (t - j) * LANES : (t - j + 1) * LANES]

    glin = r.zglin.at[st.block(st.z, tok), :] if last else r.glin
    if last:
        for h in range(2):
            r1[h].sum_into(t1[h])
        own_rest = Rest(st, t1, (r.l2c, r.l2d), (r.t2c, r.t2d), (r.g1c, r.g1d), (r.ha, r.hb), 0)
    r.need("cos", "sa", "sb", "x", "small")
    cos, sa, sb = r.cos[...], r.sa[...], r.sb[...]
    for t in range(TILES):
        gq = gathered_tile(r.gq_s[:, t * LANES : (t + 1) * LANES], t).T * HEAD_DIM ** (-0.5)
        glin[:, t * LANES : (t + 1) * LANES] = unrope(gq, cos, sa, sb).astype(BF16)
    if last:
        factors = attention.whole(r.zglin, slice(0, D))
        r.need("n1z1", "dout1")
        qswap = attention.swap(before, r.n1z1, r.all_glin, r.all_small, r.dout1, r.qv, r.ql)
        own_rest.advance()
        attention.fold(qswap, r.qv, r.ql, (r.qpa, r.qpb))
        few = Few(st, r, "")
    else:
        out_gradient()
        arrived(qkv_factor)
        r.flush("dout", "n1z")

    def take(k, total):
        sum_copy(k).wait_recv()
        return total + r.land_k[k].astype(F32)

    own = lax.fori_loop(1, n, take, own)
    glin[:, D : D + LANES] = unrope(own[:, :LANES], cos, sa, sb).astype(BF16)
    glin[:, D + LANES :] = own[:, LANES:].astype(BF16)
    if last:
        factors += attention.whole(r.zglin, slice(D, QKV))
        own_rest.advance()
        few.second_sum()
    else:
        r.flush("glin")
    gn1 = mm_nt(glin[...], r.gu[0, :, :QKV])
    x = r.x[...]
    r1_ = lax.rsqrt(jnp.mean(x * x, -1, keepdims=True) + EPS)
    unit = x * r1_
    dg1 = col_sum(gn1 * unit)
    dbias = col_sum(glin[...].astype(F32))
    gsmall = r.zsmall.at[st.block(st.z, 2 * UNIT), :] if last else r.gsmall
    gsmall[...] = jnp.zeros(gsmall.shape, F32)
    row = 0
    for part in (dg1, dg2, dbias):
        for t in range(part.shape[1] // LANES):
            gsmall[row : row + 1, :] = part[:, t * LANES : (t + 1) * LANES]
            row += 1
    if last:
        factors += attention.whole(r.zsmall)
        own_rest.advance()
        few.first_gather()
    else:
        r.flush("gsmall")
    dz = gn1 * r.small[layer][:, :D]
    r.gx[...] = r.gm_s[...] + r1_ * (dz - unit * jnp.mean(dz * unit, -1, keepdims=True))
    if last:
        below = Delivery(st, 0, r.gx, r.input_grad)
        out = (r.qa, r.qb)
        out_gradient()
        arrived(qkv_factor)
        zswap = attention.swap(factors, r.n1z, r.zglin, r.zsmall, r.dout, r.zv, r.zl)
        own_rest.relay()
        attention.fold(zswap, r.zv, r.zl, (r.qp0a, r.qp0b))
        last_few = Few(st, r, "0")
        own_rest.give(slice(SIDE // 2, SIDE))
        ends = few.hand_over(out, 1)
        last_few.second_sum()
        own_rest.relay()
        for end in ends:
            end.relay()
        last_few.first_gather()
        final = last_few.hand_over(out, 0)
        rest.finish()
        for end in final:
            end.relay()
        for end in ends:
            end.finish()
        own_rest.finish()
        for end in final:
            end.finish()
        above.finish()
        below.finish()
    else:
        for h in range(2):
            r1[h].sum_into(t1[h])
    st.drain()

    def done(k, c):
        sum_copy(k).wait_send()
        return c

    lax.fori_loop(1, n, done, 0)
    r.close()


class Refs(types.SimpleNamespace):
    def load(self):
        for c in self.coming.values():
            c.start()

    def need(self, *names):
        for k in names:
            if k not in self.here:
                self.coming[k].wait()
                self.here.add(k)

    def flush(self, *names):
        for k in names:
            self.going[k].start()
            self.gone.add(k)

    def close(self):
        self.need(*self.coming)
        self.flush(*[k for k in self.going if k not in self.gone])
        for c in self.going.values():
            c.wait()


def call(kernel, layer, cid, name, ins, outs, scratch, sems, hbm=(), flops=10**10, picked=(), whole=(), scalars=()):
    staged = [k for k in ins if k not in hbm + whole + scalars]
    made = [k for k in outs if k not in hbm]
    dma = pltpu.SemaphoreType.DMA
    counts = dict(ssem=sems, rsem=sems, lsem=20, csem=16, csem2=16, psem=16, psem2=16, isem=len(staged), osem=len(made))
    if name == "forward":
        counts.update(csem1=16, csem21=16)
    places = [pltpu.VMEM(ins[k].shape[2 if k in picked else 0 :], ins[k].dtype) for k in staged] + [pltpu.VMEM(*outs[k]) for k in made]
    names = ["in_" + k for k in ins] + ["out_" + k for k in outs] + staged + made + list(scratch) + list(counts)

    def body(*refs):
        r = Refs(**dict(zip(names, refs)))
        for k in hbm + whole + scalars:
            if k in ins or k in outs:
                setattr(r, k, getattr(r, ("in_" if k in ins else "out_") + k))
        r.here, r.gone = set(), set()
        def source(k):
            ref = getattr(r, "in_" + k)
            return ref.at[lax.axis_index("section"), 0] if k in picked else ref

        r.coming = {k: pltpu.make_async_copy(source(k), getattr(r, k), r.isem.at[i]) for i, k in enumerate(staged)}
        r.going = {
            k: pltpu.make_async_copy(getattr(r, k), getattr(r, "out_" + k), r.osem.at[i]) for i, k in enumerate(made)
        }
        kernel(layer, r)

    anywhere = pl.BlockSpec(memory_space=pl.ANY)
    places_in = {k: pl.BlockSpec(memory_space=pltpu.VMEM) for k in whole}
    places_in.update({k: pl.BlockSpec(memory_space=pltpu.SMEM) for k in scalars})
    got = pl.pallas_call(
        body,
        out_shape=[jax.ShapeDtypeStruct(s, t) for s, t in outs.values()],
        in_specs=[places_in.get(k, anywhere) for k in ins],
        out_specs=[anywhere] * len(outs),
        scratch_shapes=places + [pltpu.VMEM(s, t) for s, t in scratch.values()] + [dma((k,)) for k in counts.values()],
        compiler_params=pltpu.CompilerParams(
            collective_id=cid, has_side_effects=True, vmem_limit_bytes=VMEM_LIMIT
        ),
        cost_estimate=pl.CostEstimate(flops=flops, bytes_accessed=20 * 2**20, transcendentals=0),
        name=name,
    )(*ins.values())
    return dict(zip(outs, got))


FAR = ("ga", "gb", "ha", "hb", "qa", "qb", "input_grad", "wa")
FA_ROWS = tuple((4 * g + d) * UNIT for g, d in zip(GATE_PER, DOWN_PER))
RQ = Q_ROWS // 2 // 16
SIDES = (SIDE, SIDE)
WIDE = HEADS * HEAD_DIM


def bf(*shape):
    return (shape, BF16)


def f4(*shape):
    return (shape, F32)


def rest_scratch():
    made = {}
    for h, rows in zip("ab", FA_ROWS):
        made["l2" + h] = bf(SIDE - 1, rows, LANES)
        made["t2" + h] = bf(rows, LANES)
        made["g1" + h] = bf(SIDE, rows, LANES)
    return made


def rest_outs():
    return {"g" + h: bf(2, *SIDES, rows, LANES) for h, rows in zip("ab", FA_ROWS)}


def assemble_kernel(nz, *refs):
    given, results, held, outs, sem, osem = (refs[:2], refs[2:4]), refs[6:14], refs[14:16] + refs[4:6], refs[16:24], refs[24], refs[25]
    s = lax.axis_index("section")
    copies = [pltpu.make_async_copy(a, b, osem.at[i]) for i, (a, b) in enumerate(zip(outs, results))]
    for layer in range(2):
        @pl.when(s == layer)
        def _():
            moving = [pltpu.make_async_copy(a, b, sem.at[i]) for i, (a, b) in enumerate(zip(given[layer], held))]
            for c in moving:
                c.start()
            for c in moving:
                c.wait()

    gate_ref, up_ref, down_ref, qkv_ref, out_ref = outs[:5]
    share = D // nz
    starts = window_starts(nz)

    def units(refs, section, base, per, first, count):
        rows = []
        for part, piece, slot, _, m in unit_runs(first, count, per):
            at = base[part] + slot * UNIT
            rows.append(refs[part][section, piece // SIDE, piece % SIDE, at : at + m * UNIT, :].astype(F32))
        return jnp.concatenate(rows, 0) if len(rows) > 1 else rows[0]

    for section, ref in ((0, gate_ref), (1, up_ref)):
        tiles = {}
        for w, a in enumerate(starts):
            for t in range(WIN // LANES):
                tiles.setdefault(a // LANES + t, []).append((w, t))
        for col, sources in tiles.items():
            total = None
            for w, t in sources:
                base = [w * per * UNIT for per in GATE_PER]
                got = units(held[:2], section, base, GATE_PER, t * (share // UNIT), share // UNIT)
                total = got if total is None else total + got
            ref[:, col * LANES : (col + 1) * LANES] = total
        copies[section].start()
    base = [nz * per * UNIT for per in GATE_PER]
    half = FF // nz // 2
    for section in range(2):
        for t in range(TILES):
            got = units(held[:2], section, base, DOWN_PER, t * (half // UNIT), half // UNIT)
            down_ref[section * half : (section + 1) * half, t * LANES : (t + 1) * LANES] = got
    copies[2].start()
    for t in range(QKV // LANES + TILES):
        got = units(held[2:], t // 8, (0, 0), Q_PER, (t % 8) * (share // UNIT), share // UNIT)
        if t < QKV // LANES:
            qkv_ref[:, t * LANES : (t + 1) * LANES] = got
        else:
            u = t - QKV // LANES
            out_ref[:, u * LANES : (u + 1) * LANES] = got
    small = units(held[2:], 0, (0, 0), Q_PER, 8 * (share // UNIT), 2)
    z = lax.axis_index("fsdp")
    row = 0
    for ref, size in zip(outs[5:], (D, D, QKV)):
        tiles = size // LANES
        line = jnp.concatenate([small[row + t : row + t + 1, :] for t in range(tiles)], 1)
        part = size // nz
        ref[...] = pltpu.roll(jnp.broadcast_to(line, (8, size)), lax.rem(size - z * part, size), 1)[:1, :part]
        row += tiles
    for c in copies[3:]:
        c.start()
    for c in copies:
        c.wait()


def assemble(zero, one, attn):
    nz = lax.axis_size("fsdp")
    vm = pl.BlockSpec(memory_space=pltpu.VMEM)
    anywhere = pl.BlockSpec(memory_space=pl.ANY)
    share = D // nz
    shapes = [(share, FF), (share, FF), (FF // nz, D), (share, QKV), (share, D), (1, share), (1, share), (1, QKV // nz)]
    return pl.pallas_call(
        functools.partial(assemble_kernel, nz),
        out_shape=[jax.ShapeDtypeStruct(a, F32) for a in shapes],
        in_specs=[anywhere] * 4 + [vm] * 2,
        out_specs=[anywhere] * len(shapes),
        scratch_shapes=[pltpu.VMEM(a.shape, a.dtype) for a in zero]
        + [pltpu.VMEM(a, F32) for a in shapes]
        + [pltpu.SemaphoreType.DMA((2,)), pltpu.SemaphoreType.DMA((len(shapes),))],
        compiler_params=pltpu.CompilerParams(vmem_limit_bytes=VMEM_LIMIT),
        name="assemble",
    )(*zero, *one, *attn)


def window_starts(n):
    share = FF // n
    return [(i * share // LANES) * LANES for i in range(n)]


def forward(tokens, cotangent, shards, gains, pair_of):
    n, nz = lax.axis_size("ctx"), lax.axis_size("fsdp")
    tok = tokens.shape[2]
    freq = np.arange(HEAD_DIM // 2, dtype=np.float64)
    inverse = jnp.asarray(np.tile(THETA ** (-2.0 * freq / HEAD_DIM), 4)[None, :].astype(np.float32))
    ins = dict(gains, pair=pair_of, inverse=inverse, x0=tokens, gy=cotangent)
    hbm = {k + "_shard": v for k, v in shards.items()}
    ins.update(hbm)
    outs = dict(
        small=f4(2, 1, SMALL), pairs=((n, 8, 2 * LANES), jnp.int32), cos=f4(tok, LANES), sa=f4(tok, LANES), sb=f4(tok, LANES),
        x1=f4(tok, D), gy_all=bf(nz * tok, D), layer_out=f4(2, tok, D),
    )
    scratch = dict(m_s=f4(2, WIDE), l_s=f4(2, WIDE), acc_s=f4(2 * LANES, WIDE), att_s=bf(tok, D), parts=f4(2, nz, 1, SMALL))
    for l in "01":
        each = dict(
            mid=f4(tok, D), n1t=bf(D, tok), qst=bf(2 * LANES, WIDE), kv=bf(n, tok, 2 * LANES), lse=f4(2, WIDE),
            attt=bf(D, tok), gu=bf(2, D, WIN), down=bf(WIN, D), wa=bf(D, QKV + D),
            all=bf(nz, tok, D), gate=bf(nz, tok, WIN), up=bf(nz, tok, WIN),
        )
        outs.update({k + l: v for k, v in each.items()})
        scratch.update({"y" + l: f4(tok, D), "send_s" + l: bf(nz, tok, D), "land_s" + l: bf(nz, tok, D)})
    return call(forward_kernel, 0, 1, "forward", ins, outs, scratch, 200, tuple(hbm) + ("layer_out",), picked=("x0", "gy"), whole=tuple(gains), scalars=("pair",))


def backward(layer, gy, f, before):
    n, nz = lax.axis_size("ctx"), lax.axis_size("fsdp")
    tok = gy.shape[-2]
    share = D // nz
    own = {k: f[k + str(layer)] for k in ("down", "gate", "up", "gu", "all", "mid", "attt", "n1t", "qst", "lse", "kv", "wa")}
    ins = dict(gy=gy)
    outs = {}
    factors = dict(n1z=bf(share, nz * tok), dout=bf(TILES * share, LANES))
    scratch = dict(
        hid_s=bf(nz * tok, WIN), g_s=bf(2, nz * tok, WIN), gm_s=f4(tok, D),
        own_s=f4(tok, D), send_s=bf(nz, tok, D), land_s=bf(nz, tok, D),
        delta_s=f4(2, WIDE), gq_s=f4(2 * LANES, WIDE), all_gm=bf(nz * tok, D), attz=bf(share, nz * tok),
        send_k=bf(n, tok, 2 * LANES), land_k=bf(n, tok, 2 * LANES),
    )
    for h, rows in zip("ab", FA_ROWS):
        scratch["f" + h] = bf(2, *SIDES, rows, LANES)
        scratch["sl" + h] = bf(*SIDES, rows, LANES)
        scratch["l1" + h] = bf(SIDE - 1, SIDE, rows, LANES)
    if layer == 0:
        scratch["gx"] = f4(tok, D)
        outs["input_grad"] = f4(2, tok, D)
        scratch["all_s"] = bf(nz * tok, D)
        ins.update(p1a=before["t1a"], p1b=before["t1b"])
        scratch.update(rest_scratch())
        outs.update(rest_outs())
    else:
        ins["all_s"] = f["gy_all"]
        outs["gx"] = f4(tok, D)
    ins.update(down=own["down"], gate=own["gate"], up=own["up"], gu=own["gu"], n2_all=own["all"], mid=own["mid"])
    ins["small"] = f["small"]
    ins.update({k: own[k] for k in ("attt", "n1t")})
    if layer == 0:
        ins.update(glin1=before["glin"], gsmall1=before["gsmall"], n1z1=before["n1z"], dout1=before["dout"])
        scratch.update(factors)
        scratch.update(all_glin=bf(nz * tok, QKV), all_small=f4(nz * 2 * UNIT, LANES), qv=bf(2, Q_ROWS, LANES), ql=bf(Q_ROWS, LANES))
        scratch.update(zglin=bf(nz * tok, QKV), zsmall=f4(nz * 2 * UNIT, LANES), zv=bf(2, Q_ROWS, LANES), zl=bf(Q_ROWS, LANES))
        scratch.update(t1a=bf(SIDE, FA_ROWS[0], LANES), t1b=bf(SIDE, FA_ROWS[1], LANES))
        for g, h, rows in zip("ab", "cd", FA_ROWS):
            scratch["l2" + h] = bf(SIDE - 1, rows, LANES)
            scratch["t2" + h] = bf(rows, LANES)
            scratch["g1" + h] = bf(SIDE, rows, LANES)
            outs["h" + g] = bf(2, *SIDES, rows, LANES)
            outs["q" + g] = bf(2, *SIDES, RQ, LANES)
            for tag in ("", "0"):
                scratch["qp" + tag + g] = bf(*SIDES, RQ, LANES)
                scratch["qm" + tag + g] = bf(SIDE - 1, SIDE, RQ, LANES)
                scratch["qw" + tag + g] = bf(SIDE - 1, RQ, LANES)
                scratch["qe" + tag + g] = bf(SIDE, RQ, LANES)
                scratch["qh" + tag + g] = bf(SIDE, RQ, LANES)
    else:
        outs.update(factors)
        outs.update(glin=bf(tok, QKV), gsmall=f4(2 * UNIT, LANES), t1a=bf(SIDE, FA_ROWS[0], LANES), t1b=bf(SIDE, FA_ROWS[1], LANES))
    ins.update({k: own[k] for k in ("qst", "lse", "kv", "wa")})
    ins.update({k: f[k] for k in ("pairs", "cos", "sa", "sb")})
    ins["x"] = f["x" + str(layer)] if layer else before["x0"]
    return call(backward_kernel, layer, 2 + layer, f"backward_{layer}", ins, outs, scratch, 256, FAR, 3 * 10**10, ("x",) if layer == 0 else ("gy",))


def local(
    tokens, cotangent, pair_of, attn_gain, ffn_gain, qkv_weight, qkv_bias, out_weight, gate_weight, up_weight, down_weight,
):
    shards = dict(qkv=qkv_weight, out=out_weight, gate=gate_weight, up=up_weight, down=down_weight)

    gains = dict(attn_gain=attn_gain, ffn_gain=ffn_gain, qkv_bias=qkv_bias)
    f = forward(tokens, cotangent, shards, gains, pair_of)
    c1 = backward(1, cotangent, f, None)
    c0 = backward(0, c1["gx"], f, dict(c1, x0=tokens))
    dgate, dup, ddown, dqkv, dout, dg1, dg2, dbias = assemble((c0["ha"], c0["hb"]), (c0["ga"], c0["gb"]), (c0["qa"], c0["qb"]))
    return (
        f["layer_out"][None, :, None],
        c0["input_grad"][None, :, None],
        dg1,
        dg2,
        dqkv[None],
        dbias,
        dout[None],
        dgate[None],
        dup[None],
        ddown[None],
    )


def solution(mesh):
    return jax.shard_map(
        local,
        mesh=mesh,
        in_specs=(
            P(None, "fsdp", "ctx", None),
            P(None, "fsdp", "ctx", None),
            P("ctx"),
            P("section", "fsdp"),
            P("section", "fsdp"),
            P("section", "fsdp", None),
            P("section", "fsdp"),
            P("section", "fsdp", None),
            P("section", "fsdp", None),
            P("section", "fsdp", None),
            P("section", "fsdp", None),
        ),
        out_specs=(
            P("section", None, "fsdp", "ctx", None),
            P("section", None, "fsdp", "ctx", None),
            P("section", "fsdp"),
            P("section", "fsdp"),
            P("section", "fsdp", None),
            P("section", "fsdp"),
            P("section", "fsdp", None),
            P("section", "fsdp", None),
            P("section", "fsdp", None),
            P("section", "fsdp", None),
        ),
        check_vma=False,
    )
```

```python
import functools
import types

import jax
import jax.numpy as jnp
import numpy as np
from jax import lax
from jax.experimental import pallas as pl
from jax.experimental.pallas import tpu as pltpu
from jax.sharding import PartitionSpec as P

D = 896
HEADS = 14
KV_HEADS = 2
HEAD_DIM = 64
GROUP = HEADS // KV_HEADS
FF = 4864
QKV = 1152
EPS = 1e-06
THETA = 1000000.0
LANES = 128
TILES = D // LANES
WIN = 1280
NEG = -1e30
F32 = jnp.float32
BF16 = jnp.bfloat16
MESH = pl.DeviceIdType.MESH
VMEM_LIMIT = 60 * 2**20
UNIT = 16
SIDE = 4
GATE_PER = (5, 4)
DOWN_PER = (8, 9)
Q_PER = (4, 4)
Q_ROWS = 16 * sum(Q_PER) * UNIT


def mm(a, b):
    return jnp.dot(a, b, preferred_element_type=F32)


def mm_nt(a, b):
    return lax.dot_general(a, b, (((1,), (1,)), ((), ())), preferred_element_type=F32)


def mm_tn(a, b):
    return lax.dot_general(a, b, (((0,), (0,)), ((), ())), preferred_element_type=F32)


ORDER = (1, 3, 2)
SMALL = 2 * D + QKV
AXES = (("x", "y"), ("y", "x"))
BATCH = 3
GROUPS = tuple(slice(a, min(a + 2 * LANES, HEADS * HEAD_DIM)) for a in range(0, HEADS * HEAD_DIM, 2 * LANES))


def push(src, dst, ssem, rsem, axis, to):
    return pltpu.make_async_remote_copy(
        src_ref=src,
        dst_ref=dst,
        send_sem=ssem,
        recv_sem=rsem,
        device_id={axis: to},
        device_id_type=MESH,
    )


def rope(u, cos, sa, sb):
    return u * cos + pltpu.roll(u, 96, 1) * sa + pltpu.roll(u, 32, 1) * sb


def unrope(u, cos, sa, sb):
    return u * cos - pltpu.roll(u, 96, 1) * sa - pltpu.roll(u, 32, 1) * sb


def halves(a0, a1):
    lane = lax.broadcasted_iota(jnp.int32, a0.shape, 1) < HEAD_DIM
    low = jnp.where(lane, a0, pltpu.roll(a1, HEAD_DIM, 1))
    high = jnp.where(lane, pltpu.roll(a0, HEAD_DIM, 1), a1)
    return low, high


def spread(ref, t, tile_t):
    half = HEAD_DIM
    zero = jnp.zeros((half, LANES), F32)
    cols = slice(t * LANES, (t + 1) * LANES)
    for g in range(KV_HEADS):
        pair = [tile_t[j * half : (j + 1) * half, :] if (2 * t + j) // GROUP == g else zero for j in range(2)]
        for part, content in enumerate(halves(*pair)):
            ref[part * LANES + g * half : part * LANES + (g + 1) * half, cols] = content.astype(BF16)


def gathered_tile(wide, t):
    half = HEAD_DIM
    rows = []
    for j in range(2):
        g = (2 * t + j) // GROUP
        low = wide[g * half : (g + 1) * half, :]
        high = wide[LANES + g * half : LANES + (g + 1) * half, :]
        rows.append(halves(low, high)[j])
    return jnp.concatenate(rows, 0)


def dealt(a_per, b_per):
    where = [(0, u // a_per, u % a_per) for u in range(16 * a_per)]
    return where + [(1, v // b_per, v % b_per) for v in range(16 * b_per)]


def unit_runs(first, count, per):
    where = dealt(*per)
    found = []
    for i in range(count):
        part, piece, slot = where[first + i]
        if found and found[-1][0] == part and found[-1][1] == piece:
            found[-1][4] += 1
        else:
            found.append([part, piece, slot, i, 1])
    return found


def put_units(refs, section, base, per, first, rows):
    for part, piece, slot, i, m in unit_runs(first, rows.shape[0] // UNIT, per):
        at = base[part] + slot * UNIT
        refs[part][section, piece // SIDE, piece % SIDE, at : at + m * UNIT, :] = rows[i * UNIT : (i + m) * UNIT, :]


class Stages:
    def __init__(self, r):
        self.s = lax.axis_index("section")
        self.c = lax.axis_index("ctx")
        self.nc = lax.axis_size("ctx")
        self.x, self.y = self.c // SIDE, lax.rem(self.c, SIDE)
        self.z = lax.axis_index("fsdp")
        self.nz = lax.axis_size("fsdp")
        self.ssem, self.rsem, self.lsem = r.ssem, r.rsem, r.lsem
        self.used = 0
        self.local_used = 0
        self.sent = []

    def along(self, axis, k):
        own, n = {
            "x": (self.x, SIDE),
            "y": (self.y, SIDE),
            "z": (self.z, self.nz),
            "c": (self.c, self.nc),
        }[axis]
        return lax.rem(own + n + k, n)

    def peer(self, axis, k, section=None):
        if axis == "s":
            return {"section": 1 - self.s}
        if axis == "z":
            to = {"fsdp": self.along("z", k)}
        elif axis == "c":
            to = {"ctx": self.along("c", k)}
        elif axis == "x":
            to = {"ctx": self.along("x", k) * SIDE + self.y}
        else:
            to = {"ctx": self.x * SIDE + self.along("y", k)}
        if section is not None:
            to["section"] = section
        return to

    def hail(self, ids, ring=False):
        bar = pltpu.get_barrier_semaphore()
        for i in ids:
            pl.semaphore_signal(bar, inc=1, device_id=i, device_id_type=MESH)
        self.expected = len(ids)
        if ring:
            def one(k, c):
                pl.semaphore_signal(bar, inc=1, device_id=self.peer("c", k), device_id_type=MESH)
                return c

            lax.fori_loop(1, self.nc, one, 0)
            self.expected += self.nc - 1
        self.bar = bar

    def met(self):
        pl.semaphore_wait(self.bar, self.expected)

    def beside(self):
        return [self.peer("s", 0)]

    def upright(self, both=False):
        ids = [self.peer("z", k) for k in range(1, self.nz)]
        return ids + ([self.peer("z", k, 1 - self.s) for k in range(1, self.nz)] if both else [])

    def flat(self, both=False):
        ids = [self.peer(a, k) for a in "xy" for k in range(1, SIDE)]
        return ids + ([self.peer(a, k, 1 - self.s) for a in "xy" for k in range(1, SIDE)] if both else [])

    def take(self, count):
        self.used += count
        return self.used - count

    def copy(self, src, dst, at, to, recv_at=None):
        return pltpu.make_async_remote_copy(
            src_ref=src,
            dst_ref=dst,
            send_sem=self.ssem.at[at],
            recv_sem=self.rsem.at[at if recv_at is None else recv_at],
            device_id=to,
            device_id_type=MESH,
        )

    def begin(self, copies):
        for c in copies:
            c.start()
        self.sent += copies
        return copies

    def drain(self):
        for c in self.sent:
            c.wait_send()

    def swap(self, src, land):
        return self.begin([self.copy(src.at[1 - self.s], land, self.take(1), self.peer("s", 0))])

    def scatter(self, axis, src, land):
        n = self.nz if axis == "z" else SIDE
        at = self.take(n - 1)
        return self.begin(
            [self.copy(src.at[self.along(axis, k)], land.at[k - 1], at + k - 1, self.peer(axis, k)) for k in range(1, n)]
        )

    def gather(self, axis, ref):
        at = self.take(SIDE - 1)
        mine = ref.at[self.along(axis, 0)]
        return self.begin([self.copy(mine, mine, at + k - 1, self.peer(axis, k)) for k in range(1, SIDE)])

    def deal(self, src, dst, rows):
        at = self.take(self.nz - 1)
        mine = dst.at[self.block(self.z, rows), :]
        return self.begin(
            [
                self.copy(src.at[self.block(self.along("z", k), rows), :], mine, at + k - 1, self.peer("z", k))
                for k in range(1, self.nz)
            ]
        )

    def block(self, i, rows):
        return pl.ds(pl.multiple_of(i * rows, UNIT), rows)

    def aside(self, j):
        x = lax.rem(self.x + (1 - self.s) * j, SIDE)
        y = lax.rem(self.y + self.s * j, SIDE)
        return {"ctx": x * SIDE + y}

    def quarter(self):
        return self.x * (1 - self.s) + self.y * self.s

    def hand_over(self, axis, src, dst, layer, part=None):
        return Handover(self, axis, src, dst, layer, part)


class Handover:
    def __init__(self, st, axis, src, dst, layer, part=None):
        self.st, self.axis, self.layer = st, axis, layer
        self.at = st.take(2 * SIDE)
        mine = dst.at[st.s, st.along(axis, 0)]
        if part is not None:
            src, mine = src.at[part], mine.at[part]
        self.src, self.mine, self.dst, self.part = src, mine, dst, part
        st.begin(
            [st.copy(src, mine, self.at + k, st.peer(axis, k, layer), self.at + st.s * SIDE + k) for k in (1, SIDE - 1)]
        )
        self.beside = st.copy(src, mine, self.at, {"section": layer}, self.at + st.s * SIDE)
        self.within = pltpu.make_async_copy(src, mine, st.lsem.at[st.local_used])
        st.local_used += 1
        pl.when(st.s != layer)(self.beside.start)
        pl.when(st.s == layer)(self.within.start)

    def arrival(self, half, k):
        return self.st.copy(self.src, self.mine, self.at, {"section": self.layer}, self.at + half * SIDE + k)

    def passing(self, half):
        st = self.st
        way = 1 - 2 * half
        p = self.dst.at[half, st.along(self.axis, -way)]
        if self.part is not None:
            p = p.at[self.part]
        at = self.at + half * SIDE + 2
        return st.copy(p, p, at, st.peer(self.axis, way), at)

    def relay(self):
        @pl.when(self.st.s == self.layer)
        def _():
            for half, k in ((0, 1), (1, SIDE - 1)):
                self.arrival(half, k).wait_recv()
                self.passing(half).start()

    def finish(self):
        @pl.when(self.st.s == self.layer)
        def _():
            self.within.wait()
            for half, k in ((0, SIDE - 1), (1, 1), (0, 2), (1, 2), (1 - self.layer, 0)):
                self.arrival(half, k).wait_recv()
            for half in range(2):
                self.passing(half).wait_send()

        pl.when(self.st.s != self.layer)(self.beside.wait_send)


class Scatter:
    def __init__(self, st, axis, src, land):
        self.st, self.axis, self.src, self.land = st, axis, src, land
        self.at = st.take(6)
        low, high = slice(0, SIDE // 2), slice(SIDE // 2, SIDE)
        far = src.at[st.along(axis, 2)]
        self.through = [
            self.send(far.at[low], land.at[2, low], 0, 1),
            self.send(far.at[high], land.at[2, high], 1, -1),
        ]
        self.straight = [
            self.send(src.at[st.along(axis, 1), high], land.at[0, high], 2, 1),
            self.send(src.at[st.along(axis, -1), low], land.at[1, low], 3, -1),
        ]
        st.begin(self.through + self.straight)

    def send(self, src, dst, i, way):
        return self.st.copy(src, dst, self.at + i, self.st.peer(self.axis, way))

    def pass_on(self):
        st = self.st
        low, high = slice(0, SIDE // 2), slice(SIDE // 2, SIDE)
        self.late = []
        for i, (part, way) in enumerate(((low, 1), (high, -1))):
            self.through[i].wait_recv()
            mine = self.src.at[st.along(self.axis, way), part]
            add_into(mine, [mine, self.land.at[2, part]])
            self.late.append(self.send(mine, self.land.at[i, part], 4 + i, way))
        st.begin(self.late)

    def sum_into(self, out):
        arrived(self.straight + self.late)
        add_into(out, [self.src.at[self.st.along(self.axis, 0)], self.land.at[0], self.land.at[1]])


class Feed:
    def __init__(self, st, layer, sources, piece, band):
        self.st, self.layer, self.sources, self.piece, self.band = st, layer, sources, piece, band
        steps = st.nz - 1
        self.across = st.take(2 * steps)
        self.sideways = st.take((SIDE - 1) * steps)
        self.passed = st.take(steps)
        self.own = st.take(2)

    def beside(self, h):
        b = self.band(self.st.z, h)
        return self.st.copy(b, b, self.own + h, self.st.peer("s", 0))

    def send(self, h, k, src):
        st = self.st
        dst = self.piece(st.z, h, (st.x, st.y)[h])
        return st.copy(dst if src is None else src, dst, self.across + 2 * (k - 1) + h, st.peer("z", k, h))

    def start_beside(self):
        @pl.when(self.st.s == self.layer)
        def _():
            for h in range(2):
                self.beside(h).start()

    def start(self):
        st = self.st

        @pl.when(st.s == self.layer)
        def _():
            for k in ORDER:
                for h in range(2):
                    for needed, src in self.sources(h, (st.x, st.y)[h], st.along("z", k)):
                        if needed is None:
                            self.send(h, k, src).start()
                        else:
                            pl.when(needed)(self.send(h, k, src).start)

    def relay(self, k):
        st = self.st
        p = self.piece(st.along("z", -k), st.s, st.quarter())
        st.copy(p, p, self.across + 2 * (k - 1) + st.s, st.peer("s", 0)).wait_recv()
        at = self.sideways + (SIDE - 1) * (k - 1) - 1
        st.begin([st.copy(p, p, at + j, st.aside(j)) for j in range(1, SIDE)])

    def collect(self, k):
        st = self.st
        z = st.along("z", -k)
        at = self.sideways + (SIDE - 1) * (k - 1) - 1
        for j in range(1, SIDE):
            p = self.piece(z, st.s, lax.rem(st.quarter() + SIDE - j, SIDE))
            st.copy(p, p, at + j, st.aside(j)).wait_recv()
        b = self.band(z, st.s)
        st.begin([st.copy(b, b, self.passed + k - 1, st.peer("s", 0))])

    def finish(self):
        st = self.st
        for k in ORDER:
            b = self.band(st.along("z", -k), 1 - st.s)
            st.copy(b, b, self.passed + k - 1, st.peer("s", 0)).wait_recv()

        @pl.when(st.s == self.layer)
        def _():
            for h in range(2):
                for k in ORDER:
                    self.send(h, k, None).wait_send()
                self.beside(h).wait_send()

        @pl.when(st.s != self.layer)
        def _():
            for h in range(2):
                self.beside(h).wait_recv()


class FeedDown:
    def __init__(self, st, layer, src, dst):
        self.st, self.layer = st, layer
        share = src.shape[1]
        spare = WIN - share
        odd = lax.rem(st.z, 2)
        place = dst.at[pl.ds(pl.multiple_of(odd * spare, UNIT), share), :]
        dst[pl.ds(pl.multiple_of((1 - odd) * share, UNIT), spare), :] = jnp.zeros((spare, D), BF16)
        self.local = pltpu.make_async_copy(src.at[0], place, st.lsem.at[st.local_used])
        st.local_used += 1
        self.remote = st.copy(src.at[0], place, st.take(1), st.peer("s", 0))

    def start(self):
        @pl.when(self.st.s == self.layer)
        def _():
            self.local.start()
            self.remote.start()

    def finish(self):
        @pl.when(self.st.s == self.layer)
        def _():
            self.local.wait()
            self.remote.wait_send()

        @pl.when(self.st.s != self.layer)
        def _():
            self.remote.wait_recv()


class Delivery:
    def __init__(self, st, layer, src, out):
        self.st, self.layer = st, layer
        mine = out.at[st.s]
        self.within = pltpu.make_async_copy(src, mine, st.lsem.at[st.local_used])
        st.local_used += 1
        self.over = st.copy(src, mine, st.take(1), st.peer("s", 0))
        pl.when(st.s == layer)(self.within.start)
        pl.when(st.s != layer)(self.over.start)

    def finish(self):
        @pl.when(self.st.s == self.layer)
        def _():
            self.within.wait()
            self.over.wait_recv()

        pl.when(self.st.s != self.layer)(self.over.wait_send)


class Local:
    def __init__(self, st, layer, pairs):
        self.st, self.layer = st, layer
        self.copies = [pltpu.make_async_copy(a, b, st.lsem.at[st.local_used + i]) for i, (a, b) in enumerate(pairs)]
        st.local_used += len(pairs)

        @pl.when(st.s == layer)
        def _():
            for c in self.copies:
                c.start()

    def wait(self):
        @pl.when(self.st.s == self.layer)
        def _():
            for c in self.copies:
                c.wait()


def half_rows(z, h, share):
    return pl.ds(pl.multiple_of(z * share + h * (share // 2), UNIT), share // 2)


def feed_attention(st, layer, qkv, out, dst):
    share = qkv.shape[1]
    rows = st.block(st.z, share)
    local = Local(st, layer, [(qkv.at[0], dst.at[rows, :QKV]), (out.at[0], dst.at[rows, QKV:])])
    whole = QKV + D
    split = whole // 4 * 3

    def feed(low, high):
        width = (high - low) // SIDE

        def piece(z, h, q):
            return dst.at[half_rows(z, h, share), pl.ds(pl.multiple_of(low + q * width, LANES), width)]

        def band(z, h):
            return dst.at[half_rows(z, h, share), low:high]

        return Feed(st, layer, lambda h, q, z_to: [(None, None)], piece, band)

    return local, feed(0, split), feed(split, whole)


def feed_windows(st, layer, gate, up, dst):
    share = gate.shape[1]
    pace = FF // st.nz // (LANES // 2)
    width = WIN // 2

    def window(z):
        return pl.multiple_of(z * pace // 2 * LANES, LANES)

    rows = st.block(st.z, share)
    local = Local(st, layer, [(w.at[0, :, pl.ds(window(st.z), WIN)], dst.at[i, rows, :]) for i, w in enumerate((gate, up))])

    def sources(h, q, z_to):
        at = pl.multiple_of(window(z_to) + lax.rem(q, 2) * width, LANES)
        part = slice(h * (share // 2), (h + 1) * (share // 2))
        return [(q < 2, gate.at[0, part, pl.ds(at, width)]), (q >= 2, up.at[0, part, pl.ds(at, width)])]

    def piece(z, h, q):
        return dst.at[q // 2, half_rows(z, h, share), pl.ds(pl.multiple_of(lax.rem(q, 2) * width, LANES), width)]

    def band(z, h):
        return dst.at[:, half_rows(z, h, share), :]

    return local, Feed(st, layer, sources, piece, band)


class Ring:
    def __init__(self, st, place, rows):
        self.st, self.place, self.rows = st, place, rows
        self.at = st.take(4)
        mine = place(st.z, 0, rows)
        self.near = st.begin([self.send(mine, i, way) for i, way in enumerate((1, -1))])

    def send(self, ref, i, way):
        return self.st.copy(ref, ref, self.at + i, self.st.peer("z", way))

    def pass_on(self):
        st, half = self.st, self.rows // 2
        arrived(self.near)
        self.far = st.begin(
            [
                self.send(self.place(st.along("z", -1), 0, half), 2, 1),
                self.send(self.place(st.along("z", 1), half, half), 3, -1),
            ]
        )

    def finish(self):
        arrived(self.far)


def arrived(copies):
    for c in copies:
        c.wait_recv()


def add_into(dst, parts):
    def one(i, c):
        total = parts[0][i].astype(F32)
        for p in parts[1:]:
            total = total + p[i].astype(F32)
        dst[i] = total.astype(dst.dtype)
        return c

    lax.fori_loop(0, dst.shape[0], one, 0)


def add_rows(dst, parts):
    total = parts[0][...].astype(F32)
    for p in parts[1:]:
        total = total + p[...].astype(F32)
    dst[...] = total.astype(dst.dtype)


def swapped_sum(st, copies, given, land):
    arrived(copies)
    for i in range(SIDE):
        add_into(land.at[i], [given.at[st.s, i], land.at[i]])


def sides(tile, chosen):
    half = HEAD_DIM
    low, high = tile[:half], tile[half:]
    zero = jnp.zeros_like(low)
    below = jnp.concatenate([jnp.where(chosen, low, zero), jnp.where(chosen, zero, high)], 1)
    return jnp.concatenate([jnp.concatenate([zero, low], 1), below], 0).astype(BF16)


def sides_t(tile_t, chosen):
    lane = lax.broadcasted_iota(jnp.int32, tile_t.shape, 1) < HEAD_DIM
    upper = jnp.where(jnp.logical_or(lane, jnp.logical_not(chosen)), 0.0, pltpu.roll(tile_t, HEAD_DIM, 1))
    lower = jnp.where(jnp.logical_or(lane, jnp.logical_not(chosen)), tile_t, 0.0)
    return jnp.concatenate([upper, lower], 0).astype(BF16)


def own_sides(tile):
    low, high = tile[:HEAD_DIM], tile[HEAD_DIM:]
    zero = jnp.zeros_like(low)
    rows = [[zero, low], [low, zero], [zero, high]]
    return jnp.concatenate([jnp.concatenate(p, 1) for p in rows], 0).astype(BF16)


def own_bias(width):
    key = lax.broadcasted_iota(jnp.int32, (HEAD_DIM, width), 0)
    query = lax.rem(lax.broadcasted_iota(jnp.int32, (HEAD_DIM, width), 1), HEAD_DIM)
    return jnp.where(key <= query, 0.0, NEG)


def earlier(pairs_ref, src, me, width):
    return pairs_ref[src, 0:1, :width] < pairs_ref[me, 0:1, :width]


def col_max(a):
    return jnp.max(a, 0, keepdims=True)


def col_sum(a):
    return jnp.sum(a, 0, keepdims=True)


class View:
    def __init__(self, r, layer):
        self.r, self.layer = r, layer

    def named(self, k):
        own = k + str(self.layer)
        return own if hasattr(self.r, own) else k

    def __getattr__(self, k):
        return getattr(self.r, self.named(k))

    def need(self, *names):
        self.r.need(*[self.named(k) for k in names])

    def flush(self, *names):
        self.r.flush(*[self.named(k) for k in names])


def forward_kernel(_, r):
    st = Stages(r)
    n, me = st.nc, st.c
    st.hail(st.beside() + st.upright(True), ring=True)
    r.load()
    wa, gu, down = [None, None], [None, None], [None, None]
    for l in range(2):
        v = View(r, l)
        wa[l] = feed_attention(st, l, r.qkv_shard, r.out_shard, v.wa)
        gu[l] = feed_windows(st, l, r.gate_shard, r.up_shard, v.gu)
        down[l] = FeedDown(st, l, r.down_shard, v.down)
    r.need("inverse", "x0")
    r.pairs[me] = jnp.full(r.pairs.shape[1:], r.pair[0], jnp.int32)
    at = 0
    for part, size in ((r.attn_gain, D), (r.ffn_gain, D), (r.qkv_bias, QKV)):
        share = part.shape[1]
        line = jnp.concatenate([part[...].astype(F32), jnp.zeros((1, size - share), F32)], 1)
        line = pltpu.roll(jnp.broadcast_to(line, (8, size)), st.z * share, 1)
        r.parts[st.s, st.z, :, at : at + size] = line[:1]
        at += size
    wa[0][0].wait()
    st.met()
    wa[0][1].start()
    wa[0][1].start_beside()
    at = st.take(2 * st.nz)
    mine = r.parts.at[st.s, st.z]
    st.begin(
        [st.copy(mine, mine, at + k, st.peer("z", k, st.s), at + st.s * st.nz + k) for k in range(1, st.nz)]
        + [st.copy(mine, mine, at + st.nz + k, st.peer("z", k, 1 - st.s), at + st.s * st.nz + k) for k in range(1, st.nz)]
        + [st.copy(mine, mine, at, st.peer("s", 0), at + st.s * st.nz)]
    )

    def tell(k, c):
        p = r.pairs.at[me]
        push(p, p, r.psem.at[k], r.psem2.at[k], "ctx", lax.rem(me + k, n)).start()
        return c

    lax.fori_loop(1, n, tell, 0)
    block = LANES // 2
    i = lax.broadcasted_iota(jnp.int32, (LANES, LANES), 0)
    pair = r.pairs[me, 0:1, :LANES]
    pos = jnp.where(i < block, pair * block + i, (2 * n - 1 - pair) * block + i - block)
    angle = pos.astype(F32) * r.inverse[...]
    lane = lax.rem(lax.broadcasted_iota(jnp.int32, (LANES, LANES), 1), HEAD_DIM)
    sine = jnp.sin(angle)
    r.cos[...] = jnp.cos(angle)
    r.sa[...] = jnp.where(lane < HEAD_DIM // 2, -sine, 0.0)
    r.sb[...] = jnp.where(lane < HEAD_DIM // 2, 0.0, sine)
    r.flush("cos", "sa", "sb")
    for h in (st.s, 1 - st.s):
        for k in range(st.nz):
            if h is st.s and k == 0:
                continue
            st.copy(mine, mine, at, st.peer("s", 0), at + h * st.nz + k).wait_recv()
    for h in range(2):
        total = r.parts[h, 0]
        for k in range(1, st.nz):
            total = total + r.parts[h, k]
        r.small[h] = total
    r.flush("small")
    for k in ORDER:
        wa[0][1].relay(k)
    wa[0][2].start()
    gu[0][0].wait()
    gu[0][1].start()
    for k in ORDER:
        wa[0][1].collect(k)
    wa[0][2].start_beside()
    gu[0][1].start_beside()
    down[0].start()

    def begin_next():
        wa[1][0].wait()
        gu[1][0].wait()
        for feed in (wa[1][1], wa[1][2], gu[1][1]):
            feed.start()

    def besides_next():
        for feed in (wa[1][1], wa[1][2], gu[1][1]):
            feed.start_beside()
        down[1].start()

    def relays(*steps):
        def go():
            for feed, name, k in steps:
                getattr(feed, name)(k)

        return go

    g0, w0, w1, w2, g1 = gu[0][1], wa[0][2], wa[1][1], wa[1][2], gu[1][1]
    wa[0][1].finish()
    v = View(r, 0)

    def out_ready():
        w0.finish()
        v.flush("wa")

    nothing = lambda: None
    ahead = relays((w0, "relay", 1), (w0, "relay", 3), (w0, "relay", 2), (g0, "relay", 1), (g0, "relay", 3))
    attention_forward(
        st, v, 0,
        (
            lambda: (ahead(), begin_next()),
            relays((g0, "relay", 2), (w0, "collect", 1), (w0, "collect", 3), (w0, "collect", 2)),
            nothing,
            nothing,
            out_ready,
        ),
    )

    def ready_0():
        relays((g0, "collect", 1), (g0, "collect", 3), (g0, "collect", 2))()
        g0.finish()
        down[0].finish()
        v.flush("gu", "down")

    first = relays((w1, "relay", 1), (w1, "relay", 3), (w1, "relay", 2))
    ffn_forward(
        st, v, ready_0,
        (
            lambda: (besides_next(), first()),
            relays((w2, "relay", 1), (w2, "relay", 3), (w2, "relay", 2), (g1, "relay", 1), (g1, "relay", 3)),
            relays((g1, "relay", 2), (w1, "collect", 1), (w1, "collect", 3), (w1, "collect", 2)),
            relays((w2, "collect", 1), (w2, "collect", 3), (w2, "collect", 2)),
        ),
    )
    r.x1[...] = r.y0[...].astype(BF16).astype(F32)
    r.flush("x1")
    done_0 = Delivery(st, 0, r.y0, r.layer_out)
    r.need("gy")
    tok = r.gy.shape[0]
    rows = st.block(st.z, tok)
    r.gy_all[rows, :] = r.gy[...].astype(BF16)
    at = st.take(st.nz - 1)
    mine_gy = r.gy_all.at[rows, :]
    gy_moving = st.begin([st.copy(mine_gy, mine_gy, at + k - 1, st.peer("z", k)) for k in range(1, st.nz)])
    w1.finish()
    w2.finish()
    v = View(r, 1)
    v.flush("wa")
    attention_forward(
        st, v, 1,
        (nothing, relays((g1, "collect", 1)), relays((g1, "collect", 3)), relays((g1, "collect", 2)), nothing),
    )

    def ready_1():
        g1.finish()
        down[1].finish()
        v.flush("gu", "down")

    ffn_forward(st, v, ready_1, (nothing,) * 4)
    done_1 = Delivery(st, 1, r.y1, r.layer_out)
    arrived(gy_moving)
    r.flush("gy_all")
    done_0.finish()
    done_1.finish()
    st.drain()

    def done(k, c):
        p = r.pairs.at[me]
        push(p, p, r.psem.at[k], r.psem2.at[k], "ctx", lax.rem(me + k, n)).wait_send()
        return c

    lax.fori_loop(1, n, done, 0)
    r.close()


def attention_forward(st, r, layer, between):
    n, me = st.nc, st.c
    x = r.x[...]
    r1 = lax.rsqrt(jnp.mean(x * x, -1, keepdims=True) + EPS)
    small = r.small[layer]
    n1_f = x * r1 * small[:, :D]
    n1 = n1_f.astype(BF16)
    bias = small[:, 2 * D :]
    cos, sa, sb = r.cos[...], r.sa[...], r.sb[...]
    lin = mm(n1, r.wa[:, D:QKV]) + bias[:, D:]
    r.kv[me] = jnp.concatenate([rope(lin[:, :LANES], cos, sa, sb), lin[:, LANES:]], 1).astype(BF16)

    def keys_copy(k, src):
        return push(r.kv.at[src], r.kv.at[src], r.csem.at[k], r.csem2.at[k], "ctx", lax.rem(me + k, n))

    def start(k, c):
        keys_copy(k, me).start()
        return c

    lax.fori_loop(1, n, start, 0)
    linq = mm(n1, r.wa[:, :D]) + bias[:, :D]
    for t in range(TILES):
        tile = slice(t * LANES, (t + 1) * LANES)
        q = rope(linq[:, tile], cos, sa, sb) * HEAD_DIM ** (-0.5)
        spread(r.qst, t, q.T)
        r.n1t[tile, :] = n1_f[:, tile].T.astype(BF16)
    r.flush("qst", "n1t")
    between[0]()
    half = HEAD_DIM
    own_k = own_sides(r.kv[me, :, :LANES].astype(F32))
    own_vt = own_sides(r.kv[me, :, LANES:].astype(F32)).astype(F32).T.astype(BF16)
    for cols in GROUPS:
        width = cols.stop - cols.start
        bias = own_bias(width)
        sc = mm(own_k, r.qst[:, cols])
        s_a, s_l, s_h = sc[:half], sc[half : 2 * half] + bias, sc[2 * half :] + bias
        m_lo = col_max(s_l)
        m_hi = jnp.maximum(col_max(s_a), col_max(s_h))
        p_a, p_l, p_h = jnp.exp(s_a - m_hi), jnp.exp(s_l - m_lo), jnp.exp(s_h - m_hi)
        r.m_s[0:1, cols], r.m_s[1:2, cols] = m_lo, m_hi
        r.l_s[0:1, cols], r.l_s[1:2, cols] = col_sum(p_l), col_sum(p_a) + col_sum(p_h)
        r.acc_s[:, cols] = mm(own_vt, jnp.concatenate([p_a, p_l, p_h], 0).astype(BF16))

    def step(i, c):
        kx, vt, sel = [], [], []
        for j in range(BATCH):
            k = i * BATCH + 1 + j
            src = lax.rem(me + n - k, n)
            keys_copy(k, src).wait_recv()
            if layer == 0:
                p = r.pairs.at[src]
                push(p, p, r.psem.at[k], r.psem2.at[k], "ctx", lax.rem(me + k, n)).wait_recv()
            sel.append(src)
            chosen = earlier(r.pairs, src, me, LANES)
            kx.append(sides(r.kv[src, :, :LANES].astype(F32), chosen))
            vt.append(sides_t(r.kv[src, :, LANES:].astype(F32).T, chosen))
        kx = jnp.concatenate(kx, 0)
        vt = jnp.concatenate(vt, 1)
        for cols in GROUPS:
            width = cols.stop - cols.start
            sc = mm(kx, r.qst[:, cols])
            m_lo, m_hi = r.m_s[0:1, cols], r.m_s[1:2, cols]
            n_lo, n_hi = m_lo, m_hi
            chosen = [earlier(r.pairs, src, me, width) for src in sel]
            for j in range(BATCH):
                top = col_max(sc[(2 * j + 1) * half : (2 * j + 2) * half])
                n_hi = jnp.maximum(n_hi, col_max(sc[2 * j * half : (2 * j + 1) * half]))
                n_hi = jnp.where(chosen[j], n_hi, jnp.maximum(n_hi, top))
                n_lo = jnp.where(chosen[j], jnp.maximum(n_lo, top), n_lo)
            a_lo, a_hi = jnp.exp(m_lo - n_lo), jnp.exp(m_hi - n_hi)
            l_lo, l_hi = r.l_s[0:1, cols] * a_lo, r.l_s[1:2, cols] * a_hi
            ps = []
            for j in range(BATCH):
                p_a = jnp.exp(sc[2 * j * half : (2 * j + 1) * half] - n_hi)
                p_s = jnp.exp(sc[(2 * j + 1) * half : (2 * j + 2) * half] - jnp.where(chosen[j], n_lo, n_hi))
                total = col_sum(p_s)
                l_hi = l_hi + col_sum(p_a) + jnp.where(chosen[j], 0.0, total)
                l_lo = l_lo + jnp.where(chosen[j], total, 0.0)
                ps += [p_a.astype(BF16), p_s.astype(BF16)]
            r.m_s[0:1, cols], r.m_s[1:2, cols] = n_lo, n_hi
            r.l_s[0:1, cols], r.l_s[1:2, cols] = l_lo, l_hi
            new = mm(vt, jnp.concatenate(ps, 0))
            r.acc_s[:LANES, cols] = r.acc_s[:LANES, cols] * a_lo + new[:LANES]
            r.acc_s[LANES:, cols] = r.acc_s[LANES:, cols] * a_hi + new[LANES:]
        return c

    lax.fori_loop(0, 1, step, 0)
    between[1]()
    lax.fori_loop(1, 2, step, 0)
    between[2]()
    lax.fori_loop(2, 4, step, 0)
    between[3]()
    lax.fori_loop(4, (n - 1) // BATCH, step, 0)
    between[4]()
    r.flush("kv")
    if layer == 0:
        r.flush("pairs")
    r.lse[...] = r.m_s[...] + jnp.log(r.l_s[...])
    for t in range(TILES):
        cols = slice(t * LANES, (t + 1) * LANES)
        wide = jnp.concatenate([r.acc_s[:LANES, cols] / r.l_s[0:1, cols], r.acc_s[LANES:, cols] / r.l_s[1:2, cols]], 0)
        tile_t = gathered_tile(wide, t)
        r.attt[cols, :] = tile_t.astype(BF16)
        r.att_s[:, cols] = tile_t.T.astype(BF16)
    r.flush("lse", "attt")
    mid = x + mm(r.att_s[...], r.wa[:, QKV:])
    r.mid[...] = mid
    r2 = lax.rsqrt(jnp.mean(mid * mid, -1, keepdims=True) + EPS)
    r.all[st.z] = (mid * r2 * small[:, D : 2 * D]).astype(BF16)
    r.flush("mid")

    def done(k, c):
        keys_copy(k, me).wait_send()
        return c

    lax.fori_loop(1, n, done, 0)


def ffn_forward(st, r, ready, between):
    n, me = st.nz, st.z
    tok = r.mid.shape[0]
    at = st.take(n)

    def second(k):
        return st.copy(r.send_s.at[k], r.land_s.at[k], at + k, st.peer("z", -k))

    ring = Ring(st, lambda z, row, rows: r.all.at[z, row : row + rows, :], tok)
    ready()

    def block(sources):
        a = jnp.concatenate([r.all[i] for i in sources], 0) if len(sources) > 1 else r.all[sources[0]]
        gate = mm(a, r.gu[0])
        up = mm(a, r.gu[1])
        for j, i in enumerate(sources):
            r.gate[i] = gate[j * tok : (j + 1) * tok].astype(BF16)
            r.up[i] = up[j * tok : (j + 1) * tok].astype(BF16)
        hidden = (gate * jax.nn.sigmoid(gate) * up).astype(BF16)
        return mm(hidden, r.down[...])

    r.y[...] = r.mid[...] + block([me])
    between[0]()
    ring.pass_on()
    both = block([st.along("z", -1), st.along("z", -3)]).astype(BF16)
    for i, k in enumerate((1, 3)):
        r.send_s[k] = both[i * tok : (i + 1) * tok]
        second(k).start()
    between[1]()
    ring.finish()
    r.send_s[2] = block([st.along("z", -2)]).astype(BF16)
    second(2).start()
    between[2]()
    r.flush("all", "gate", "up")
    between[3]()
    for k in ORDER:
        second(k).wait_recv()
        r.y[...] += r.land_s[k].astype(F32)
    for k in ORDER:
        second(k).wait_send()


class Attention:
    def __init__(self, st):
        self.st = st

    def columns(self, src, dst):
        st = self.st
        share = dst.shape[0]
        at = st.take(st.nz - 1)
        mine = dst.at[:, pl.ds(pl.multiple_of(st.z * LANES, LANES), LANES)]
        moving = st.begin(
            [
                st.copy(src.at[st.block(st.along("z", k), share), :], mine, at + k - 1, st.peer("z", k))
                for k in range(1, st.nz)
            ]
        )
        mine[...] = src[st.block(st.z, share), :]
        return moving

    def whole(self, dst, cols=slice(None)):
        st = self.st
        rows = dst.shape[0] // st.nz
        at = st.take(st.nz - 1)
        mine = dst.at[pl.ds(pl.multiple_of(st.z * rows, UNIT), rows), cols]
        return st.begin([st.copy(mine, mine, at + k - 1, st.peer("z", k)) for k in range(1, st.nz)])

    def begin(self, glin, small, all_glin, all_small):
        st = self.st
        tok = glin.shape[0]
        all_glin[st.block(st.z, tok), :] = glin[...]
        all_small[st.block(st.z, 2 * UNIT), :] = small[...]
        return self.whole(all_glin) + self.whole(all_small)

    def swap(self, moving, n1z, all_glin, all_small, dout, made, land):
        st = self.st
        arrived(moving)
        share = n1z.shape[0]
        per = 8
        for j in range(0, QKV // LANES, 2):
            cols = slice(j * LANES, min(j + 2, QKV // LANES) * LANES)
            d = mm(n1z[...], all_glin[:, cols]).astype(BF16)
            for t in range(j, min(j + 2, QKV // LANES)):
                made[t // per, (t % per) * share : (t % per + 1) * share, :] = d[:, (t - j) * LANES : (t - j + 1) * LANES]
        made[1, share : 8 * share, :] = dout[...]
        small = jnp.zeros((2 * UNIT, LANES), F32)
        for i in range(st.nz):
            small = small + all_small[i * 2 * UNIT : (i + 1) * 2 * UNIT, :]
        made[0, 8 * share : 8 * share + 2 * UNIT, :] = small.astype(BF16)
        made[0, 8 * share + 2 * UNIT :, :] = jnp.zeros((Q_ROWS - 8 * share - 2 * UNIT, LANES), BF16)
        made[1, 8 * share :, :] = jnp.zeros((Q_ROWS - 8 * share, LANES), BF16)
        return st.swap(made, land)

    def fold(self, moving, made, land, out):
        st = self.st
        arrived(moving)
        rows = Q_ROWS // 2 // 16
        for h in range(2):
            for i in range(16):
                at = slice((h * 16 + i) * rows, (h * 16 + i + 1) * rows)
                total = made[st.s, at, :].astype(F32) + land[at, :].astype(F32)
                out[h][i // SIDE, i % SIDE] = total.astype(BF16)


class Rest:
    def __init__(self, st, t1, l2, t2, g1, out, layer):
        self.st, self.t1, self.l2, self.t2, self.g1, self.out, self.layer = st, t1, l2, t2, g1, out, layer
        self.stage = 0
        self.moving = [st.scatter(AXES[h][1], t1[h], l2[h]) for h in range(2)]

    def advance(self):
        st = self.st
        for h in range(2):
            second = AXES[h][1]
            arrived(self.moving[h])
            mine = self.g1[h].at[st.along(second, 0)]
            if self.stage == 0:
                t2 = self.t2[h]
                add_rows(t2, [self.t1[h].at[st.along(second, 0)]] + [self.l2[h].at[k] for k in range(SIDE - 1)])
                per = GATE_PER[h] * UNIT
                self.moving[h] = st.deal(t2, mine, per)
                mine[st.block(st.z, per), :] = t2[st.block(st.z, per), :]
                mine[st.nz * per :, :] = t2[st.nz * per :, :]
            elif self.stage == 1:
                self.moving[h] = st.gather(second, self.g1[h])
        if self.stage == 2:
            self.ends = []
            self.open = []
            self.give(slice(0, SIDE // 2))
        self.stage += 1

    def give(self, part):
        made = [self.st.hand_over(AXES[h][0], self.g1[h], self.out[h], self.layer, part) for h in range(2)]
        self.ends += made
        self.open += made

    def relay(self, count=None):
        for one in self.open[:count]:
            one.relay()
        self.open = self.open[count:] if count else []

    def finish(self):
        for one in self.ends:
            one.finish()


class Few:
    def __init__(self, st, r, tag):
        self.st = st

        def both(name):
            return tuple(getattr(r, name + tag + h) for h in "ab")

        self.qp, self.land, self.part, self.land2, self.wide = both("qp"), both("qm"), both("qe"), both("qw"), both("qh")
        self.moving = [st.scatter(AXES[h][0], self.qp[h], self.land[h]) for h in range(2)]

    def second_sum(self):
        st = self.st
        for h in range(2):
            arrived(self.moving[h])
            own = self.qp[h].at[st.along(AXES[h][0], 0)]
            add_into(self.part[h], [own] + [self.land[h].at[k] for k in range(SIDE - 1)])
            self.moving[h] = st.scatter(AXES[h][1], self.part[h], self.land2[h])

    def first_gather(self):
        st = self.st
        for h in range(2):
            arrived(self.moving[h])
            i = st.along(AXES[h][1], 0)
            add_rows(self.wide[h].at[i], [self.part[h].at[i]] + [self.land2[h].at[k] for k in range(SIDE - 1)])
            self.moving[h] = st.gather(AXES[h][1], self.wide[h])

    def hand_over(self, out, layer):
        for h in range(2):
            arrived(self.moving[h])
        return [self.st.hand_over(AXES[h][0], self.wide[h], out[h], layer) for h in range(2)]


def backward_kernel(layer, r):
    st = Stages(r)
    n, me = st.nz, st.z
    carry = layer == 0
    ids = st.upright() + st.beside()
    if carry:
        ids += [st.peer(a, k, 1 - st.s) for a in "xy" for k in range(1, SIDE)]
    st.hail(ids, ring=True)
    r.load()
    tok = r.gy.shape[0]

    def rows_of(i):
        return pl.ds(pl.multiple_of(i * tok, tok), tok)

    r.need("gy")
    gyb = r.gy[...].astype(BF16)
    gy = gyb.astype(F32) if carry else r.gy[...]
    above = None
    if carry:
        r.all_s[rows_of(me), :] = gyb
    else:
        r.need("all_s")
    st.met()
    at = st.take(2 * n)

    def second(k):
        return st.copy(r.send_s.at[k], r.land_s.at[k], at + n + k, st.peer("z", -k))

    if carry:
        ring = Ring(st, lambda z, row, rows: r.all_s.at[pl.ds(pl.multiple_of(z * tok + row, UNIT), rows), :], tok)
        above = Delivery(st, 1, r.gy, r.input_grad)
        r.need("p1a", "p1b")
        rest = Rest(st, (r.p1a, r.p1b), (r.l2a, r.l2b), (r.t2a, r.t2b), (r.g1a, r.g1b), (r.ga, r.gb), 1)
    r.need("down", "gate", "up", "gu")

    def block(sources):
        def stacked(ref):
            parts = [ref[rows_of(i), :] for i in sources]
            return jnp.concatenate(parts, 0) if len(parts) > 1 else parts[0]

        def picked(ref):
            parts = [ref[i].astype(F32) for i in sources]
            return jnp.concatenate(parts, 0) if len(parts) > 1 else parts[0]

        def keep(ref, value):
            for j, i in enumerate(sources):
                ref[rows_of(i), :] = value[j * tok : (j + 1) * tok]

        gh = mm_nt(stacked(r.all_s), r.down[...])
        gate, up = picked(r.gate), picked(r.up)
        sg = jax.nn.sigmoid(gate)
        act = gate * sg
        keep(r.hid_s, (act * up).astype(BF16))
        ggate = (gh * up * sg * (1.0 + gate * (1.0 - sg))).astype(BF16)
        gup = (gh * act).astype(BF16)
        keep(r.g_s.at[0], ggate)
        keep(r.g_s.at[1], gup)
        return mm_nt(ggate, r.gu[0]) + mm_nt(gup, r.gu[1])

    r.own_s[...] = block([me])
    if carry:
        rest.advance()
        ring.pass_on()
    both = block([st.along("z", -1), st.along("z", -3)]).astype(BF16)
    for i, k in enumerate((1, 3)):
        r.send_s[k] = both[i * tok : (i + 1) * tok]
        second(k).start()
    if carry:
        rest.advance()
        ring.finish()
    r.send_s[2] = block([st.along("z", -2)]).astype(BF16)
    second(2).start()
    attention = Attention(st)
    before = None
    if carry:
        r.need("glin1", "gsmall1")
        before = attention.begin(r.glin1, r.gsmall1, r.all_glin, r.all_small)
        rest.advance()

    late = [
        pltpu.make_async_copy(r.wa.at[:, :QKV], r.gu.at[0, :, :QKV], st.lsem.at[st.local_used]),
        pltpu.make_async_copy(r.wa.at[:, QKV:], r.gu.at[1, :, :D], st.lsem.at[st.local_used + 1]),
    ]
    st.local_used += 2
    for c in late:
        c.start()
    refs = (r.fa, r.fb)
    share = D // n
    for j in range(WIN // (2 * LANES)):
        cols = slice(2 * j * LANES, 2 * (j + 1) * LANES)
        r.down[cols, :] = mm_tn(r.hid_s[:, cols], r.all_s[...]).astype(BF16)
    pad = (WIN - FF // n) * lax.rem(me, 2)
    half = FF // n // 2
    base = [n * per * UNIT for per in GATE_PER]
    for section in range(2):
        rows = r.down[pl.ds(pl.multiple_of(pad + section * half, UNIT), half), :]
        for t in range(TILES):
            put_units(refs, section, base, DOWN_PER, t * (half // UNIT), rows[:, t * LANES : (t + 1) * LANES])
        used = TILES * (half // UNIT)
        extra = 16 * sum(DOWN_PER) - used
        put_units(refs, section, base, DOWN_PER, used, jnp.zeros((extra * UNIT, LANES), BF16))
    if carry:
        rest.give(slice(SIDE // 2, SIDE))
    r.need("n2_all")
    normed = jnp.concatenate([r.n2_all[i] for i in range(n)], 0)

    def product(section):
        for j in range(WIN // (2 * LANES)):
            d = mm_tn(normed, r.g_s[section, :, 2 * j * LANES : 2 * (j + 1) * LANES]).astype(BF16)
            for t in (2 * j, 2 * j + 1):
                tile = d[:, (t % 2) * LANES : (t % 2 + 1) * LANES]
                for i in range(n):
                    base = [i * per * UNIT for per in GATE_PER]
                    put_units(refs, section, base, GATE_PER, t * (share // UNIT), tile[i * share : (i + 1) * share, :])
        used = WIN // LANES * (share // UNIT)
        extra = 16 * sum(GATE_PER) - used
        for i in range(n):
            base = [i * per * UNIT for per in GATE_PER]
            put_units(refs, section, base, GATE_PER, used, jnp.zeros((extra * UNIT, LANES), BF16))

    product(1 - st.s)
    if carry:
        rest.relay(2)
    swaps = [st.swap(refs[h], (r.sla, r.slb)[h]) for h in range(2)]
    product(st.s)
    r1 = []
    if carry:
        for h in range(2):
            swapped_sum(st, swaps[h], refs[h], (r.sla, r.slb)[h])
            r1.append(Scatter(st, AXES[h][0], (r.sla, r.slb)[h], (r.l1a, r.l1b)[h]))
    for k in ORDER:
        second(k).wait_recv()
        r.own_s[...] += r.land_s[k].astype(F32)
    gn2 = r.own_s[...]
    r.need("mid", "small")
    mid = r.mid[...]
    r2 = lax.rsqrt(jnp.mean(mid * mid, -1, keepdims=True) + EPS)
    unit = mid * r2
    dg2 = col_sum(gn2 * unit)
    dz = gn2 * r.small[layer][:, D : 2 * D]
    gm = gy + r2 * (dz - unit * jnp.mean(dz * unit, -1, keepdims=True))
    r.gm_s[...] = gm
    for k in ORDER:
        second(k).wait_send()
    attention_backward(st, r, layer, gm, dg2, refs, swaps, rest if carry else None, above, late, attention, before, r1)


def attention_backward(st, r, layer, gm, dg2, refs, swaps, rest, above, late, attention, before, r1):
    n, me = st.nc, st.c
    last = layer == 0
    half = HEAD_DIM
    gmb = gm.astype(BF16)
    tok = gm.shape[0]
    r.all_gm[st.block(st.z, tok), :] = gmb
    sl, l1, t1 = (r.sla, r.slb), (r.l1a, r.l1b), (r.t1a, r.t1b)
    r.need("attt", "n1t")
    size = 2 * BATCH * half
    pr, ds, gst = r.g_s.at[0, :size, :WIDE], r.g_s.at[1, :size, :WIDE], r.hid_s.at[: 2 * LANES, :WIDE]
    out_factors = attention.whole(r.all_gm) + attention.columns(r.attt, r.attz)
    qkv_factor = attention.columns(r.n1t, r.n1z)
    if not last:
        for h in range(2):
            swapped_sum(st, swaps[h], refs[h], sl[h])
            r1.append(Scatter(st, AXES[h][0], sl[h], l1[h]))
    r.need("qst", "lse", "kv", "pairs")
    for c in late:
        c.wait()
    ga = mm_nt(gmb, r.gu[1, :, :D])
    for t in range(TILES):
        tile = slice(t * LANES, (t + 1) * LANES)
        ga_t = ga[:, tile].T
        spread(gst, t, ga_t)
        prod = ga_t * r.attt[tile, :].astype(F32)
        low, high = halves(col_sum(prod[:half]), col_sum(prod[half:]))
        r.delta_s[0:1, tile], r.delta_s[1:2, tile] = low, high

    def own_block():
        keys, vals = r.kv[me, :, :LANES].astype(F32), r.kv[me, :, LANES:].astype(F32)
        kx, vx = own_sides(keys), own_sides(vals)
        kt = kx.astype(F32).T.astype(BF16)
        rows = slice(0, 3 * half)
        for cols in GROUPS:
            bias = own_bias(cols.stop - cols.start)
            sc = mm(kx, r.qst[:, cols])
            dp = mm(vx, gst[:, cols])
            lo, hi = (r.lse[0:1, cols], r.delta_s[0:1, cols]), (r.lse[1:2, cols], r.delta_s[1:2, cols])
            parts = [(sc[:half], hi), (sc[half : 2 * half] + bias, lo), (sc[2 * half :] + bias, hi)]
            for i, (part, (lse, delta)) in enumerate(parts):
                p = jnp.exp(part - lse)
                at = slice(i * half, (i + 1) * half)
                pr[at, cols] = p.astype(BF16)
                ds[at, cols] = (p * (dp[at] - delta)).astype(BF16)
            r.gq_s[:, cols] = mm(kt, ds[rows, cols])
        made = []
        for w, q in ((ds, r.qst), (pr, gst)):
            e = mm_nt(w[rows, :], q[...])
            low = e[:half, LANES:] + e[half : 2 * half, :LANES]
            made.append(jnp.concatenate([low, e[2 * half :, LANES:]], 0))
        return jnp.concatenate(made, 1)

    def sum_copy(k):
        return push(r.send_k.at[k], r.land_k.at[k], r.csem.at[k], r.csem2.at[k], "ctx", lax.rem(me + k, n))

    def step(i):
        kx, vx, kt, sel = [], [], [], []
        for j in range(BATCH):
            src = lax.rem(me + i * BATCH + 1 + j, n)
            sel.append(src)
            chosen = earlier(r.pairs, src, me, LANES)
            keys = r.kv[src, :, :LANES].astype(F32)
            kx.append(sides(keys, chosen))
            vx.append(sides(r.kv[src, :, LANES:].astype(F32), chosen))
            kt.append(sides_t(keys.T, chosen))
        kx, vx, kt = jnp.concatenate(kx, 0), jnp.concatenate(vx, 0), jnp.concatenate(kt, 1)
        rows = slice(0, 2 * BATCH * half)
        for cols in GROUPS:
            width = cols.stop - cols.start
            sc = mm(kx, r.qst[:, cols])
            dp = mm(vx, gst[:, cols])
            for j in range(BATCH):
                chosen = earlier(r.pairs, sel[j], me, width)
                for part in range(2):
                    lse, delta = r.lse[1:2, cols], r.delta_s[1:2, cols]
                    if part:
                        lse = jnp.where(chosen, r.lse[0:1, cols], lse)
                        delta = jnp.where(chosen, r.delta_s[0:1, cols], delta)
                    at = slice((2 * j + part) * half, (2 * j + part + 1) * half)
                    p = jnp.exp(sc[at] - lse)
                    pr[at, cols] = p.astype(BF16)
                    ds[at, cols] = (p * (dp[at] - delta)).astype(BF16)
            r.gq_s[:, cols] += mm(kt, ds[rows, cols])
        ek = mm_nt(ds[rows, :], r.qst[...])
        ev = mm_nt(pr[rows, :], gst[...])
        for j in range(BATCH):
            chosen = earlier(r.pairs, sel[j], me, LANES)
            k = i * BATCH + 1 + j
            for e, lanes in ((ek, slice(0, LANES)), (ev, slice(LANES, 2 * LANES))):
                top = e[2 * j * half : (2 * j + 1) * half]
                low = e[(2 * j + 1) * half : (2 * j + 2) * half]
                r.send_k[k, :half, lanes] = (top[:, LANES:] + jnp.where(chosen, low[:, :LANES], 0.0)).astype(BF16)
                r.send_k[k, half:, lanes] = jnp.where(chosen, 0.0, low[:, LANES:]).astype(BF16)
            sum_copy(k).start()

    own = own_block()
    for i in range((n - 1) // BATCH):
        step(i)
        if i == 0:
            for one in r1:
                one.pass_on()
            if last:
                rest.relay()

    def out_gradient():
        arrived(out_factors)
        share = D // st.nz
        for j in range(0, TILES, 2):
            cols = slice(j * LANES, min(j + 2, TILES) * LANES)
            d = mm(r.attz[...], r.all_gm[:, cols]).astype(BF16)
            for t in range(j, min(j + 2, TILES)):
                r.dout[t * share : (t + 1) * share, :] = d[:, (t - j) * LANES : (t - j + 1) * LANES]

    glin = r.zglin.at[st.block(st.z, tok), :] if last else r.glin
    if last:
        for h in range(2):
            r1[h].sum_into(t1[h])
        own_rest = Rest(st, t1, (r.l2c, r.l2d), (r.t2c, r.t2d), (r.g1c, r.g1d), (r.ha, r.hb), 0)
    r.need("cos", "sa", "sb", "x", "small")
    cos, sa, sb = r.cos[...], r.sa[...], r.sb[...]
    for t in range(TILES):
        gq = gathered_tile(r.gq_s[:, t * LANES : (t + 1) * LANES], t).T * HEAD_DIM ** (-0.5)
        glin[:, t * LANES : (t + 1) * LANES] = unrope(gq, cos, sa, sb).astype(BF16)
    if last:
        factors = attention.whole(r.zglin, slice(0, D))
        r.need("n1z1", "dout1")
        qswap = attention.swap(before, r.n1z1, r.all_glin, r.all_small, r.dout1, r.qv, r.ql)
        own_rest.advance()
        attention.fold(qswap, r.qv, r.ql, (r.qpa, r.qpb))
        few = Few(st, r, "")
    else:
        out_gradient()
        arrived(qkv_factor)
        r.flush("dout", "n1z")

    def take(k, total):
        sum_copy(k).wait_recv()
        return total + r.land_k[k].astype(F32)

    own = lax.fori_loop(1, n, take, own)
    glin[:, D : D + LANES] = unrope(own[:, :LANES], cos, sa, sb).astype(BF16)
    glin[:, D + LANES :] = own[:, LANES:].astype(BF16)
    if last:
        factors += attention.whole(r.zglin, slice(D, QKV))
        own_rest.advance()
        few.second_sum()
    else:
        r.flush("glin")
    gn1 = mm_nt(glin[...], r.gu[0, :, :QKV])
    x = r.x[...]
    r1_ = lax.rsqrt(jnp.mean(x * x, -1, keepdims=True) + EPS)
    unit = x * r1_
    dg1 = col_sum(gn1 * unit)
    dbias = col_sum(glin[...].astype(F32))
    gsmall = r.zsmall.at[st.block(st.z, 2 * UNIT), :] if last else r.gsmall
    gsmall[...] = jnp.zeros(gsmall.shape, F32)
    row = 0
    for part in (dg1, dg2, dbias):
        for t in range(part.shape[1] // LANES):
            gsmall[row : row + 1, :] = part[:, t * LANES : (t + 1) * LANES]
            row += 1
    if last:
        factors += attention.whole(r.zsmall)
        own_rest.advance()
        few.first_gather()
    else:
        r.flush("gsmall")
    dz = gn1 * r.small[layer][:, :D]
    r.gx[...] = r.gm_s[...] + r1_ * (dz - unit * jnp.mean(dz * unit, -1, keepdims=True))
    if last:
        below = Delivery(st, 0, r.gx, r.input_grad)
        out = (r.qa, r.qb)
        out_gradient()
        arrived(qkv_factor)
        zswap = attention.swap(factors, r.n1z, r.zglin, r.zsmall, r.dout, r.zv, r.zl)
        own_rest.relay()
        attention.fold(zswap, r.zv, r.zl, (r.qp0a, r.qp0b))
        last_few = Few(st, r, "0")
        own_rest.give(slice(SIDE // 2, SIDE))
        ends = few.hand_over(out, 1)
        last_few.second_sum()
        own_rest.relay()
        for end in ends:
            end.relay()
        last_few.first_gather()
        final = last_few.hand_over(out, 0)
        rest.finish()
        for end in final:
            end.relay()
        for end in ends:
            end.finish()
        own_rest.finish()
        for end in final:
            end.finish()
        above.finish()
        below.finish()
    else:
        for h in range(2):
            r1[h].sum_into(t1[h])
    st.drain()

    def done(k, c):
        sum_copy(k).wait_send()
        return c

    lax.fori_loop(1, n, done, 0)
    r.close()


class Refs(types.SimpleNamespace):
    def load(self):
        for c in self.coming.values():
            c.start()

    def need(self, *names):
        for k in names:
            if k not in self.here:
                self.coming[k].wait()
                self.here.add(k)

    def flush(self, *names):
        for k in names:
            self.going[k].start()
            self.gone.add(k)

    def close(self):
        self.need(*self.coming)
        self.flush(*[k for k in self.going if k not in self.gone])
        for c in self.going.values():
            c.wait()


def call(kernel, layer, cid, name, ins, outs, scratch, sems, hbm=(), flops=10**10, picked=(), whole=(), scalars=()):
    staged = [k for k in ins if k not in hbm + whole + scalars]
    made = [k for k in outs if k not in hbm]
    dma = pltpu.SemaphoreType.DMA
    counts = dict(ssem=sems, rsem=sems, lsem=20, csem=16, csem2=16, psem=16, psem2=16, isem=len(staged), osem=len(made))
    if name == "forward":
        counts.update(csem1=16, csem21=16)
    places = [pltpu.VMEM(ins[k].shape[2 if k in picked else 0 :], ins[k].dtype) for k in staged] + [pltpu.VMEM(*outs[k]) for k in made]
    names = ["in_" + k for k in ins] + ["out_" + k for k in outs] + staged + made + list(scratch) + list(counts)

    def body(*refs):
        r = Refs(**dict(zip(names, refs)))
        for k in hbm + whole + scalars:
            if k in ins or k in outs:
                setattr(r, k, getattr(r, ("in_" if k in ins else "out_") + k))
        r.here, r.gone = set(), set()
        def source(k):
            ref = getattr(r, "in_" + k)
            return ref.at[lax.axis_index("section"), 0] if k in picked else ref

        r.coming = {k: pltpu.make_async_copy(source(k), getattr(r, k), r.isem.at[i]) for i, k in enumerate(staged)}
        r.going = {
            k: pltpu.make_async_copy(getattr(r, k), getattr(r, "out_" + k), r.osem.at[i]) for i, k in enumerate(made)
        }
        kernel(layer, r)

    anywhere = pl.BlockSpec(memory_space=pl.ANY)
    places_in = {k: pl.BlockSpec(memory_space=pltpu.VMEM) for k in whole}
    places_in.update({k: pl.BlockSpec(memory_space=pltpu.SMEM) for k in scalars})
    got = pl.pallas_call(
        body,
        out_shape=[jax.ShapeDtypeStruct(s, t) for s, t in outs.values()],
        in_specs=[places_in.get(k, anywhere) for k in ins],
        out_specs=[anywhere] * len(outs),
        scratch_shapes=places + [pltpu.VMEM(s, t) for s, t in scratch.values()] + [dma((k,)) for k in counts.values()],
        compiler_params=pltpu.CompilerParams(
            collective_id=cid, has_side_effects=True, vmem_limit_bytes=VMEM_LIMIT
        ),
        cost_estimate=pl.CostEstimate(flops=flops, bytes_accessed=20 * 2**20, transcendentals=0),
        name=name,
    )(*ins.values())
    return dict(zip(outs, got))


FAR = ("ga", "gb", "ha", "hb", "qa", "qb", "input_grad", "wa")
FA_ROWS = tuple((4 * g + d) * UNIT for g, d in zip(GATE_PER, DOWN_PER))
RQ = Q_ROWS // 2 // 16
SIDES = (SIDE, SIDE)
WIDE = HEADS * HEAD_DIM


def bf(*shape):
    return (shape, BF16)


def f4(*shape):
    return (shape, F32)


def rest_scratch():
    made = {}
    for h, rows in zip("ab", FA_ROWS):
        made["l2" + h] = bf(SIDE - 1, rows, LANES)
        made["t2" + h] = bf(rows, LANES)
        made["g1" + h] = bf(SIDE, rows, LANES)
    return made


def rest_outs():
    return {"g" + h: bf(2, *SIDES, rows, LANES) for h, rows in zip("ab", FA_ROWS)}


def assemble_kernel(nz, *refs):
    given, results, held, outs, sem, osem = (refs[:2], refs[2:4]), refs[6:14], refs[14:16] + refs[4:6], refs[16:24], refs[24], refs[25]
    s = lax.axis_index("section")

    def loads(layer, half):
        return [
            pltpu.make_async_copy(a.at[half], b.at[half], sem.at[2 * half + i])
            for i, (a, b) in enumerate(zip(given[layer], held))
        ]

    copies = [pltpu.make_async_copy(a, b, osem.at[i]) for i, (a, b) in enumerate(zip(outs, results))]
    for layer in range(2):
        @pl.when(s == layer)
        def _():
            for half in range(2):
                for c in loads(layer, half):
                    c.start()

    gate_ref, up_ref, down_ref, qkv_ref, out_ref = outs[:5]
    share = D // nz
    starts = window_starts(nz)

    def units(refs, section, base, per, first, count):
        rows = []
        for part, piece, slot, _, m in unit_runs(first, count, per):
            at = base[part] + slot * UNIT
            rows.append(refs[part][section, piece // SIDE, piece % SIDE, at : at + m * UNIT, :].astype(F32))
        return jnp.concatenate(rows, 0) if len(rows) > 1 else rows[0]

    for section, ref in ((0, gate_ref), (1, up_ref)):
        for c in loads(0, section):
            c.wait()
        tiles = {}
        for w, a in enumerate(starts):
            for t in range(WIN // LANES):
                tiles.setdefault(a // LANES + t, []).append((w, t))
        for col, sources in tiles.items():
            total = None
            for w, t in sources:
                base = [w * per * UNIT for per in GATE_PER]
                got = units(held[:2], section, base, GATE_PER, t * (share // UNIT), share // UNIT)
                total = got if total is None else total + got
            ref[:, col * LANES : (col + 1) * LANES] = total
        copies[section].start()
    base = [nz * per * UNIT for per in GATE_PER]
    half = FF // nz // 2
    for section in range(2):
        for t in range(TILES):
            got = units(held[:2], section, base, DOWN_PER, t * (half // UNIT), half // UNIT)
            down_ref[section * half : (section + 1) * half, t * LANES : (t + 1) * LANES] = got
    copies[2].start()
    for t in range(QKV // LANES + TILES):
        got = units(held[2:], t // 8, (0, 0), Q_PER, (t % 8) * (share // UNIT), share // UNIT)
        if t < QKV // LANES:
            qkv_ref[:, t * LANES : (t + 1) * LANES] = got
        else:
            u = t - QKV // LANES
            out_ref[:, u * LANES : (u + 1) * LANES] = got
    small = units(held[2:], 0, (0, 0), Q_PER, 8 * (share // UNIT), 2)
    z = lax.axis_index("fsdp")
    row = 0
    for ref, size in zip(outs[5:], (D, D, QKV)):
        tiles = size // LANES
        line = jnp.concatenate([small[row + t : row + t + 1, :] for t in range(tiles)], 1)
        part = size // nz
        ref[...] = pltpu.roll(jnp.broadcast_to(line, (8, size)), lax.rem(size - z * part, size), 1)[:1, :part]
        row += tiles
    for c in copies[3:]:
        c.start()
    for c in copies:
        c.wait()


def assemble(zero, one, attn):
    nz = lax.axis_size("fsdp")
    vm = pl.BlockSpec(memory_space=pltpu.VMEM)
    anywhere = pl.BlockSpec(memory_space=pl.ANY)
    share = D // nz
    shapes = [(share, FF), (share, FF), (FF // nz, D), (share, QKV), (share, D), (1, share), (1, share), (1, QKV // nz)]
    return pl.pallas_call(
        functools.partial(assemble_kernel, nz),
        out_shape=[jax.ShapeDtypeStruct(a, F32) for a in shapes],
        in_specs=[anywhere] * 4 + [vm] * 2,
        out_specs=[anywhere] * len(shapes),
        scratch_shapes=[pltpu.VMEM(a.shape, a.dtype) for a in zero]
        + [pltpu.VMEM(a, F32) for a in shapes]
        + [pltpu.SemaphoreType.DMA((4,)), pltpu.SemaphoreType.DMA((len(shapes),))],
        compiler_params=pltpu.CompilerParams(vmem_limit_bytes=VMEM_LIMIT),
        name="assemble",
    )(*zero, *one, *attn)


def window_starts(n):
    share = FF // n
    return [(i * share // LANES) * LANES for i in range(n)]


def forward(tokens, cotangent, shards, gains, pair_of):
    n, nz = lax.axis_size("ctx"), lax.axis_size("fsdp")
    tok = tokens.shape[2]
    freq = np.arange(HEAD_DIM // 2, dtype=np.float64)
    inverse = jnp.asarray(np.tile(THETA ** (-2.0 * freq / HEAD_DIM), 4)[None, :].astype(np.float32))
    ins = dict(gains, pair=pair_of, inverse=inverse, x0=tokens, gy=cotangent)
    hbm = {k + "_shard": v for k, v in shards.items()}
    ins.update(hbm)
    outs = dict(
        small=f4(2, 1, SMALL), pairs=((n, 8, 2 * LANES), jnp.int32), cos=f4(tok, LANES), sa=f4(tok, LANES), sb=f4(tok, LANES),
        x1=f4(tok, D), gy_all=bf(nz * tok, D), layer_out=f4(2, tok, D),
    )
    scratch = dict(m_s=f4(2, WIDE), l_s=f4(2, WIDE), acc_s=f4(2 * LANES, WIDE), att_s=bf(tok, D), parts=f4(2, nz, 1, SMALL))
    for l in "01":
        each = dict(
            mid=f4(tok, D), n1t=bf(D, tok), qst=bf(2 * LANES, WIDE), kv=bf(n, tok, 2 * LANES), lse=f4(2, WIDE),
            attt=bf(D, tok), gu=bf(2, D, WIN), down=bf(WIN, D), wa=bf(D, QKV + D),
            all=bf(nz, tok, D), gate=bf(nz, tok, WIN), up=bf(nz, tok, WIN),
        )
        outs.update({k + l: v for k, v in each.items()})
        scratch.update({"y" + l: f4(tok, D), "send_s" + l: bf(nz, tok, D), "land_s" + l: bf(nz, tok, D)})
    return call(forward_kernel, 0, 1, "forward", ins, outs, scratch, 200, tuple(hbm) + ("layer_out",), picked=("x0", "gy"), whole=tuple(gains), scalars=("pair",))


def backward(layer, gy, f, before):
    n, nz = lax.axis_size("ctx"), lax.axis_size("fsdp")
    tok = gy.shape[-2]
    share = D // nz
    own = {k: f[k + str(layer)] for k in ("down", "gate", "up", "gu", "all", "mid", "attt", "n1t", "qst", "lse", "kv", "wa")}
    ins = dict(gy=gy)
    outs = {}
    factors = dict(n1z=bf(share, nz * tok), dout=bf(TILES * share, LANES))
    scratch = dict(
        hid_s=bf(nz * tok, WIN), g_s=bf(2, nz * tok, WIN), gm_s=f4(tok, D),
        own_s=f4(tok, D), send_s=bf(nz, tok, D), land_s=bf(nz, tok, D),
        delta_s=f4(2, WIDE), gq_s=f4(2 * LANES, WIDE), all_gm=bf(nz * tok, D), attz=bf(share, nz * tok),
        send_k=bf(n, tok, 2 * LANES), land_k=bf(n, tok, 2 * LANES),
    )
    for h, rows in zip("ab", FA_ROWS):
        scratch["f" + h] = bf(2, *SIDES, rows, LANES)
        scratch["sl" + h] = bf(*SIDES, rows, LANES)
        scratch["l1" + h] = bf(SIDE - 1, SIDE, rows, LANES)
    if layer == 0:
        scratch["gx"] = f4(tok, D)
        outs["input_grad"] = f4(2, tok, D)
        scratch["all_s"] = bf(nz * tok, D)
        ins.update(p1a=before["t1a"], p1b=before["t1b"])
        scratch.update(rest_scratch())
        outs.update(rest_outs())
    else:
        ins["all_s"] = f["gy_all"]
        outs["gx"] = f4(tok, D)
    ins.update(down=own["down"], gate=own["gate"], up=own["up"], gu=own["gu"], n2_all=own["all"], mid=own["mid"])
    ins["small"] = f["small"]
    ins.update({k: own[k] for k in ("attt", "n1t")})
    if layer == 0:
        ins.update(glin1=before["glin"], gsmall1=before["gsmall"], n1z1=before["n1z"], dout1=before["dout"])
        scratch.update(factors)
        scratch.update(all_glin=bf(nz * tok, QKV), all_small=f4(nz * 2 * UNIT, LANES), qv=bf(2, Q_ROWS, LANES), ql=bf(Q_ROWS, LANES))
        scratch.update(zglin=bf(nz * tok, QKV), zsmall=f4(nz * 2 * UNIT, LANES), zv=bf(2, Q_ROWS, LANES), zl=bf(Q_ROWS, LANES))
        scratch.update(t1a=bf(SIDE, FA_ROWS[0], LANES), t1b=bf(SIDE, FA_ROWS[1], LANES))
        for g, h, rows in zip("ab", "cd", FA_ROWS):
            scratch["l2" + h] = bf(SIDE - 1, rows, LANES)
            scratch["t2" + h] = bf(rows, LANES)
            scratch["g1" + h] = bf(SIDE, rows, LANES)
            outs["h" + g] = bf(2, *SIDES, rows, LANES)
            outs["q" + g] = bf(2, *SIDES, RQ, LANES)
            for tag in ("", "0"):
                scratch["qp" + tag + g] = bf(*SIDES, RQ, LANES)
                scratch["qm" + tag + g] = bf(SIDE - 1, SIDE, RQ, LANES)
                scratch["qw" + tag + g] = bf(SIDE - 1, RQ, LANES)
                scratch["qe" + tag + g] = bf(SIDE, RQ, LANES)
                scratch["qh" + tag + g] = bf(SIDE, RQ, LANES)
    else:
        outs.update(factors)
        outs.update(glin=bf(tok, QKV), gsmall=f4(2 * UNIT, LANES), t1a=bf(SIDE, FA_ROWS[0], LANES), t1b=bf(SIDE, FA_ROWS[1], LANES))
    ins.update({k: own[k] for k in ("qst", "lse", "kv", "wa")})
    ins.update({k: f[k] for k in ("pairs", "cos", "sa", "sb")})
    ins["x"] = f["x" + str(layer)] if layer else before["x0"]
    return call(backward_kernel, layer, 2 + layer, f"backward_{layer}", ins, outs, scratch, 256, FAR, 3 * 10**10, ("x",) if layer == 0 else ("gy",))


def local(
    tokens, cotangent, pair_of, attn_gain, ffn_gain, qkv_weight, qkv_bias, out_weight, gate_weight, up_weight, down_weight,
):
    shards = dict(qkv=qkv_weight, out=out_weight, gate=gate_weight, up=up_weight, down=down_weight)

    gains = dict(attn_gain=attn_gain, ffn_gain=ffn_gain, qkv_bias=qkv_bias)
    f = forward(tokens, cotangent, shards, gains, pair_of)
    c1 = backward(1, cotangent, f, None)
    c0 = backward(0, c1["gx"], f, dict(c1, x0=tokens))
    dgate, dup, ddown, dqkv, dout, dg1, dg2, dbias = assemble((c0["ha"], c0["hb"]), (c0["ga"], c0["gb"]), (c0["qa"], c0["qb"]))
    return (
        f["layer_out"][None, :, None],
        c0["input_grad"][None, :, None],
        dg1,
        dg2,
        dqkv[None],
        dbias,
        dout[None],
        dgate[None],
        dup[None],
        ddown[None],
    )


def solution(mesh):
    return jax.shard_map(
        local,
        mesh=mesh,
        in_specs=(
            P(None, "fsdp", "ctx", None),
            P(None, "fsdp", "ctx", None),
            P("ctx"),
            P("section", "fsdp"),
            P("section", "fsdp"),
            P("section", "fsdp", None),
            P("section", "fsdp"),
            P("section", "fsdp", None),
            P("section", "fsdp", None),
            P("section", "fsdp", None),
            P("section", "fsdp", None),
        ),
        out_specs=(
            P("section", None, "fsdp", "ctx", None),
            P("section", None, "fsdp", "ctx", None),
            P("section", "fsdp"),
            P("section", "fsdp"),
            P("section", "fsdp", None),
            P("section", "fsdp"),
            P("section", "fsdp", None),
            P("section", "fsdp", None),
            P("section", "fsdp", None),
            P("section", "fsdp", None),
        ),
        check_vma=False,
    )
```
